32 devices in a mesh: dp: 4 (over z), mp: 8 (over y, x, core).
Axes of the slice: x: 2, y: 2, z: 4, core: 2. Of those that a mesh axis runs over, the one named last changes fastest.
Arguments:
- tokens: int32 [8, 1024], P('dp'), may hold values from 0 to 49151
- targets: int32 [8, 256], P('dp'), may hold values from 0 to 49151
- pair_order: int32 [8], replicated, may hold values from 0 to 7, each once
- lengths: int32 [8], P('dp'), may hold values from 1 to 256
- loss_mask: int32 [8, 256], P('dp'), may hold values 0 or 1
- start_pos: int32 [8], P('dp'), may hold values from 0 to 4095
- owner_map: int32 [8, 512], P('mp'), may hold values from 0 to 511, as said below
- block_master: float32 [8, 512, 128, 128], P('mp', 'dp')
- left_stat: float32 [8, 512, 128, 128], P('mp', 'dp')
- right_stat: float32 [8, 512, 128, 128], P('mp', 'dp')
- left_root: float32 [8, 512, 128, 128], P('mp', 'dp')
- right_root: float32 [8, 512, 128, 128], P('mp', 'dp')
- table_master: float32 [49152, 2048], P('mp', 'dp')
- table_moment: float32 [49152, 2048], P('mp', 'dp')
- table_second: float32 [49152, 2048], P('mp', 'dp')
- gain_master: float32 [3, 2048], P(None, 'dp')
- gain_moment: float32 [3, 2048], P(None, 'dp')
- gain_second: float32 [3, 2048], P(None, 'dp')
Outputs:
- loss_total: float32 [], replicated
- clip_norm: float32 [], replicated
- block_new: float32 [8, 512, 128, 128], P('mp', 'dp')
- block_copy: bfloat16 [8, 512, 128, 128], P('mp', 'dp')
- block_grad: float32 [8, 512, 128, 128], P('mp', 'dp')
- left_new: float32 [8, 512, 128, 128], P('mp', 'dp')
- right_new: float32 [8, 512, 128, 128], P('mp', 'dp')
- table_new: float32 [49152, 2048], P('mp', 'dp')
- table_copy: bfloat16 [49152, 2048], P('mp', 'dp')
- table_moment_new: float32 [49152, 2048], P('mp', 'dp')
- table_second_new: float32 [49152, 2048], P('mp', 'dp')
- gain_new: float32 [3, 2048], P(None, 'dp')
- gain_moment_new: float32 [3, 2048], P(None, 'dp')
- gain_second_new: float32 [3, 2048], P(None, 'dp')
The draws below stay inside these ranges and needn't reach their ends.
Inputs may be any that keep to these rules, and one draw needn't show every extreme that they name: Items whose pair_order values share the quotient by 2 form a pair. `owner_map`: each row is a permutation of 0 to 511.
All inputs are finite; a program needn't handle non-finite values. No bound on the sum of `loss_mask` on one device may be relied on, other than what follows from the above.
Results may differ from the reference program's by a relative error of at most 0.012.
The reference program's roundings to bfloat16 on the way count: a program that leaves them out, or rounds other values in their place, can miss the bound.
Values may be sent and summed in bfloat16 or wider, within the bound.
A program may use at most 512 MiB of HBM per device.

```python
import math
import jax
import jax.numpy as jnp
import numpy as np
from jax import lax

D = 2048
HEADS = 32
HD = 64
FF = 8192
V = 49152
LEN = 1024
ANS = 256
MB = 2
SEQ_MB = 1
B = 128
STEP = 5
ITEMS = 8
GROUPS = 4
N_DP = 4
N_MP = 8


CLIP_NORM = 0.01


STAT_DECAY = 0.95


ADAM_ONE = 0.9


ADAM_TWO = 0.95


def grad_entry():
    return CLIP_NORM / math.sqrt(4 * D * D + 3 * D * FF + V * D + 3 * D)


def owner_table(key):
    number = D * (4 * D + 3 * FF) // (N_MP * B * B)
    keys = jax.random.split(jax.random.fold_in(key, 77), N_MP)
    return jax.vmap(lambda single: jax.random.permutation(single, number))(keys).astype(jnp.int32)


def stat_tile(noise, key, lower, upper, offdiag, overall):
    eye = jnp.eye(B, dtype=jnp.float32)
    diag = jnp.exp(jax.random.uniform(key, noise.shape[:-1], jnp.float32, math.log(lower), math.log(upper)))
    sym = (noise + jnp.swapaxes(noise, -1, -2)) * (offdiag / math.sqrt(2.0 * B))
    return overall * (diag[..., None] * eye + sym * (1.0 - eye))


def stat_scale():
    return (1.0 - STAT_DECAY) / STAT_DECAY * B * grad_entry() ** 2


def tile_shape():
    return (N_MP, D * (4 * D + 3 * FF) // (N_MP * B * B), B, B)


def draw_owner_map(key, part):
    shared = owner_table(key)
    return shared


def draw_block_master(key, part):
    owners = owner_table(key)
    key = jax.random.fold_in(key, 2)
    width = D // N_MP
    units = FF // N_MP
    n_qkv = D * 3 * width // (B * B)
    n_out = width * D // (B * B)
    n_gate = D * 2 * units // (B * B)
    scale = jnp.where(owners < n_qkv, D ** (-0.5), jnp.where(owners < n_qkv + n_out, math.sqrt(LEN / 8.0) * D ** (-0.5), jnp.where(owners < n_qkv + n_out + n_gate, D ** (-0.5), FF ** (-0.5))))
    shape = (N_MP, owners.shape[1], B, B)
    noise = jax.random.normal(key, shape, jnp.float32)
    return noise * scale[:, :, None, None].astype(jnp.float32)


def draw_left_stat(key, part):
    key = jax.random.fold_in(key, 3)
    first, second = jax.random.split(key)
    noise = jax.random.normal(first, tile_shape(), jnp.float32)
    return stat_tile(noise, second, 1.0, 4.0, 0.3, stat_scale())


def draw_right_stat(key, part):
    key = jax.random.fold_in(key, 4)
    first, second = jax.random.split(key)
    noise = jax.random.normal(first, tile_shape(), jnp.float32)
    return stat_tile(noise, second, 1.0, 4.0, 0.3, stat_scale())


def draw_left_root(key, part):
    key = jax.random.fold_in(key, 5)
    first, second = jax.random.split(key)
    noise = jax.random.normal(first, tile_shape(), jnp.float32)
    return stat_tile(noise, second, 0.5, 2.0, 0.5, stat_scale() ** (-0.25))


def draw_right_root(key, part):
    key = jax.random.fold_in(key, 6)
    first, second = jax.random.split(key)
    noise = jax.random.normal(first, tile_shape(), jnp.float32)
    return stat_tile(noise, second, 0.5, 2.0, 0.5, stat_scale() ** (-0.25))


def draw_table_master(key, part):
    key = jax.random.fold_in(key, 7)
    rows = jnp.arange(V, dtype=jnp.float32)[:, None] / V
    noise = jax.random.normal(key, (V, D), jnp.float32)
    return noise * (1.0 + 2.0 * rows) * D ** (-0.5)


def draw_table_moment(key, part):
    key = jax.random.fold_in(key, 8)
    noise = jax.random.normal(key, (V, D), jnp.float32)
    return noise * ((1.0 - ADAM_ONE) / ADAM_ONE * grad_entry())


def draw_table_second(key, part):
    key = jax.random.fold_in(key, 10)
    factor = jnp.exp(jax.random.uniform(key, (V, D), jnp.float32, 0.0, math.log(4.0)))
    return factor * ((1.0 - ADAM_TWO) / ADAM_TWO * grad_entry() ** 2)


def draw_gain_master(key, part):
    key = jax.random.fold_in(key, 11)
    ramp = 0.6 + 0.8 * jnp.arange(D, dtype=jnp.float32)[None, :] / D
    noise = jax.random.normal(key, (3, D), jnp.float32)
    return ramp * (1.0 + 0.1 * noise)


def draw_gain_moment(key, part):
    key = jax.random.fold_in(key, 12)
    noise = jax.random.normal(key, (3, D), jnp.float32)
    return noise * ((1.0 - ADAM_ONE) / ADAM_ONE * 3.0 * grad_entry())


def draw_gain_second(key, part):
    key = jax.random.fold_in(key, 13)
    factor = jnp.exp(jax.random.uniform(key, (3, D), jnp.float32, 0.0, math.log(4.0)))
    return factor * ((1.0 - ADAM_TWO) / ADAM_TWO * 9.0 * grad_entry() ** 2)


def draw_lengths(key, part):
    key = jax.random.fold_in(key, 9)
    index = jnp.arange(ITEMS)
    rank = index // (MB * SEQ_MB)
    upper = jnp.maximum(ANS * (rank + 2) // (N_DP + 1), 1)
    drawn = jax.random.randint(key, (ITEMS,), 1, upper + 1)
    return drawn.at[ITEMS - 1].set(ANS).astype(jnp.int32)


def set_ends(entries, own_key, least, high):
    spot = [jax.random.randint(jax.random.fold_in(own_key, axis), (), 0, length) for axis, length in enumerate(entries.shape)]
    main_axis = entries.shape.index(max(entries.shape))
    neighbour = spot[:main_axis] + [(spot[main_axis] + 1) % entries.shape[main_axis]] + spot[main_axis + 1:]
    return entries.at[tuple(spot)].set(least).at[tuple(neighbour)].set(high)


def cumulative_ranks(count, skew):
    weights = [(1 << 20) // math.isqrt(grade ** skew) + 1 for grade in range(1, count + 1)]
    deviation = 1 + sum(weights) // (1 << 30)
    return np.cumsum(np.array([max(1, weight // deviation) for weight in weights]))


def skewed_ids(stream_key, extent, number_of, lean):
    listing = cumulative_ranks(number_of, lean)
    pick = jax.random.randint(jax.random.fold_in(stream_key, 1), extent, 0, int(listing[number_of - 1]))
    rank = jnp.searchsorted(jnp.asarray(listing, jnp.int32), pick, side="right")
    return jax.random.permutation(jax.random.fold_in(stream_key, 2), number_of)[rank].astype(jnp.int32)


def setup_inputs(seed: int = 0) -> dict:
    streams_of = jax.random.split(jax.random.key(seed), 19)
    return {
        "tokens": set_ends(skewed_ids(streams_of[0], (ITEMS, LEN), V, 2), jax.random.fold_in(streams_of[0], 3), 0, V - 1).astype(jnp.int32),
        "targets": set_ends(skewed_ids(streams_of[1], (ITEMS, ANS), V, 2), jax.random.fold_in(streams_of[1], 3), 0, V - 1).astype(jnp.int32),
        "pair_order": jax.random.permutation(streams_of[2], ITEMS).astype(jnp.int32),
        "lengths": draw_lengths(jax.random.fold_in(streams_of[18], 71), 0),
        "loss_mask": set_ends((jax.random.randint(streams_of[4], (ITEMS, ANS), 0, 4) < 3).astype(jnp.int32), jax.random.fold_in(streams_of[4], 1), 0, 1),
        "start_pos": set_ends(jax.random.randint(streams_of[5], (ITEMS,), 0, 4096), jax.random.fold_in(streams_of[5], 1), 0, 4095).astype(jnp.int32),
        "owner_map": draw_owner_map(jax.random.fold_in(streams_of[18], 71), 0),
        "block_master": draw_block_master(jax.random.fold_in(streams_of[18], 71), 0),
        "left_stat": draw_left_stat(jax.random.fold_in(streams_of[18], 71), 0),
        "right_stat": draw_right_stat(jax.random.fold_in(streams_of[18], 71), 0),
        "left_root": draw_left_root(jax.random.fold_in(streams_of[18], 71), 0),
        "right_root": draw_right_root(jax.random.fold_in(streams_of[18], 71), 0),
        "table_master": draw_table_master(jax.random.fold_in(streams_of[18], 71), 0),
        "table_moment": draw_table_moment(jax.random.fold_in(streams_of[18], 71), 0),
        "table_second": draw_table_second(jax.random.fold_in(streams_of[18], 71), 0),
        "gain_master": draw_gain_master(jax.random.fold_in(streams_of[18], 71), 0),
        "gain_moment": draw_gain_moment(jax.random.fold_in(streams_of[18], 71), 0),
        "gain_second": draw_gain_second(jax.random.fold_in(streams_of[18], 71), 0),
    }


EPS_NORM = 1e-05
ROPE_BASE = 130000.0
CLIP_NORM = 0.01
STAT_DECAY = 0.95
LR_MATRIX = 0.05
DECAY_MATRIX = 0.1
LR_TABLE = 0.03
DECAY_TABLE = 0.1
LR_GAIN = 0.2
ADAM_ONE = 0.9
ADAM_TWO = 0.95
ADAM_EPS = 1e-08
MASKED = -1e+30
HIGHEST = lax.Precision.HIGHEST

@jax.custom_vjp
def low(v):
    return lax.optimization_barrier(v.astype(jnp.bfloat16)).astype(jnp.float32)

@jax.custom_vjp
def low_back(v):
    return v

def low_keep(v):
    return (low(v), None)

def low_pass(kept, grad):
    return (grad,)

def back_keep(v):
    return (v, None)

def back_low(kept, grad):
    return (low(grad),)
low.defvjp(low_keep, low_pass)
low_back.defvjp(back_keep, back_low)

def from_blocks(blocks, rows, cols):
    size = blocks.shape[-1]
    return blocks.reshape(rows // size, cols // size, size, size).transpose(0, 2, 1, 3).reshape(rows, cols)

def to_blocks(matrix, size):
    rows, cols = matrix.shape
    return matrix.reshape(rows // size, size, cols // size, size).transpose(0, 2, 1, 3).reshape(-1, size, size)

def shard_mats(blocks, width, hidden):
    shapes = ((D, 3 * width), (width, D), (D, 2 * hidden), (hidden, D))
    size = blocks.shape[-1]
    result = []
    start = 0
    for rows, cols in shapes:
        number = rows * cols // (size * size)
        result.append(from_blocks(blocks[start:start + number], rows, cols))
        start += number
    return tuple(result)

def rms_norm(x, gain):
    return x * lax.rsqrt(lax.optimization_barrier(jnp.mean(x * x, axis=-1, keepdims=True)) + EPS_NORM) * gain

def rotate(x, cosine, sine):
    half = x.shape[-1] // 2
    first = x[..., :half]
    second = x[..., half:]
    return jnp.concatenate([first * cosine - second * sine, second * cosine + first * sine], axis=-1)

def adam(master, moment, second, grad, rate, decay):
    moment_new = ADAM_ONE * moment + (1.0 - ADAM_ONE) * grad
    second_new = ADAM_TWO * second + (1.0 - ADAM_TWO) * grad * grad
    corrected = moment_new / (1.0 - ADAM_ONE ** STEP) / (jnp.sqrt(second_new / (1.0 - ADAM_TWO ** STEP)) + ADAM_EPS)
    return (master - rate * (corrected + decay * master), moment_new, second_new)

def reference(tokens, targets, pair_order, lengths, loss_mask, start_pos, owner_map, block_master, left_stat, right_stat, left_root, right_root, table_master, table_moment, table_second, gain_master, gain_moment, gain_second):
    width = D // N_MP
    units = FF // N_MP
    heads_dev = HEADS // N_MP
    number = owner_map.shape[1]
    inverse = jax.vmap(lambda perm: jnp.zeros_like(perm).at[perm].set(jnp.arange(number, dtype=jnp.int32)))(owner_map)
    ordered = jnp.take_along_axis(block_master, inverse[:, :, None, None], axis=1)
    copies = ordered.astype(jnp.bfloat16).astype(jnp.float32)
    wqkv, wout, wgate, wdown = jax.vmap(lambda blocks: shard_mats(blocks, width, units))(copies)
    table = table_master.astype(jnp.bfloat16).astype(jnp.float32)
    gains = gain_master.astype(jnp.bfloat16).astype(jnp.float32)
    pairs = pair_order // 2
    column = jnp.arange(ANS)[None, :]
    weights = jnp.where(column == 0, 1.0, jnp.where(column < lengths[:, None], loss_mask.astype(jnp.float32), 0.0)).astype(jnp.float32)
    counts = jax.ops.segment_sum(lax.optimization_barrier(jnp.sum(weights, axis=1)), pairs, num_segments=GROUPS)
    row_scale = weights / (counts[pairs][:, None] * GROUPS)
    half = HD // 2
    freq = ROPE_BASE ** (-jnp.arange(half).astype(jnp.float32) * 2.0 / HD)
    causal = jnp.arange(LEN)[:, None] >= jnp.arange(LEN)[None, :]

    def total_loss(wqkv, wout, wgate, wdown, table, gains):

        def item(inputs):
            tok, tgt, scale_row, start = inputs
            angle = (start + jnp.arange(LEN)).astype(jnp.float32)[:, None] * freq[None, :]
            cosine = jnp.cos(angle)[:, None, :]
            sine = jnp.sin(angle)[:, None, :]
            x0 = jnp.take(table, tok, axis=0)
            h1 = low(rms_norm(x0, gains[0]))
            qkv = low_back(jnp.einsum('td,mde->tme', h1, wqkv, precision=HIGHEST)).reshape(LEN, N_MP, 3, heads_dev, HD)
            query = low(rotate(qkv[:, :, 0].reshape(LEN, HEADS, HD), cosine, sine))
            key = low(rotate(qkv[:, :, 1].reshape(LEN, HEADS, HD), cosine, sine))
            value = low(qkv[:, :, 2].reshape(LEN, HEADS, HD))
            scores = low_back(HD ** (-0.5) * jnp.einsum('qhe,khe->hqk', query, key, precision=HIGHEST))
            probs = low(jax.nn.softmax(jnp.where(causal[None], scores, MASKED), axis=-1))
            attended = low(low_back(jnp.einsum('hqk,khe->qhe', probs, value, precision=HIGHEST)))
            attn = low_back(jnp.einsum('tmw,mwd->td', attended.reshape(LEN, N_MP, width), wout, precision=HIGHEST))
            x1 = x0 + attn
            h2 = low(rms_norm(x1, gains[1]))
            gate_up = low_back(jnp.einsum('td,mdf->tmf', h2, wgate, precision=HIGHEST))
            hidden = low(jax.nn.silu(gate_up[..., :units]) * gate_up[..., units:])
            x2 = x1 + low_back(jnp.einsum('tmf,mfd->td', hidden, wdown, precision=HIGHEST))
            final = low(rms_norm(x2[LEN - ANS:], gains[2]))
            logits = low_back(jnp.dot(final, table.T, precision=HIGHEST))
            lse = jax.nn.logsumexp(logits, axis=-1)
            picked = jnp.take_along_axis(logits, tgt[:, None], axis=1)[:, 0]
            return jnp.sum(scale_row * (lse - picked))
        per_item = lax.map(jax.checkpoint(item), (tokens, targets, row_scale, start_pos))
        return jnp.sum(per_item)
    loss, pullback = jax.vjp(total_loss, wqkv, wout, wgate, wdown, table, gains)
    grad_qkv, grad_out, grad_gate, grad_down, grad_table, grad_gains = pullback(jnp.ones((), loss.dtype))
    canon = jax.vmap(lambda a, b, c, d: jnp.concatenate([to_blocks(a, B), to_blocks(b, B), to_blocks(c, B), to_blocks(d, B)], axis=0))(grad_qkv, grad_out, grad_gate, grad_down)
    slots = jnp.take_along_axis(canon, owner_map[:, :, None, None], axis=1)
    norm = jnp.sqrt(jnp.sum(slots * slots) + jnp.sum(grad_table * grad_table) + jnp.sum(grad_gains * grad_gains))
    factor = CLIP_NORM / jnp.maximum(norm, CLIP_NORM)
    grad_slots = factor * slots
    left_new = STAT_DECAY * left_stat + (1.0 - STAT_DECAY) * jnp.einsum('mnij,mnkj->mnik', grad_slots, grad_slots, precision=HIGHEST)
    right_new = STAT_DECAY * right_stat + (1.0 - STAT_DECAY) * jnp.einsum('mnji,mnjk->mnik', grad_slots, grad_slots, precision=HIGHEST)
    direction = jnp.einsum('mnij,mnjk->mnik', jnp.einsum('mnij,mnjk->mnik', left_root, grad_slots, precision=HIGHEST), right_root, precision=HIGHEST)
    block_new = block_master - LR_MATRIX * (direction + DECAY_MATRIX * block_master)
    table_new, table_moment_new, table_second_new = adam(table_master, table_moment, table_second, factor * grad_table, LR_TABLE, DECAY_TABLE)
    gain_new, gain_moment_new, gain_second_new = adam(gain_master, gain_moment, gain_second, factor * grad_gains, LR_GAIN, 0.0)
    return (loss * GROUPS, norm, block_new, block_new.astype(jnp.bfloat16), grad_slots, left_new, right_new, table_new, table_new.astype(jnp.bfloat16), table_moment_new, table_second_new, gain_new, gain_moment_new, gain_second_new)
```

```python
import jax
import jax.numpy as jnp
from jax import lax
from jax.sharding import PartitionSpec as P

D = 2048
HD = 64
FF = 8192
ANS = 256
STEP = 5


EPS_NORM = 1e-05
ROPE_BASE = 130000.0
CLIP_NORM = 0.01
STAT_DECAY = 0.95
LR_MATRIX = 0.05
DECAY_MATRIX = 0.1
LR_TABLE = 0.03
DECAY_TABLE = 0.1
LR_GAIN = 0.2
ADAM_ONE = 0.9
ADAM_TWO = 0.95
ADAM_EPS = 1e-08
MASKED = -1e30
HIGHEST = lax.Precision.HIGHEST
F32 = jnp.float32
BF16 = jnp.bfloat16


def dot(spec, a, b):
    return jnp.einsum(spec, a, b, preferred_element_type=F32)


def cube_bits(n):
    bits = [1 << i for i in range(n.bit_length() - 1)]
    return bits[1:] + bits[:1]


def cube_order(n):
    order = [0]
    for bit in cube_bits(n):
        order = order + [o ^ bit for o in order]
    return order


def swap(x, axis, bit):
    n = lax.axis_size(axis)
    return lax.ppermute(x, axis, [(i, i ^ bit) for i in range(n)])


def cube_gather(x):
    n = lax.axis_size("mp")
    if n != 8:
        held = x[None]
        for bit in cube_bits(n):
            held = jnp.concatenate([held, swap(held, "mp", bit)])
        return held
    half = x.shape[0] // 2
    over_x = swap(x, "mp", 2)
    over_y = swap(x, "mp", 4)
    far = jnp.concatenate([swap(over_x[:half], "mp", 4), swap(over_y[half:], "mp", 2)])
    held = jnp.stack([x, over_x, over_y, far])
    return jnp.concatenate([held, swap(held, "mp", 1)])


def cube_scatter(parts):
    n = lax.axis_size("mp")
    if n != 8:
        held = parts
        for bit in reversed(cube_bits(n)):
            keep = held.shape[0] // 2
            other = swap(held[keep:].astype(BF16), "mp", bit)
            held = held[:keep].astype(F32) + other.astype(F32)
        return held[0]
    got = swap(parts[4:], "mp", 1)
    held = (parts[:4].astype(F32) + got.astype(F32)).astype(BF16)
    half = held.shape[1] // 2
    one, two = held[:, :half], held[:, half:]
    one_x = swap(one[1::2], "mp", 2)
    two_y = swap(two[2:], "mp", 4)
    one = one[0::2].astype(F32) + one_x.astype(F32)
    two = two[:2].astype(F32) + two_y.astype(F32)
    one_y = swap(one[1].astype(BF16), "mp", 4)
    two_x = swap(two[1].astype(BF16), "mp", 2)
    return jnp.concatenate([one[0] + one_y.astype(F32), two[0] + two_x.astype(F32)])


def shift(x, by):
    n = lax.axis_size("dp")
    return lax.ppermute(x, "dp", [(i, (i + by) % n) for i in range(n)])


def line_gather(x):
    n = lax.axis_size("dp")
    return [x] + [shift(x, n - o) for o in range(1, n)]


def line_exchange(parts):
    n = lax.axis_size("dp")
    return [parts[0]] + [shift(parts[n - o], n - o) for o in range(1, n)]


def combine_stats(a, b):
    top = jnp.maximum(a[0], b[0])
    total = a[1] * jnp.exp(a[0] - top) + b[1] * jnp.exp(b[0] - top)
    return jnp.stack([top, total, a[2] + b[2]])


def everywhere(x, op):
    for axis in ("mp", "dp"):
        bit = 1
        while bit < lax.axis_size(axis):
            x = op(x, swap(x, axis, bit))
            bit *= 2
    return x


def stats_everywhere(x, rows):
    n_mp, n_dp = lax.axis_size("mp"), lax.axis_size("dp")
    bits = cube_bits(n_mp)
    split = (3,) + (2,) * len(bits) + (n_dp * rows,)
    x = x.reshape(split)
    for i, bit in enumerate(bits):
        x = combine_stats(x, jnp.flip(swap(x, "mp", bit), len(bits) - i))
    x = x.reshape(3, n_mp, n_dp, rows)
    total = x
    for o, other in enumerate(line_gather(x)):
        if o:
            total = combine_stats(total, jnp.roll(other, o, axis=2))
    return total.reshape(3, -1)


def from_blocks(blocks, rows, cols):
    size = blocks.shape[-1]
    return (
        blocks.reshape(rows // size, cols // size, size, size)
        .transpose(0, 2, 1, 3)
        .reshape(rows, cols)
    )


def to_blocks(matrix, size):
    rows, cols = matrix.shape
    return (
        matrix.reshape(rows // size, size, cols // size, size)
        .transpose(0, 2, 1, 3)
        .reshape(-1, size, size)
    )


def shard_mats(blocks, width, hidden):
    shapes = ((D, 3 * width), (width, D), (D, 2 * hidden), (hidden, D))
    size = blocks.shape[-1]
    result = []
    start = 0
    for rows, cols in shapes:
        number = rows * cols // (size * size)
        result.append(from_blocks(blocks[start : start + number], rows, cols))
        start += number
    return tuple(result)


def norm_forward(x):
    inverse = lax.rsqrt(jnp.mean(x * x, axis=-1, keepdims=True) + EPS_NORM)
    return (x * inverse, inverse)


def norm_backward(grad, normed, inverse, gain):
    scaled = grad * gain
    dgain = jnp.sum(grad * normed, axis=0)
    dx = inverse * (scaled - normed * jnp.mean(scaled * normed, axis=-1, keepdims=True))
    return (dx, dgain)


def rotate(x, cosine, sine):
    half = x.shape[-1] // 2
    first = x[..., :half]
    second = x[..., half:]
    return jnp.concatenate(
        [first * cosine - second * sine, second * cosine + first * sine], axis=-1
    )


def adam(master, moment, second, grad, rate, decay):
    moment_new = ADAM_ONE * moment + (1.0 - ADAM_ONE) * grad
    second_new = ADAM_TWO * second + (1.0 - ADAM_TWO) * grad * grad
    corrected = (
        moment_new
        / (1.0 - ADAM_ONE**STEP)
        / (jnp.sqrt(second_new / (1.0 - ADAM_TWO**STEP)) + ADAM_EPS)
    )
    return (master - rate * (corrected + decay * master), moment_new, second_new)


def body(
    tokens,
    targets,
    pair_order,
    lengths,
    loss_mask,
    start_pos,
    owner_map,
    block_master,
    left_stat,
    right_stat,
    left_root,
    right_root,
    table_master,
    table_moment,
    table_second,
    gain_master,
    gain_moment,
    gain_second,
):
    dp = lax.axis_index("dp")
    mp = lax.axis_index("mp")
    n_mp = lax.axis_size("mp")
    n_dp = lax.axis_size("dp")
    items, length = tokens.shape
    context = length - ANS
    n_ans = ANS // n_mp
    n_ctx = context // n_mp
    rows_ans = items * n_ans
    rows_own = items * (n_ans + n_ctx)
    width = D // n_mp
    units = FF // n_mp
    heads = width // HD
    vocab_part, cols = table_master.shape
    sub = vocab_part // n_dp
    perm = owner_map[0]
    number = perm.shape[0]
    who = mp ^ jnp.array(cube_order(n_mp), jnp.int32)
    near = lax.rem(dp + jnp.arange(n_dp, dtype=jnp.int32), n_dp)

    slots = lax.all_gather(block_master[0].astype(BF16), "dp", axis=0, tiled=True)
    gains = line_gather(gain_master.astype(BF16))
    wide = jnp.zeros((3, D), BF16)
    for o in range(n_dp):
        wide = lax.dynamic_update_slice(wide, gains[o], (0, near[o] * cols))
    gains = wide.astype(F32)
    table_low = table_master.astype(BF16)

    packed = jnp.concatenate([tokens, targets, loss_mask, lengths[:, None]], axis=1)
    packed = jnp.stack(line_gather(packed))
    all_tokens = packed[:, :, :length]
    all_targets = packed[:, :, length : length + ANS]
    all_mask = packed[:, :, length + ANS : length + 2 * ANS]
    all_lengths = packed[:, :, -1]
    column = jnp.arange(ANS)
    weights = jnp.where(
        column == 0,
        1.0,
        jnp.where(column < all_lengths[..., None], all_mask.astype(F32), 0.0),
    )
    pairs_all = pair_order.shape[0] // 2
    pairs = (pair_order // 2).reshape(n_dp, items)[near]
    member = (pairs[..., None] == jnp.arange(pairs_all)).astype(F32)
    counts = jnp.einsum("oip,oi->p", member, jnp.sum(weights, axis=-1))
    scale = weights / (jnp.sum(member * counts, axis=-1)[..., None] * pairs_all)

    def by_owner(x):
        split = x.reshape(n_dp, items, n_mp, n_ans)[:, :, who]
        return split.transpose(2, 0, 1, 3)

    row_scale = by_owner(scale).reshape(-1)
    row_target = by_owner(all_targets).reshape(-1)
    tok_ans = all_tokens[:, :, context:].reshape(n_dp, items, n_mp, n_ans)[:, :, who]
    tok_ctx = all_tokens[:, :, :context].reshape(n_dp, items, n_mp, n_ctx)[:, :, who]
    tok = jnp.concatenate(
        [
            tok_ans.transpose(2, 0, 1, 3).reshape(n_mp, n_dp, -1),
            tok_ctx.transpose(2, 0, 1, 3).reshape(n_mp, n_dp, -1),
        ],
        axis=2,
    )

    local = tok - mp * vocab_part
    valid = (local >= 0) & (local < vocab_part)
    safe = jnp.clip(local, 0, vocab_part - 1)
    looked = jnp.where(valid[..., None], jnp.take(table_low, safe, axis=0), 0)
    own_cols = cube_scatter(looked).astype(BF16)
    pieces = line_exchange([own_cols[o] for o in range(n_dp)])
    x0 = jnp.zeros((rows_own, D), BF16)
    for o in range(n_dp):
        x0 = lax.dynamic_update_slice(x0, pieces[o], (0, near[o] * cols))
    x0 = x0.astype(F32)
    normed1, inverse1 = norm_forward(x0)
    h1 = cube_gather((normed1 * gains[0]).astype(BF16))
    h1_ans = h1[:, :rows_ans].reshape(-1, D)
    h1_all = h1.reshape(-1, D)

    inverse = jnp.zeros_like(perm).at[perm].set(jnp.arange(number, dtype=jnp.int32))
    wqkv, wout, wgate, wdown = shard_mats(jnp.take(slots, inverse, axis=0), width, units)
    wq, wkv = wqkv[:, :width], wqkv[:, width:]

    late, table_late = lax.optimization_barrier((slots[0, 0, 0], table_low))
    parts = [
        lax.dynamic_slice_in_dim(table_late, near[o] * sub, sub) for o in range(n_dp)
    ]
    pieces = line_exchange(parts)
    head = jnp.zeros((sub, D), BF16)
    for o in range(n_dp):
        head = lax.dynamic_update_slice(head, pieces[o], (0, near[o] * cols))

    half = HD // 2
    freq = ROPE_BASE ** (-jnp.arange(half).astype(F32) * 2.0 / HD)
    t_ans = context + who[:, None] * n_ans + jnp.arange(n_ans)
    t_ctx = who[:, None] * n_ctx + jnp.arange(n_ctx)

    def angles(t):
        place = (start_pos[None, :, None] + t[:, None, :]).astype(F32)
        angle = place.reshape(n_mp, -1)[..., None] * freq
        return jnp.cos(angle), jnp.sin(angle)

    cos_a, sin_a = angles(t_ans)
    cos_c, sin_c = angles(t_ctx)
    cos_all = jnp.concatenate([cos_a, cos_c], axis=1)[:, :, None]
    sin_all = jnp.concatenate([sin_a, sin_c], axis=1)[:, :, None]
    cos_a, sin_a = cos_a[:, :, None], sin_a[:, :, None]

    def ans_heads(x):
        x = x.reshape(n_mp, items, n_ans, heads, HD).transpose(1, 3, 0, 2, 4)
        return x.reshape(items, heads, ANS, HD)

    def ctx_heads(x):
        x = x.reshape(n_mp, items, n_ctx, heads, HD).transpose(1, 3, 0, 2, 4)
        return x.reshape(items, heads, context, HD)

    def ans_rows(x):
        x = x.reshape(items, heads, n_mp, n_ans, HD).transpose(2, 0, 3, 1, 4)
        return x.reshape(n_mp, rows_ans, heads, HD)

    def ctx_rows(x):
        x = x.reshape(items, heads, n_mp, n_ctx, HD).transpose(2, 0, 3, 1, 4)
        return x.reshape(n_mp, items * n_ctx, heads, HD)

    def key_heads(x):
        return jnp.concatenate([ctx_heads(x[:, rows_ans:]), ans_heads(x[:, :rows_ans])], axis=2)

    def key_rows(x):
        return jnp.concatenate([ans_rows(x[:, :, context:]), ctx_rows(x[:, :, :context])], axis=1)

    q = dot("td,de->te", h1_ans, wq).reshape(n_mp, rows_ans, heads, HD)
    kv = dot("td,de->te", h1_all, wkv).reshape(n_mp, rows_own, 2, heads, HD)
    query = ans_heads(rotate(q, cos_a, sin_a).astype(BF16))
    key = key_heads(rotate(kv[:, :, 0], cos_all, sin_all).astype(BF16))
    value = key_heads(kv[:, :, 1].astype(BF16))
    t_query = t_ans.reshape(-1)
    t_key = jnp.concatenate([jnp.full((context,), -1, jnp.int32), t_query])
    causal = t_query[:, None] >= t_key[None, :]
    scores = HD ** (-0.5) * dot("nhqe,nhke->nhqk", query, key)
    scores = jnp.where(causal, scores, MASKED)
    top = jnp.max(scores, axis=-1, keepdims=True)
    expo = jnp.exp(scores - top)
    exact = expo / jnp.sum(expo, axis=-1, keepdims=True)
    probs = exact.astype(BF16)
    attended = dot("nhqk,nhke->nhqe", probs, value).astype(BF16)
    o_rows = ans_rows(attended).reshape(-1, width)
    x1 = x0[:rows_ans] + cube_scatter(
        dot("tw,wd->td", o_rows, wout).astype(BF16).reshape(n_mp, rows_ans, D)
    )

    normed2, inverse2 = norm_forward(x1)
    h2 = cube_gather((normed2 * gains[1]).astype(BF16)).reshape(-1, D)
    gate_up = dot("td,df->tf", h2, wgate)
    gate, upward = gate_up[:, :units], gate_up[:, units:]
    hidden = (jax.nn.silu(gate) * upward).astype(BF16)
    x2 = x1 + cube_scatter(
        dot("tf,fd->td", hidden, wdown).astype(BF16).reshape(n_mp, rows_ans, D)
    )
    normed3, inverse3 = norm_forward(x2)
    final_own = (normed3 * gains[2]).astype(BF16)

    final = cube_gather(jnp.stack(line_gather(final_own)).reshape(-1, D))
    final = final.reshape(-1, D)
    logits = dot("rd,vd->rv", final, head)
    first = mp * vocab_part + dp * sub
    hit = jnp.arange(sub, dtype=jnp.int32)[None, :] == (row_target - first)[:, None]
    top = jnp.max(logits, axis=1)
    total = jnp.sum(jnp.exp(logits - top[:, None]), axis=1)
    picked = jnp.sum(jnp.where(hit, logits, 0.0), axis=1)
    top, total, picked = stats_everywhere(jnp.stack([top, total, picked]), rows_ans)
    lse = top + jnp.log(total)
    loss_total = jnp.sum(row_scale * (lse - picked)) * pairs_all
    dlogits = (
        row_scale[:, None] * (jnp.exp(logits - lse[:, None]) - hit.astype(F32))
    ).astype(BF16)
    danswer = dot("rv,vd->rd", dlogits, head).astype(BF16)
    mine = cube_scatter(danswer.reshape(n_mp, n_dp * rows_ans, D)).astype(BF16)
    mine = line_exchange(list(mine.reshape(n_dp, rows_ans, D)))
    dfinal = sum(piece.astype(F32) for piece in mine)
    head_grad = dot("rv,rd->vd", dlogits, final).astype(BF16)
    pieces = line_exchange(
        [lax.dynamic_slice_in_dim(head_grad, near[o] * cols, cols, 1) for o in range(n_dp)]
    )
    table_grad = jnp.zeros((vocab_part, cols), BF16)
    for o in range(n_dp):
        table_grad = lax.dynamic_update_slice(table_grad, pieces[o], (near[o] * sub, 0))

    dx2, dgain3 = norm_backward(dfinal, normed3, inverse3, gains[2])
    down_in = cube_gather(dx2.astype(BF16)).reshape(-1, D)
    dhidden = dot("td,fd->tf", down_in, wdown)
    sigma = jax.nn.sigmoid(gate)
    dgate_up = jnp.concatenate(
        [dhidden * upward * sigma * (1.0 + gate * (1.0 - sigma)), dhidden * gate * sigma],
        axis=-1,
    ).astype(BF16)
    dnormed2 = cube_scatter(
        dot("tf,df->td", dgate_up, wgate).astype(BF16).reshape(n_mp, rows_ans, D)
    )
    grad_down = dot("tf,td->fd", hidden, down_in).astype(BF16)
    grad_gate = dot("td,tf->df", h2, dgate_up).astype(BF16)
    dx_mlp, dgain2 = norm_backward(dnormed2, normed2, inverse2, gains[1])
    dx1 = dx2 + dx_mlp
    out_in = cube_gather(dx1.astype(BF16)).reshape(-1, D)
    dattended = dot("td,wd->tw", out_in, wout).astype(BF16)
    dattended = ans_heads(dattended.reshape(n_mp, rows_ans, heads, HD))
    grad_out = dot("tw,td->wd", o_rows, out_in).astype(BF16)
    dvalue = dot("nhqk,nhqe->nhke", probs, dattended)
    dprobs = dot("nhqe,nhke->nhqk", dattended, value)
    dscores = (exact * (dprobs - jnp.sum(exact * dprobs, axis=-1, keepdims=True))).astype(BF16)
    dquery = HD ** (-0.5) * dot("nhqk,nhke->nhqe", dscores, key)
    dkey = HD ** (-0.5) * dot("nhqk,nhqe->nhke", dscores, query)
    dq = rotate(ans_rows(dquery), cos_a, -sin_a).astype(BF16).reshape(-1, width)
    dk = rotate(key_rows(dkey), cos_all, -sin_all).astype(BF16)
    dkv = jnp.stack([dk, key_rows(dvalue).astype(BF16)], axis=2).reshape(-1, 2 * width)
    dh1 = dot("te,de->td", dkv, wkv).reshape(n_mp, rows_own, D)
    dh1_ans = dh1[:, :rows_ans] + dot("te,de->td", dq, wq).reshape(n_mp, rows_ans, D)
    dh1 = jnp.concatenate([dh1_ans, dh1[:, rows_ans:]], axis=1).astype(BF16)
    dnormed1 = cube_scatter(dh1)
    grad_qkv = jnp.concatenate(
        [dot("td,te->de", h1_ans, dq), dot("td,te->de", h1_all, dkv)], axis=1
    ).astype(BF16)
    dx0, dgain1 = norm_backward(dnormed1, normed1, inverse1, gains[0])
    dx0 = jnp.concatenate([dx0[:rows_ans] + dx1, dx0[rows_ans:]]).astype(BF16)

    size = block_master.shape[-1]
    all_blocks = jnp.concatenate(
        [to_blocks(grad, size) for grad in (grad_qkv, grad_out, grad_gate, grad_down)]
    )
    own_slots = lax.psum_scatter(
        jnp.take(all_blocks, perm, axis=0), "dp", scatter_dimension=0, tiled=True
    ).astype(F32)

    pieces = line_exchange(
        [lax.dynamic_slice_in_dim(dx0, near[o] * cols, cols, 1) for o in range(n_dp)]
    )
    rows_back = cube_gather(jnp.stack(pieces).reshape(-1, cols)).reshape(safe.shape + (cols,))
    picked_rows = jnp.where(valid[..., None], rows_back, 0).astype(F32)
    own_table = table_grad.astype(F32).at[safe.reshape(-1)].add(picked_rows.reshape(-1, cols))

    gain_grad = jnp.stack([dgain1, dgain2, dgain3])
    gain_total = everywhere(gain_grad, jnp.add)
    own_gain = lax.dynamic_slice_in_dim(gain_total, dp * cols, cols, 1)
    first_mp = (mp == 0).astype(F32)
    squares = (
        jnp.sum(own_slots * own_slots)
        + jnp.sum(own_table * own_table)
        + first_mp * jnp.sum(own_gain * own_gain)
    )
    squares_all = everywhere(squares.reshape(1, 1), jnp.add)[0, 0]
    norm = jnp.sqrt(squares_all)
    factor = CLIP_NORM / jnp.maximum(norm, CLIP_NORM)
    grad_slots = factor * own_slots
    left_new = STAT_DECAY * left_stat[0] + (1.0 - STAT_DECAY) * jnp.einsum(
        "nij,nkj->nik", grad_slots, grad_slots, precision=HIGHEST
    )
    right_new = STAT_DECAY * right_stat[0] + (1.0 - STAT_DECAY) * jnp.einsum(
        "nji,njk->nik", grad_slots, grad_slots, precision=HIGHEST
    )
    direction = jnp.einsum(
        "nij,njk->nik",
        jnp.einsum("nij,njk->nik", left_root[0], grad_slots, precision=HIGHEST),
        right_root[0],
        precision=HIGHEST,
    )
    block_new = block_master[0] - LR_MATRIX * (direction + DECAY_MATRIX * block_master[0])
    table_new, table_moment_new, table_second_new = adam(
        table_master, table_moment, table_second, factor * own_table, LR_TABLE, DECAY_TABLE
    )
    gain_new, gain_moment_new, gain_second_new = adam(
        gain_master, gain_moment, gain_second, factor * own_gain, LR_GAIN, 0.0
    )
    return (
        loss_total,
        norm,
        block_new[None],
        block_new.astype(BF16)[None],
        grad_slots[None],
        left_new[None],
        right_new[None],
        table_new,
        table_new.astype(BF16),
        table_moment_new,
        table_second_new,
        gain_new,
        gain_moment_new,
        gain_second_new,
    )


def solution(mesh):
    in_specs = (
        P("dp", None),
        P("dp", None),
        P(),
        P("dp"),
        P("dp", None),
        P("dp"),
        P("mp", None),
        P("mp", "dp", None, None),
        P("mp", "dp", None, None),
        P("mp", "dp", None, None),
        P("mp", "dp", None, None),
        P("mp", "dp", None, None),
        P("mp", "dp"),
        P("mp", "dp"),
        P("mp", "dp"),
        P(None, "dp"),
        P(None, "dp"),
        P(None, "dp"),
    )
    out_specs = (
        P(),
        P(),
        P("mp", "dp", None, None),
        P("mp", "dp", None, None),
        P("mp", "dp", None, None),
        P("mp", "dp", None, None),
        P("mp", "dp", None, None),
        P("mp", "dp"),
        P("mp", "dp"),
        P("mp", "dp"),
        P("mp", "dp"),
        P(None, "dp"),
        P(None, "dp"),
        P(None, "dp"),
    )
    return jax.shard_map(body, mesh=mesh, in_specs=in_specs, out_specs=out_specs, check_vma=False)
```

```python
import functools

import jax
import jax.numpy as jnp
from jax import lax
from jax.experimental import pallas as pl
from jax.experimental.pallas import tpu as pltpu
from jax.sharding import PartitionSpec as P

D = 2048
HD = 64
FF = 8192
ANS = 256
STEP = 5


EPS_NORM = 1e-05
ROPE_BASE = 130000.0
CLIP_NORM = 0.01
STAT_DECAY = 0.95
LR_MATRIX = 0.05
DECAY_MATRIX = 0.1
LR_TABLE = 0.03
DECAY_TABLE = 0.1
LR_GAIN = 0.2
ADAM_ONE = 0.9
ADAM_TWO = 0.95
ADAM_EPS = 1e-08
MASKED = -1e30
F32 = jnp.float32
BF16 = jnp.bfloat16


def dot(spec, a, b):
    return jnp.einsum(spec, a, b, preferred_element_type=F32)


def cube_bits(n):
    bits = [1 << i for i in range(n.bit_length() - 1)]
    return bits[1:] + bits[:1]


def cube_order(n):
    order = [0]
    for bit in cube_bits(n):
        order = order + [o ^ bit for o in order]
    return order


def swap(x, axis, bit):
    n = lax.axis_size(axis)
    return lax.ppermute(x, axis, [(i, i ^ bit) for i in range(n)])


def cube_gather(x):
    n = lax.axis_size("mp")
    if n != 8:
        held = x[None]
        for bit in cube_bits(n):
            held = jnp.concatenate([held, swap(held, "mp", bit)])
        return held
    half = x.shape[0] // 2
    over_x = swap(x, "mp", 2)
    over_y = swap(x, "mp", 4)
    far = jnp.concatenate([swap(over_x[:half], "mp", 4), swap(over_y[half:], "mp", 2)])
    held = jnp.stack([x, over_x, over_y, far])
    return jnp.concatenate([held, swap(held, "mp", 1)])


def cube_scatter(parts):
    n = lax.axis_size("mp")
    if n != 8:
        held = parts
        for bit in reversed(cube_bits(n)):
            keep = held.shape[0] // 2
            other = swap(held[keep:].astype(BF16), "mp", bit)
            held = held[:keep].astype(F32) + other.astype(F32)
        return held[0]
    got = swap(parts[4:], "mp", 1)
    held = (parts[:4].astype(F32) + got.astype(F32)).astype(BF16)
    half = held.shape[1] // 2
    one, two = held[:, :half], held[:, half:]
    one_x = swap(one[1::2], "mp", 2)
    two_y = swap(two[2:], "mp", 4)
    one = one[0::2].astype(F32) + one_x.astype(F32)
    two = two[:2].astype(F32) + two_y.astype(F32)
    one_y = swap(one[1].astype(BF16), "mp", 4)
    two_x = swap(two[1].astype(BF16), "mp", 2)
    return jnp.concatenate([one[0] + one_y.astype(F32), two[0] + two_x.astype(F32)])


def shift(x, by):
    n = lax.axis_size("dp")
    return lax.ppermute(x, "dp", [(i, (i + by) % n) for i in range(n)])


def line_gather(x):
    n = lax.axis_size("dp")
    return [x] + [shift(x, n - o) for o in range(1, n)]


def line_exchange(parts):
    n = lax.axis_size("dp")
    return [parts[0]] + [shift(parts[n - o], n - o) for o in range(1, n)]


def combine_stats(a, b):
    top = jnp.maximum(a[0], b[0])
    total = a[1] * jnp.exp(a[0] - top) + b[1] * jnp.exp(b[0] - top)
    return jnp.stack([top, total, a[2] + b[2]])


def everywhere(x, op):
    for axis in ("mp", "dp"):
        bit = 1
        while bit < lax.axis_size(axis):
            x = op(x, swap(x, axis, bit))
            bit *= 2
    return x


def stats_everywhere(x, rows):
    n_mp, n_dp = lax.axis_size("mp"), lax.axis_size("dp")
    bits = cube_bits(n_mp)
    split = (3,) + (2,) * len(bits) + (n_dp * rows,)
    x = x.reshape(split)
    for i, bit in enumerate(bits):
        x = combine_stats(x, jnp.flip(swap(x, "mp", bit), len(bits) - i))
    x = x.reshape(3, n_mp, n_dp, rows)
    total = x
    for o, other in enumerate(line_gather(x)):
        if o:
            total = combine_stats(total, jnp.roll(other, o, axis=2))
    return total.reshape(3, -1)


def peer_copy(src, dst, sems, k, **device):
    return pltpu.make_async_remote_copy(
        src_ref=src,
        dst_ref=dst,
        send_sem=sems.at[0, k],
        recv_sem=sems.at[1, k],
        device_id=device,
        device_id_type=pl.DeviceIdType.MESH,
    )


def greet(n_dp):
    me = lax.axis_index("mp")
    a = lax.axis_index("dp")
    barrier = pltpu.get_barrier_semaphore()
    partners = [{"mp": me ^ bit} for bit in (1, 2, 4)]
    partners += [{"dp": lax.rem(a + o, n_dp)} for o in range(1, n_dp)]
    for partner in partners:
        pl.semaphore_signal(barrier, 1, device_id=partner, device_id_type=pl.DeviceIdType.MESH)
    pl.semaphore_wait(barrier, len(partners))


def by_rows(count, step):
    @pl.loop(0, count // 16)
    def _(i):
        step(pl.ds(pl.multiple_of(i * 16, 16), 16), pl.multiple_of(i * 16, 16))


def sum_steps(parts, own, core, held, near, last, sems, first):
    me = lax.axis_index("mp")
    half = own.shape[0] // 2
    top, low = pl.ds(0, half), pl.ds(half, half)
    x, y = {"mp": me ^ 2}, {"mp": me ^ 4}
    order = (3, 1, 2, 0)
    at_core = {s: peer_copy(parts.at[4 + s], core.at[s], sems, first + s, mp=me ^ 1) for s in order}
    for s in order:
        at_core[s].start()
    far_x = peer_copy(held.at[3, top], near.at[0], sems, first + 4, **x)
    far_y = peer_copy(held.at[3, low], near.at[1], sems, first + 5, **y)
    one_x = peer_copy(held.at[1, top], near.at[2], sems, first + 6, **x)
    two_y = peer_copy(held.at[2, low], near.at[3], sems, first + 7, **y)
    mid_y = peer_copy(held.at[2, top], last.at[0], sems, first + 8, **y)
    mid_x = peer_copy(held.at[1, low], last.at[1], sems, first + 9, **x)
    for s, sent in ((3, (far_x, far_y)), (1, (one_x,)), (2, (two_y,))):
        at_core[s].wait_recv()

        def add(rows, _, s=s):
            held[s, rows] = (parts[s, rows].astype(F32) + core[s, rows].astype(F32)).astype(BF16)

        by_rows(2 * half, add)
        for copy in sent:
            copy.start()
    far_x.wait_recv()

    def add_x(rows, _):
        held[2, rows] = (held[2, rows].astype(F32) + near[0, rows].astype(F32)).astype(BF16)

    by_rows(half, add_x)
    mid_y.start()
    far_y.wait_recv()

    def add_y(rows, at):
        below = pl.ds(half + at, 16)
        held[1, below] = (held[1, below].astype(F32) + near[1, rows].astype(F32)).astype(BF16)

    by_rows(half, add_y)
    mid_x.start()
    for copy in (at_core[0], one_x, two_y, mid_y, mid_x):
        copy.wait_recv()

    def total(rows, at):
        below = pl.ds(half + at, 16)
        own[rows] = (
            (parts[0, rows].astype(F32) + core[0, rows].astype(F32))
            + near[2, rows].astype(F32)
            + last[0, rows].astype(F32)
        )
        own[below] = (
            (parts[0, below].astype(F32) + core[0, below].astype(F32))
            + near[3, rows].astype(F32)
            + last[1, rows].astype(F32)
        )

    by_rows(half, total)
    for copy in (*at_core.values(), far_x, far_y, one_x, two_y, mid_y, mid_x):
        copy.wait_send()


def spread_steps(x, out, sems, first):
    me = lax.axis_index("mp")
    half = x.shape[0] // 2
    top, low = pl.ds(0, half), pl.ds(half, half)
    over_x, over_y, core = {"mp": me ^ 2}, {"mp": me ^ 4}, {"mp": me ^ 1}

    def copy(src, slot, rows, k, to):
        return peer_copy(src, out.at[slot, rows], sems, first + k, **to)

    x_top = copy(x.at[top], 1, top, 0, over_x)
    y_low = copy(x.at[low], 2, low, 1, over_y)
    x_low = copy(x.at[low], 1, low, 2, over_x)
    y_top = copy(x.at[top], 2, top, 3, over_y)
    own = peer_copy(x, out.at[4], sems, first + 4, **core)
    for c in (x_top, y_low, x_low, y_top, own):
        c.start()

    def keep(rows, _):
        out[0, rows] = x[rows]

    by_rows(2 * half, keep)
    far_y = copy(out.at[1, top], 3, top, 5, over_y)
    far_x = copy(out.at[2, low], 3, low, 6, over_x)
    to_core = {
        (s, r): copy(out.at[s, rows], 4 + s, rows, 7 + 2 * (s - 1) + r, core)
        for s in (1, 2, 3)
        for r, rows in enumerate((top, low))
    }
    x_top.wait_recv()
    far_y.start()
    to_core[1, 0].start()
    y_low.wait_recv()
    far_x.start()
    to_core[2, 1].start()
    x_low.wait_recv()
    to_core[1, 1].start()
    y_top.wait_recv()
    to_core[2, 0].start()
    far_y.wait_recv()
    to_core[3, 0].start()
    far_x.wait_recv()
    to_core[3, 1].start()
    own.wait_recv()
    for c in to_core.values():
        c.wait_recv()
    for c in (x_top, y_low, x_low, y_top, own, far_y, far_x, *to_core.values()):
        c.wait_send()


def norm_step(x, gain):
    return (x * lax.rsqrt(jnp.mean(x * x, axis=1, keepdims=True) + EPS_NORM)) * gain


def norm_back_step(grad, x, gain):
    inverse = lax.rsqrt(jnp.mean(x * x, axis=1, keepdims=True) + EPS_NORM)
    normed = x * inverse
    scaled = grad * gain
    dx = inverse * (scaled - normed * jnp.mean(scaled * normed, axis=1, keepdims=True))
    return dx, jnp.sum(grad * normed, axis=0, keepdims=True)


def forward_kernel(n_dp, wide, parts, res, gain, x_out, out, own, core, held, near, last, *more):
    *more, sems = more
    greet(n_dp)
    sum_steps(parts, own, core, held, near, last, sems, 0)
    x = res[...] + own[...]
    x_out[...] = x
    low = norm_step(x, gain[...]).astype(BF16)
    (mine,) = more
    rows = x.shape[0]
    mine[pl.ds(0, rows)] = low
    if wide:
        a = lax.axis_index("dp")
        copies = [
            peer_copy(
                mine.at[pl.ds(0, rows)],
                mine.at[pl.ds((n_dp - o) * rows, rows)],
                sems,
                22 + o,
                dp=lax.rem(a + o, n_dp),
            )
            for o in range(1, n_dp)
        ]
        for copy in copies:
            copy.start()
        for copy in copies:
            copy.wait()
    spread_steps(mine, out, sems, 10)


def backward_kernel(n_dp, wide, parts, x_in, gain, *refs):
    if wide:
        dx_out, dgain, out, own, core, held, near, last, mine, sent, got, sems = refs
    else:
        res, dx_out, dgain, out, own, core, held, near, last, mine, sems = refs
    greet(n_dp)
    sum_steps(parts, own, core, held, near, last, sems, 0)
    rows = x_in.shape[0]
    if wide:
        a = lax.axis_index("dp")
        sent[...] = own[...].astype(BF16)
        copies = [
            peer_copy(
                sent.at[pl.ds(o * rows, rows)],
                got.at[o - 1],
                sems,
                22 + o,
                dp=lax.rem(a + o, n_dp),
            )
            for o in range(1, n_dp)
        ]
        for copy in copies:
            copy.start()
        for copy in copies:
            copy.wait()
        grad = own[pl.ds(0, rows)]
        for o in range(1, n_dp):
            grad = grad + got[o - 1].astype(F32)
    else:
        grad = own[...]
    dx, dg = norm_back_step(grad, x_in[...], gain[...])
    if not wide:
        dx = dx + res[...]
    dx_out[...] = dx
    dgain[...] = dg
    mine[...] = dx.astype(BF16)
    spread_steps(mine, out, sems, 10)


def exchange(kernel, name, number, n_dp, wide_in, wide_out, outs, *args):
    parts = args[0]
    total = parts.shape[1]
    half = total // 2
    scratch = [
        pltpu.VMEM((total, D), F32),
        pltpu.VMEM((4, total, D), BF16),
        pltpu.VMEM((4, total, D), BF16),
        pltpu.VMEM((4, half, D), BF16),
        pltpu.VMEM((2, half, D), BF16),
        pltpu.VMEM((outs[-1][0][1], D), BF16),
    ]
    if wide_in:
        rows = total // n_dp
        scratch += [pltpu.VMEM((total, D), BF16), pltpu.VMEM((n_dp - 1, rows, D), BF16)]
    return pl.pallas_call(
        functools.partial(kernel, n_dp, wide_in or wide_out),
        out_shape=[jax.ShapeDtypeStruct(shape, dtype) for shape, dtype in outs],
        in_specs=[pl.BlockSpec(memory_space=pltpu.VMEM)] * len(args),
        out_specs=[pl.BlockSpec(memory_space=pltpu.VMEM)] * len(outs),
        scratch_shapes=scratch + [pltpu.SemaphoreType.DMA((2, 23 + n_dp))],
        compiler_params=pltpu.CompilerParams(
            collective_id=number, has_side_effects=True, vmem_limit_bytes=56 << 20
        ),
        cost_estimate=pl.CostEstimate(flops=0, bytes_accessed=1 << 20, transcendentals=0),
        name=name,
    )(*args)


def greet_all(n_dp):
    me = lax.axis_index("mp")
    a = lax.axis_index("dp")
    barrier = pltpu.get_barrier_semaphore()
    partners = [{"mp": me ^ k} for k in range(1, 8)]
    partners += [{"dp": lax.rem(a + o, n_dp)} for o in range(1, n_dp)]
    for partner in partners:
        pl.semaphore_signal(barrier, 1, device_id=partner, device_id_type=pl.DeviceIdType.MESH)
    pl.semaphore_wait(barrier, len(partners))


def stats_kernel(n_dp, x_ref, out_ref, plane, mid, line, sems):
    me = lax.axis_index("mp")
    a = lax.axis_index("dp")
    order = cube_order(8)
    greet_all(n_dp)
    copies = [
        peer_copy(x_ref, plane.at[s - 1], sems, s - 1, mp=me ^ order[s]) for s in range(1, 8)
    ]
    for copy in copies:
        copy.start()

    def join(have, new):
        top = jnp.maximum(have[0], new[0])
        total = have[1] * jnp.exp(have[0] - top) + new[1] * jnp.exp(new[0] - top)
        return top, total, have[2] + new[2]

    have = tuple(x_ref[k] for k in range(3))
    for s in range(1, 8):
        copies[s - 1].wait_recv()
        rows = [order.index(order[t] ^ order[s]) for t in range(8)]
        got = [plane[s - 1, k] for k in range(3)]
        got = [jnp.concatenate([v[r : r + 1] for r in rows], axis=0) for v in got]
        have = join(have, got)
    for k in range(3):
        mid[k] = have[k]
    across = [
        peer_copy(mid, line.at[o - 1], sems, 6 + o, dp=lax.rem(a + o, n_dp)) for o in range(1, n_dp)
    ]
    for copy in across:
        copy.start()
    rows = x_ref.shape[2] // n_dp
    for o in range(1, n_dp):
        across[o - 1].wait_recv()
        got = [line[o - 1, k] for k in range(3)]
        got = [jnp.concatenate([v[:, o * rows :], v[:, : o * rows]], axis=1) for v in got]
        have = join(have, got)
    out_ref[0] = have[0] + jnp.log(have[1])
    out_ref[1] = have[2]
    for copy in copies + across:
        copy.wait_send()


def stats_exchange(x, n_dp):
    shape = x.shape
    return pl.pallas_call(
        functools.partial(stats_kernel, n_dp),
        out_shape=jax.ShapeDtypeStruct((2,) + shape[1:], F32),
        in_specs=[pl.BlockSpec(memory_space=pltpu.VMEM)],
        out_specs=pl.BlockSpec(memory_space=pltpu.VMEM),
        scratch_shapes=[
            pltpu.VMEM((7,) + shape, F32),
            pltpu.VMEM(shape, F32),
            pltpu.VMEM((n_dp - 1,) + shape, F32),
            pltpu.SemaphoreType.DMA((2, 6 + n_dp)),
        ],
        compiler_params=pltpu.CompilerParams(collective_id=5, has_side_effects=True),
        cost_estimate=pl.CostEstimate(flops=0, bytes_accessed=1 << 16, transcendentals=0),
        name="stats",
    )(x)


def total_kernel(n_dp, one_ref, two_ref, more_ref, out_ref, plane, line, sems):
    me = lax.axis_index("mp")
    a = lax.axis_index("dp")
    greet_all(n_dp)

    def squares(ref):
        def add(k, have):
            g = ref[k].astype(F32)
            return have + jnp.sum((g * g).reshape(-1, 8, 128), axis=0)

        return lax.fori_loop(0, ref.shape[0], add, jnp.zeros((8, 128), F32))

    plane[me, 0] = squares(one_ref) + squares(two_ref) + more_ref[0]
    plane[me, 1] = more_ref[1]
    copies = [peer_copy(plane.at[me], plane.at[me], sems, k - 1, mp=me ^ k) for k in range(1, 8)]
    for copy in copies:
        copy.start()
    for copy in copies:
        copy.wait()
    line[a] = jnp.sum(plane[...], axis=0)
    across = [
        peer_copy(line.at[a], line.at[a], sems, 6 + o, dp=lax.rem(a + o, n_dp))
        for o in range(1, n_dp)
    ]
    for copy in across:
        copy.start()
    for copy in across:
        copy.wait()
    out_ref[...] = jnp.sum(line[...], axis=0)


def total_exchange(one, two, more, n_dp):
    return pl.pallas_call(
        functools.partial(total_kernel, n_dp),
        out_shape=jax.ShapeDtypeStruct(more.shape, F32),
        in_specs=[pl.BlockSpec(memory_space=pltpu.VMEM)] * 3,
        out_specs=pl.BlockSpec(memory_space=pltpu.VMEM),
        scratch_shapes=[
            pltpu.VMEM((8,) + more.shape, F32),
            pltpu.VMEM((n_dp,) + more.shape, F32),
            pltpu.SemaphoreType.DMA((2, 6 + n_dp)),
        ],
        compiler_params=pltpu.CompilerParams(collective_id=6, has_side_effects=True),
        name="total",
    )(one, two, more)


def mat_shapes(n_mp):
    width, units = D // n_mp, FF // n_mp
    return ((D, 3 * width), (width, D), (D, 2 * units), (units, D))


def tile_views(shapes, refs, size):
    first = 0
    views = []
    for (rows, cols), ref in zip(shapes, refs):
        wide = cols // size

        def view(tile, ref=ref, wide=wide):
            row = pl.multiple_of(lax.div(tile, wide) * size, size)
            col = pl.multiple_of(lax.rem(tile, wide) * size, size)
            return ref.at[pl.ds(row, size), pl.ds(col, size)]

        number = (rows // size) * wide
        views.append((first, number, view))
        first += number
    return views


def place_kernel(shapes, map_ref, slots_ref, *refs):
    mats, sem = refs[:-1], refs[-1]
    number, size, _ = slots_ref.shape
    views = tile_views(shapes, mats, size)

    @pl.loop(0, number)
    def _(slot):
        tile = map_ref[slot]
        for first, count, view in views:

            @pl.when((tile >= first) & (tile < first + count))
            def _(first=first, view=view):
                pltpu.make_async_copy(slots_ref.at[slot], view(tile - first), sem).start()

    pltpu.make_async_copy(slots_ref, slots_ref, sem).wait()


def place_tiles(perm, slots, shapes):
    anywhere = pl.BlockSpec(memory_space=pl.ANY)
    return pl.pallas_call(
        functools.partial(place_kernel, shapes),
        out_shape=[jax.ShapeDtypeStruct(shape, slots.dtype) for shape in shapes],
        in_specs=[pl.BlockSpec(memory_space=pltpu.SMEM), anywhere],
        out_specs=[pl.BlockSpec(memory_space=pltpu.VMEM)] * len(shapes),
        scratch_shapes=[pltpu.SemaphoreType.DMA],
        compiler_params=pltpu.CompilerParams(vmem_limit_bytes=40 << 20),
        cost_estimate=pl.CostEstimate(flops=0, bytes_accessed=slots.size * 2, transcendentals=0),
        name="place_tiles",
    )(perm, slots)


def collect_kernel(shapes, chosen, n_dp, map_ref, *refs):
    mats = refs[: len(chosen)]
    one_ref, two_ref, sem = refs[-3:]
    size = one_ref.shape[-1]
    half = one_ref.shape[0] // n_dp
    full = [None] * len(shapes)
    for place, ref in zip(chosen, mats):
        full[place] = ref
    views = [v for k, v in enumerate(tile_views(shapes, full, size)) if k in chosen]

    for owner in range(n_dp):
        for part, out_ref in enumerate((one_ref, two_ref)):

            @pl.loop(0, half)
            def _(j, owner=owner, part=part, out_ref=out_ref):
                tile = map_ref[(2 * owner + part) * half + j]
                for first, count, view in views:

                    @pl.when((tile >= first) & (tile < first + count))
                    def _(first=first, view=view):
                        to = out_ref.at[owner * half + j]
                        pltpu.make_async_copy(view(tile - first), to, sem).start()

    for ref in mats:
        pltpu.make_async_copy(ref, ref, sem).wait()


def collect_tiles(perm, mats, shapes, chosen, n_dp, given=(), after=()):
    size = 128
    anywhere = pl.BlockSpec(memory_space=pl.ANY)
    out = jax.ShapeDtypeStruct((perm.shape[0] // 2, size, size), BF16)
    return pl.pallas_call(
        functools.partial(collect_kernel, shapes, chosen, n_dp),
        out_shape=[out, out],
        in_specs=[pl.BlockSpec(memory_space=pltpu.SMEM)]
        + [pl.BlockSpec(memory_space=pltpu.VMEM)] * len(mats)
        + [anywhere] * (len(given) + len(after)),
        out_specs=[anywhere, anywhere],
        scratch_shapes=[pltpu.SemaphoreType.DMA],
        compiler_params=pltpu.CompilerParams(vmem_limit_bytes=40 << 20),
        input_output_aliases={1 + len(mats) + k: k for k in range(len(given))},
        cost_estimate=pl.CostEstimate(flops=0, bytes_accessed=1 << 20, transcendentals=0),
        name="collect_tiles",
    )(perm, *mats, *given, *after)


def split(x):
    high = x.astype(BF16)
    return high, (x - high.astype(F32)).astype(BF16)


def tile_step_kernel(blocks, factor_ref, one_ref, two_ref, *refs):
    master, left, right, l_root, r_root, new, copy, grad, left_new, right_new = refs
    factor = factor_ref[0, 0]

    def step(g_ref):
        for k in range(g_ref.shape[0]):
            g = g_ref[k]
            grad[k] = factor * g.astype(F32)
            outer = (mm(g, g, CONTRACT_LAST) * factor) * factor
            inner = (mm(g, g, CONTRACT_FIRST) * factor) * factor
            left_new[k] = STAT_DECAY * left[k] + (1.0 - STAT_DECAY) * outer
            right_new[k] = STAT_DECAY * right[k] + (1.0 - STAT_DECAY) * inner
            l_high, l_low = split(l_root[k])
            r_high, r_low = split(r_root[k])
            t_high, t_low = split((mm(l_high, g) + mm(l_low, g)) * factor)
            direction = mm(t_high, r_high) + (mm(t_low, r_high) + mm(t_high, r_low))
            value = master[k] - LR_MATRIX * (direction + DECAY_MATRIX * master[k])
            new[k] = value
            copy[k] = value.astype(BF16)

    at = pl.program_id(0)
    pl.when(at < blocks)(lambda: step(one_ref))
    pl.when(at >= blocks)(lambda: step(two_ref))


def tile_step(factor, one, two, *state):
    number, size, _ = state[0].shape
    group = 8
    blocks = number // group // 2

    def block(index):
        return pl.BlockSpec((group, size, size), lambda i: (index(i), 0, 0))

    whole = block(lambda i: i)
    shape = (number, size, size)
    kinds = (F32, BF16, F32, F32, F32)
    return pl.pallas_call(
        functools.partial(tile_step_kernel, blocks),
        grid=(2 * blocks,),
        out_shape=[jax.ShapeDtypeStruct(shape, kind) for kind in kinds],
        in_specs=[
            pl.BlockSpec(memory_space=pltpu.SMEM),
            block(lambda i: jnp.minimum(i, blocks - 1)),
            block(lambda i: jnp.maximum(i - blocks, 0)),
        ]
        + [whole] * 5,
        out_specs=[whole] * 5,
        compiler_params=pltpu.CompilerParams(vmem_limit_bytes=40 << 20),
        name="tile_step",
    )(factor, one, two, *state)


CONTRACT_LAST = (((1,), (1,)), ((), ()))
CONTRACT_FIRST = (((0,), (0,)), ((), ()))


def mm(a, b, dims=(((1,), (0,)), ((), ()))):
    return lax.dot_general(a, b, dims, preferred_element_type=F32)


def turn(x, cosine, sine):
    lane = lax.broadcasted_iota(jnp.int32, x.shape, 1)
    other = jnp.where(
        lax.rem(lane, HD) < HD // 2, pltpu.roll(x, 128 - HD // 2, 1), pltpu.roll(x, HD // 2, 1)
    )
    return x * cosine + other * sine


def flat(x):
    return x.reshape(x.shape[0] * x.shape[1], x.shape[2])


def head_probs(q, k_ctx, k_ans, causal):
    s_ctx = mm(q, k_ctx, CONTRACT_LAST) * HD ** (-0.5)
    s_ans = jnp.where(causal, mm(q, k_ans, CONTRACT_LAST) * HD ** (-0.5), MASKED)
    top = jnp.maximum(
        jnp.max(s_ctx, axis=1, keepdims=True), jnp.max(s_ans, axis=1, keepdims=True)
    )
    e_ctx = jnp.exp(s_ctx - top)
    e_ans = jnp.exp(s_ans - top)
    total = jnp.sum(e_ctx, axis=1, keepdims=True) + jnp.sum(e_ans, axis=1, keepdims=True)
    return e_ctx / total, e_ans / total


def attend_kernel(items, qkv_ref, cos_ref, sin_ref, col_ref, row_ref, *outs):
    o_ref, qo_ref, ko_ref, vo_ref = outs
    n, rows_ans, width = o_ref.shape
    n_ans = rows_ans // items
    n_ctx = qkv_ref.shape[1] // items - n_ans
    causal = col_ref[...] >= row_ref[...]
    lane = lax.broadcasted_iota(jnp.int32, (1, 128), 1)

    for item in range(items):
        ans = pl.ds(item * n_ans, n_ans)
        ctx = pl.ds(rows_ans + item * n_ctx, n_ctx)
        turns = [(flat(cos_ref[:, r]), flat(sin_ref[:, r])) for r in (ans, ctx)]
        for g in range(width // 128):
            lanes = pl.ds(g * 128, 128)
            klanes = pl.ds(width + g * 128, 128)
            vlanes = pl.ds(2 * width + g * 128, 128)
            q = turn(flat(qkv_ref[:, ans, lanes]), *turns[0]).astype(BF16)
            k_ans = turn(flat(qkv_ref[:, ans, klanes]), *turns[0]).astype(BF16)
            k_ctx = turn(flat(qkv_ref[:, ctx, klanes]), *turns[1]).astype(BF16)
            v_ans = flat(qkv_ref[:, ans, vlanes]).astype(BF16)
            v_ctx = flat(qkv_ref[:, ctx, vlanes]).astype(BF16)
            qo_ref[:, ans, lanes] = q.reshape(n, n_ans, 128)
            ko_ref[:, ans, lanes] = k_ans.reshape(n, n_ans, 128)
            ko_ref[:, ctx, lanes] = k_ctx.reshape(n, n_ctx, 128)
            vo_ref[:, ans, lanes] = v_ans.reshape(n, n_ans, 128)
            vo_ref[:, ctx, lanes] = v_ctx.reshape(n, n_ctx, 128)
            got = []
            for first in (True, False):
                own = (lane < HD) == first
                p_ctx, p_ans = head_probs(jnp.where(own, q, 0), k_ctx, k_ans, causal)
                got.append(mm(p_ctx.astype(BF16), v_ctx) + mm(p_ans.astype(BF16), v_ans))
            o = jnp.where(lane < HD, got[0], got[1]).astype(BF16)
            o_ref[:, ans, lanes] = o.reshape(n, n_ans, 128)


def attend_back_kernel(items, *refs):
    q_ref, k_ref, v_ref, do_ref, cos_ref, sin_ref, col_ref, row_ref, d_ref = refs
    n, rows_ans, width = q_ref.shape
    n_ans = rows_ans // items
    n_ctx = k_ref.shape[1] // items - n_ans
    causal = col_ref[...] >= row_ref[...]
    lane = lax.broadcasted_iota(jnp.int32, (1, 128), 1)
    root = HD ** (-0.5)

    for item in range(items):
        ans = pl.ds(item * n_ans, n_ans)
        ctx = pl.ds(rows_ans + item * n_ctx, n_ctx)
        turns = [(flat(cos_ref[:, r]), -flat(sin_ref[:, r])) for r in (ans, ctx)]
        d_ref[:, ctx, pl.ds(0, width)] = jnp.zeros((n, n_ctx, width), BF16)
        for g in range(width // 128):
            lanes = pl.ds(g * 128, 128)
            klanes = pl.ds(width + g * 128, 128)
            vlanes = pl.ds(2 * width + g * 128, 128)
            q, do = flat(q_ref[:, ans, lanes]), flat(do_ref[:, ans, lanes])
            k_ans, k_ctx = flat(k_ref[:, ans, lanes]), flat(k_ref[:, ctx, lanes])
            v_ans, v_ctx = flat(v_ref[:, ans, lanes]), flat(v_ref[:, ctx, lanes])
            dq, sums = [], None
            for first in (True, False):
                own = (lane < HD) == first
                q_own, do_own = jnp.where(own, q, 0), jnp.where(own, do, 0)
                p_ctx, p_ans = head_probs(q_own, k_ctx, k_ans, causal)
                dp_ctx = mm(do_own, v_ctx, CONTRACT_LAST)
                dp_ans = mm(do_own, v_ans, CONTRACT_LAST)
                mean = jnp.sum(p_ctx * dp_ctx, axis=1, keepdims=True) + jnp.sum(
                    p_ans * dp_ans, axis=1, keepdims=True
                )
                ds_ctx = (p_ctx * (dp_ctx - mean)).astype(BF16)
                ds_ans = (p_ans * (dp_ans - mean)).astype(BF16)
                dq.append(mm(ds_ctx, k_ctx) + mm(ds_ans, k_ans))
                new = [
                    mm(ds_ctx, q_own, CONTRACT_FIRST),
                    mm(ds_ans, q_own, CONTRACT_FIRST),
                    mm(p_ctx.astype(BF16), do_own, CONTRACT_FIRST),
                    mm(p_ans.astype(BF16), do_own, CONTRACT_FIRST),
                ]
                sums = new if sums is None else [a + b for a, b in zip(sums, new)]
            dq = turn(jnp.where(lane < HD, dq[0], dq[1]) * root, *turns[0])
            dk_ctx = turn(sums[0] * root, *turns[1])
            dk_ans = turn(sums[1] * root, *turns[0])
            d_ref[:, ans, lanes] = dq.astype(BF16).reshape(n, n_ans, 128)
            d_ref[:, ans, klanes] = dk_ans.astype(BF16).reshape(n, n_ans, 128)
            d_ref[:, ctx, klanes] = dk_ctx.astype(BF16).reshape(n, n_ctx, 128)
            d_ref[:, ans, vlanes] = sums[3].astype(BF16).reshape(n, n_ans, 128)
            d_ref[:, ctx, vlanes] = sums[2].astype(BF16).reshape(n, n_ctx, 128)


def in_vmem(kernel, name, outs, *args):
    return pl.pallas_call(
        kernel,
        out_shape=[jax.ShapeDtypeStruct(shape, dtype) for shape, dtype in outs],
        in_specs=[pl.BlockSpec(memory_space=pltpu.VMEM)] * len(args),
        out_specs=[pl.BlockSpec(memory_space=pltpu.VMEM)] * len(outs),
        compiler_params=pltpu.CompilerParams(vmem_limit_bytes=48 << 20),
        cost_estimate=pl.CostEstimate(flops=0, bytes_accessed=1 << 20, transcendentals=0),
        name=name,
    )(*args)


def norm_forward(x):
    inverse = lax.rsqrt(jnp.mean(x * x, axis=-1, keepdims=True) + EPS_NORM)
    return (x * inverse, inverse)


def norm_backward(grad, normed, inverse, gain):
    scaled = grad * gain
    dgain = jnp.sum(grad * normed, axis=0)
    dx = inverse * (scaled - normed * jnp.mean(scaled * normed, axis=-1, keepdims=True))
    return (dx, dgain)


def adam(master, moment, second, grad, rate, decay):
    moment_new = ADAM_ONE * moment + (1.0 - ADAM_ONE) * grad
    second_new = ADAM_TWO * second + (1.0 - ADAM_TWO) * grad * grad
    corrected = (
        moment_new
        / (1.0 - ADAM_ONE**STEP)
        / (jnp.sqrt(second_new / (1.0 - ADAM_TWO**STEP)) + ADAM_EPS)
    )
    return (master - rate * (corrected + decay * master), moment_new, second_new)


def body(
    tokens,
    targets,
    pair_order,
    lengths,
    loss_mask,
    start_pos,
    owner_map,
    block_master,
    left_stat,
    right_stat,
    left_root,
    right_root,
    table_master,
    table_moment,
    table_second,
    gain_master,
    gain_moment,
    gain_second,
):
    dp = lax.axis_index("dp")
    mp = lax.axis_index("mp")
    n_mp = lax.axis_size("mp")
    n_dp = lax.axis_size("dp")
    items, length = tokens.shape
    context = length - ANS
    n_ans = ANS // n_mp
    n_ctx = context // n_mp
    rows_ans = items * n_ans
    rows_own = items * (n_ans + n_ctx)
    width = D // n_mp
    units = FF // n_mp
    heads = width // HD
    vocab_part, cols = table_master.shape
    sub = vocab_part // n_dp
    perm = owner_map[0]
    who = mp ^ jnp.array(cube_order(n_mp), jnp.int32)
    near = lax.rem(dp + jnp.arange(n_dp, dtype=jnp.int32), n_dp)

    slots = lax.all_gather(block_master[0].astype(BF16), "dp", axis=0, tiled=True)
    gains = line_gather(gain_master.astype(BF16))
    wide = jnp.zeros((3, D), BF16)
    for o in range(n_dp):
        wide = lax.dynamic_update_slice(wide, gains[o], (0, near[o] * cols))
    gains = wide.astype(F32)
    table_low = table_master.astype(BF16)

    packed = jnp.concatenate([tokens, targets, loss_mask, lengths[:, None]], axis=1)
    packed = jnp.stack(line_gather(packed))
    all_tokens = packed[:, :, :length]
    all_targets = packed[:, :, length : length + ANS]
    all_mask = packed[:, :, length + ANS : length + 2 * ANS]
    all_lengths = packed[:, :, -1]
    column = jnp.arange(ANS)
    weights = jnp.where(
        column == 0,
        1.0,
        jnp.where(column < all_lengths[..., None], all_mask.astype(F32), 0.0),
    )
    pairs_all = pair_order.shape[0] // 2
    pairs = (pair_order // 2).reshape(n_dp, items)[near]
    member = (pairs[..., None] == jnp.arange(pairs_all)).astype(F32)
    counts = jnp.einsum("oip,oi->p", member, jnp.sum(weights, axis=-1))
    scale = weights / (jnp.sum(member * counts, axis=-1)[..., None] * pairs_all)

    def by_owner(x):
        split = x.reshape(n_dp, items, n_mp, n_ans)[:, :, who]
        return split.transpose(2, 0, 1, 3)

    row_scale = by_owner(scale).reshape(-1)
    row_target = by_owner(all_targets).reshape(-1)
    tok_ans = all_tokens[:, :, context:].reshape(n_dp, items, n_mp, n_ans)[:, :, who]
    tok_ctx = all_tokens[:, :, :context].reshape(n_dp, items, n_mp, n_ctx)[:, :, who]
    tok = jnp.concatenate(
        [
            tok_ans.transpose(2, 0, 1, 3).reshape(n_mp, n_dp, -1),
            tok_ctx.transpose(2, 0, 1, 3).reshape(n_mp, n_dp, -1),
        ],
        axis=2,
    )

    local = tok - mp * vocab_part
    valid = (local >= 0) & (local < vocab_part)
    safe = jnp.clip(local, 0, vocab_part - 1)
    looked = jnp.where(valid[..., None], jnp.take(table_low, safe, axis=0), 0)
    own_cols = cube_scatter(looked).astype(BF16)
    pieces = line_exchange([own_cols[o] for o in range(n_dp)])
    x0 = jnp.zeros((rows_own, D), BF16)
    for o in range(n_dp):
        x0 = lax.dynamic_update_slice(x0, pieces[o], (0, near[o] * cols))
    x0 = x0.astype(F32)
    normed1, inverse1 = norm_forward(x0)
    h1 = cube_gather((normed1 * gains[0]).astype(BF16))
    h1_all = h1.reshape(-1, D)

    shapes = mat_shapes(n_mp)
    wqkv, wout, wgate, wdown = place_tiles(perm, slots, shapes)

    after = 0.0 * slots[0, 0, 0].astype(F32) + 0.0 * h1[-1, 0, 0].astype(F32)
    table_late = (table_master + after).astype(BF16)
    pieces = lax.all_to_all(table_late.reshape(n_dp, sub, cols), "dp", 0, 0)
    head = jnp.concatenate([pieces[a] for a in range(n_dp)], axis=1)

    half = HD // 2
    freq = ROPE_BASE ** (-jnp.arange(half).astype(F32) * 2.0 / HD)
    t_ans = context + who[:, None] * n_ans + jnp.arange(n_ans)
    t_ctx = who[:, None] * n_ctx + jnp.arange(n_ctx)

    def angles(t):
        place = (start_pos[None, :, None] + t[:, None, :]).astype(F32)
        angle = place.reshape(n_mp, -1)[..., None] * freq
        return jnp.cos(angle), jnp.sin(angle)

    cosine, sine = (jnp.concatenate(pair, axis=1) for pair in zip(angles(t_ans), angles(t_ctx)))
    cosine = jnp.concatenate([cosine] * 4, axis=-1)
    sine = jnp.concatenate([-sine, sine] * 2, axis=-1)
    t_query = t_ans.reshape(-1)
    place = (t_query[:, None], t_query[None, :])

    qkv = dot("td,de->te", h1_all, wqkv).reshape(n_mp, rows_own, 3 * width)
    ans_shape = ((n_mp, rows_ans, width), BF16)
    key_shape = ((n_mp, rows_own, width), BF16)
    o_rows, query, key, value = in_vmem(
        functools.partial(attend_kernel, items),
        "attend",
        (ans_shape, ans_shape, key_shape, key_shape),
        *(qkv, cosine, sine, *place),
    )
    o_rows = o_rows.reshape(-1, width)
    parts = dot("tw,wd->td", o_rows, wout).astype(BF16).reshape(n_mp, rows_ans, D)
    own = ((rows_ans, D), F32)
    gain_row = ((1, D), F32)
    plane = ((n_mp, rows_ans, D), BF16)
    if n_mp == 8:
        x1, h2 = exchange(
            forward_kernel, "attend_sum", 1, n_dp, False, False, (own, plane),
            *(parts, x0[:rows_ans], gains[1:2]),
        )
    else:
        x1 = x0[:rows_ans] + cube_scatter(parts)
        h2 = cube_gather((norm_forward(x1)[0] * gains[1]).astype(BF16))
    h2 = h2.reshape(-1, D)

    gate_up = dot("td,df->tf", h2, wgate)
    gate, upward = gate_up[:, :units], gate_up[:, units:]
    hidden = (jax.nn.silu(gate) * upward).astype(BF16)
    parts = dot("tf,fd->td", hidden, wdown).astype(BF16).reshape(n_mp, rows_ans, D)

    if n_mp == 8:
        x2, final = exchange(
            forward_kernel, "units_sum", 2, n_dp, False, True,
            (own, ((n_mp, n_dp * rows_ans, D), BF16)),
            *(parts, x1, gains[2:3]),
        )
    else:
        x2 = x1 + cube_scatter(parts)
        final = (norm_forward(x2)[0] * gains[2]).astype(BF16)
        final = cube_gather(jnp.stack(line_gather(final)).reshape(-1, D))
    final = final.reshape(-1, D)
    logits = dot("rd,vd->rv", final, head)
    first = mp * vocab_part + dp * sub
    hit = jnp.arange(sub, dtype=jnp.int32)[None, :] == (row_target - first)[:, None]
    top = jnp.max(logits, axis=1)
    total = jnp.sum(jnp.exp(logits - top[:, None]), axis=1)
    picked = jnp.sum(jnp.where(hit, logits, 0.0), axis=1)
    stats = jnp.stack([top, total, picked])
    if n_mp == 8:
        lse, picked = stats_exchange(stats.reshape(3, n_mp, n_dp * rows_ans), n_dp)
        lse, picked = lse.reshape(-1), picked.reshape(-1)
    else:
        top, total, picked = stats_everywhere(stats, rows_ans)
        lse = top + jnp.log(total)
    loss_own = jnp.sum((row_scale * (lse - picked))[:rows_ans]) * pairs_all
    dlogits = (
        row_scale[:, None] * (jnp.exp(logits - lse[:, None]) - hit.astype(F32))
    ).astype(BF16)
    danswer = dot("rv,vd->rd", dlogits, head).astype(BF16)

    def head_grad(rows, after):
        grads = [
            dot("rv,rd->vd", dlogits[:, rows], final[:, a * cols : (a + 1) * cols]) + after
            for a in range(n_dp)
        ]
        return lax.all_to_all(jnp.stack(grads).astype(BF16), "dp", 0, 0)

    half_grads = [head_grad(slice(0, sub // 2), 0.0)]

    parts = danswer.reshape(n_mp, n_dp * rows_ans, D)
    if n_mp == 8:
        dx2, dgain3, down_in = exchange(
            backward_kernel, "head_sum", 3, n_dp, True, False, (own, gain_row, plane),
            *(parts, x2, gains[2:3]),
        )
        dgain3 = dgain3[0]
    else:
        mine = cube_scatter(parts).astype(BF16)
        mine = line_exchange(list(mine.reshape(n_dp, rows_ans, D)))
        dfinal = sum(piece.astype(F32) for piece in mine)
        dx2, dgain3 = norm_backward(dfinal, *norm_forward(x2), gains[2])
        down_in = cube_gather(dx2.astype(BF16))
    down_in = down_in.reshape(-1, D)
    half_grads.append(head_grad(slice(sub // 2, sub), 0.0 * dx2[0, 0]))
    table_grad = jnp.concatenate(half_grads, axis=1).reshape(vocab_part, cols)
    dhidden = dot("td,fd->tf", down_in, wdown)
    sigma = jax.nn.sigmoid(gate)
    dgate_up = jnp.concatenate(
        [dhidden * upward * sigma * (1.0 + gate * (1.0 - sigma)), dhidden * gate * sigma],
        axis=-1,
    ).astype(BF16)
    parts = dot("tf,df->td", dgate_up, wgate).astype(BF16).reshape(n_mp, rows_ans, D)
    grad_down = dot("tf,td->fd", hidden, down_in).astype(BF16)
    grad_gate = dot("td,tf->df", h2, dgate_up).astype(BF16)
    if n_mp == 8:
        dx1, dgain2, out_in = exchange(
            backward_kernel, "gate_sum", 4, n_dp, False, False, (own, gain_row, plane),
            *(parts, x1, gains[1:2], dx2),
        )
        dgain2 = dgain2[0]
    else:
        dx_mlp, dgain2 = norm_backward(cube_scatter(parts), *norm_forward(x1), gains[1])
        dx1 = dx2 + dx_mlp
        out_in = cube_gather(dx1.astype(BF16))
    out_in = out_in.reshape(-1, D)
    dattended = dot("td,wd->tw", out_in, wout).astype(BF16)
    grad_out = dot("tw,td->wd", o_rows, out_in).astype(BF16)
    (dqkv,) = in_vmem(
        functools.partial(attend_back_kernel, items),
        "attend_back",
        (((n_mp, rows_own, 3 * width), BF16),),
        *(query, key, value, dattended.reshape(n_mp, rows_ans, width), cosine, sine, *place),
    )
    dqkv = dqkv.reshape(-1, 3 * width)
    dh1 = dot("te,de->td", dqkv, wqkv).astype(BF16).reshape(n_mp, rows_own, D)
    dnormed1 = cube_scatter(dh1)
    grad_qkv = dot("td,te->de", h1_all, dqkv).astype(BF16)
    dx0, dgain1 = norm_backward(dnormed1, normed1, inverse1, gains[0])
    dx0 = jnp.concatenate([dx0[:rows_ans] + dx1, dx0[rows_ans:]]).astype(BF16)

    halves = collect_tiles(perm, (grad_gate, grad_down), shapes, (2, 3), n_dp)
    one, two = collect_tiles(
        perm, (grad_qkv, grad_out), shapes, (0, 1), n_dp, halves, half_grads
    )
    one = lax.psum_scatter(one, "dp", scatter_dimension=0, tiled=True)

    pieces = line_exchange(
        [lax.dynamic_slice_in_dim(dx0, near[o] * cols, cols, 1) for o in range(n_dp)]
    )
    after = sum(0.0 * piece[0, 0].astype(F32) for piece in pieces)
    two = (two.astype(F32) + after).astype(BF16)
    two = lax.psum_scatter(two, "dp", scatter_dimension=0, tiled=True)
    rows_back = cube_gather(jnp.stack(pieces).reshape(-1, cols)).reshape(safe.shape + (cols,))
    picked_rows = jnp.where(valid[..., None], rows_back, 0).astype(F32)
    own_table = table_grad.astype(F32).at[safe.reshape(-1)].add(picked_rows.reshape(-1, cols))

    gain_grad = jnp.stack([dgain1, dgain2, dgain3])
    gain_total = everywhere(gain_grad, jnp.add)
    own_gain = lax.dynamic_slice_in_dim(gain_total, dp * cols, cols, 1)
    first_mp = (mp == 0).astype(F32)
    squares = jnp.sum(own_table * own_table) + first_mp * jnp.sum(own_gain * own_gain)
    if n_mp == 8:
        more = jnp.zeros((2, 8, 128), F32).at[:, 0, 0].set(jnp.stack([squares, loss_own]))
        squares_all, loss_total = jnp.sum(total_exchange(one, two, more, n_dp), axis=(1, 2))
    else:
        squares = squares + sum(jnp.sum(jnp.square(g.astype(F32))) for g in (one, two))
        more = everywhere(jnp.stack([squares, loss_own])[None], jnp.add)[0]
        squares_all, loss_total = more
    norm = jnp.sqrt(squares_all)
    factor = CLIP_NORM / jnp.maximum(norm, CLIP_NORM)
    block_new, block_copy, grad_slots, left_new, right_new = tile_step(
        factor.reshape(1, 1),
        *(one, two, block_master[0], left_stat[0], right_stat[0], left_root[0], right_root[0]),
    )
    table_new, table_moment_new, table_second_new = adam(
        table_master, table_moment, table_second, factor * own_table, LR_TABLE, DECAY_TABLE
    )
    gain_new, gain_moment_new, gain_second_new = adam(
        gain_master, gain_moment, gain_second, factor * own_gain, LR_GAIN, 0.0
    )
    return (
        loss_total,
        norm,
        block_new[None],
        block_copy[None],
        grad_slots[None],
        left_new[None],
        right_new[None],
        table_new,
        table_new.astype(BF16),
        table_moment_new,
        table_second_new,
        gain_new,
        gain_moment_new,
        gain_second_new,
    )


def solution(mesh):
    in_specs = (
        P("dp", None),
        P("dp", None),
        P(),
        P("dp"),
        P("dp", None),
        P("dp"),
        P("mp", None),
        P("mp", "dp", None, None),
        P("mp", "dp", None, None),
        P("mp", "dp", None, None),
        P("mp", "dp", None, None),
        P("mp", "dp", None, None),
        P("mp", "dp"),
        P("mp", "dp"),
        P("mp", "dp"),
        P(None, "dp"),
        P(None, "dp"),
        P(None, "dp"),
    )
    out_specs = (
        P(),
        P(),
        P("mp", "dp", None, None),
        P("mp", "dp", None, None),
        P("mp", "dp", None, None),
        P("mp", "dp", None, None),
        P("mp", "dp", None, None),
        P("mp", "dp"),
        P("mp", "dp"),
        P("mp", "dp"),
        P("mp", "dp"),
        P(None, "dp"),
        P(None, "dp"),
        P(None, "dp"),
    )
    return jax.shard_map(body, mesh=mesh, in_specs=in_specs, out_specs=out_specs, check_vma=False)
```

```python
import functools

import jax
import jax.numpy as jnp
from jax import lax
from jax.experimental import pallas as pl
from jax.experimental.pallas import tpu as pltpu
from jax.sharding import PartitionSpec as P

D = 2048
HD = 64
FF = 8192
ANS = 256
STEP = 5


EPS_NORM = 1e-05
ROPE_BASE = 130000.0
CLIP_NORM = 0.01
STAT_DECAY = 0.95
LR_MATRIX = 0.05
DECAY_MATRIX = 0.1
LR_TABLE = 0.03
DECAY_TABLE = 0.1
LR_GAIN = 0.2
ADAM_ONE = 0.9
ADAM_TWO = 0.95
ADAM_EPS = 1e-08
MASKED = -1e30
F32 = jnp.float32
BF16 = jnp.bfloat16


def dot(spec, a, b):
    return jnp.einsum(spec, a, b, preferred_element_type=F32)


def cube_bits(n):
    bits = [1 << i for i in range(n.bit_length() - 1)]
    return bits[1:] + bits[:1]


def cube_order(n):
    order = [0]
    for bit in cube_bits(n):
        order = order + [o ^ bit for o in order]
    return order


def swap(x, axis, bit):
    n = lax.axis_size(axis)
    return lax.ppermute(x, axis, [(i, i ^ bit) for i in range(n)])


def cube_gather(x):
    n = lax.axis_size("mp")
    if n != 8:
        held = x[None]
        for bit in cube_bits(n):
            held = jnp.concatenate([held, swap(held, "mp", bit)])
        return held
    half = x.shape[0] // 2
    over_x = swap(x, "mp", 2)
    over_y = swap(x, "mp", 4)
    far = jnp.concatenate([swap(over_x[:half], "mp", 4), swap(over_y[half:], "mp", 2)])
    held = jnp.stack([x, over_x, over_y, far])
    return jnp.concatenate([held, swap(held, "mp", 1)])


def cube_scatter(parts):
    n = lax.axis_size("mp")
    if n != 8:
        held = parts
        for bit in reversed(cube_bits(n)):
            keep = held.shape[0] // 2
            other = swap(held[keep:].astype(BF16), "mp", bit)
            held = held[:keep].astype(F32) + other.astype(F32)
        return held[0]
    got = swap(parts[4:], "mp", 1)
    held = (parts[:4].astype(F32) + got.astype(F32)).astype(BF16)
    half = held.shape[1] // 2
    one, two = held[:, :half], held[:, half:]
    one_x = swap(one[1::2], "mp", 2)
    two_y = swap(two[2:], "mp", 4)
    one = one[0::2].astype(F32) + one_x.astype(F32)
    two = two[:2].astype(F32) + two_y.astype(F32)
    one_y = swap(one[1].astype(BF16), "mp", 4)
    two_x = swap(two[1].astype(BF16), "mp", 2)
    return jnp.concatenate([one[0] + one_y.astype(F32), two[0] + two_x.astype(F32)])


def line_gather(x):
    return [x] + [swap(x, "dp", o) for o in range(1, lax.axis_size("dp"))]


def line_exchange(parts):
    return [parts[0]] + [swap(parts[o], "dp", o) for o in range(1, len(parts))]


def combine_stats(a, b):
    top = jnp.maximum(a[0], b[0])
    total = a[1] * jnp.exp(a[0] - top) + b[1] * jnp.exp(b[0] - top)
    return jnp.stack([top, total, a[2] + b[2]])


def everywhere(x, op):
    for axis in ("mp", "dp"):
        bit = 1
        while bit < lax.axis_size(axis):
            x = op(x, swap(x, axis, bit))
            bit *= 2
    return x


def stats_everywhere(x, rows):
    n_mp, n_dp = lax.axis_size("mp"), lax.axis_size("dp")
    bits = cube_bits(n_mp)
    split = (3,) + (2,) * len(bits) + (n_dp * rows,)
    x = x.reshape(split)
    for i, bit in enumerate(bits):
        x = combine_stats(x, jnp.flip(swap(x, "mp", bit), len(bits) - i))
    x = x.reshape(3, n_mp, n_dp, rows)
    total = x
    for o, other in enumerate(line_gather(x)):
        if o:
            order = [e ^ o for e in range(n_dp)]
            total = combine_stats(total, jnp.stack([other[:, :, e] for e in order], axis=2))
    return total.reshape(3, -1)


def peer_copy(src, dst, sems, k, **device):
    return pltpu.make_async_remote_copy(
        src_ref=src,
        dst_ref=dst,
        send_sem=sems.at[0, k],
        recv_sem=sems.at[1, k],
        device_id=device,
        device_id_type=pl.DeviceIdType.MESH,
    )


def greet(n_dp, bits=(1, 2, 4)):
    me = lax.axis_index("mp")
    a = lax.axis_index("dp")
    barrier = pltpu.get_barrier_semaphore()
    partners = [{"mp": me ^ bit} for bit in bits]
    partners += [{"dp": a ^ o} for o in range(1, n_dp)]
    for partner in partners:
        pl.semaphore_signal(barrier, 1, device_id=partner, device_id_type=pl.DeviceIdType.MESH)
    pl.semaphore_wait(barrier, len(partners))


def by_rows(count, step):
    @pl.loop(0, count // 16)
    def _(i):
        step(pl.multiple_of(i * 16, 16))


class PlaneSum:
    def __init__(self, parts, own, core, held, near, last, sems, first, blocks):
        me = lax.axis_index("mp")
        self.refs = parts, own, core, held, near, last
        self.rows = own.shape[0] // blocks
        self.half = half = self.rows // 2
        self.at_core = {
            s: peer_copy(parts.at[4 + s], core.at[s], sems, first + s, mp=me ^ 1)
            for s in range(4)
        }
        self.blocks = []
        for b in range(blocks):
            top, low = pl.ds(b * self.rows, half), pl.ds(b * self.rows + half, half)
            spot = pl.ds(b * half, half)
            k = first + 4 + 6 * b
            sends = (
                (3, top, near, 0, 2),
                (3, low, near, 1, 4),
                (1, top, near, 2, 2),
                (2, low, near, 3, 4),
                (2, top, last, 0, 4),
                (1, low, last, 1, 2),
            )
            self.blocks.append(
                [
                    peer_copy(held.at[s, rows], to.at[at, spot], sems, k + e, mp=me ^ bit)
                    for e, (s, rows, to, at, bit) in enumerate(sends)
                ]
            )

    def send_core(self, s):
        self.at_core[s].start()

    def await_core(self, s):
        self.at_core[s].wait_recv()

    def first_sends(self, b):
        parts, _, core, held, _, _ = self.refs
        copies = self.blocks[b]
        for s, sent in ((3, copies[:2]), (1, copies[2:3]), (2, copies[3:4])):

            def add(at, s=s):
                rows = pl.ds(b * self.rows + at, 16)
                value = parts[s, rows].astype(F32) + core[s, rows].astype(F32)
                held[s, rows] = value.astype(BF16)

            by_rows(self.rows, add)
            for copy in sent:
                copy.start()

    def second_sends(self, b):
        _, _, _, held, near, _ = self.refs
        copies = self.blocks[b]
        for e, s, offset in ((0, 2, 0), (1, 1, self.half)):
            copies[e].wait_recv()

            def add(at, e=e, s=s, offset=offset):
                rows = pl.ds(b * self.rows + offset + at, 16)
                value = held[s, rows].astype(F32) + near[e, pl.ds(b * self.half + at, 16)].astype(F32)
                held[s, rows] = value.astype(BF16)

            by_rows(self.half, add)
            copies[4 + e].start()

    def finish(self, b):
        parts, own, core, _, near, last = self.refs
        for copy in self.blocks[b][2:]:
            copy.wait_recv()

        def total(at):
            spot = pl.ds(b * self.half + at, 16)
            for e, offset in ((0, 0), (1, self.half)):
                rows = pl.ds(b * self.rows + offset + at, 16)
                own[rows] = (
                    (parts[0, rows].astype(F32) + core[0, rows].astype(F32))
                    + near[2 + e, spot].astype(F32)
                    + last[e, spot].astype(F32)
                )

        by_rows(self.half, total)

    def close(self):
        for copy in self.at_core.values():
            copy.wait_send()
        for copies in self.blocks:
            for copy in copies:
                copy.wait_send()

    def run(self):
        for s in (3, 1, 2, 0):
            self.send_core(s)
        for s in (3, 1, 2):
            self.await_core(s)
        for b in range(len(self.blocks)):
            self.first_sends(b)
        for b in range(len(self.blocks)):
            self.second_sends(b)
        self.await_core(0)
        for b in range(len(self.blocks)):
            self.finish(b)
        self.close()


class PlaneSpread:
    def __init__(self, x, out, sems, k, start, rows):
        me = lax.axis_index("mp")
        half = rows // 2
        top, low, whole = pl.ds(start, half), pl.ds(start + half, half), pl.ds(start, rows)
        self.own = x, out, start, rows

        def copy(src, slot, part, e, bit):
            return peer_copy(src, out.at[slot, part], sems, k + e, mp=me ^ bit)

        self.x_top = copy(x.at[top], 1, top, 0, 2)
        self.y_low = copy(x.at[low], 2, low, 1, 4)
        self.x_low = copy(x.at[low], 1, low, 2, 2)
        self.y_top = copy(x.at[top], 2, top, 3, 4)
        self.core = copy(x.at[whole], 4, whole, 4, 1)
        self.far_y = copy(out.at[1, top], 3, top, 5, 4)
        self.far_x = copy(out.at[2, low], 3, low, 6, 2)
        self.to_core = {
            (s, r): copy(out.at[s, part], 4 + s, part, 7 + 2 * (s - 1) + r, 1)
            for s in (1, 2, 3)
            for r, part in enumerate((top, low))
        }

    def begin(self):
        for c in (self.x_top, self.y_low, self.x_low, self.y_top, self.core):
            c.start()
        x, out, start, rows = self.own

        def keep(at):
            part = pl.ds(start + at, 16)
            out[0, part] = x[part]

        by_rows(rows, keep)

    def relay(self):
        self.x_top.wait_recv()
        self.far_y.start()
        self.to_core[1, 0].start()
        self.y_low.wait_recv()
        self.far_x.start()
        self.to_core[2, 1].start()
        self.x_low.wait_recv()
        self.to_core[1, 1].start()
        self.y_top.wait_recv()
        self.to_core[2, 0].start()

    def relay_far(self):
        self.far_y.wait_recv()
        self.to_core[3, 0].start()
        self.far_x.wait_recv()
        self.to_core[3, 1].start()

    def arrive(self):
        self.core.wait_recv()
        for c in self.to_core.values():
            c.wait_recv()

    def close(self):
        sent = (self.x_top, self.y_low, self.x_low, self.y_top, self.core, self.far_y, self.far_x)
        for c in (*sent, *self.to_core.values()):
            c.wait_send()

    def run(self):
        self.begin()
        self.relay()
        self.relay_far()
        self.arrive()
        self.close()


def norm_step(x, gain):
    return (x * lax.rsqrt(jnp.mean(x * x, axis=1, keepdims=True) + EPS_NORM)) * gain


def norm_back_step(grad, x, gain):
    inverse = lax.rsqrt(jnp.mean(x * x, axis=1, keepdims=True) + EPS_NORM)
    normed = x * inverse
    scaled = grad * gain
    dx = inverse * (scaled - normed * jnp.mean(scaled * normed, axis=1, keepdims=True))
    return dx, jnp.sum(grad * normed, axis=0, keepdims=True)


def forward_kernel(n_dp, spread, parts, res, gain, x_out, out, *refs):
    *refs, mine, sems = refs
    greet(1)
    PlaneSum(parts, *refs, sems, 0, 1).run()
    x = res[...] + refs[0][...]
    x_out[...] = x
    low = norm_step(x, gain[...]).astype(BF16)
    if spread:
        mine[...] = low
        PlaneSpread(mine, out, sems, 10, 0, mine.shape[0]).run()
    else:
        out[...] = low


def head_kernel(n_dp, rows_ref, head_ref, target_ref, scale_ref, *refs):
    final, dlogits, seen, mine, logits, stats, plane, mid, line, sems = refs
    rows, vocab = rows_ref.shape[0], logits.shape[2]
    wide = head_ref.shape[2]
    a = lax.axis_index("dp")
    greet(n_dp, range(1, 8))
    mine[pl.ds(0, rows)] = rows_ref[...]
    across = [
        peer_copy(rows_ref, mine.at[pl.ds(o * rows, rows)], sems, 13 * n_dp + o, dp=a ^ o)
        for o in range(1, n_dp)
    ]
    for copy in across:
        copy.start()
    blocks = [PlaneSpread(mine, final, sems, 13 * o, o * rows, rows) for o in range(n_dp)]
    tile = 512 if vocab % 512 == 0 else vocab

    def use(b):
        part = pl.ds(b * rows, rows)

        @pl.loop(0, vocab // tile)
        def _(v):
            at = pl.ds(pl.multiple_of(v * tile, tile), tile)
            value = None
            for p in range(n_dp):
                x = flat(final[:, part, pl.ds(p * wide, wide)])
                term = mm(x, head_ref[p, at, :], CONTRACT_LAST)
                value = term if value is None else value + term
            logits[:, part, at] = value.reshape(8, rows, tile)

        value = flat(logits[:, part, :])
        top = jnp.max(value, axis=1, keepdims=True)
        expo = jnp.sum(jnp.exp(value - top), axis=1, keepdims=True)
        column = lax.broadcasted_iota(jnp.int32, value.shape, 1)
        hit = jnp.sum(jnp.where(column == target_ref[b], value, 0.0), axis=1, keepdims=True)
        lane = lax.broadcasted_iota(jnp.int32, (8 * rows, 128), 1)
        packed = jnp.where(lane == 0, top, jnp.where(lane == 1, expo, hit)).T
        for k in range(3):
            stats[k, b : b + 1, :] = packed[k : k + 1]

    blocks[0].begin()
    for b in range(1, n_dp):
        across[b - 1].wait_recv()
        blocks[b].begin()
        blocks[b - 1].relay()
        blocks[b - 1].relay_far()
        if b > 1:
            blocks[b - 2].arrive()
            use(b - 2)
    blocks[n_dp - 1].relay()
    blocks[n_dp - 1].relay_far()
    for b in range(max(n_dp - 2, 0), n_dp):
        blocks[b].arrive()
        use(b)
    stats_steps(n_dp, stats, seen, plane, mid, line, sems, 14 * n_dp)

    @pl.loop(0, n_dp)
    def _(b):
        part = pl.ds(pl.multiple_of(b * rows, rows), rows)
        lse = jnp.broadcast_to(seen[0, pl.ds(b, 1), :], (128, 8 * rows)).T[:, :1]
        value = flat(logits[:, part, :])
        column = lax.broadcasted_iota(jnp.int32, value.shape, 1)
        hit = (column == target_ref[b]).astype(F32)
        grad = (scale_ref[b] * (jnp.exp(value - lse) - hit)).astype(BF16)
        dlogits[:, part, :] = grad.reshape(8, rows, vocab)

    for copy in across:
        copy.wait_send()
    for block in blocks:
        block.close()


def head_call(n_dp, rows, head, target, scale):
    total = n_dp * rows.shape[0]
    vocab = head.shape[1]
    stats = (3, n_dp, 8 * rows.shape[0])
    outs = [((8, total, D), BF16), ((8, total, vocab), BF16), ((2,) + stats[1:], F32)]
    return pl.pallas_call(
        functools.partial(head_kernel, n_dp),
        out_shape=[jax.ShapeDtypeStruct(shape, dtype) for shape, dtype in outs],
        in_specs=[pl.BlockSpec(memory_space=pltpu.VMEM)] * 4,
        out_specs=[pl.BlockSpec(memory_space=pltpu.VMEM)] * 3,
        scratch_shapes=[
            pltpu.VMEM((total, D), BF16),
            pltpu.VMEM((8, total, vocab), F32),
            pltpu.VMEM(stats, F32),
            pltpu.VMEM((7,) + stats, F32),
            pltpu.VMEM(stats, F32),
            pltpu.VMEM((n_dp - 1,) + stats, F32),
            pltpu.SemaphoreType.DMA((2, 14 * n_dp + 6 + n_dp)),
        ],
        compiler_params=pltpu.CompilerParams(
            collective_id=5, has_side_effects=True, vmem_limit_bytes=56 << 20
        ),
        cost_estimate=pl.CostEstimate(flops=0, bytes_accessed=1 << 20, transcendentals=0),
        name="head",
    )(rows, head, target, scale)


def head_back_kernel(n_dp, dlogits, final, head, x_in, gain, dx_out, dgain, out, grads, *refs):
    own, core, held, near, last, mine, sent, got, parts, sems = refs
    a = lax.axis_index("dp")
    rows = x_in.shape[0]
    wide, vocab = head.shape[2], head.shape[1]
    greet(n_dp)
    plan = PlaneSum(parts, own, core, held, near, last, sems, 0, n_dp)

    def make(s):
        for p in range(n_dp):
            parts[s, :, pl.ds(p * wide, wide)] = mm(dlogits[s], head[p]).astype(BF16)

    tile = 512 if vocab % 512 == 0 else vocab
    left = [(p, v) for p in range(n_dp) for v in range(vocab // tile)]

    def fill(count):
        for _ in range(min(count, len(left))):
            p, v = left.pop(0)
            at = pl.ds(v * tile, tile)
            value = mm(flat(dlogits[:, :, at]), flat(final[:, :, pl.ds(p * wide, wide)]), CONTRACT_FIRST)
            grads[p, at, :] = value.astype(BF16)

    for s in (3, 1, 2, 0):
        make(4 + s)
        plan.send_core(s)
    for s in (3, 1, 2):
        make(s)
    for s in (3, 1, 2):
        plan.await_core(s)
    across = {
        b: peer_copy(
            sent.at[pl.ds(b * rows, rows)], got.at[b - 1], sems, 17 + 6 * n_dp + b, dp=a ^ b
        )
        for b in range(1, n_dp)
    }

    def finish(b):
        plan.finish(b)
        if b:
            part = pl.ds(b * rows, rows)
            sent[part] = own[part].astype(BF16)
            across[b].start()

    order = [*range(2, n_dp), *range(1, min(2, n_dp)), 0]
    for b in order[:2]:
        plan.first_sends(b)
    make(0)
    plan.await_core(0)
    for at in range(2, n_dp + 2):
        plan.second_sends(order[at - 2])
        if at < n_dp:
            plan.first_sends(order[at])
        fill(2)
        finish(order[at - 2])
        fill(1)
    fill(len(left))
    for copy in across.values():
        copy.wait()
    grad = own[pl.ds(0, rows)]
    for o in range(1, n_dp):
        grad = grad + got[o - 1].astype(F32)
    dx, dg = norm_back_step(grad, x_in[...], gain[...])
    dx_out[...] = dx
    dgain[...] = dg
    mine[...] = dx.astype(BF16)
    PlaneSpread(mine, out, sems, 4 + 6 * n_dp, 0, rows).run()
    plan.close()


def backward_kernel(n_dp, _, parts, x_in, gain, res, dx_out, dgain, out, *refs):
    *refs, mine, sems = refs
    greet(1)
    PlaneSum(parts, *refs, sems, 0, 1).run()
    dx, dg = norm_back_step(refs[0][...], x_in[...], gain[...])
    dx = dx + res[...]
    dx_out[...] = dx
    dgain[...] = dg
    mine[...] = dx.astype(BF16)
    PlaneSpread(mine, out, sems, 10, 0, mine.shape[0]).run()


def exchange(kernel, name, number, n_dp, how, total, outs, *args):
    half = total // 2
    rows = outs[0][0][0]
    scratch = [
        pltpu.VMEM((total, D), F32),
        pltpu.VMEM((4, total, D), BF16),
        pltpu.VMEM((4, total, D), BF16),
        pltpu.VMEM((4, half, D), BF16),
        pltpu.VMEM((2, half, D), BF16),
        pltpu.VMEM((rows, D), BF16),
    ]
    if kernel is head_back_kernel:
        body = functools.partial(kernel, n_dp)
        scratch += [pltpu.VMEM((total, D), BF16), pltpu.VMEM((n_dp - 1, rows, D), BF16)]
        scratch += [pltpu.VMEM((8, total, D), BF16)]
        sems = 17 + 7 * n_dp
    else:
        body = functools.partial(kernel, n_dp, how)
        sems = 23
    return pl.pallas_call(
        body,
        out_shape=[jax.ShapeDtypeStruct(shape, dtype) for shape, dtype in outs],
        in_specs=[pl.BlockSpec(memory_space=pltpu.VMEM)] * len(args),
        out_specs=[pl.BlockSpec(memory_space=pltpu.VMEM)] * len(outs),
        scratch_shapes=scratch + [pltpu.SemaphoreType.DMA((2, sems))],
        compiler_params=pltpu.CompilerParams(
            collective_id=number, has_side_effects=True, vmem_limit_bytes=62 << 20
        ),
        cost_estimate=pl.CostEstimate(flops=0, bytes_accessed=1 << 20, transcendentals=0),
        name=name,
    )(*args)


def stats_steps(n_dp, x_ref, out_ref, plane, mid, line, sems, first):
    me = lax.axis_index("mp")
    a = lax.axis_index("dp")
    order = cube_order(8)
    rows = x_ref.shape[2] // 8
    copies = [
        peer_copy(x_ref, plane.at[s - 1], sems, first + s - 1, mp=me ^ order[s])
        for s in range(1, 8)
    ]
    for copy in copies:
        copy.start()

    def join(have, new):
        top = jnp.maximum(have[0], new[0])
        total = have[1] * jnp.exp(have[0] - top) + new[1] * jnp.exp(new[0] - top)
        return top, total, have[2] + new[2]

    have = tuple(x_ref[k] for k in range(3))
    for s in range(1, 8):
        copies[s - 1].wait_recv()
        got = [plane[s - 1, k] for k in range(3)]
        got = [
            jnp.concatenate([v[:, (e ^ s) * rows : (e ^ s) * rows + rows] for e in range(8)], axis=1)
            for v in got
        ]
        have = join(have, got)
    for k in range(3):
        mid[k] = have[k]
    across = [
        peer_copy(mid, line.at[o - 1], sems, first + 6 + o, dp=a ^ o) for o in range(1, n_dp)
    ]
    for copy in across:
        copy.start()
    for o in range(1, n_dp):
        across[o - 1].wait_recv()
        got = [line[o - 1, k] for k in range(3)]
        got = [jnp.concatenate([v[e ^ o : (e ^ o) + 1] for e in range(n_dp)], axis=0) for v in got]
        have = join(have, got)
    out_ref[0] = have[0] + jnp.log(have[1])
    out_ref[1] = have[2]
    for copy in copies + across:
        copy.wait_send()


def total_kernel(n_dp, one_ref, two_ref, more_ref, out_ref, plane, line, sems):
    me = lax.axis_index("mp")
    a = lax.axis_index("dp")
    greet(n_dp, range(1, 8))

    def squares(ref):
        def add(k, have):
            g = ref[k].astype(F32)
            return have + jnp.sum((g * g).reshape(-1, 8, 128), axis=0)

        return lax.fori_loop(0, ref.shape[0], add, jnp.zeros((8, 128), F32))

    plane[me, 0] = squares(one_ref) + squares(two_ref) + more_ref[0]
    plane[me, 1] = more_ref[1]
    copies = [peer_copy(plane.at[me], plane.at[me], sems, k - 1, mp=me ^ k) for k in range(1, 8)]
    for copy in copies:
        copy.start()
    for copy in copies:
        copy.wait()
    line[a] = jnp.sum(plane[...], axis=0)
    across = [
        peer_copy(line.at[a], line.at[a], sems, 6 + o, dp=a ^ o)
        for o in range(1, n_dp)
    ]
    for copy in across:
        copy.start()
    for copy in across:
        copy.wait()
    out_ref[...] = jnp.sum(line[...], axis=0)


def total_exchange(one, two, more, n_dp):
    return pl.pallas_call(
        functools.partial(total_kernel, n_dp),
        out_shape=jax.ShapeDtypeStruct(more.shape, F32),
        in_specs=[pl.BlockSpec(memory_space=pltpu.VMEM)] * 3,
        out_specs=pl.BlockSpec(memory_space=pltpu.VMEM),
        scratch_shapes=[
            pltpu.VMEM((8,) + more.shape, F32),
            pltpu.VMEM((n_dp,) + more.shape, F32),
            pltpu.SemaphoreType.DMA((2, 6 + n_dp)),
        ],
        compiler_params=pltpu.CompilerParams(collective_id=6, has_side_effects=True),
        name="total",
    )(one, two, more)


def mat_shapes(n_mp):
    width, units = D // n_mp, FF // n_mp
    return ((D, 3 * width), (width, D), (D, 2 * units), (units, D))


def each_tile(shape, size, first, step):
    rows, cols = shape

    @pl.loop(0, rows // size)
    def _(r):
        row = pl.ds(pl.multiple_of(r * size, size), size)
        for c in range(cols // size):
            step(first + r * (cols // size) + c, (row, pl.ds(c * size, size)))


def first_tiles(shapes, size):
    firsts = [0]
    for rows, cols in shapes:
        firsts.append(firsts[-1] + rows * cols // (size * size))
    return firsts


def place_kernel(shapes, slot_ref, slots_ref, *refs):
    count = len(shapes)
    outs, mats, sems = refs[:count], refs[count : 2 * count], refs[-1]
    size = slots_ref.shape[1]
    for k, (shape, first) in enumerate(zip(shapes, first_tiles(shapes, size))):

        def fetch(tile, view, k=k):
            pltpu.make_async_copy(
                slots_ref.at[slot_ref[tile]], mats[k].at[view], sems.at[0, k]
            ).start()

        each_tile(shape, size, first, fetch)
    for k in range(count):
        pltpu.make_async_copy(mats[k], mats[k], sems.at[0, k]).wait()
        pltpu.make_async_copy(mats[k], outs[k], sems.at[1, k]).start()
    for k in range(count):
        pltpu.make_async_copy(mats[k], outs[k], sems.at[1, k]).wait()


def place_tiles(slot_of, slots, shapes):
    anywhere = pl.BlockSpec(memory_space=pl.ANY)
    return pl.pallas_call(
        functools.partial(place_kernel, shapes),
        out_shape=[jax.ShapeDtypeStruct(shape, slots.dtype) for shape in shapes],
        in_specs=[pl.BlockSpec(memory_space=pltpu.SMEM), anywhere],
        out_specs=[anywhere] * len(shapes),
        scratch_shapes=[pltpu.VMEM(shape, slots.dtype) for shape in shapes]
        + [pltpu.SemaphoreType.DMA((2, len(shapes)))],
        compiler_params=pltpu.CompilerParams(vmem_limit_bytes=40 << 20),
        cost_estimate=pl.CostEstimate(flops=0, bytes_accessed=1 << 20, transcendentals=0),
        name="place_tiles",
    )(slot_of, slots)


def collect_kernel(shapes, chosen, to_ref, *refs):
    mats = refs[: len(chosen)]
    one_ref, two_ref, sem = refs[-3:]
    number, size, _ = one_ref.shape
    firsts = first_tiles(shapes, size)
    for k, ref in zip(chosen, mats):

        def send(tile, view, ref=ref):
            to = to_ref[tile]

            @pl.when(to < number)
            def _():
                pltpu.make_async_copy(ref.at[view], one_ref.at[to], sem).start()

            @pl.when(to >= number)
            def _():
                pltpu.make_async_copy(ref.at[view], two_ref.at[to - number], sem).start()

        each_tile(shapes[k], size, firsts[k], send)
    for ref in mats:
        pltpu.make_async_copy(ref, ref, sem).wait()


def collect_tiles(to, mats, shapes, chosen, given=(), after=()):
    size = 128
    anywhere = pl.BlockSpec(memory_space=pl.ANY)
    out = jax.ShapeDtypeStruct((to.shape[0] // 2, size, size), BF16)
    return pl.pallas_call(
        functools.partial(collect_kernel, shapes, chosen),
        out_shape=[out, out],
        in_specs=[pl.BlockSpec(memory_space=pltpu.SMEM)]
        + [pl.BlockSpec(memory_space=pltpu.VMEM)] * len(mats)
        + [anywhere] * (len(given) + len(after)),
        out_specs=[anywhere, anywhere],
        scratch_shapes=[pltpu.SemaphoreType.DMA],
        compiler_params=pltpu.CompilerParams(vmem_limit_bytes=40 << 20),
        input_output_aliases={1 + len(mats) + k: k for k in range(len(given))},
        cost_estimate=pl.CostEstimate(flops=0, bytes_accessed=1 << 20, transcendentals=0),
        name="collect_tiles",
    )(to, *mats, *given, *after)


def after(x, *others):
    anywhere = pl.BlockSpec(memory_space=pl.ANY)
    return pl.pallas_call(
        lambda *refs: None,
        out_shape=jax.ShapeDtypeStruct(x.shape, x.dtype),
        in_specs=[anywhere] * (1 + len(others)),
        out_specs=anywhere,
        input_output_aliases={0: 0},
        cost_estimate=pl.CostEstimate(flops=0, bytes_accessed=0, transcendentals=0),
        name="after",
    )(x, *others)


def split(x):
    high = x.astype(BF16)
    return high, (x - high.astype(F32)).astype(BF16)


def tile_step_kernel(blocks, factor_ref, one_ref, two_ref, *refs):
    master, left, right, l_root, r_root, new, copy, grad, left_new, right_new = refs
    factor = factor_ref[0, 0]

    def step(g_ref):
        for k in range(g_ref.shape[0]):
            g = g_ref[k]
            grad[k] = factor * g.astype(F32)
            outer = (mm(g, g, CONTRACT_LAST) * factor) * factor
            inner = (mm(g, g, CONTRACT_FIRST) * factor) * factor
            left_new[k] = STAT_DECAY * left[k] + (1.0 - STAT_DECAY) * outer
            right_new[k] = STAT_DECAY * right[k] + (1.0 - STAT_DECAY) * inner
            l_high, l_low = split(l_root[k])
            r_high, r_low = split(r_root[k])
            t_high, t_low = split((mm(l_high, g) + mm(l_low, g)) * factor)
            direction = mm(t_high, r_high) + (mm(t_low, r_high) + mm(t_high, r_low))
            value = master[k] - LR_MATRIX * (direction + DECAY_MATRIX * master[k])
            new[k] = value
            copy[k] = value.astype(BF16)

    at = pl.program_id(0)
    pl.when(at < blocks)(lambda: step(one_ref))
    pl.when(at >= blocks)(lambda: step(two_ref))


def tile_step(factor, one, two, *state):
    number, size, _ = state[0].shape
    group = 8
    blocks = number // group // 2

    def block(index):
        return pl.BlockSpec((group, size, size), lambda i: (index(i), 0, 0))

    whole = block(lambda i: i)
    shape = (number, size, size)
    kinds = (F32, BF16, F32, F32, F32)
    return pl.pallas_call(
        functools.partial(tile_step_kernel, blocks),
        grid=(2 * blocks,),
        out_shape=[jax.ShapeDtypeStruct(shape, kind) for kind in kinds],
        in_specs=[
            pl.BlockSpec(memory_space=pltpu.SMEM),
            block(lambda i: jnp.minimum(i, blocks - 1)),
            block(lambda i: jnp.maximum(i - blocks, 0)),
        ]
        + [whole] * 5,
        out_specs=[whole] * 5,
        compiler_params=pltpu.CompilerParams(vmem_limit_bytes=40 << 20),
        name="tile_step",
    )(factor, one, two, *state)


CONTRACT_LAST = (((1,), (1,)), ((), ()))
CONTRACT_FIRST = (((0,), (0,)), ((), ()))


def mm(a, b, dims=(((1,), (0,)), ((), ()))):
    return lax.dot_general(a, b, dims, preferred_element_type=F32)


def turn(x, cosine, sine):
    lane = lax.broadcasted_iota(jnp.int32, x.shape, 1)
    other = jnp.where(
        lax.rem(lane, HD) < HD // 2, pltpu.roll(x, 128 - HD // 2, 1), pltpu.roll(x, HD // 2, 1)
    )
    return x * cosine + other * sine


def flat(x):
    return x.reshape(x.shape[0] * x.shape[1], x.shape[2])


def head_probs(q, k_ctx, k_ans, causal):
    s_ctx = mm(q, k_ctx, CONTRACT_LAST) * HD ** (-0.5)
    s_ans = jnp.where(causal, mm(q, k_ans, CONTRACT_LAST) * HD ** (-0.5), MASKED)
    top = jnp.maximum(
        jnp.max(s_ctx, axis=1, keepdims=True), jnp.max(s_ans, axis=1, keepdims=True)
    )
    e_ctx = jnp.exp(s_ctx - top)
    e_ans = jnp.exp(s_ans - top)
    total = jnp.sum(e_ctx, axis=1, keepdims=True) + jnp.sum(e_ans, axis=1, keepdims=True)
    return e_ctx / total, e_ans / total


def attend_kernel(items, qkv_ref, cos_ref, sin_ref, col_ref, row_ref, *outs):
    o_ref, qo_ref, ko_ref, vo_ref = outs
    n, rows_ans, width = o_ref.shape
    n_ans = rows_ans // items
    n_ctx = qkv_ref.shape[1] // items - n_ans
    causal = col_ref[...] >= row_ref[...]
    lane = lax.broadcasted_iota(jnp.int32, (1, 128), 1)

    for item in range(items):
        ans = pl.ds(item * n_ans, n_ans)
        ctx = pl.ds(rows_ans + item * n_ctx, n_ctx)
        turns = [(flat(cos_ref[:, r]), flat(sin_ref[:, r])) for r in (ans, ctx)]
        for g in range(width // 128):
            lanes = pl.ds(g * 128, 128)
            klanes = pl.ds(width + g * 128, 128)
            vlanes = pl.ds(2 * width + g * 128, 128)
            q = turn(flat(qkv_ref[:, ans, lanes]), *turns[0]).astype(BF16)
            k_ans = turn(flat(qkv_ref[:, ans, klanes]), *turns[0]).astype(BF16)
            k_ctx = turn(flat(qkv_ref[:, ctx, klanes]), *turns[1]).astype(BF16)
            v_ans = flat(qkv_ref[:, ans, vlanes]).astype(BF16)
            v_ctx = flat(qkv_ref[:, ctx, vlanes]).astype(BF16)
            qo_ref[:, ans, lanes] = q.reshape(n, n_ans, 128)
            ko_ref[:, ans, lanes] = k_ans.reshape(n, n_ans, 128)
            ko_ref[:, ctx, lanes] = k_ctx.reshape(n, n_ctx, 128)
            vo_ref[:, ans, lanes] = v_ans.reshape(n, n_ans, 128)
            vo_ref[:, ctx, lanes] = v_ctx.reshape(n, n_ctx, 128)
            got = []
            for first in (True, False):
                own = (lane < HD) == first
                p_ctx, p_ans = head_probs(jnp.where(own, q, 0), k_ctx, k_ans, causal)
                got.append(mm(p_ctx.astype(BF16), v_ctx) + mm(p_ans.astype(BF16), v_ans))
            o = jnp.where(lane < HD, got[0], got[1]).astype(BF16)
            o_ref[:, ans, lanes] = o.reshape(n, n_ans, 128)


def attend_back_kernel(items, *refs):
    q_ref, k_ref, v_ref, do_ref, cos_ref, sin_ref, col_ref, row_ref, d_ref = refs
    n, rows_ans, width = q_ref.shape
    n_ans = rows_ans // items
    n_ctx = k_ref.shape[1] // items - n_ans
    causal = col_ref[...] >= row_ref[...]
    lane = lax.broadcasted_iota(jnp.int32, (1, 128), 1)
    root = HD ** (-0.5)

    for item in range(items):
        ans = pl.ds(item * n_ans, n_ans)
        ctx = pl.ds(rows_ans + item * n_ctx, n_ctx)
        turns = [(flat(cos_ref[:, r]), -flat(sin_ref[:, r])) for r in (ans, ctx)]
        d_ref[:, ctx, pl.ds(0, width)] = jnp.zeros((n, n_ctx, width), BF16)
        for g in range(width // 128):
            lanes = pl.ds(g * 128, 128)
            klanes = pl.ds(width + g * 128, 128)
            vlanes = pl.ds(2 * width + g * 128, 128)
            q, do = flat(q_ref[:, ans, lanes]), flat(do_ref[:, ans, lanes])
            k_ans, k_ctx = flat(k_ref[:, ans, lanes]), flat(k_ref[:, ctx, lanes])
            v_ans, v_ctx = flat(v_ref[:, ans, lanes]), flat(v_ref[:, ctx, lanes])
            dq, sums = [], None
            for first in (True, False):
                own = (lane < HD) == first
                q_own, do_own = jnp.where(own, q, 0), jnp.where(own, do, 0)
                p_ctx, p_ans = head_probs(q_own, k_ctx, k_ans, causal)
                dp_ctx = mm(do_own, v_ctx, CONTRACT_LAST)
                dp_ans = mm(do_own, v_ans, CONTRACT_LAST)
                mean = jnp.sum(p_ctx * dp_ctx, axis=1, keepdims=True) + jnp.sum(
                    p_ans * dp_ans, axis=1, keepdims=True
                )
                ds_ctx = (p_ctx * (dp_ctx - mean)).astype(BF16)
                ds_ans = (p_ans * (dp_ans - mean)).astype(BF16)
                dq.append(mm(ds_ctx, k_ctx) + mm(ds_ans, k_ans))
                new = [
                    mm(ds_ctx, q_own, CONTRACT_FIRST),
                    mm(ds_ans, q_own, CONTRACT_FIRST),
                    mm(p_ctx.astype(BF16), do_own, CONTRACT_FIRST),
                    mm(p_ans.astype(BF16), do_own, CONTRACT_FIRST),
                ]
                sums = new if sums is None else [a + b for a, b in zip(sums, new)]
            dq = turn(jnp.where(lane < HD, dq[0], dq[1]) * root, *turns[0])
            dk_ctx = turn(sums[0] * root, *turns[1])
            dk_ans = turn(sums[1] * root, *turns[0])
            d_ref[:, ans, lanes] = dq.astype(BF16).reshape(n, n_ans, 128)
            d_ref[:, ans, klanes] = dk_ans.astype(BF16).reshape(n, n_ans, 128)
            d_ref[:, ctx, klanes] = dk_ctx.astype(BF16).reshape(n, n_ctx, 128)
            d_ref[:, ans, vlanes] = sums[3].astype(BF16).reshape(n, n_ans, 128)
            d_ref[:, ctx, vlanes] = sums[2].astype(BF16).reshape(n, n_ctx, 128)


def in_vmem(kernel, name, outs, *args):
    return pl.pallas_call(
        kernel,
        out_shape=[jax.ShapeDtypeStruct(shape, dtype) for shape, dtype in outs],
        in_specs=[pl.BlockSpec(memory_space=pltpu.VMEM)] * len(args),
        out_specs=[pl.BlockSpec(memory_space=pltpu.VMEM)] * len(outs),
        compiler_params=pltpu.CompilerParams(vmem_limit_bytes=48 << 20),
        cost_estimate=pl.CostEstimate(flops=0, bytes_accessed=1 << 20, transcendentals=0),
        name=name,
    )(*args)


def norm_forward(x):
    inverse = lax.rsqrt(jnp.mean(x * x, axis=-1, keepdims=True) + EPS_NORM)
    return (x * inverse, inverse)


def norm_backward(grad, normed, inverse, gain):
    scaled = grad * gain
    dgain = jnp.sum(grad * normed, axis=0)
    dx = inverse * (scaled - normed * jnp.mean(scaled * normed, axis=-1, keepdims=True))
    return (dx, dgain)


def adam(master, moment, second, grad, rate, decay):
    moment_new = ADAM_ONE * moment + (1.0 - ADAM_ONE) * grad
    second_new = ADAM_TWO * second + (1.0 - ADAM_TWO) * grad * grad
    corrected = (
        moment_new
        / (1.0 - ADAM_ONE**STEP)
        / (jnp.sqrt(second_new / (1.0 - ADAM_TWO**STEP)) + ADAM_EPS)
    )
    return (master - rate * (corrected + decay * master), moment_new, second_new)


def body(
    tokens,
    targets,
    pair_order,
    lengths,
    loss_mask,
    start_pos,
    owner_map,
    block_master,
    left_stat,
    right_stat,
    left_root,
    right_root,
    table_master,
    table_moment,
    table_second,
    gain_master,
    gain_moment,
    gain_second,
):
    dp = lax.axis_index("dp")
    mp = lax.axis_index("mp")
    n_mp = lax.axis_size("mp")
    n_dp = lax.axis_size("dp")
    items, length = tokens.shape
    context = length - ANS
    n_ans = ANS // n_mp
    n_ctx = context // n_mp
    rows_ans = items * n_ans
    rows_own = items * (n_ans + n_ctx)
    width = D // n_mp
    units = FF // n_mp
    heads = width // HD
    vocab_part, cols = table_master.shape
    sub = vocab_part // n_dp
    perm = owner_map[0]
    who = mp ^ jnp.array(cube_order(n_mp), jnp.int32)
    near = dp ^ jnp.arange(n_dp, dtype=jnp.int32)

    slots = lax.all_gather(block_master[0].astype(BF16), "dp", axis=0, tiled=True)
    gains = line_gather(gain_master.astype(BF16))
    wide = jnp.zeros((3, D), BF16)
    for o in range(n_dp):
        wide = lax.dynamic_update_slice(wide, gains[o], (0, near[o] * cols))
    gains = wide.astype(F32)
    table_low = table_master.astype(BF16)

    packed = jnp.concatenate([tokens, targets, loss_mask, lengths[:, None]], axis=1)
    packed = jnp.stack(line_gather(packed))
    all_tokens = packed[:, :, :length]
    all_targets = packed[:, :, length : length + ANS]
    all_mask = packed[:, :, length + ANS : length + 2 * ANS]
    all_lengths = packed[:, :, -1]
    column = jnp.arange(ANS)
    weights = jnp.where(
        column == 0,
        1.0,
        jnp.where(column < all_lengths[..., None], all_mask.astype(F32), 0.0),
    )
    pairs_all = pair_order.shape[0] // 2
    pairs = (pair_order // 2).reshape(n_dp, items)[near]
    member = (pairs[..., None] == jnp.arange(pairs_all)).astype(F32)
    counts = jnp.einsum("oip,oi->p", member, jnp.sum(weights, axis=-1))
    scale = weights / (jnp.sum(member * counts, axis=-1)[..., None] * pairs_all)

    def by_owner(x):
        split = x.reshape(n_dp, items, n_mp, n_ans)[:, :, who]
        return split.transpose(2, 0, 1, 3)

    row_scale = by_owner(scale).reshape(-1)
    row_target = by_owner(all_targets).reshape(-1)
    tok_ans = all_tokens[:, :, context:].reshape(n_dp, items, n_mp, n_ans)[:, :, who]
    tok_ctx = all_tokens[:, :, :context].reshape(n_dp, items, n_mp, n_ctx)[:, :, who]
    tok = jnp.concatenate(
        [
            tok_ans.transpose(2, 0, 1, 3).reshape(n_mp, n_dp, -1),
            tok_ctx.transpose(2, 0, 1, 3).reshape(n_mp, n_dp, -1),
        ],
        axis=2,
    )

    shapes = mat_shapes(n_mp)
    number = perm.shape[0]
    slot_of = jnp.zeros_like(perm).at[perm].set(jnp.arange(number, dtype=jnp.int32))
    split_slots = slot_of.reshape(1, -1)
    each = number // n_dp
    owner, at = split_slots // each, split_slots % each
    half_slots = each // 2
    sent_to = (at // half_slots) * (number // 2) + owner * half_slots + at % half_slots
    sent_to = sent_to.reshape(-1)

    local = tok - mp * vocab_part
    valid = (local >= 0) & (local < vocab_part)
    safe = jnp.clip(local, 0, vocab_part - 1)
    looked = jnp.where(valid[..., None], jnp.take(table_low, safe, axis=0), 0)
    own_cols = cube_scatter(looked).astype(BF16)
    pieces = line_exchange([own_cols[o] for o in range(n_dp)])
    x0 = jnp.zeros((rows_own, D), BF16)
    for o in range(n_dp):
        x0 = lax.dynamic_update_slice(x0, pieces[o], (0, near[o] * cols))
    x0 = x0.astype(F32)
    normed1, inverse1 = norm_forward(x0)
    h1 = cube_gather((normed1 * gains[0]).astype(BF16))
    h1_all = h1.reshape(-1, D)

    wqkv, wout, wgate, wdown = place_tiles(slot_of, slots, shapes)

    table_late = after(table_low, slots, h1)
    head_parts = lax.all_to_all(table_late.reshape(n_dp, sub, cols), "dp", 0, 0)

    half = HD // 2
    freq = ROPE_BASE ** (-jnp.arange(half).astype(F32) * 2.0 / HD)
    t_ans = context + who[:, None] * n_ans + jnp.arange(n_ans)
    t_ctx = who[:, None] * n_ctx + jnp.arange(n_ctx)

    def angles(t):
        place = (start_pos[None, :, None] + t[:, None, :]).astype(F32)
        angle = place.reshape(n_mp, -1)[..., None] * freq
        return jnp.cos(angle), jnp.sin(angle)

    cosine, sine = (jnp.concatenate(pair, axis=1) for pair in zip(angles(t_ans), angles(t_ctx)))
    cosine = jnp.concatenate([cosine] * 4, axis=-1)
    sine = jnp.concatenate([-sine, sine] * 2, axis=-1)
    t_query = t_ans.reshape(-1)
    place = (t_query[:, None], t_query[None, :])

    qkv = dot("td,de->te", h1_all, wqkv).reshape(n_mp, rows_own, 3 * width)
    ans_shape = ((n_mp, rows_ans, width), BF16)
    key_shape = ((n_mp, rows_own, width), BF16)
    o_rows, query, key, value = in_vmem(
        functools.partial(attend_kernel, items),
        "attend",
        (ans_shape, ans_shape, key_shape, key_shape),
        *(qkv, cosine, sine, *place),
    )
    o_rows = o_rows.reshape(-1, width)
    parts = dot("tw,wd->td", o_rows, wout).astype(BF16).reshape(n_mp, rows_ans, D)
    own = ((rows_ans, D), F32)
    gain_row = ((1, D), F32)
    plane = ((n_mp, rows_ans, D), BF16)
    if n_mp == 8:
        x1, h2 = exchange(
            forward_kernel, "attend_sum", 1, n_dp, True, rows_ans, (own, plane),
            *(parts, x0[:rows_ans], gains[1:2]),
        )
    else:
        x1 = x0[:rows_ans] + cube_scatter(parts)
        h2 = cube_gather((norm_forward(x1)[0] * gains[1]).astype(BF16))
    h2 = h2.reshape(-1, D)

    gate_up = dot("td,df->tf", h2, wgate)
    gate, upward = gate_up[:, :units], gate_up[:, units:]
    hidden = (jax.nn.silu(gate) * upward).astype(BF16)
    parts = dot("tf,fd->td", hidden, wdown).astype(BF16).reshape(n_mp, rows_ans, D)

    def by_line(x):
        return x.reshape(n_mp, n_dp, rows_ans).transpose(1, 0, 2).reshape(n_dp, -1, 1)

    first = mp * vocab_part + dp * sub
    if n_mp == 8:
        x2, final = exchange(
            forward_kernel, "units_sum", 2, n_dp, False, rows_ans,
            (own, ((rows_ans, D), BF16)), *(parts, x1, gains[2:3]),
        )
        final, dlogits, seen = head_call(
            n_dp,
            final,
            head_parts,
            by_line(row_target - first),
            by_line(row_scale),
        )
        lse, picked = seen[0, 0], seen[1, 0]
        dlogits = dlogits.reshape(-1, sub)
        final = final.reshape(-1, D)
    else:
        head = jnp.concatenate([head_parts[a] for a in range(n_dp)], axis=1)
        x2 = x1 + cube_scatter(parts)
        final = (norm_forward(x2)[0] * gains[2]).astype(BF16)
        final = cube_gather(jnp.stack(line_gather(final)).reshape(-1, D))
        final = final.reshape(-1, D)
        logits = dot("rd,vd->rv", final, head)
        hit = jnp.arange(sub, dtype=jnp.int32)[None, :] == (row_target - first)[:, None]
        top = jnp.max(logits, axis=1)
        total = jnp.sum(jnp.exp(logits - top[:, None]), axis=1)
        picked = jnp.sum(jnp.where(hit, logits, 0.0), axis=1)
        top, total, picked = stats_everywhere(jnp.stack([top, total, picked]), rows_ans)
        lse = top + jnp.log(total)
        dlogits = (
            row_scale[:, None] * (jnp.exp(logits - lse[:, None]) - hit.astype(F32))
        ).astype(BF16)
    loss_own = jnp.sum(row_scale[:rows_ans] * (lse - picked)[:rows_ans]) * pairs_all

    if n_mp == 8:
        grads = ((n_dp, sub, cols), BF16)
        dx2, dgain3, down_in, head_grad = exchange(
            head_back_kernel, "head_sum", 3, n_dp, True, n_dp * rows_ans,
            (own, gain_row, plane, grads),
            *(dlogits.reshape(n_mp, -1, sub), final.reshape(n_mp, -1, D), head_parts),
            *(x2, gains[2:3]),
        )
        dgain3 = dgain3[0]
    else:
        parts = dot("rv,vd->rd", dlogits, head).astype(BF16)
        mine = cube_scatter(parts.reshape(n_mp, n_dp * rows_ans, D)).astype(BF16)
        mine = line_exchange(list(mine.reshape(n_dp, rows_ans, D)))
        dfinal = sum(piece.astype(F32) for piece in mine)
        dx2, dgain3 = norm_backward(dfinal, *norm_forward(x2), gains[2])
        down_in = cube_gather(dx2.astype(BF16))
        head_grad = jnp.stack(
            [
                dot("rv,rd->vd", dlogits, final[:, a * cols : (a + 1) * cols]).astype(BF16)
                for a in range(n_dp)
            ]
        )
    down_in = down_in.reshape(-1, D)
    table_grad = lax.all_to_all(head_grad, "dp", 0, 0)
    dhidden = dot("td,fd->tf", down_in, wdown)
    sigma = jax.nn.sigmoid(gate)
    dgate_up = jnp.concatenate(
        [dhidden * upward * sigma * (1.0 + gate * (1.0 - sigma)), dhidden * gate * sigma],
        axis=-1,
    ).astype(BF16)
    parts = dot("tf,df->td", dgate_up, wgate).astype(BF16).reshape(n_mp, rows_ans, D)
    grad_down = dot("tf,td->fd", hidden, down_in).astype(BF16)
    grad_gate = dot("td,tf->df", h2, dgate_up).astype(BF16)
    if n_mp == 8:
        dx1, dgain2, out_in = exchange(
            backward_kernel, "gate_sum", 4, n_dp, False, rows_ans, (own, gain_row, plane),
            *(parts, x1, gains[1:2], dx2),
        )
        dgain2 = dgain2[0]
    else:
        dx_mlp, dgain2 = norm_backward(cube_scatter(parts), *norm_forward(x1), gains[1])
        dx1 = dx2 + dx_mlp
        out_in = cube_gather(dx1.astype(BF16))
    out_in = out_in.reshape(-1, D)
    dattended = dot("td,wd->tw", out_in, wout).astype(BF16)
    grad_out = dot("tw,td->wd", o_rows, out_in).astype(BF16)
    (dqkv,) = in_vmem(
        functools.partial(attend_back_kernel, items),
        "attend_back",
        (((n_mp, rows_own, 3 * width), BF16),),
        *(query, key, value, dattended.reshape(n_mp, rows_ans, width), cosine, sine, *place),
    )
    dqkv = dqkv.reshape(-1, 3 * width)
    dh1 = dot("te,de->td", dqkv, wqkv).astype(BF16).reshape(n_mp, rows_own, D)
    dnormed1 = cube_scatter(dh1)
    grad_qkv = dot("td,te->de", h1_all, dqkv).astype(BF16)
    dx0, dgain1 = norm_backward(dnormed1, normed1, inverse1, gains[0])
    dx0 = jnp.concatenate([dx0[:rows_ans] + dx1, dx0[rows_ans:]]).astype(BF16)

    halves = collect_tiles(sent_to, (grad_gate, grad_down), shapes, (2, 3))
    one, two = collect_tiles(
        sent_to, (grad_qkv, grad_out), shapes, (0, 1), halves, (table_grad,)
    )
    one = lax.psum_scatter(one, "dp", scatter_dimension=0, tiled=True)

    pieces = line_exchange(
        [lax.dynamic_slice_in_dim(dx0, near[o] * cols, cols, 1) for o in range(n_dp)]
    )
    two = after(two, *pieces)
    two = lax.psum_scatter(two, "dp", scatter_dimension=0, tiled=True)
    rows_back = cube_gather(jnp.stack(pieces).reshape(-1, cols)).reshape(safe.shape + (cols,))
    picked_rows = jnp.where(valid[..., None], rows_back, 0).astype(F32)
    own_table = table_grad.reshape(vocab_part, cols).astype(F32).at[safe.reshape(-1)].add(picked_rows.reshape(-1, cols))

    gain_grad = jnp.stack([dgain1, dgain2, dgain3])
    gain_total = everywhere(gain_grad, jnp.add)
    own_gain = lax.dynamic_slice_in_dim(gain_total, dp * cols, cols, 1)
    first_mp = (mp == 0).astype(F32)
    squares = jnp.sum(own_table * own_table) + first_mp * jnp.sum(own_gain * own_gain)
    if n_mp == 8:
        more = jnp.zeros((2, 8, 128), F32).at[:, 0, 0].set(jnp.stack([squares, loss_own]))
        squares_all, loss_total = jnp.sum(total_exchange(one, two, more, n_dp), axis=(1, 2))
    else:
        squares = squares + sum(jnp.sum(jnp.square(g.astype(F32))) for g in (one, two))
        more = everywhere(jnp.stack([squares, loss_own])[None], jnp.add)[0]
        squares_all, loss_total = more
    norm = jnp.sqrt(squares_all)
    factor = CLIP_NORM / jnp.maximum(norm, CLIP_NORM)
    block_new, block_copy, grad_slots, left_new, right_new = tile_step(
        factor.reshape(1, 1),
        *(one, two, block_master[0], left_stat[0], right_stat[0], left_root[0], right_root[0]),
    )
    table_new, table_moment_new, table_second_new = adam(
        table_master, table_moment, table_second, factor * own_table, LR_TABLE, DECAY_TABLE
    )
    gain_new, gain_moment_new, gain_second_new = adam(
        gain_master, gain_moment, gain_second, factor * own_gain, LR_GAIN, 0.0
    )
    return (
        loss_total,
        norm,
        block_new[None],
        block_copy[None],
        grad_slots[None],
        left_new[None],
        right_new[None],
        table_new,
        table_new.astype(BF16),
        table_moment_new,
        table_second_new,
        gain_new,
        gain_moment_new,
        gain_second_new,
    )


def solution(mesh):
    in_specs = (
        P("dp", None),
        P("dp", None),
        P(),
        P("dp"),
        P("dp", None),
        P("dp"),
        P("mp", None),
        P("mp", "dp", None, None),
        P("mp", "dp", None, None),
        P("mp", "dp", None, None),
        P("mp", "dp", None, None),
        P("mp", "dp", None, None),
        P("mp", "dp"),
        P("mp", "dp"),
        P("mp", "dp"),
        P(None, "dp"),
        P(None, "dp"),
        P(None, "dp"),
    )
    out_specs = (
        P(),
        P(),
        P("mp", "dp", None, None),
        P("mp", "dp", None, None),
        P("mp", "dp", None, None),
        P("mp", "dp", None, None),
        P("mp", "dp", None, None),
        P("mp", "dp"),
        P("mp", "dp"),
        P("mp", "dp"),
        P("mp", "dp"),
        P(None, "dp"),
        P(None, "dp"),
        P(None, "dp"),
    )
    return jax.shard_map(body, mesh=mesh, in_specs=in_specs, out_specs=out_specs, check_vma=False)
```

```python
import functools

import jax
import jax.numpy as jnp
from jax import lax
from jax.experimental import pallas as pl
from jax.experimental.pallas import tpu as pltpu
from jax.sharding import PartitionSpec as P

D = 2048
HD = 64
FF = 8192
ANS = 256
STEP = 5


EPS_NORM = 1e-05
ROPE_BASE = 130000.0
CLIP_NORM = 0.01
STAT_DECAY = 0.95
LR_MATRIX = 0.05
DECAY_MATRIX = 0.1
LR_TABLE = 0.03
DECAY_TABLE = 0.1
LR_GAIN = 0.2
ADAM_ONE = 0.9
ADAM_TWO = 0.95
ADAM_EPS = 1e-08
MASKED = -1e30
F32 = jnp.float32
BF16 = jnp.bfloat16


def dot(spec, a, b):
    return jnp.einsum(spec, a, b, preferred_element_type=F32)


def cube_bits(n):
    bits = [1 << i for i in range(n.bit_length() - 1)]
    return bits[1:] + bits[:1]


def cube_order(n):
    order = [0]
    for bit in cube_bits(n):
        order = order + [o ^ bit for o in order]
    return order


def swap(x, axis, bit):
    n = lax.axis_size(axis)
    return lax.ppermute(x, axis, [(i, i ^ bit) for i in range(n)])


def cube_gather(x):
    n = lax.axis_size("mp")
    if n != 8:
        held = x[None]
        for bit in cube_bits(n):
            held = jnp.concatenate([held, swap(held, "mp", bit)])
        return held
    half = x.shape[0] // 2
    over_x = swap(x, "mp", 2)
    over_y = swap(x, "mp", 4)
    far = jnp.concatenate([swap(over_x[:half], "mp", 4), swap(over_y[half:], "mp", 2)])
    held = jnp.stack([x, over_x, over_y, far])
    return jnp.concatenate([held, swap(held, "mp", 1)])


def cube_scatter(parts):
    n = lax.axis_size("mp")
    if n != 8:
        held = parts
        for bit in reversed(cube_bits(n)):
            keep = held.shape[0] // 2
            other = swap(held[keep:].astype(BF16), "mp", bit)
            held = held[:keep].astype(F32) + other.astype(F32)
        return held[0]
    got = swap(parts[4:], "mp", 1)
    held = (parts[:4].astype(F32) + got.astype(F32)).astype(BF16)
    half = held.shape[1] // 2
    one, two = held[:, :half], held[:, half:]
    one_x = swap(one[1::2], "mp", 2)
    two_y = swap(two[2:], "mp", 4)
    one = one[0::2].astype(F32) + one_x.astype(F32)
    two = two[:2].astype(F32) + two_y.astype(F32)
    one_y = swap(one[1].astype(BF16), "mp", 4)
    two_x = swap(two[1].astype(BF16), "mp", 2)
    return jnp.concatenate([one[0] + one_y.astype(F32), two[0] + two_x.astype(F32)])


def line_gather(x):
    return [x] + [swap(x, "dp", o) for o in range(1, lax.axis_size("dp"))]


def line_exchange(parts):
    return [parts[0]] + [swap(parts[o], "dp", o) for o in range(1, len(parts))]


def combine_stats(a, b):
    top = jnp.maximum(a[0], b[0])
    total = a[1] * jnp.exp(a[0] - top) + b[1] * jnp.exp(b[0] - top)
    return jnp.stack([top, total, a[2] + b[2]])


def everywhere(x, op):
    for axis in ("mp", "dp"):
        bit = 1
        while bit < lax.axis_size(axis):
            x = op(x, swap(x, axis, bit))
            bit *= 2
    return x


def stats_everywhere(x, rows):
    n_mp, n_dp = lax.axis_size("mp"), lax.axis_size("dp")
    bits = cube_bits(n_mp)
    split = (3,) + (2,) * len(bits) + (n_dp * rows,)
    x = x.reshape(split)
    for i, bit in enumerate(bits):
        x = combine_stats(x, jnp.flip(swap(x, "mp", bit), len(bits) - i))
    x = x.reshape(3, n_mp, n_dp, rows)
    total = x
    for o, other in enumerate(line_gather(x)):
        if o:
            order = [e ^ o for e in range(n_dp)]
            total = combine_stats(total, jnp.stack([other[:, :, e] for e in order], axis=2))
    return total.reshape(3, -1)


def peer_copy(src, dst, sems, k, **device):
    return pltpu.make_async_remote_copy(
        src_ref=src,
        dst_ref=dst,
        send_sem=sems.at[0, k],
        recv_sem=sems.at[1, k],
        device_id=device,
        device_id_type=pl.DeviceIdType.MESH,
    )


def greet(n_dp, bits=(1, 2, 4)):
    me = lax.axis_index("mp")
    a = lax.axis_index("dp")
    barrier = pltpu.get_barrier_semaphore()
    partners = [{"mp": me ^ bit} for bit in bits]
    partners += [{"dp": a ^ o} for o in range(1, n_dp)]
    for partner in partners:
        pl.semaphore_signal(barrier, 1, device_id=partner, device_id_type=pl.DeviceIdType.MESH)
    pl.semaphore_wait(barrier, len(partners))


def by_rows(count, step):
    @pl.loop(0, count // 16)
    def _(i):
        step(pl.multiple_of(i * 16, 16))


class PlaneSum:
    def __init__(self, parts, own, core, held, near, last, sems, first, blocks):
        me = lax.axis_index("mp")
        self.refs = parts, own, core, held, near, last
        self.rows = own.shape[0] // blocks
        self.half = half = self.rows // 2
        self.at_core = []
        self.blocks = []
        for b in range(blocks):
            whole = pl.ds(b * self.rows, self.rows)
            top, low = pl.ds(b * self.rows, half), pl.ds(b * self.rows + half, half)
            spot = pl.ds(b * half, half)
            k = first + 7 * b
            self.at_core.append(
                peer_copy(parts.at[4:8, whole], core.at[:, whole], sems, k, mp=me ^ 1)
            )
            sends = (
                (3, top, near, 0, 2),
                (3, low, near, 1, 4),
                (1, top, near, 2, 2),
                (2, low, near, 3, 4),
                (2, top, last, 0, 4),
                (1, low, last, 1, 2),
            )
            self.blocks.append(
                [
                    peer_copy(held.at[s, rows], to.at[at, spot], sems, k + 1 + e, mp=me ^ bit)
                    for e, (s, rows, to, at, bit) in enumerate(sends)
                ]
            )

    def first_sends(self, b):
        self.at_core[b].wait_recv()
        parts, _, core, held, _, _ = self.refs
        copies = self.blocks[b]
        for s, sent in ((3, copies[:2]), (1, copies[2:3]), (2, copies[3:4])):

            def add(at, s=s):
                rows = pl.ds(b * self.rows + at, 16)
                value = parts[s, rows].astype(F32) + core[s, rows].astype(F32)
                held[s, rows] = value.astype(BF16)

            by_rows(self.rows, add)
            for copy in sent:
                copy.start()

    def second_sends(self, b):
        _, _, _, held, near, _ = self.refs
        copies = self.blocks[b]
        for e, s, offset in ((0, 2, 0), (1, 1, self.half)):
            copies[e].wait_recv()

            def add(at, e=e, s=s, offset=offset):
                rows = pl.ds(b * self.rows + offset + at, 16)
                value = held[s, rows].astype(F32) + near[e, pl.ds(b * self.half + at, 16)].astype(F32)
                held[s, rows] = value.astype(BF16)

            by_rows(self.half, add)
            copies[4 + e].start()

    def finish(self, b):
        parts, own, core, _, near, last = self.refs
        for copy in self.blocks[b][2:]:
            copy.wait_recv()

        def total(at):
            spot = pl.ds(b * self.half + at, 16)
            for e, offset in ((0, 0), (1, self.half)):
                rows = pl.ds(b * self.rows + offset + at, 16)
                own[rows] = (
                    (parts[0, rows].astype(F32) + core[0, rows].astype(F32))
                    + near[2 + e, spot].astype(F32)
                    + last[e, spot].astype(F32)
                )

        by_rows(self.half, total)

    def close(self):
        for core, copies in zip(self.at_core, self.blocks):
            core.wait_send()
            for copy in copies:
                copy.wait_send()

    def run(self):
        for b in range(len(self.blocks)):
            self.at_core[b].start()
        for step in (self.first_sends, self.second_sends, self.finish):
            for b in range(len(self.blocks)):
                step(b)
        self.close()


class PlaneSpread:
    def __init__(self, x, out, sems, k, start, rows):
        me = lax.axis_index("mp")
        half = rows // 2
        top, low, whole = pl.ds(start, half), pl.ds(start + half, half), pl.ds(start, rows)
        self.own = x, out, start, rows

        def copy(src, slot, part, e, bit):
            return peer_copy(src, out.at[slot, part], sems, k + e, mp=me ^ bit)

        self.x_top = copy(x.at[top], 1, top, 0, 2)
        self.y_low = copy(x.at[low], 2, low, 1, 4)
        self.x_low = copy(x.at[low], 1, low, 2, 2)
        self.y_top = copy(x.at[top], 2, top, 3, 4)
        self.core = copy(x.at[whole], 4, whole, 4, 1)
        self.far_y = copy(out.at[1, top], 3, top, 5, 4)
        self.far_x = copy(out.at[2, low], 3, low, 6, 2)
        self.to_core = {
            (s, r): copy(out.at[s, part], 4 + s, part, 7 + 2 * (s - 1) + r, 1)
            for s in (1, 2, 3)
            for r, part in enumerate((top, low))
        }

    def begin(self):
        for c in (self.x_top, self.y_low, self.x_low, self.y_top, self.core):
            c.start()
        x, out, start, rows = self.own

        def keep(at):
            part = pl.ds(start + at, 16)
            out[0, part] = x[part]

        by_rows(rows, keep)

    def relay(self):
        self.x_top.wait_recv()
        self.far_y.start()
        self.to_core[1, 0].start()
        self.y_low.wait_recv()
        self.far_x.start()
        self.to_core[2, 1].start()
        self.x_low.wait_recv()
        self.to_core[1, 1].start()
        self.y_top.wait_recv()
        self.to_core[2, 0].start()

    def relay_far(self):
        self.far_y.wait_recv()
        self.to_core[3, 0].start()
        self.far_x.wait_recv()
        self.to_core[3, 1].start()

    def arrive(self):
        self.core.wait_recv()
        for c in self.to_core.values():
            c.wait_recv()

    def close(self):
        sent = (self.x_top, self.y_low, self.x_low, self.y_top, self.core, self.far_y, self.far_x)
        for c in (*sent, *self.to_core.values()):
            c.wait_send()

    def run(self):
        self.begin()
        self.relay()
        self.relay_far()
        self.arrive()
        self.close()


def norm_step(x, gain):
    return (x * lax.rsqrt(jnp.mean(x * x, axis=1, keepdims=True) + EPS_NORM)) * gain


def norm_back_step(grad, x, gain):
    inverse = lax.rsqrt(jnp.mean(x * x, axis=1, keepdims=True) + EPS_NORM)
    normed = x * inverse
    scaled = grad * gain
    dx = inverse * (scaled - normed * jnp.mean(scaled * normed, axis=1, keepdims=True))
    return dx, jnp.sum(grad * normed, axis=0, keepdims=True)


def by_columns(step, width=512):
    for c in range(D // width):
        step(pl.ds(c * width, width))


def forward_step(refs, res, gain, x_out):
    own, core, held, near, last, parts, _, sems = refs
    PlaneSum(parts, own, core, held, near, last, sems, 0, 1).run()
    x = res[...] + own[...]
    x_out[...] = x
    return norm_step(x, gain[...]).astype(BF16)


def attend_sum_kernel(o, wout, res, gain, x_out, out, *refs):
    *_, parts, mine, sems = refs
    greet(1)

    def make(c):
        parts[:, :, c] = mm(flat(o[...]), wout[:, c]).astype(BF16).reshape(8, -1, c.size)

    by_columns(make)
    mine[...] = forward_step(refs, res, gain, x_out)
    PlaneSpread(mine, out, sems, 7, 0, mine.shape[0]).run()


def units_sum_kernel(h2, wgate, wdown, res, gain, x_out, gate_up, hidden, out, *refs):
    *_, parts, _, _ = refs
    units = wdown.shape[0]
    greet(1)
    x = flat(h2[...])
    step = min(units, 512)
    for c in range(2 * units // step):
        at = pl.ds(c * step, step)
        gate_up[:, at] = mm(x, wgate[:, at])
    for c in range(units // step):
        at, up = pl.ds(c * step, step), pl.ds(units + c * step, step)
        gate = gate_up[:, at]
        hidden[:, at] = (gate / (1.0 + jnp.exp(-gate)) * gate_up[:, up]).astype(BF16)

    def make(c):
        parts[:, :, c] = mm(hidden[...], wdown[:, c]).astype(BF16).reshape(8, -1, c.size)

    by_columns(make)
    out[...] = forward_step(refs, res, gain, x_out)


def gate_sum_kernel(
    down_in, wdown, wgate, gate_up, x_in, gain, res, dx_out, dgain, dgate_up, out, *refs
):
    own, core, held, near, last, parts, mine, sems = refs
    units = wdown.shape[0]
    greet(1)
    x = flat(down_in[...])
    step = min(units, 512)
    for c in range(units // step):
        at, up = pl.ds(c * step, step), pl.ds(units + c * step, step)
        grad = mm(x, wdown[at, :], CONTRACT_LAST)
        gate, upward = gate_up[:, at], gate_up[:, up]
        sigma = 1.0 / (1.0 + jnp.exp(-gate))
        dgate = grad * upward * sigma * (1.0 + gate * (1.0 - sigma))
        dgate_up[:, at] = dgate.astype(BF16)
        dgate_up[:, up] = (grad * gate * sigma).astype(BF16)

    def make(c):
        value = mm(dgate_up[...], wgate[c, :], CONTRACT_LAST)
        parts[:, :, c] = value.astype(BF16).reshape(8, -1, c.size)

    by_columns(make)
    PlaneSum(parts, own, core, held, near, last, sems, 0, 1).run()
    dx, dg = norm_back_step(own[...], x_in[...], gain[...])
    dx = dx + res[...]
    dx_out[...] = dx
    dgain[...] = dg
    mine[...] = dx.astype(BF16)
    PlaneSpread(mine, out, sems, 7, 0, mine.shape[0]).run()


def head_kernel(n_dp, rows_ref, target_ref, scale_ref, *refs):
    head_ref, final_out, dlogits, seen, final, head, mine, logits, *refs = refs
    stats, plane, mid, line, sems, own_sems = refs
    rows, vocab = rows_ref.shape[0], logits.shape[2]
    wide = head.shape[2]
    load = pltpu.make_async_copy(head_ref, head, own_sems.at[0])
    store = pltpu.make_async_copy(final, final_out, own_sems.at[1])
    load.start()
    a = lax.axis_index("dp")
    greet(n_dp, range(1, 8))
    mine[pl.ds(0, rows)] = rows_ref[...]
    block = [pl.ds(o * rows, rows) for o in range(4)]
    across = [
        peer_copy(rows_ref, mine.at[block[1]], sems, 53, dp=a ^ 1),
        peer_copy(rows_ref, mine.at[block[2]], sems, 54, dp=a ^ 2),
        peer_copy(mine.at[block[2]], mine.at[block[3]], sems, 55, dp=a ^ 1),
    ]
    across[0].start()
    across[1].start()
    blocks = [PlaneSpread(mine, final, sems, 13 * o, o * rows, rows) for o in range(n_dp)]
    tile = 512 if vocab % 512 == 0 else vocab

    def use(b):
        part = pl.ds(b * rows, rows)

        @pl.loop(0, vocab // tile)
        def _(v):
            at = pl.ds(pl.multiple_of(v * tile, tile), tile)
            value = None
            for p in range(n_dp):
                x = flat(final[:, part, pl.ds(p * wide, wide)])
                term = mm(x, head[p, at, :], CONTRACT_LAST)
                value = term if value is None else value + term
            logits[:, part, at] = value.reshape(8, rows, tile)

        value = flat(logits[:, part, :])
        top = jnp.max(value, axis=1, keepdims=True)
        expo = jnp.sum(jnp.exp(value - top), axis=1, keepdims=True)
        column = lax.broadcasted_iota(jnp.int32, value.shape, 1)
        hit = jnp.sum(jnp.where(column == target_ref[b], value, 0.0), axis=1, keepdims=True)
        lane = lax.broadcasted_iota(jnp.int32, (8 * rows, 128), 1)
        packed = jnp.where(lane == 0, top, jnp.where(lane == 1, expo, hit)).T
        for k in range(3):
            stats[k, b : b + 1, :] = packed[k : k + 1]

    blocks[0].begin()
    across[0].wait_recv()
    blocks[1].begin()
    blocks[0].relay()
    across[1].wait_recv()
    across[2].start()
    blocks[2].begin()
    blocks[1].relay()
    blocks[0].relay_far()
    across[2].wait_recv()
    blocks[3].begin()
    blocks[2].relay()
    blocks[1].relay_far()
    blocks[0].arrive()
    load.wait()
    use(0)
    blocks[3].relay()
    blocks[2].relay_far()
    blocks[1].arrive()
    use(1)
    blocks[3].relay_far()
    blocks[2].arrive()
    use(2)
    blocks[3].arrive()
    store.start()
    use(3)
    stats_steps(n_dp, stats, seen, plane, mid, line, sems, 14 * n_dp)

    @pl.loop(0, n_dp)
    def _(b):
        part = pl.ds(pl.multiple_of(b * rows, rows), rows)
        lse = jnp.broadcast_to(seen[0, pl.ds(b, 1), :], (128, 8 * rows)).T[:, :1]
        value = flat(logits[:, part, :])
        column = lax.broadcasted_iota(jnp.int32, value.shape, 1)
        hit = (column == target_ref[b]).astype(F32)
        grad = (scale_ref[b] * (jnp.exp(value - lse) - hit)).astype(BF16)
        dlogits[:, part, :] = grad.reshape(8, rows, vocab)

    for copy in across:
        copy.wait_send()
    for each in blocks:
        each.close()
    store.wait()


def head_call(n_dp, rows, head, target, scale):
    total = n_dp * rows.shape[0]
    vocab = head.shape[1]
    stats = (3, n_dp, 8 * rows.shape[0])
    outs = [((8, total, D), BF16), ((8, total, vocab), BF16), ((2,) + stats[1:], F32)]
    anywhere = pl.BlockSpec(memory_space=pl.ANY)
    return pl.pallas_call(
        functools.partial(head_kernel, n_dp),
        out_shape=[jax.ShapeDtypeStruct(shape, dtype) for shape, dtype in outs],
        in_specs=[pl.BlockSpec(memory_space=pltpu.VMEM)] * 3 + [anywhere],
        out_specs=[anywhere] + [pl.BlockSpec(memory_space=pltpu.VMEM)] * 2,
        scratch_shapes=[
            pltpu.VMEM((8, total, D), BF16),
            pltpu.VMEM(head.shape, BF16),
            pltpu.VMEM((total, D), BF16),
            pltpu.VMEM((8, total, vocab), F32),
            pltpu.VMEM(stats, F32),
            pltpu.VMEM((7,) + stats, F32),
            pltpu.VMEM(stats, F32),
            pltpu.VMEM((n_dp - 1,) + stats, F32),
            pltpu.SemaphoreType.DMA((2, 14 * n_dp + 6 + n_dp)),
            pltpu.SemaphoreType.DMA((2,)),
        ],
        compiler_params=pltpu.CompilerParams(
            collective_id=5, has_side_effects=True, vmem_limit_bytes=56 << 20
        ),
        cost_estimate=pl.CostEstimate(flops=0, bytes_accessed=1 << 20, transcendentals=0),
        name="head",
    )(rows, target, scale, head)


def head_back_kernel(n_dp, cut, dlogits, head, x_in, gain, final_ref, *refs):
    dx_out, dgain, out, early, grads, own, core, held, near, last, parts, *refs = refs
    mine, sent, got, final, ready, sems, own_sem = refs
    a = lax.axis_index("dp")
    rows = x_in.shape[0]
    _, vocab, wide = head.shape
    load = pltpu.make_async_copy(final_ref, final, own_sem)
    load.start()
    greet(n_dp)
    plan = PlaneSum(parts, own, core, held, near, last, sems, 0, n_dp)

    def make(b):
        part = pl.ds(b * rows, rows)
        x = flat(dlogits[:, part, :])
        for p in range(n_dp):
            value = mm(x, head[p]).astype(BF16)
            parts[:, part, pl.ds(p * wide, wide)] = value.reshape(8, rows, wide)
        plan.at_core[b].start()

    def table_part(p, first, number):
        x = flat(final[:, :, pl.ds(pl.multiple_of(p * wide, 128), wide)])
        return mm(flat(dlogits[:, :, pl.ds(first, number)]), x, CONTRACT_FIRST).astype(BF16)

    left = [(p, v) for p in range(n_dp) for v in range(cut, vocab, 256)]

    def fill(count):
        for _ in range(min(count, len(left))):
            p, v = left.pop(0)
            grads[p, pl.ds(v - cut, 256), :] = table_part(p, v, 256)

    first_rows = [
        peer_copy(ready.at[o - 1], early.at[a], sems, 12 + 8 * n_dp + o, dp=a ^ o)
        for o in range(1, n_dp)
    ]
    across = {
        b: peer_copy(
            sent.at[pl.ds(b * rows, rows)], got.at[b - 1], sems, 13 + 7 * n_dp + b, dp=a ^ b
        )
        for b in range(1, n_dp)
    }

    def finish(b):
        plan.finish(b)
        if b:
            part = pl.ds(b * rows, rows)
            sent[part] = own[part].astype(BF16)
            across[b].start()

    make(2)
    load.wait()
    for o in range(1, n_dp):
        ready[o - 1] = table_part(a ^ o, 0, cut)
        first_rows[o - 1].start()
    plan.first_sends(2)
    make(3)
    plan.second_sends(2)
    plan.first_sends(3)
    make(1)
    early[a] = table_part(a, 0, cut)
    plan.first_sends(1)
    plan.second_sends(3)
    make(0)
    finish(2)
    plan.first_sends(0)
    fill(2)
    plan.second_sends(1)
    finish(3)
    fill(6)
    plan.second_sends(0)
    finish(1)
    fill(7)
    finish(0)
    fill(len(left))
    for copy in first_rows:
        copy.wait()
    for copy in across.values():
        copy.wait()
    grad = own[pl.ds(0, rows)]
    for o in range(1, n_dp):
        grad = grad + got[o - 1].astype(F32)
    dx, dg = norm_back_step(grad, x_in[...], gain[...])
    dx_out[...] = dx
    dgain[...] = dg
    mine[...] = dx.astype(BF16)
    PlaneSpread(mine, out, sems, 7 * n_dp, 0, rows).run()
    plan.close()


def input_back_kernel(dqkv, wqkv, h1, x_in, gain, res, dx_out, dgain, grads, *refs):
    own, core, held, near, last, parts, _, sems = refs
    rows = res.shape[0]
    blocks = x_in.shape[0] // rows
    greet(1)
    plan = PlaneSum(parts, own, core, held, near, last, sems, 0, blocks)

    def make(b):
        part = pl.ds(b * rows, rows)
        x = flat(dqkv[:, part, :])
        for c in range(D // 512):
            value = mm(x, wqkv[pl.ds(c * 512, 512), :], CONTRACT_LAST).astype(BF16)
            parts[:, part, pl.ds(c * 512, 512)] = value.reshape(8, rows, 512)
        plan.at_core[b].start()

    left = list(range(D // 512))

    def fill():
        c = pl.ds(left.pop(0) * 512, 512)
        grads[c, :] = mm(flat(h1[:, :, c]), flat(dqkv[...]), CONTRACT_FIRST).astype(BF16)

    def close(b):
        plan.finish(b)
        part = pl.ds(b * rows, rows)
        dx, dg = norm_back_step(own[part], x_in[part], gain[...])
        if b == 0:
            dx = dx + res[...]
            dgain[...] = dg
        else:
            dgain[...] += dg
        dx_out[part] = dx.astype(BF16)

    make(0)
    make(1)
    plan.first_sends(0)
    make(2)
    plan.first_sends(1)
    plan.second_sends(0)
    make(3)
    plan.first_sends(2)
    plan.second_sends(1)
    plan.first_sends(3)
    fill()
    close(0)
    plan.second_sends(2)
    fill()
    close(1)
    plan.second_sends(3)
    fill()
    close(2)
    fill()
    close(3)
    plan.close()


def exchange(kernel, name, number, n_dp, total, outs, *args, more=(), sems=20, far=0):
    half = total // 2
    rows = outs[0][0][0]
    scratch = [
        pltpu.VMEM((total, D), F32),
        pltpu.VMEM((4, total, D), BF16),
        pltpu.VMEM((4, total, D), BF16),
        pltpu.VMEM((4, half, D), BF16),
        pltpu.VMEM((2, half, D), BF16),
        pltpu.VMEM((8, total, D), BF16),
        pltpu.VMEM((rows, D), BF16),
    ]
    scratch += [pltpu.VMEM(shape, BF16) for shape in more]
    return pl.pallas_call(
        kernel,
        out_shape=[jax.ShapeDtypeStruct(shape, dtype) for shape, dtype in outs],
        in_specs=[pl.BlockSpec(memory_space=pltpu.VMEM)] * (len(args) - far)
        + [pl.BlockSpec(memory_space=pl.ANY)] * far,
        out_specs=[pl.BlockSpec(memory_space=pltpu.VMEM)] * len(outs),
        scratch_shapes=scratch
        + [pltpu.SemaphoreType.DMA((2, sems))]
        + [pltpu.SemaphoreType.DMA] * far,
        compiler_params=pltpu.CompilerParams(
            collective_id=number, has_side_effects=True, vmem_limit_bytes=62 << 20
        ),
        cost_estimate=pl.CostEstimate(flops=0, bytes_accessed=1 << 10, transcendentals=0),
        name=name,
    )(*args)


def stats_steps(n_dp, x_ref, out_ref, plane, mid, line, sems, first):
    me = lax.axis_index("mp")
    a = lax.axis_index("dp")
    order = cube_order(8)
    rows = x_ref.shape[2] // 8
    copies = [
        peer_copy(x_ref, plane.at[s - 1], sems, first + s - 1, mp=me ^ order[s])
        for s in range(1, 8)
    ]
    for copy in copies:
        copy.start()

    def join(have, new):
        top = jnp.maximum(have[0], new[0])
        total = have[1] * jnp.exp(have[0] - top) + new[1] * jnp.exp(new[0] - top)
        return top, total, have[2] + new[2]

    have = tuple(x_ref[k] for k in range(3))
    for s in range(1, 8):
        copies[s - 1].wait_recv()
        got = [plane[s - 1, k] for k in range(3)]
        got = [
            jnp.concatenate([v[:, (e ^ s) * rows : (e ^ s) * rows + rows] for e in range(8)], axis=1)
            for v in got
        ]
        have = join(have, got)
    for k in range(3):
        mid[k] = have[k]
    across = [
        peer_copy(mid, line.at[o - 1], sems, first + 6 + o, dp=a ^ o) for o in range(1, n_dp)
    ]
    for copy in across:
        copy.start()
    for o in range(1, n_dp):
        across[o - 1].wait_recv()
        got = [line[o - 1, k] for k in range(3)]
        got = [jnp.concatenate([v[e ^ o : (e ^ o) + 1] for e in range(n_dp)], axis=0) for v in got]
        have = join(have, got)
    out_ref[0] = have[0] + jnp.log(have[1])
    out_ref[1] = have[2]
    for copy in copies + across:
        copy.wait_send()


def total_kernel(n_dp, slots_ref, more_ref, out_ref, plane, line, sems):
    me = lax.axis_index("mp")
    a = lax.axis_index("dp")
    greet(n_dp, range(1, 8))

    def add(k, have):
        g = slots_ref[pl.ds(k * 8, 8)].astype(F32)
        return have + jnp.sum((g * g).reshape(-1, 8, 128), axis=0)

    start = jnp.zeros((8, 128), F32)
    plane[me, 0] = lax.fori_loop(0, slots_ref.shape[0] // 8, add, start) + more_ref[0]
    plane[me, 1] = more_ref[1]
    copies = [peer_copy(plane.at[me], plane.at[me], sems, k - 1, mp=me ^ k) for k in range(1, 8)]
    for copy in copies:
        copy.start()
    for copy in copies:
        copy.wait()
    line[a] = jnp.sum(plane[...], axis=0)
    across = [
        peer_copy(line.at[a], line.at[a], sems, 6 + o, dp=a ^ o)
        for o in range(1, n_dp)
    ]
    for copy in across:
        copy.start()
    for copy in across:
        copy.wait()
    out_ref[...] = jnp.sum(line[...], axis=0)


def total_exchange(slots, more, n_dp):
    return pl.pallas_call(
        functools.partial(total_kernel, n_dp),
        out_shape=jax.ShapeDtypeStruct(more.shape, F32),
        in_specs=[pl.BlockSpec(memory_space=pltpu.VMEM)] * 2,
        out_specs=pl.BlockSpec(memory_space=pltpu.VMEM),
        scratch_shapes=[
            pltpu.VMEM((8,) + more.shape, F32),
            pltpu.VMEM((n_dp,) + more.shape, F32),
            pltpu.SemaphoreType.DMA((2, 6 + n_dp)),
        ],
        compiler_params=pltpu.CompilerParams(collective_id=6, has_side_effects=True),
        name="total",
    )(slots, more)


def mat_shapes(n_mp):
    width, units = D // n_mp, FF // n_mp
    return ((D, 3 * width), (width, D), (D, 2 * units), (units, D))


def each_tile(shape, size, first, step):
    rows, cols = shape

    @pl.loop(0, rows // size)
    def _(r):
        row = pl.ds(pl.multiple_of(r * size, size), size)
        for c in range(cols // size):
            step(first + r * (cols // size) + c, (row, pl.ds(c * size, size)))


def first_tiles(shapes, size):
    firsts = [0]
    for rows, cols in shapes:
        firsts.append(firsts[-1] + rows * cols // (size * size))
    return firsts


def place_kernel(shapes, slot_ref, slots_ref, *refs):
    count = len(shapes)
    outs, mats, sems = refs[:count], refs[count : 2 * count], refs[-1]
    size = slots_ref.shape[1]
    for k, (shape, first) in enumerate(zip(shapes, first_tiles(shapes, size))):

        def fetch(tile, view, k=k):
            pltpu.make_async_copy(
                slots_ref.at[slot_ref[tile]], mats[k].at[view], sems.at[0, k]
            ).start()

        each_tile(shape, size, first, fetch)
    for k in range(count):
        pltpu.make_async_copy(mats[k], mats[k], sems.at[0, k]).wait()
        pltpu.make_async_copy(mats[k], outs[k], sems.at[1, k]).start()
    for k in range(count):
        pltpu.make_async_copy(mats[k], outs[k], sems.at[1, k]).wait()


def place_tiles(slot_of, slots, shapes):
    anywhere = pl.BlockSpec(memory_space=pl.ANY)
    return pl.pallas_call(
        functools.partial(place_kernel, shapes),
        out_shape=[jax.ShapeDtypeStruct(shape, slots.dtype) for shape in shapes],
        in_specs=[pl.BlockSpec(memory_space=pltpu.SMEM), anywhere],
        out_specs=[anywhere] * len(shapes),
        scratch_shapes=[pltpu.VMEM(shape, slots.dtype) for shape in shapes]
        + [pltpu.SemaphoreType.DMA((2, len(shapes)))],
        compiler_params=pltpu.CompilerParams(vmem_limit_bytes=40 << 20),
        cost_estimate=pl.CostEstimate(flops=0, bytes_accessed=1 << 20, transcendentals=0),
        name="place_tiles",
    )(slot_of, slots)


def collect_kernel(shapes, chosen, slot_ref, *refs):
    mats = refs[: len(chosen)]
    slots_ref, sem = refs[-2:]
    size = slots_ref.shape[1]
    firsts = first_tiles(shapes, size)
    for k, ref in zip(chosen, mats):

        def send(tile, view, ref=ref):
            pltpu.make_async_copy(ref.at[view], slots_ref.at[slot_ref[tile]], sem).start()

        each_tile(shapes[k], size, firsts[k], send)
    for ref in mats:
        pltpu.make_async_copy(ref, ref, sem).wait()


def collect_tiles(slot_of, mats, shapes, chosen, given=()):
    size = 128
    anywhere = pl.BlockSpec(memory_space=pl.ANY)
    return pl.pallas_call(
        functools.partial(collect_kernel, shapes, chosen),
        out_shape=jax.ShapeDtypeStruct((slot_of.shape[0], size, size), BF16),
        in_specs=[pl.BlockSpec(memory_space=pltpu.SMEM)]
        + [pl.BlockSpec(memory_space=pltpu.VMEM)] * len(mats)
        + [anywhere] * len(given),
        out_specs=anywhere,
        scratch_shapes=[pltpu.SemaphoreType.DMA],
        compiler_params=pltpu.CompilerParams(vmem_limit_bytes=40 << 20),
        input_output_aliases={1 + len(mats): 0} if given else {},
        cost_estimate=pl.CostEstimate(flops=0, bytes_accessed=1 << 20, transcendentals=0),
        name="collect_tiles",
    )(slot_of, *mats, *given)


def after(x, *others):
    anywhere = pl.BlockSpec(memory_space=pl.ANY)
    return pl.pallas_call(
        lambda *refs: None,
        out_shape=jax.ShapeDtypeStruct(x.shape, x.dtype),
        in_specs=[anywhere] * (1 + len(others)),
        out_specs=anywhere,
        input_output_aliases={0: 0},
        cost_estimate=pl.CostEstimate(flops=0, bytes_accessed=0, transcendentals=0),
        name="after",
    )(x, *others)


def split(x):
    high = x.astype(BF16)
    return high, (x - high.astype(F32)).astype(BF16)


def adam(master, moment, second, grad, rate, decay):
    moment_new = ADAM_ONE * moment + (1.0 - ADAM_ONE) * grad
    second_new = ADAM_TWO * second + (1.0 - ADAM_TWO) * grad * grad
    corrected = (
        moment_new
        / (1.0 - ADAM_ONE**STEP)
        / (jnp.sqrt(second_new / (1.0 - ADAM_TWO**STEP)) + ADAM_EPS)
    )
    return (master - rate * (corrected + decay * master), moment_new, second_new)


def owner_step_kernel(steps, factor_ref, *refs):
    g_ref, master, left, right, l_root, r_root = refs[:6]
    t_grad, t_master, t_moment, t_second = refs[6:10]
    new, copy, grad, left_new, right_new = refs[10:15]
    t_new, t_copy, t_moment_new, t_second_new = refs[15:]
    factor = factor_ref[0, 0]

    @pl.when(pl.program_id(0) < steps)
    def _():
        for k in range(g_ref.shape[0]):
            g = g_ref[k]
            grad[k] = factor * g.astype(F32)
            outer = (mm(g, g, CONTRACT_LAST) * factor) * factor
            inner = (mm(g, g, CONTRACT_FIRST) * factor) * factor
            left_new[k] = STAT_DECAY * left[k] + (1.0 - STAT_DECAY) * outer
            right_new[k] = STAT_DECAY * right[k] + (1.0 - STAT_DECAY) * inner
            l_high, l_low = split(l_root[k])
            r_high, r_low = split(r_root[k])
            t_high, t_low = split((mm(l_high, g) + mm(l_low, g)) * factor)
            direction = mm(t_high, r_high) + (mm(t_low, r_high) + mm(t_high, r_low))
            value = master[k] - LR_MATRIX * (direction + DECAY_MATRIX * master[k])
            new[k] = value
            copy[k] = value.astype(BF16)

    @pl.when(pl.program_id(0) >= steps)
    def _():
        value, moment, second = adam(
            t_master[...],
            t_moment[...],
            t_second[...],
            factor * t_grad[...],
            LR_TABLE,
            DECAY_TABLE,
        )
        t_new[...] = value
        t_copy[...] = value.astype(BF16)
        t_moment_new[...] = moment
        t_second_new[...] = second


def owner_step(factor, tiles, table):
    number, size, _ = tiles[0].shape
    rows, cols = table[0].shape
    group, band = 16, 512
    steps = number // group

    tile = pl.BlockSpec((group, size, size), lambda i: (jnp.minimum(i, steps - 1), 0, 0))
    part = pl.BlockSpec((band, cols), lambda i: (jnp.maximum(i - steps, 0), 0))
    kinds = (F32, BF16, F32, F32, F32)
    out_shape = [jax.ShapeDtypeStruct((number, size, size), kind) for kind in kinds]
    out_shape += [jax.ShapeDtypeStruct((rows, cols), kind) for kind in kinds[:4]]
    return pl.pallas_call(
        functools.partial(owner_step_kernel, steps),
        grid=(steps + rows // band,),
        out_shape=out_shape,
        in_specs=[pl.BlockSpec(memory_space=pltpu.SMEM)] + [tile] * 6 + [part] * 4,
        out_specs=[tile] * 5 + [part] * 4,
        compiler_params=pltpu.CompilerParams(vmem_limit_bytes=56 << 20),
        name="owner_step",
    )(factor, *tiles, *table)


CONTRACT_LAST = (((1,), (1,)), ((), ()))
CONTRACT_FIRST = (((0,), (0,)), ((), ()))


def mm(a, b, dims=(((1,), (0,)), ((), ()))):
    return lax.dot_general(a, b, dims, preferred_element_type=F32)


def turn(x, cosine, sine):
    lane = lax.broadcasted_iota(jnp.int32, x.shape, 1)
    other = jnp.where(
        lax.rem(lane, HD) < HD // 2, pltpu.roll(x, 128 - HD // 2, 1), pltpu.roll(x, HD // 2, 1)
    )
    return x * cosine + other * sine


def flat(x):
    return x.reshape(x.shape[0] * x.shape[1], x.shape[2])


def head_probs(q, k_ctx, k_ans, causal):
    s_ctx = mm(q, k_ctx, CONTRACT_LAST) * HD ** (-0.5)
    s_ans = jnp.where(causal, mm(q, k_ans, CONTRACT_LAST) * HD ** (-0.5), MASKED)
    top = jnp.maximum(
        jnp.max(s_ctx, axis=1, keepdims=True), jnp.max(s_ans, axis=1, keepdims=True)
    )
    e_ctx = jnp.exp(s_ctx - top)
    e_ans = jnp.exp(s_ans - top)
    total = jnp.sum(e_ctx, axis=1, keepdims=True) + jnp.sum(e_ans, axis=1, keepdims=True)
    return e_ctx / total, e_ans / total


def attend_kernel(items, h1_ref, w_ref, cos_ref, sin_ref, col_ref, row_ref, *outs):
    o_ref, qo_ref, ko_ref, vo_ref, qkv_ref = outs

    @pl.loop(0, h1_ref.shape[0])
    def _(s):
        qkv_ref[s] = mm(h1_ref[s], w_ref[...])

    n, rows_ans, width = o_ref.shape
    n_ans = rows_ans // items
    n_ctx = qkv_ref.shape[1] // items - n_ans
    causal = col_ref[...] >= row_ref[...]
    lane = lax.broadcasted_iota(jnp.int32, (1, 128), 1)

    for item in range(items):
        ans = pl.ds(item * n_ans, n_ans)
        ctx = pl.ds(rows_ans + item * n_ctx, n_ctx)
        turns = [(flat(cos_ref[:, r]), flat(sin_ref[:, r])) for r in (ans, ctx)]
        for g in range(width // 128):
            lanes = pl.ds(g * 128, 128)
            klanes = pl.ds(width + g * 128, 128)
            vlanes = pl.ds(2 * width + g * 128, 128)
            q = turn(flat(qkv_ref[:, ans, lanes]), *turns[0]).astype(BF16)
            k_ans = turn(flat(qkv_ref[:, ans, klanes]), *turns[0]).astype(BF16)
            k_ctx = turn(flat(qkv_ref[:, ctx, klanes]), *turns[1]).astype(BF16)
            v_ans = flat(qkv_ref[:, ans, vlanes]).astype(BF16)
            v_ctx = flat(qkv_ref[:, ctx, vlanes]).astype(BF16)
            qo_ref[:, ans, lanes] = q.reshape(n, n_ans, 128)
            ko_ref[:, ans, lanes] = k_ans.reshape(n, n_ans, 128)
            ko_ref[:, ctx, lanes] = k_ctx.reshape(n, n_ctx, 128)
            vo_ref[:, ans, lanes] = v_ans.reshape(n, n_ans, 128)
            vo_ref[:, ctx, lanes] = v_ctx.reshape(n, n_ctx, 128)
            got = []
            for first in (True, False):
                own = (lane < HD) == first
                p_ctx, p_ans = head_probs(jnp.where(own, q, 0), k_ctx, k_ans, causal)
                got.append(mm(p_ctx.astype(BF16), v_ctx) + mm(p_ans.astype(BF16), v_ans))
            o = jnp.where(lane < HD, got[0], got[1]).astype(BF16)
            o_ref[:, ans, lanes] = o.reshape(n, n_ans, 128)


def attend_back_kernel(items, *refs):
    q_ref, k_ref, v_ref, dx_ref, w_ref, cos_ref, sin_ref, col_ref, row_ref, d_ref, do_ref = refs
    n, rows_ans, width = q_ref.shape
    do_ref[...] = mm(flat(dx_ref[...]), w_ref[...], CONTRACT_LAST).astype(BF16).reshape(q_ref.shape)
    n_ans = rows_ans // items
    n_ctx = k_ref.shape[1] // items - n_ans
    causal = col_ref[...] >= row_ref[...]
    lane = lax.broadcasted_iota(jnp.int32, (1, 128), 1)
    root = HD ** (-0.5)

    for item in range(items):
        ans = pl.ds(item * n_ans, n_ans)
        ctx = pl.ds(rows_ans + item * n_ctx, n_ctx)
        turns = [(flat(cos_ref[:, r]), -flat(sin_ref[:, r])) for r in (ans, ctx)]
        d_ref[:, ctx, pl.ds(0, width)] = jnp.zeros((n, n_ctx, width), BF16)
        for g in range(width // 128):
            lanes = pl.ds(g * 128, 128)
            klanes = pl.ds(width + g * 128, 128)
            vlanes = pl.ds(2 * width + g * 128, 128)
            q, do = flat(q_ref[:, ans, lanes]), flat(do_ref[:, ans, lanes])
            k_ans, k_ctx = flat(k_ref[:, ans, lanes]), flat(k_ref[:, ctx, lanes])
            v_ans, v_ctx = flat(v_ref[:, ans, lanes]), flat(v_ref[:, ctx, lanes])
            dq, sums = [], None
            for first in (True, False):
                own = (lane < HD) == first
                q_own, do_own = jnp.where(own, q, 0), jnp.where(own, do, 0)
                p_ctx, p_ans = head_probs(q_own, k_ctx, k_ans, causal)
                dp_ctx = mm(do_own, v_ctx, CONTRACT_LAST)
                dp_ans = mm(do_own, v_ans, CONTRACT_LAST)
                mean = jnp.sum(p_ctx * dp_ctx, axis=1, keepdims=True) + jnp.sum(
                    p_ans * dp_ans, axis=1, keepdims=True
                )
                ds_ctx = (p_ctx * (dp_ctx - mean)).astype(BF16)
                ds_ans = (p_ans * (dp_ans - mean)).astype(BF16)
                dq.append(mm(ds_ctx, k_ctx) + mm(ds_ans, k_ans))
                new = [
                    mm(ds_ctx, q_own, CONTRACT_FIRST),
                    mm(ds_ans, q_own, CONTRACT_FIRST),
                    mm(p_ctx.astype(BF16), do_own, CONTRACT_FIRST),
                    mm(p_ans.astype(BF16), do_own, CONTRACT_FIRST),
                ]
                sums = new if sums is None else [a + b for a, b in zip(sums, new)]
            dq = turn(jnp.where(lane < HD, dq[0], dq[1]) * root, *turns[0])
            dk_ctx = turn(sums[0] * root, *turns[1])
            dk_ans = turn(sums[1] * root, *turns[0])
            d_ref[:, ans, lanes] = dq.astype(BF16).reshape(n, n_ans, 128)
            d_ref[:, ans, klanes] = dk_ans.astype(BF16).reshape(n, n_ans, 128)
            d_ref[:, ctx, klanes] = dk_ctx.astype(BF16).reshape(n, n_ctx, 128)
            d_ref[:, ans, vlanes] = sums[3].astype(BF16).reshape(n, n_ans, 128)
            d_ref[:, ctx, vlanes] = sums[2].astype(BF16).reshape(n, n_ctx, 128)


def in_vmem(kernel, name, outs, scratch, *args):
    return pl.pallas_call(
        kernel,
        out_shape=[jax.ShapeDtypeStruct(shape, dtype) for shape, dtype in outs],
        in_specs=[pl.BlockSpec(memory_space=pltpu.VMEM)] * len(args),
        out_specs=[pl.BlockSpec(memory_space=pltpu.VMEM)] * len(outs),
        scratch_shapes=[pltpu.VMEM(shape, dtype) for shape, dtype in scratch],
        compiler_params=pltpu.CompilerParams(vmem_limit_bytes=48 << 20),
        cost_estimate=pl.CostEstimate(flops=0, bytes_accessed=1 << 10, transcendentals=0),
        name=name,
    )(*args)


def norm_forward(x):
    inverse = lax.rsqrt(jnp.mean(x * x, axis=-1, keepdims=True) + EPS_NORM)
    return (x * inverse, inverse)


def norm_backward(grad, normed, inverse, gain):
    scaled = grad * gain
    dgain = jnp.sum(grad * normed, axis=0)
    dx = inverse * (scaled - normed * jnp.mean(scaled * normed, axis=-1, keepdims=True))
    return (dx, dgain)


def body(
    tokens,
    targets,
    pair_order,
    lengths,
    loss_mask,
    start_pos,
    owner_map,
    block_master,
    left_stat,
    right_stat,
    left_root,
    right_root,
    table_master,
    table_moment,
    table_second,
    gain_master,
    gain_moment,
    gain_second,
):
    dp = lax.axis_index("dp")
    mp = lax.axis_index("mp")
    n_mp = lax.axis_size("mp")
    n_dp = lax.axis_size("dp")
    fused = (n_mp, n_dp) == (8, 4)
    items, length = tokens.shape
    context = length - ANS
    n_ans = ANS // n_mp
    n_ctx = context // n_mp
    rows_ans = items * n_ans
    rows_own = items * (n_ans + n_ctx)
    width = D // n_mp
    units = FF // n_mp
    heads = width // HD
    vocab_part, cols = table_master.shape
    sub = vocab_part // n_dp
    perm = owner_map[0]
    who = mp ^ jnp.array(cube_order(n_mp), jnp.int32)
    near = dp ^ jnp.arange(n_dp, dtype=jnp.int32)

    slots = lax.all_gather(block_master[0].astype(BF16), "dp", axis=0, tiled=True)
    gains = line_gather(gain_master.astype(BF16))
    wide = jnp.zeros((3, D), BF16)
    for o in range(n_dp):
        wide = lax.dynamic_update_slice(wide, gains[o], (0, near[o] * cols))
    gains = wide.astype(F32)
    table_low = table_master.astype(BF16)

    packed = jnp.concatenate([tokens, targets, loss_mask, lengths[:, None]], axis=1)
    packed = jnp.stack(line_gather(packed))
    all_tokens = packed[:, :, :length]
    all_targets = packed[:, :, length : length + ANS]
    all_mask = packed[:, :, length + ANS : length + 2 * ANS]
    all_lengths = packed[:, :, -1]
    column = jnp.arange(ANS)
    weights = jnp.where(
        column == 0,
        1.0,
        jnp.where(column < all_lengths[..., None], all_mask.astype(F32), 0.0),
    )
    pairs_all = pair_order.shape[0] // 2
    pairs = (pair_order // 2).reshape(n_dp, items)[near]
    member = (pairs[..., None] == jnp.arange(pairs_all)).astype(F32)
    counts = jnp.einsum("oip,oi->p", member, jnp.sum(weights, axis=-1))
    scale = weights / (jnp.sum(member * counts, axis=-1)[..., None] * pairs_all)

    def by_owner(x):
        split = x.reshape(n_dp, items, n_mp, n_ans)[:, :, who]
        return split.transpose(2, 0, 1, 3)

    row_scale = by_owner(scale).reshape(-1)
    row_target = by_owner(all_targets).reshape(-1)
    tok_ans = all_tokens[:, :, context:].reshape(n_dp, items, n_mp, n_ans)[:, :, who]
    tok_ctx = all_tokens[:, :, :context].reshape(n_dp, items, n_mp, n_ctx)[:, :, who]
    tok = jnp.concatenate(
        [
            tok_ans.transpose(2, 0, 1, 3).reshape(n_mp, n_dp, -1),
            tok_ctx.transpose(2, 0, 1, 3).reshape(n_mp, n_dp, -1),
        ],
        axis=2,
    )

    shapes = mat_shapes(n_mp)
    number = perm.shape[0]
    slot_of = jnp.zeros_like(perm).at[perm].set(jnp.arange(number, dtype=jnp.int32))

    local = tok - mp * vocab_part
    valid = (local >= 0) & (local < vocab_part)
    safe = jnp.clip(local, 0, vocab_part - 1)
    looked = jnp.where(valid[..., None], jnp.take(table_low, safe, axis=0), 0)
    own_cols = cube_scatter(looked).astype(BF16)
    pieces = line_exchange([own_cols[o] for o in range(n_dp)])
    x0 = jnp.zeros((rows_own, D), BF16)
    for o in range(n_dp):
        x0 = lax.dynamic_update_slice(x0, pieces[o], (0, near[o] * cols))
    x0 = x0.astype(F32)
    normed1, inverse1 = norm_forward(x0)
    h1 = cube_gather((normed1 * gains[0]).astype(BF16))
    h1_all = h1.reshape(-1, D)

    wqkv, wout, wgate, wdown = place_tiles(slot_of, slots, shapes)

    table_late = after(table_low, slots, h1)
    head_parts = lax.all_to_all(table_late.reshape(n_dp, sub, cols), "dp", 0, 0)

    half = HD // 2
    freq = ROPE_BASE ** (-jnp.arange(half).astype(F32) * 2.0 / HD)
    t_ans = context + who[:, None] * n_ans + jnp.arange(n_ans)
    t_ctx = who[:, None] * n_ctx + jnp.arange(n_ctx)

    def angles(t):
        place = (start_pos[None, :, None] + t[:, None, :]).astype(F32)
        angle = place.reshape(n_mp, -1)[..., None] * freq
        return jnp.cos(angle), jnp.sin(angle)

    cosine, sine = (jnp.concatenate(pair, axis=1) for pair in zip(angles(t_ans), angles(t_ctx)))
    cosine = jnp.concatenate([cosine] * 4, axis=-1)
    sine = jnp.concatenate([-sine, sine] * 2, axis=-1)
    t_query = t_ans.reshape(-1)
    place = (t_query[:, None], t_query[None, :])

    ans_shape = ((n_mp, rows_ans, width), BF16)
    key_shape = ((n_mp, rows_own, width), BF16)
    o_rows, query, key, value = in_vmem(
        functools.partial(attend_kernel, items),
        "attend",
        (ans_shape, ans_shape, key_shape, key_shape),
        (((n_mp, rows_own, 3 * width), F32),),
        *(h1, wqkv, cosine, sine, *place),
    )
    own = ((rows_ans, D), F32)
    gain_row = ((1, D), F32)
    plane = ((n_mp, rows_ans, D), BF16)
    if fused:
        x1, h2 = exchange(
            attend_sum_kernel, "attend_sum", 1, n_dp, rows_ans, (own, plane),
            *(o_rows, wout, x0[:rows_ans], gains[1:2]),
        )
    else:
        parts = dot("tw,wd->td", o_rows.reshape(-1, width), wout).astype(BF16)
        x1 = x0[:rows_ans] + cube_scatter(parts.reshape(n_mp, rows_ans, D))
        h2 = cube_gather((norm_forward(x1)[0] * gains[1]).astype(BF16))
    o_rows = o_rows.reshape(-1, width)

    if fused:
        flat_units = n_mp * rows_ans
        x2, gate_up, hidden, final = exchange(
            units_sum_kernel, "units_sum", 2, n_dp, rows_ans,
            (
                own,
                ((flat_units, 2 * units), F32),
                ((flat_units, units), BF16),
                ((rows_ans, D), BF16),
            ),
            *(h2, wgate, wdown, x1, gains[2:3]),
        )
        h2 = h2.reshape(-1, D)
    else:
        h2 = h2.reshape(-1, D)
        gate_up = dot("td,df->tf", h2, wgate)
        gate, upward = gate_up[:, :units], gate_up[:, units:]
        hidden = (jax.nn.silu(gate) * upward).astype(BF16)
        parts = dot("tf,fd->td", hidden, wdown).astype(BF16)
        x2 = x1 + cube_scatter(parts.reshape(n_mp, rows_ans, D))

    def by_line(x):
        return x.reshape(n_mp, n_dp, rows_ans).transpose(1, 0, 2).reshape(n_dp, -1, 1)

    first = mp * vocab_part + dp * sub
    if fused:
        final, dlogits, seen = head_call(
            n_dp, final, head_parts, by_line(row_target - first), by_line(row_scale)
        )
        lse, picked = seen[0, 0], seen[1, 0]
        dlogits = dlogits.reshape(-1, sub)
        final = final.reshape(-1, D)
    else:
        head = jnp.concatenate([head_parts[a] for a in range(n_dp)], axis=1)
        final = (norm_forward(x2)[0] * gains[2]).astype(BF16)
        final = cube_gather(jnp.stack(line_gather(final)).reshape(-1, D))
        final = final.reshape(-1, D)
        logits = dot("rd,vd->rv", final, head)
        hit = jnp.arange(sub, dtype=jnp.int32)[None, :] == (row_target - first)[:, None]
        top = jnp.max(logits, axis=1)
        total = jnp.sum(jnp.exp(logits - top[:, None]), axis=1)
        picked = jnp.sum(jnp.where(hit, logits, 0.0), axis=1)
        top, total, picked = stats_everywhere(jnp.stack([top, total, picked]), rows_ans)
        lse = top + jnp.log(total)
        dlogits = (
            row_scale[:, None] * (jnp.exp(logits - lse[:, None]) - hit.astype(F32))
        ).astype(BF16)
    loss_own = jnp.sum(row_scale[:rows_ans] * (lse - picked)[:rows_ans]) * pairs_all

    if fused:
        cut = 256
        total = n_dp * rows_ans
        dx2, dgain3, down_in, early_grad, head_grad = exchange(
            functools.partial(head_back_kernel, n_dp, cut), "head_sum", 3, n_dp, total,
            (
                own,
                gain_row,
                plane,
                ((n_dp, cut, cols), BF16),
                ((n_dp, sub - cut, cols), BF16),
            ),
            *(dlogits.reshape(n_mp, -1, sub), head_parts, x2, gains[2:3]),
            final.reshape(n_mp, -1, D),
            more=(
                (total, D),
                (n_dp - 1, rows_ans, D),
                (n_mp, total, D),
                (n_dp - 1, cut, cols),
            ),
            sems=13 + 9 * n_dp,
            far=1,
        )
        dgain3 = dgain3[0]
    else:
        parts = dot("rv,vd->rd", dlogits, head).astype(BF16)
        mine = cube_scatter(parts.reshape(n_mp, n_dp * rows_ans, D)).astype(BF16)
        mine = line_exchange(list(mine.reshape(n_dp, rows_ans, D)))
        dfinal = sum(piece.astype(F32) for piece in mine)
        dx2, dgain3 = norm_backward(dfinal, *norm_forward(x2), gains[2])
        down_in = cube_gather(dx2.astype(BF16))
        head_grad = jnp.stack(
            [
                dot("rv,rd->vd", dlogits, final[:, a * cols : (a + 1) * cols]).astype(BF16)
                for a in range(n_dp)
            ]
        )
    table_grad = lax.all_to_all(head_grad, "dp", 0, 0)
    if fused:
        dx1, dgain2, dgate_up, out_in = exchange(
            gate_sum_kernel, "gate_sum", 4, n_dp, rows_ans,
            (own, gain_row, (gate_up.shape, BF16), plane),
            *(down_in, wdown, wgate, gate_up, x1, gains[1:2], dx2),
        )
        dgain2 = dgain2[0]
        down_in = down_in.reshape(-1, D)
    else:
        down_in = down_in.reshape(-1, D)
        dhidden = dot("td,fd->tf", down_in, wdown)
        sigma = jax.nn.sigmoid(gate)
        dgate = dhidden * upward * sigma * (1.0 + gate * (1.0 - sigma))
        dgate_up = jnp.concatenate([dgate, dhidden * gate * sigma], axis=-1).astype(BF16)
        parts = dot("tf,df->td", dgate_up, wgate).astype(BF16)
        dnormed2 = cube_scatter(parts.reshape(n_mp, rows_ans, D))
        dx_mlp, dgain2 = norm_backward(dnormed2, *norm_forward(x1), gains[1])
        dx1 = dx2 + dx_mlp
        out_in = cube_gather(dx1.astype(BF16))
    grad_down = dot("tf,td->fd", hidden, down_in).astype(BF16)
    grad_gate = dot("td,tf->df", h2, dgate_up).astype(BF16)
    grad_out = dot("tw,td->wd", o_rows, out_in.reshape(-1, D)).astype(BF16)
    (dqkv,) = in_vmem(
        functools.partial(attend_back_kernel, items),
        "attend_back",
        (((n_mp, rows_own, 3 * width), BF16),),
        (ans_shape,),
        *(query, key, value, out_in, wout, cosine, sine, *place),
    )
    dqkv = dqkv.reshape(-1, 3 * width)
    if fused:
        dx0, dgain1, grad_qkv = exchange(
            input_back_kernel, "input_sum", 7, n_dp, rows_own,
            (((rows_own, D), BF16), gain_row, (wqkv.shape, BF16)),
            *(dqkv.reshape(n_mp, rows_own, -1), wqkv, h1, x0, gains[:1], dx1),
            sems=7 * (rows_own // rows_ans),
        )
        dgain1 = dgain1[0]
    else:
        dh1 = dot("te,de->td", dqkv, wqkv).astype(BF16).reshape(n_mp, rows_own, D)
        grad_qkv = dot("td,te->de", h1_all, dqkv).astype(BF16)
        dx0, dgain1 = norm_backward(cube_scatter(dh1), *norm_forward(x0), gains[0])
        dx0 = jnp.concatenate([dx0[:rows_ans] + dx1, dx0[rows_ans:]]).astype(BF16)

    rows_over = line_exchange(
        [lax.dynamic_slice_in_dim(dx0, near[o] * cols, cols, 1) for o in range(n_dp)]
    )

    slots = collect_tiles(slot_of, (grad_gate, grad_down), shapes, (2, 3))
    slots = collect_tiles(slot_of, (grad_qkv, grad_out), shapes, (0, 1), (slots,))
    slots = after(slots, table_grad, *rows_over)
    own_slots = lax.psum_scatter(slots, "dp", scatter_dimension=0, tiled=True)

    if fused:
        table_grad = jnp.concatenate([early_grad, table_grad], axis=1)
    rows_back = cube_gather(jnp.stack(rows_over).reshape(-1, cols)).reshape(safe.shape + (cols,))
    picked_rows = jnp.where(valid[..., None], rows_back, 0).astype(F32)
    own_table = table_grad.reshape(vocab_part, cols).astype(F32).at[safe.reshape(-1)].add(picked_rows.reshape(-1, cols))

    gain_grad = jnp.stack([dgain1, dgain2, dgain3])
    gain_total = everywhere(gain_grad, jnp.add)
    own_gain = lax.dynamic_slice_in_dim(gain_total, dp * cols, cols, 1)
    first_mp = (mp == 0).astype(F32)
    squares = jnp.sum(own_table * own_table) + first_mp * jnp.sum(own_gain * own_gain)
    if fused:
        more = jnp.zeros((2, 8, 128), F32).at[:, 0, 0].set(jnp.stack([squares, loss_own]))
        squares_all, loss_total = jnp.sum(total_exchange(own_slots, more, n_dp), axis=(1, 2))
    else:
        squares = squares + jnp.sum(jnp.square(own_slots.astype(F32)))
        more = everywhere(jnp.stack([squares, loss_own])[None], jnp.add)[0]
        squares_all, loss_total = more
    norm = jnp.sqrt(squares_all)
    factor = CLIP_NORM / jnp.maximum(norm, CLIP_NORM)
    roots = (left_stat[0], right_stat[0], left_root[0], right_root[0])
    block_new, block_copy, grad_slots, left_new, right_new, *table_step = owner_step(
        factor.reshape(1, 1),
        (own_slots, block_master[0], *roots),
        (own_table, table_master, table_moment, table_second),
    )
    table_new, table_copy, table_moment_new, table_second_new = table_step
    gain_new, gain_moment_new, gain_second_new = adam(
        gain_master, gain_moment, gain_second, factor * own_gain, LR_GAIN, 0.0
    )
    return (
        loss_total,
        norm,
        block_new[None],
        block_copy[None],
        grad_slots[None],
        left_new[None],
        right_new[None],
        table_new,
        table_copy,
        table_moment_new,
        table_second_new,
        gain_new,
        gain_moment_new,
        gain_second_new,
    )


def solution(mesh):
    in_specs = (
        P("dp", None),
        P("dp", None),
        P(),
        P("dp"),
        P("dp", None),
        P("dp"),
        P("mp", None),
        P("mp", "dp", None, None),
        P("mp", "dp", None, None),
        P("mp", "dp", None, None),
        P("mp", "dp", None, None),
        P("mp", "dp", None, None),
        P("mp", "dp"),
        P("mp", "dp"),
        P("mp", "dp"),
        P(None, "dp"),
        P(None, "dp"),
        P(None, "dp"),
    )
    out_specs = (
        P(),
        P(),
        P("mp", "dp", None, None),
        P("mp", "dp", None, None),
        P("mp", "dp", None, None),
        P("mp", "dp", None, None),
        P("mp", "dp", None, None),
        P("mp", "dp"),
        P("mp", "dp"),
        P("mp", "dp"),
        P("mp", "dp"),
        P(None, "dp"),
        P(None, "dp"),
        P(None, "dp"),
    )
    return jax.shard_map(body, mesh=mesh, in_specs=in_specs, out_specs=out_specs, check_vma=False)
```

```python
import functools

import jax
import jax.numpy as jnp
from jax import lax
from jax.experimental import pallas as pl
from jax.experimental.pallas import tpu as pltpu
from jax.sharding import PartitionSpec as P

D = 2048
HD = 64
FF = 8192
ANS = 256
STEP = 5


EPS_NORM = 1e-05
ROPE_BASE = 130000.0
CLIP_NORM = 0.01
STAT_DECAY = 0.95
LR_MATRIX = 0.05
DECAY_MATRIX = 0.1
LR_TABLE = 0.03
DECAY_TABLE = 0.1
LR_GAIN = 0.2
ADAM_ONE = 0.9
ADAM_TWO = 0.95
ADAM_EPS = 1e-08
MASKED = -1e30
F32 = jnp.float32
BF16 = jnp.bfloat16


def dot(spec, a, b):
    return jnp.einsum(spec, a, b, preferred_element_type=F32)


def cube_bits(n):
    bits = [1 << i for i in range(n.bit_length() - 1)]
    return bits[1:] + bits[:1]


def cube_order(n):
    order = [0]
    for bit in cube_bits(n):
        order = order + [o ^ bit for o in order]
    return order


def swap(x, axis, bit):
    n = lax.axis_size(axis)
    return lax.ppermute(x, axis, [(i, i ^ bit) for i in range(n)])


def cube_gather(x):
    n = lax.axis_size("mp")
    if n != 8:
        held = x[None]
        for bit in cube_bits(n):
            held = jnp.concatenate([held, swap(held, "mp", bit)])
        return held
    half = x.shape[0] // 2
    over_x = swap(x, "mp", 2)
    over_y = swap(x, "mp", 4)
    far = jnp.concatenate([swap(over_x[:half], "mp", 4), swap(over_y[half:], "mp", 2)])
    held = jnp.stack([x, over_x, over_y, far])
    return jnp.concatenate([held, swap(held, "mp", 1)])


def cube_scatter(parts):
    n = lax.axis_size("mp")
    if n != 8:
        held = parts
        for bit in reversed(cube_bits(n)):
            keep = held.shape[0] // 2
            other = swap(held[keep:].astype(BF16), "mp", bit)
            held = held[:keep].astype(F32) + other.astype(F32)
        return held[0]
    got = swap(parts[4:], "mp", 1)
    held = (parts[:4].astype(F32) + got.astype(F32)).astype(BF16)
    half = held.shape[1] // 2
    one, two = held[:, :half], held[:, half:]
    one_x = swap(one[1::2], "mp", 2)
    two_y = swap(two[2:], "mp", 4)
    one = one[0::2].astype(F32) + one_x.astype(F32)
    two = two[:2].astype(F32) + two_y.astype(F32)
    one_y = swap(one[1].astype(BF16), "mp", 4)
    two_x = swap(two[1].astype(BF16), "mp", 2)
    return jnp.concatenate([one[0] + one_y.astype(F32), two[0] + two_x.astype(F32)])


def line_gather(x):
    return [x] + [swap(x, "dp", o) for o in range(1, lax.axis_size("dp"))]


def line_exchange(parts):
    return [parts[0]] + [swap(parts[o], "dp", o) for o in range(1, len(parts))]


def combine_stats(a, b):
    top = jnp.maximum(a[0], b[0])
    total = a[1] * jnp.exp(a[0] - top) + b[1] * jnp.exp(b[0] - top)
    return jnp.stack([top, total, a[2] + b[2]])


def everywhere(x, op):
    for axis in ("mp", "dp"):
        bit = 1
        while bit < lax.axis_size(axis):
            x = op(x, swap(x, axis, bit))
            bit *= 2
    return x


def stats_everywhere(x, rows):
    n_mp, n_dp = lax.axis_size("mp"), lax.axis_size("dp")
    bits = cube_bits(n_mp)
    split = (3,) + (2,) * len(bits) + (n_dp * rows,)
    x = x.reshape(split)
    for i, bit in enumerate(bits):
        x = combine_stats(x, jnp.flip(swap(x, "mp", bit), len(bits) - i))
    x = x.reshape(3, n_mp, n_dp, rows)
    total = x
    for o, other in enumerate(line_gather(x)):
        if o:
            order = [e ^ o for e in range(n_dp)]
            total = combine_stats(total, jnp.stack([other[:, :, e] for e in order], axis=2))
    return total.reshape(3, -1)


def peer_copy(src, dst, sems, k, **device):
    return pltpu.make_async_remote_copy(
        src_ref=src,
        dst_ref=dst,
        send_sem=sems.at[0, k],
        recv_sem=sems.at[1, k],
        device_id=device,
        device_id_type=pl.DeviceIdType.MESH,
    )


def greet(n_dp, bits=(1, 2, 4)):
    me = lax.axis_index("mp")
    a = lax.axis_index("dp")
    barrier = pltpu.get_barrier_semaphore()
    partners = [{"mp": me ^ bit} for bit in bits]
    partners += [{"dp": a ^ o} for o in range(1, n_dp)]
    for partner in partners:
        pl.semaphore_signal(barrier, 1, device_id=partner, device_id_type=pl.DeviceIdType.MESH)
    pl.semaphore_wait(barrier, len(partners))


def by_rows(count, step):
    @pl.loop(0, count // 16)
    def _(i):
        step(pl.multiple_of(i * 16, 16))


class PlaneSum:
    def __init__(self, parts, own, core, held, near, last, sems, first, blocks):
        me = lax.axis_index("mp")
        self.refs = parts, own, core, held, near, last
        self.rows = own.shape[0] // blocks
        self.half = half = self.rows // 2
        self.at_core = []
        self.blocks = []
        for b in range(blocks):
            whole = pl.ds(b * self.rows, self.rows)
            top, low = pl.ds(b * self.rows, half), pl.ds(b * self.rows + half, half)
            spot = pl.ds(b * half, half)
            k = first + 7 * b
            self.at_core.append(
                peer_copy(parts.at[4:8, whole], core.at[:, whole], sems, k, mp=me ^ 1)
            )
            sends = (
                (3, top, near, 0, 2),
                (3, low, near, 1, 4),
                (1, top, near, 2, 2),
                (2, low, near, 3, 4),
                (2, top, last, 0, 4),
                (1, low, last, 1, 2),
            )
            self.blocks.append(
                [
                    peer_copy(held.at[s, rows], to.at[at, spot], sems, k + 1 + e, mp=me ^ bit)
                    for e, (s, rows, to, at, bit) in enumerate(sends)
                ]
            )

    def first_sends(self, b):
        self.at_core[b].wait_recv()
        parts, _, core, held, _, _ = self.refs
        copies = self.blocks[b]
        for s, sent in ((3, copies[:2]), (1, copies[2:3]), (2, copies[3:4])):

            def add(at, s=s):
                rows = pl.ds(b * self.rows + at, 16)
                value = parts[s, rows].astype(F32) + core[s, rows].astype(F32)
                held[s, rows] = value.astype(BF16)

            by_rows(self.rows, add)
            for copy in sent:
                copy.start()

    def second_sends(self, b):
        _, _, _, held, near, _ = self.refs
        copies = self.blocks[b]
        for e, s, offset in ((0, 2, 0), (1, 1, self.half)):
            copies[e].wait_recv()

            def add(at, e=e, s=s, offset=offset):
                rows = pl.ds(b * self.rows + offset + at, 16)
                value = held[s, rows].astype(F32) + near[e, pl.ds(b * self.half + at, 16)].astype(F32)
                held[s, rows] = value.astype(BF16)

            by_rows(self.half, add)
            copies[4 + e].start()

    def finish(self, b):
        parts, own, core, _, near, last = self.refs
        for copy in self.blocks[b][2:]:
            copy.wait_recv()

        def total(at):
            spot = pl.ds(b * self.half + at, 16)
            for e, offset in ((0, 0), (1, self.half)):
                rows = pl.ds(b * self.rows + offset + at, 16)
                own[rows] = (
                    (parts[0, rows].astype(F32) + core[0, rows].astype(F32))
                    + near[2 + e, spot].astype(F32)
                    + last[e, spot].astype(F32)
                )

        by_rows(self.half, total)

    def close(self):
        for core, copies in zip(self.at_core, self.blocks):
            core.wait_send()
            for copy in copies:
                copy.wait_send()

    def run(self, fill=lambda: None):
        for b in range(len(self.blocks)):
            self.at_core[b].start()
        for step in (self.first_sends, self.second_sends, self.finish):
            fill()
            for b in range(len(self.blocks)):
                step(b)
        self.close()


class PlaneSpread:
    def __init__(self, x, out, sems, k, start, rows):
        me = lax.axis_index("mp")
        half = rows // 2
        top, low, whole = pl.ds(start, half), pl.ds(start + half, half), pl.ds(start, rows)
        self.own = x, out, start, rows

        def copy(src, slot, part, e, bit):
            return peer_copy(src, out.at[slot, part], sems, k + e, mp=me ^ bit)

        self.x_top = copy(x.at[top], 1, top, 0, 2)
        self.y_low = copy(x.at[low], 2, low, 1, 4)
        self.x_low = copy(x.at[low], 1, low, 2, 2)
        self.y_top = copy(x.at[top], 2, top, 3, 4)
        self.core = copy(x.at[whole], 4, whole, 4, 1)
        self.far_y = copy(out.at[1, top], 3, top, 5, 4)
        self.far_x = copy(out.at[2, low], 3, low, 6, 2)
        self.to_core = {
            (s, r): copy(out.at[s, part], 4 + s, part, 7 + 2 * (s - 1) + r, 1)
            for s in (1, 2, 3)
            for r, part in enumerate((top, low))
        }

    def begin(self):
        for c in (self.x_top, self.y_low, self.x_low, self.y_top, self.core):
            c.start()
        x, out, start, rows = self.own

        def keep(at):
            part = pl.ds(start + at, 16)
            out[0, part] = x[part]

        by_rows(rows, keep)

    def relay(self):
        self.x_top.wait_recv()
        self.far_y.start()
        self.to_core[1, 0].start()
        self.y_low.wait_recv()
        self.far_x.start()
        self.to_core[2, 1].start()
        self.x_low.wait_recv()
        self.to_core[1, 1].start()
        self.y_top.wait_recv()
        self.to_core[2, 0].start()

    def relay_far(self):
        self.far_y.wait_recv()
        self.to_core[3, 0].start()
        self.far_x.wait_recv()
        self.to_core[3, 1].start()

    def arrive(self):
        self.core.wait_recv()
        for c in self.to_core.values():
            c.wait_recv()

    def close(self):
        sent = (self.x_top, self.y_low, self.x_low, self.y_top, self.core, self.far_y, self.far_x)
        for c in (*sent, *self.to_core.values()):
            c.wait_send()

    def run(self, fill=lambda: None):
        self.begin()
        fill()
        self.relay()
        fill()
        self.relay_far()
        self.arrive()
        self.close()


def norm_step(x, gain):
    return (x * lax.rsqrt(jnp.mean(x * x, axis=1, keepdims=True) + EPS_NORM)) * gain


def norm_back_step(grad, x, gain):
    inverse = lax.rsqrt(jnp.mean(x * x, axis=1, keepdims=True) + EPS_NORM)
    normed = x * inverse
    scaled = grad * gain
    dx = inverse * (scaled - normed * jnp.mean(scaled * normed, axis=1, keepdims=True))
    return dx, jnp.sum(grad * normed, axis=0, keepdims=True)


def by_columns(step, width=512):
    for c in range(D // width):
        step(pl.ds(c * width, width))


def forward_step(refs, res, gain, x_out):
    own, core, held, near, last, parts, _, sems = refs
    PlaneSum(parts, own, core, held, near, last, sems, 0, 1).run()
    x = res[...] + own[...]
    x_out[...] = x
    return norm_step(x, gain[...]).astype(BF16)


def attend_sum_kernel(o, wout, res, gain, x_out, out, *refs):
    *_, parts, mine, sems = refs
    greet(1)

    def make(c):
        parts[:, :, c] = mm(flat(o[...]), wout[:, c]).astype(BF16).reshape(8, -1, c.size)

    by_columns(make)
    mine[...] = forward_step(refs, res, gain, x_out)
    PlaneSpread(mine, out, sems, 7, 0, mine.shape[0]).run()


def units_sum_kernel(h2, wgate, wdown, res, gain, x_out, gate_up, hidden, out, *refs):
    *_, parts, _, _ = refs
    units = wdown.shape[0]
    greet(1)
    x = flat(h2[...])
    step = min(units, 512)
    for c in range(2 * units // step):
        at = pl.ds(c * step, step)
        gate_up[:, at] = mm(x, wgate[:, at])
    for c in range(units // step):
        at, up = pl.ds(c * step, step), pl.ds(units + c * step, step)
        gate = gate_up[:, at]
        hidden[:, at] = (gate / (1.0 + jnp.exp(-gate)) * gate_up[:, up]).astype(BF16)

    def make(c):
        parts[:, :, c] = mm(hidden[...], wdown[:, c]).astype(BF16).reshape(8, -1, c.size)

    by_columns(make)
    out[...] = forward_step(refs, res, gain, x_out)


def gate_sum_kernel(down_in, wdown, wgate, gate_up, x_in, gain, res, h2_ref, hidden_ref, *refs):
    dx_out, dgain, dgate_up, out, down_out, gate_out, *refs = refs
    own, core, held, near, last, parts, mine, *refs = refs
    h2, hidden, down_grad, gate_grad, sems, h2_sem, hidden_sem, store_sems = refs
    units = wdown.shape[0]
    loads = [
        pltpu.make_async_copy(h2_ref, h2, h2_sem),
        pltpu.make_async_copy(hidden_ref, hidden, hidden_sem),
    ]
    stores = [
        pltpu.make_async_copy(down_grad, down_out, store_sems.at[0]),
        pltpu.make_async_copy(gate_grad, gate_out, store_sems.at[1]),
    ]
    for copy in loads:
        copy.start()
    greet(1)
    x = flat(down_in[...])
    step = min(units, 512)
    for c in range(units // step):
        at, up = pl.ds(c * step, step), pl.ds(units + c * step, step)
        grad = mm(x, wdown[at, :], CONTRACT_LAST)
        gate, upward = gate_up[:, at], gate_up[:, up]
        sigma = 1.0 / (1.0 + jnp.exp(-gate))
        dgate = grad * upward * sigma * (1.0 + gate * (1.0 - sigma))
        dgate_up[:, at] = dgate.astype(BF16)
        dgate_up[:, up] = (grad * gate * sigma).astype(BF16)

    def make(c):
        value = mm(dgate_up[...], wgate[c, :], CONTRACT_LAST)
        parts[:, :, c] = value.astype(BF16).reshape(8, -1, c.size)

    by_columns(make)
    left = [(down_grad, c) for c in range(0, D, step)]
    left += [(gate_grad, c) for c in range(0, 2 * units, step)]

    def fill(count=2):
        for _ in range(min(count, len(left))):
            grad, c = left.pop(0)
            at = pl.ds(c, step)
            if grad is down_grad:
                value = mm(hidden[...], flat(down_in[:, :, at]), CONTRACT_FIRST)
            else:
                value = mm(flat(h2[...]), dgate_up[:, at], CONTRACT_FIRST)
            grad[:, at] = value.astype(BF16)
            if not left:
                stores[1].start()
            elif grad is down_grad and left[0][0] is gate_grad:
                stores[0].start()

    for copy in loads:
        copy.wait()
    PlaneSum(parts, own, core, held, near, last, sems, 0, 1).run(fill)
    dx, dg = norm_back_step(own[...], x_in[...], gain[...])
    dx = dx + res[...]
    dx_out[...] = dx
    dgain[...] = dg
    mine[...] = dx.astype(BF16)
    PlaneSpread(mine, out, sems, 7, 0, mine.shape[0]).run(fill)
    fill(len(left))
    for copy in stores:
        copy.wait()


def head_kernel(n_dp, rows_ref, target_ref, scale_ref, *refs):
    head_ref, final_out, dlogits_out, seen, final, head, mine, logits, *refs = refs
    stats, plane, mid, line, dlogits, sems, own_sems = refs
    rows, vocab = rows_ref.shape[0], logits.shape[2]
    wide = head.shape[2]
    load = pltpu.make_async_copy(head_ref, head, own_sems.at[0])
    store = pltpu.make_async_copy(final, final_out, own_sems.at[1])
    load.start()
    a = lax.axis_index("dp")
    greet(n_dp, range(1, 8))
    mine[pl.ds(0, rows)] = rows_ref[...]
    block = [pl.ds(o * rows, rows) for o in range(4)]
    across = [
        peer_copy(rows_ref, mine.at[block[1]], sems, 53, dp=a ^ 1),
        peer_copy(rows_ref, mine.at[block[2]], sems, 54, dp=a ^ 2),
        peer_copy(mine.at[block[2]], mine.at[block[3]], sems, 55, dp=a ^ 1),
    ]
    across[0].start()
    across[1].start()
    blocks = [PlaneSpread(mine, final, sems, 13 * o, o * rows, rows) for o in range(n_dp)]
    tile = 512 if vocab % 512 == 0 else vocab

    def use(b):
        part = pl.ds(b * rows, rows)

        @pl.loop(0, vocab // tile)
        def _(v):
            at = pl.ds(pl.multiple_of(v * tile, tile), tile)
            value = None
            for p in range(n_dp):
                x = flat(final[:, part, pl.ds(p * wide, wide)])
                term = mm(x, head[p, at, :], CONTRACT_LAST)
                value = term if value is None else value + term
            logits[:, part, at] = value.reshape(8, rows, tile)

        value = flat(logits[:, part, :])
        top = jnp.max(value, axis=1, keepdims=True)
        expo = jnp.sum(jnp.exp(value - top), axis=1, keepdims=True)
        column = lax.broadcasted_iota(jnp.int32, value.shape, 1)
        hit = jnp.sum(jnp.where(column == target_ref[b], value, 0.0), axis=1, keepdims=True)
        lane = lax.broadcasted_iota(jnp.int32, (8 * rows, 128), 1)
        packed = jnp.where(lane == 0, top, jnp.where(lane == 1, expo, hit)).T
        for k in range(3):
            stats[k, b : b + 1, :] = packed[k : k + 1]

    blocks[0].begin()
    across[0].wait_recv()
    blocks[1].begin()
    blocks[0].relay()
    across[1].wait_recv()
    across[2].start()
    blocks[2].begin()
    blocks[1].relay()
    blocks[0].relay_far()
    across[2].wait_recv()
    blocks[3].begin()
    blocks[2].relay()
    blocks[1].relay_far()
    blocks[0].arrive()
    load.wait()
    use(0)
    blocks[3].relay()
    blocks[2].relay_far()
    blocks[1].arrive()
    use(1)
    blocks[3].relay_far()
    blocks[2].arrive()
    use(2)
    blocks[3].arrive()
    store.start()
    use(3)
    stats_steps(n_dp, stats, seen, plane, mid, line, sems, 14 * n_dp)

    @pl.loop(0, n_dp)
    def _(b):
        part = pl.ds(pl.multiple_of(b * rows, rows), rows)
        lse = jnp.broadcast_to(seen[0, pl.ds(b, 1), :], (128, 8 * rows)).T[:, :1]
        value = flat(logits[:, part, :])
        column = lax.broadcasted_iota(jnp.int32, value.shape, 1)
        hit = (column == target_ref[b]).astype(F32)
        grad = (scale_ref[b] * (jnp.exp(value - lse) - hit)).astype(BF16)
        dlogits[:, part, :] = grad.reshape(8, rows, vocab)
        pltpu.make_async_copy(
            dlogits.at[:, part, :], dlogits_out.at[:, part, :], own_sems.at[2 + b]
        ).start()

    for b in range(n_dp):
        part = pl.ds(b * rows, rows)
        pltpu.make_async_copy(
            dlogits.at[:, part, :], dlogits_out.at[:, part, :], own_sems.at[2 + b]
        ).wait()
    for copy in across:
        copy.wait_send()
    for each in blocks:
        each.close()
    store.wait()


def head_call(n_dp, rows, head, target, scale):
    total = n_dp * rows.shape[0]
    vocab = head.shape[1]
    stats = (3, n_dp, 8 * rows.shape[0])
    outs = [((8, total, D), BF16), ((8, total, vocab), BF16), ((2,) + stats[1:], F32)]
    anywhere = pl.BlockSpec(memory_space=pl.ANY)
    return pl.pallas_call(
        functools.partial(head_kernel, n_dp),
        out_shape=[jax.ShapeDtypeStruct(shape, dtype) for shape, dtype in outs],
        in_specs=[pl.BlockSpec(memory_space=pltpu.VMEM)] * 3 + [anywhere],
        out_specs=[anywhere, anywhere, pl.BlockSpec(memory_space=pltpu.VMEM)],
        scratch_shapes=[
            pltpu.VMEM((8, total, D), BF16),
            pltpu.VMEM(head.shape, BF16),
            pltpu.VMEM((total, D), BF16),
            pltpu.VMEM((8, total, vocab), F32),
            pltpu.VMEM(stats, F32),
            pltpu.VMEM((7,) + stats, F32),
            pltpu.VMEM(stats, F32),
            pltpu.VMEM((n_dp - 1,) + stats, F32),
            pltpu.VMEM((8, total, vocab), BF16),
            pltpu.SemaphoreType.DMA((2, 14 * n_dp + 6 + n_dp)),
            pltpu.SemaphoreType.DMA((2 + n_dp,)),
        ],
        compiler_params=pltpu.CompilerParams(
            collective_id=5, has_side_effects=True, vmem_limit_bytes=56 << 20
        ),
        cost_estimate=pl.CostEstimate(flops=0, bytes_accessed=1 << 20, transcendentals=0),
        name="head",
    )(rows, target, scale, head)


def head_back_kernel(n_dp, cut, dlogits, head, x_in, gain, final_ref, *refs):
    dx_out, dgain, out, early, grads, own, core, held, near, last, parts, *refs = refs
    mine, sent, got, final, ready, sems, own_sem = refs
    a = lax.axis_index("dp")
    rows = x_in.shape[0]
    _, vocab, wide = head.shape
    load = pltpu.make_async_copy(final_ref, final, own_sem)
    load.start()
    greet(n_dp)
    plan = PlaneSum(parts, own, core, held, near, last, sems, 0, n_dp)

    def make(b):
        part = pl.ds(b * rows, rows)
        x = flat(dlogits[:, part, :])
        for p in range(n_dp):
            value = mm(x, head[p]).astype(BF16)
            parts[:, part, pl.ds(p * wide, wide)] = value.reshape(8, rows, wide)
        plan.at_core[b].start()

    def table_part(p, first, number):
        x = flat(final[:, :, pl.ds(pl.multiple_of(p * wide, 128), wide)])
        return mm(flat(dlogits[:, :, pl.ds(first, number)]), x, CONTRACT_FIRST).astype(BF16)

    whole = cut[0] + cut[1]
    left = [(p, v) for p in range(n_dp) for v in range(whole, vocab, 384)]

    def fill(count):
        for _ in range(min(count, len(left))):
            p, v = left.pop(0)
            number = min(384, vocab - v)
            grads[p, pl.ds(v - whole, number), :] = table_part(p, v, number)

    def rows_of(e):
        return pl.ds(e * cut[0], cut[e])

    early_sends = [
        [
            peer_copy(
                ready.at[o - 1, rows_of(e)],
                early.at[a, rows_of(e)],
                sems,
                12 + (8 + e) * n_dp + o,
                dp=a ^ o,
            )
            for o in range(1, n_dp)
        ]
        for e in range(2)
    ]
    across = {
        b: peer_copy(
            sent.at[pl.ds(b * rows, rows)], got.at[b - 1], sems, 13 + 7 * n_dp + b, dp=a ^ b
        )
        for b in range(1, n_dp)
    }

    def finish(b):
        plan.finish(b)
        if b:
            part = pl.ds(b * rows, rows)
            sent[part] = own[part].astype(BF16)
            across[b].start()

    make(2)
    load.wait()
    for o in range(1, n_dp):
        ready[o - 1, rows_of(0)] = table_part(a ^ o, 0, cut[0])
        early_sends[0][o - 1].start()
    plan.first_sends(2)
    make(3)
    plan.second_sends(2)
    plan.first_sends(3)
    make(1)
    early[a, rows_of(0)] = table_part(a, 0, cut[0])
    plan.first_sends(1)
    plan.second_sends(3)
    make(0)
    finish(2)
    plan.first_sends(0)
    fill(2)
    plan.second_sends(1)
    finish(3)
    for o in range(1, n_dp):
        ready[o - 1, rows_of(1)] = table_part(a ^ o, *cut)
    early[a, rows_of(1)] = table_part(a, *cut)
    plan.second_sends(0)
    finish(1)
    for copy in early_sends[1]:
        copy.start()
    fill(7)
    finish(0)
    fill(len(left))
    for copy in across.values():
        copy.wait()
    grad = own[pl.ds(0, rows)]
    for o in range(1, n_dp):
        grad = grad + got[o - 1].astype(F32)
    dx, dg = norm_back_step(grad, x_in[...], gain[...])
    dx_out[...] = dx
    dgain[...] = dg
    mine[...] = dx.astype(BF16)
    PlaneSpread(mine, out, sems, 7 * n_dp, 0, rows).run()
    plan.close()
    for copies in early_sends:
        for copy in copies:
            copy.wait()


def input_back_kernel(n_dp, dqkv, wqkv, x_in, gain, res, h1_ref, over, dgain, grads, *refs):
    own, core, held, near, last, parts, _, dx_out, h1, sems, h1_sem = refs
    rows, wide = res.shape[0], over.shape[2]
    blocks = x_in.shape[0] // rows
    a = lax.axis_index("dp")
    load = pltpu.make_async_copy(h1_ref, h1, h1_sem)
    load.start()
    greet(n_dp)
    plan = PlaneSum(parts, own, core, held, near, last, sems, 0, blocks)
    sent = []

    def make(b):
        part = pl.ds(b * rows, rows)
        x = flat(dqkv[:, part, :])
        for c in range(D // 512):
            value = mm(x, wqkv[pl.ds(c * 512, 512), :], CONTRACT_LAST).astype(BF16)
            parts[:, part, pl.ds(c * 512, 512)] = value.reshape(8, rows, 512)
        plan.at_core[b].start()

    left = list(range(D // 512))

    def fill():
        c = pl.ds(left.pop(0) * 512, 512)
        grads[c, :] = mm(flat(h1[:, :, c]), flat(dqkv[...]), CONTRACT_FIRST).astype(BF16)

    def close(b):
        plan.finish(b)
        part = pl.ds(b * rows, rows)
        dx, dg = norm_back_step(own[part], x_in[part], gain[...])
        if b == 0:
            dx = dx + res[...]
            dgain[...] = dg
        else:
            dgain[...] += dg
        dx_out[part] = dx.astype(BF16)

        def columns(o):
            return pl.ds(pl.multiple_of((a ^ o) * wide, 128), wide)

        over[0, part] = dx_out[part, columns(0)]
        for o in range(1, n_dp):
            copy = peer_copy(
                dx_out.at[part, columns(o)], over.at[o, part], sems, 7 * blocks + len(sent), dp=a ^ o
            )
            copy.start()
            sent.append(copy)

    make(0)
    make(1)
    plan.first_sends(0)
    make(2)
    plan.first_sends(1)
    plan.second_sends(0)
    make(3)
    plan.first_sends(2)
    plan.second_sends(1)
    plan.first_sends(3)
    load.wait()
    fill()
    close(0)
    plan.second_sends(2)
    fill()
    close(1)
    plan.second_sends(3)
    fill()
    close(2)
    fill()
    close(3)
    plan.close()
    for copy in sent:
        copy.wait()


def exchange(kernel, name, number, n_dp, total, outs, *args, more=(), sems=20, far=0, stored=0):
    half = total // 2
    rows = outs[0][0][0]
    scratch = [
        pltpu.VMEM((total, D), F32),
        pltpu.VMEM((4, total, D), BF16),
        pltpu.VMEM((4, total, D), BF16),
        pltpu.VMEM((4, half, D), BF16),
        pltpu.VMEM((2, half, D), BF16),
        pltpu.VMEM((8, total, D), BF16),
        pltpu.VMEM((rows, D), BF16),
    ]
    scratch += [pltpu.VMEM(shape, BF16) for shape in more]
    return pl.pallas_call(
        kernel,
        out_shape=[jax.ShapeDtypeStruct(shape, dtype) for shape, dtype in outs],
        in_specs=[pl.BlockSpec(memory_space=pltpu.VMEM)] * (len(args) - far)
        + [pl.BlockSpec(memory_space=pl.ANY)] * far,
        out_specs=[pl.BlockSpec(memory_space=pltpu.VMEM)] * (len(outs) - stored)
        + [pl.BlockSpec(memory_space=pl.ANY)] * stored,
        scratch_shapes=scratch
        + [pltpu.SemaphoreType.DMA((2, sems))]
        + [pltpu.SemaphoreType.DMA] * far
        + [pltpu.SemaphoreType.DMA((stored,))] * (stored > 0),
        compiler_params=pltpu.CompilerParams(
            collective_id=number, has_side_effects=True, vmem_limit_bytes=62 << 20
        ),
        cost_estimate=pl.CostEstimate(flops=0, bytes_accessed=1 << 10, transcendentals=0),
        name=name,
    )(*args)


def stats_steps(n_dp, x_ref, out_ref, plane, mid, line, sems, first):
    me = lax.axis_index("mp")
    a = lax.axis_index("dp")
    order = cube_order(8)
    rows = x_ref.shape[2] // 8
    copies = [
        peer_copy(x_ref, plane.at[s - 1], sems, first + s - 1, mp=me ^ order[s])
        for s in range(1, 8)
    ]
    for copy in copies:
        copy.start()

    def join(have, new):
        top = jnp.maximum(have[0], new[0])
        total = have[1] * jnp.exp(have[0] - top) + new[1] * jnp.exp(new[0] - top)
        return top, total, have[2] + new[2]

    have = tuple(x_ref[k] for k in range(3))
    for s in range(1, 8):
        copies[s - 1].wait_recv()
        got = [plane[s - 1, k] for k in range(3)]
        got = [
            jnp.concatenate([v[:, (e ^ s) * rows : (e ^ s) * rows + rows] for e in range(8)], axis=1)
            for v in got
        ]
        have = join(have, got)
    for k in range(3):
        mid[k] = have[k]
    across = [
        peer_copy(mid, line.at[o - 1], sems, first + 6 + o, dp=a ^ o) for o in range(1, n_dp)
    ]
    for copy in across:
        copy.start()
    for o in range(1, n_dp):
        across[o - 1].wait_recv()
        got = [line[o - 1, k] for k in range(3)]
        got = [jnp.concatenate([v[e ^ o : (e ^ o) + 1] for e in range(n_dp)], axis=0) for v in got]
        have = join(have, got)
    out_ref[0] = have[0] + jnp.log(have[1])
    out_ref[1] = have[2]
    for copy in copies + across:
        copy.wait_send()


def total_kernel(n_dp, slots_ref, more_ref, out_ref, plane, line, sems):
    me = lax.axis_index("mp")
    a = lax.axis_index("dp")
    greet(n_dp, range(1, 8))

    def add(k, have):
        g = slots_ref[pl.ds(k * 8, 8)].astype(F32)
        return have + jnp.sum((g * g).reshape(-1, 8, 128), axis=0)

    start = jnp.zeros((8, 128), F32)
    plane[me, 0] = lax.fori_loop(0, slots_ref.shape[0] // 8, add, start) + more_ref[0]
    plane[me, 1] = more_ref[1]
    copies = [peer_copy(plane.at[me], plane.at[me], sems, k - 1, mp=me ^ k) for k in range(1, 8)]
    for copy in copies:
        copy.start()
    for copy in copies:
        copy.wait()
    line[a] = jnp.sum(plane[...], axis=0)
    across = [
        peer_copy(line.at[a], line.at[a], sems, 6 + o, dp=a ^ o)
        for o in range(1, n_dp)
    ]
    for copy in across:
        copy.start()
    for copy in across:
        copy.wait()
    out_ref[...] = jnp.sum(line[...], axis=0)


def total_exchange(slots, more, n_dp):
    return pl.pallas_call(
        functools.partial(total_kernel, n_dp),
        out_shape=jax.ShapeDtypeStruct(more.shape, F32),
        in_specs=[pl.BlockSpec(memory_space=pltpu.VMEM)] * 2,
        out_specs=pl.BlockSpec(memory_space=pltpu.VMEM),
        scratch_shapes=[
            pltpu.VMEM((8,) + more.shape, F32),
            pltpu.VMEM((n_dp,) + more.shape, F32),
            pltpu.SemaphoreType.DMA((2, 6 + n_dp)),
        ],
        compiler_params=pltpu.CompilerParams(collective_id=6, has_side_effects=True),
        name="total",
    )(slots, more)


def mat_shapes(n_mp):
    width, units = D // n_mp, FF // n_mp
    return ((D, 3 * width), (width, D), (D, 2 * units), (units, D))


def each_tile(shape, size, first, step):
    rows, cols = shape

    @pl.loop(0, rows // size)
    def _(r):
        row = pl.ds(pl.multiple_of(r * size, size), size)
        for c in range(cols // size):
            step(first + r * (cols // size) + c, (row, pl.ds(c * size, size)))


def first_tiles(shapes, size):
    firsts = [0]
    for rows, cols in shapes:
        firsts.append(firsts[-1] + rows * cols // (size * size))
    return firsts


def place_kernel(shapes, slot_ref, slots_ref, *refs):
    count = len(shapes)
    outs, mats, sems = refs[:count], refs[count : 2 * count], refs[-1]
    size = slots_ref.shape[1]
    for k, (shape, first) in enumerate(zip(shapes, first_tiles(shapes, size))):

        def fetch(tile, view, k=k):
            pltpu.make_async_copy(
                slots_ref.at[slot_ref[tile]], mats[k].at[view], sems.at[0, k]
            ).start()

        each_tile(shape, size, first, fetch)
    for k in range(count):
        pltpu.make_async_copy(mats[k], mats[k], sems.at[0, k]).wait()
        pltpu.make_async_copy(mats[k], outs[k], sems.at[1, k]).start()
    for k in range(count):
        pltpu.make_async_copy(mats[k], outs[k], sems.at[1, k]).wait()


def place_tiles(slot_of, slots, shapes):
    anywhere = pl.BlockSpec(memory_space=pl.ANY)
    return pl.pallas_call(
        functools.partial(place_kernel, shapes),
        out_shape=[jax.ShapeDtypeStruct(shape, slots.dtype) for shape in shapes],
        in_specs=[pl.BlockSpec(memory_space=pltpu.SMEM), anywhere],
        out_specs=[anywhere] * len(shapes),
        scratch_shapes=[pltpu.VMEM(shape, slots.dtype) for shape in shapes]
        + [pltpu.SemaphoreType.DMA((2, len(shapes)))],
        compiler_params=pltpu.CompilerParams(vmem_limit_bytes=40 << 20),
        cost_estimate=pl.CostEstimate(flops=0, bytes_accessed=1 << 20, transcendentals=0),
        name="place_tiles",
    )(slot_of, slots)


def collect_kernel(shapes, chosen, slot_ref, *refs):
    mats = refs[: len(chosen)]
    slots_ref, sem = refs[-2:]
    size = slots_ref.shape[1]
    firsts = first_tiles(shapes, size)
    for k, ref in zip(chosen, mats):

        def send(tile, view, ref=ref):
            pltpu.make_async_copy(ref.at[view], slots_ref.at[slot_ref[tile]], sem).start()

        each_tile(shapes[k], size, firsts[k], send)
    for ref in mats:
        pltpu.make_async_copy(ref, ref, sem).wait()


def collect_tiles(slot_of, mats, shapes, chosen, given=()):
    size = 128
    anywhere = pl.BlockSpec(memory_space=pl.ANY)
    return pl.pallas_call(
        functools.partial(collect_kernel, shapes, chosen),
        out_shape=jax.ShapeDtypeStruct((slot_of.shape[0], size, size), BF16),
        in_specs=[pl.BlockSpec(memory_space=pltpu.SMEM)]
        + [pl.BlockSpec(memory_space=pltpu.VMEM)] * len(mats)
        + [anywhere] * len(given),
        out_specs=anywhere,
        scratch_shapes=[pltpu.SemaphoreType.DMA],
        compiler_params=pltpu.CompilerParams(vmem_limit_bytes=40 << 20),
        input_output_aliases={1 + len(mats): 0} if given else {},
        cost_estimate=pl.CostEstimate(flops=0, bytes_accessed=1 << 20, transcendentals=0),
        name="collect_tiles",
    )(slot_of, *mats, *given)


def after(x, *others):
    anywhere = pl.BlockSpec(memory_space=pl.ANY)
    return pl.pallas_call(
        lambda *refs: None,
        out_shape=jax.ShapeDtypeStruct(x.shape, x.dtype),
        in_specs=[anywhere] * (1 + len(others)),
        out_specs=anywhere,
        input_output_aliases={0: 0},
        cost_estimate=pl.CostEstimate(flops=0, bytes_accessed=0, transcendentals=0),
        name="after",
    )(x, *others)


def split(x):
    high = x.astype(BF16)
    return high, (x - high.astype(F32)).astype(BF16)


def adam(master, moment, second, grad, rate, decay):
    moment_new = ADAM_ONE * moment + (1.0 - ADAM_ONE) * grad
    second_new = ADAM_TWO * second + (1.0 - ADAM_TWO) * grad * grad
    corrected = (
        moment_new
        / (1.0 - ADAM_ONE**STEP)
        / (jnp.sqrt(second_new / (1.0 - ADAM_TWO**STEP)) + ADAM_EPS)
    )
    return (master - rate * (corrected + decay * master), moment_new, second_new)


def owner_step_kernel(steps, factor_ref, *refs):
    g_ref, master, left, right, l_root, r_root = refs[:6]
    t_grad, t_master, t_moment, t_second = refs[6:10]
    new, copy, grad, left_new, right_new = refs[10:15]
    t_new, t_copy, t_moment_new, t_second_new = refs[15:]
    factor = factor_ref[0, 0]

    @pl.when(pl.program_id(0) < steps)
    def _():
        for k in range(g_ref.shape[0]):
            g = g_ref[k]
            grad[k] = factor * g.astype(F32)
            outer = (mm(g, g, CONTRACT_LAST) * factor) * factor
            inner = (mm(g, g, CONTRACT_FIRST) * factor) * factor
            left_new[k] = STAT_DECAY * left[k] + (1.0 - STAT_DECAY) * outer
            right_new[k] = STAT_DECAY * right[k] + (1.0 - STAT_DECAY) * inner
            l_high, l_low = split(l_root[k])
            r_high, r_low = split(r_root[k])
            t_high, t_low = split((mm(l_high, g) + mm(l_low, g)) * factor)
            direction = mm(t_high, r_high) + (mm(t_low, r_high) + mm(t_high, r_low))
            value = master[k] - LR_MATRIX * (direction + DECAY_MATRIX * master[k])
            new[k] = value
            copy[k] = value.astype(BF16)

    @pl.when(pl.program_id(0) >= steps)
    def _():
        value, moment, second = adam(
            t_master[...],
            t_moment[...],
            t_second[...],
            factor * t_grad[...],
            LR_TABLE,
            DECAY_TABLE,
        )
        t_new[...] = value
        t_copy[...] = value.astype(BF16)
        t_moment_new[...] = moment
        t_second_new[...] = second


def owner_step(factor, tiles, table):
    number, size, _ = tiles[0].shape
    rows, cols = table[0].shape
    group, band = min(32, number), 512
    steps = number // group

    tile = pl.BlockSpec((group, size, size), lambda i: (jnp.minimum(i, steps - 1), 0, 0))
    part = pl.BlockSpec((band, cols), lambda i: (jnp.maximum(i - steps, 0), 0))
    kinds = (F32, BF16, F32, F32, F32)
    out_shape = [jax.ShapeDtypeStruct((number, size, size), kind) for kind in kinds]
    out_shape += [jax.ShapeDtypeStruct((rows, cols), kind) for kind in kinds[:4]]
    return pl.pallas_call(
        functools.partial(owner_step_kernel, steps),
        grid=(steps + rows // band,),
        out_shape=out_shape,
        in_specs=[pl.BlockSpec(memory_space=pltpu.SMEM)] + [tile] * 6 + [part] * 4,
        out_specs=[tile] * 5 + [part] * 4,
        compiler_params=pltpu.CompilerParams(vmem_limit_bytes=62 << 20),
        name="owner_step",
    )(factor, *tiles, *table)


CONTRACT_LAST = (((1,), (1,)), ((), ()))
CONTRACT_FIRST = (((0,), (0,)), ((), ()))


def mm(a, b, dims=(((1,), (0,)), ((), ()))):
    return lax.dot_general(a, b, dims, preferred_element_type=F32)


def turn(x, cosine, sine):
    lane = lax.broadcasted_iota(jnp.int32, x.shape, 1)
    other = jnp.where(
        lax.rem(lane, HD) < HD // 2, pltpu.roll(x, 128 - HD // 2, 1), pltpu.roll(x, HD // 2, 1)
    )
    return x * cosine + other * sine


def flat(x):
    return x.reshape(x.shape[0] * x.shape[1], x.shape[2])


def head_probs(q, k_ctx, k_ans, causal):
    s_ctx = mm(q, k_ctx, CONTRACT_LAST) * HD ** (-0.5)
    s_ans = jnp.where(causal, mm(q, k_ans, CONTRACT_LAST) * HD ** (-0.5), MASKED)
    top = jnp.maximum(
        jnp.max(s_ctx, axis=1, keepdims=True), jnp.max(s_ans, axis=1, keepdims=True)
    )
    e_ctx = jnp.exp(s_ctx - top)
    e_ans = jnp.exp(s_ans - top)
    total = jnp.sum(e_ctx, axis=1, keepdims=True) + jnp.sum(e_ans, axis=1, keepdims=True)
    return e_ctx / total, e_ans / total


def attend_kernel(items, h1_ref, w_ref, cos_ref, sin_ref, col_ref, row_ref, *outs):
    o_ref, qo_ref, ko_ref, vo_ref, qkv_ref = outs

    @pl.loop(0, h1_ref.shape[0])
    def _(s):
        qkv_ref[s] = mm(h1_ref[s], w_ref[...])

    n, rows_ans, width = o_ref.shape
    n_ans = rows_ans // items
    n_ctx = qkv_ref.shape[1] // items - n_ans
    causal = col_ref[...] >= row_ref[...]
    lane = lax.broadcasted_iota(jnp.int32, (1, 128), 1)

    for item in range(items):
        ans = pl.ds(item * n_ans, n_ans)
        ctx = pl.ds(rows_ans + item * n_ctx, n_ctx)
        turns = [(flat(cos_ref[:, r]), flat(sin_ref[:, r])) for r in (ans, ctx)]
        for g in range(width // 128):
            lanes = pl.ds(g * 128, 128)
            klanes = pl.ds(width + g * 128, 128)
            vlanes = pl.ds(2 * width + g * 128, 128)
            q = turn(flat(qkv_ref[:, ans, lanes]), *turns[0]).astype(BF16)
            k_ans = turn(flat(qkv_ref[:, ans, klanes]), *turns[0]).astype(BF16)
            k_ctx = turn(flat(qkv_ref[:, ctx, klanes]), *turns[1]).astype(BF16)
            v_ans = flat(qkv_ref[:, ans, vlanes]).astype(BF16)
            v_ctx = flat(qkv_ref[:, ctx, vlanes]).astype(BF16)
            qo_ref[:, ans, lanes] = q.reshape(n, n_ans, 128)
            ko_ref[:, ans, lanes] = k_ans.reshape(n, n_ans, 128)
            ko_ref[:, ctx, lanes] = k_ctx.reshape(n, n_ctx, 128)
            vo_ref[:, ans, lanes] = v_ans.reshape(n, n_ans, 128)
            vo_ref[:, ctx, lanes] = v_ctx.reshape(n, n_ctx, 128)
            got = []
            for first in (True, False):
                own = (lane < HD) == first
                p_ctx, p_ans = head_probs(jnp.where(own, q, 0), k_ctx, k_ans, causal)
                got.append(mm(p_ctx.astype(BF16), v_ctx) + mm(p_ans.astype(BF16), v_ans))
            o = jnp.where(lane < HD, got[0], got[1]).astype(BF16)
            o_ref[:, ans, lanes] = o.reshape(n, n_ans, 128)


def attend_back_kernel(items, shapes, slot_ref, *refs):
    q_ref, k_ref, v_ref, dx_ref, w_ref, o_ref, cos_ref, sin_ref, col_ref, row_ref, *refs = refs
    gate_ref, down_ref, d_ref, grad_ref, slots_ref, do_ref, gate, down, load_sems, sem = refs
    loads = [
        pltpu.make_async_copy(gate_ref, gate, load_sems.at[0]),
        pltpu.make_async_copy(down_ref, down, load_sems.at[1]),
    ]
    for copy in loads:
        copy.start()
    n, rows_ans, width = q_ref.shape
    for c in range(D // 512):
        at = pl.ds(c * 512, 512)
        grad_ref[:, at] = mm(o_ref[...], flat(dx_ref[:, :, at]), CONTRACT_FIRST).astype(BF16)
    do_ref[...] = mm(flat(dx_ref[...]), w_ref[...], CONTRACT_LAST).astype(BF16).reshape(q_ref.shape)
    n_ans = rows_ans // items
    n_ctx = k_ref.shape[1] // items - n_ans
    causal = col_ref[...] >= row_ref[...]
    lane = lax.broadcasted_iota(jnp.int32, (1, 128), 1)
    root = HD ** (-0.5)

    def collect():
        size = slots_ref.shape[1]
        firsts = first_tiles(shapes, size)
        for load, k, ref in zip(loads, (2, 3), (gate, down)):
            load.wait()

            def send(tile, view, ref=ref):
                pltpu.make_async_copy(ref.at[view], slots_ref.at[slot_ref[tile]], sem).start()

            each_tile(shapes[k], size, firsts[k], send)

    for item in range(items):
        if item == 1 or items == 1:
            collect()
        ans = pl.ds(item * n_ans, n_ans)
        ctx = pl.ds(rows_ans + item * n_ctx, n_ctx)
        turns = [(flat(cos_ref[:, r]), -flat(sin_ref[:, r])) for r in (ans, ctx)]
        d_ref[:, ctx, pl.ds(0, width)] = jnp.zeros((n, n_ctx, width), BF16)
        for g in range(width // 128):
            lanes = pl.ds(g * 128, 128)
            klanes = pl.ds(width + g * 128, 128)
            vlanes = pl.ds(2 * width + g * 128, 128)
            q, do = flat(q_ref[:, ans, lanes]), flat(do_ref[:, ans, lanes])
            k_ans, k_ctx = flat(k_ref[:, ans, lanes]), flat(k_ref[:, ctx, lanes])
            v_ans, v_ctx = flat(v_ref[:, ans, lanes]), flat(v_ref[:, ctx, lanes])
            dq, sums = [], None
            for first in (True, False):
                own = (lane < HD) == first
                q_own, do_own = jnp.where(own, q, 0), jnp.where(own, do, 0)
                p_ctx, p_ans = head_probs(q_own, k_ctx, k_ans, causal)
                dp_ctx = mm(do_own, v_ctx, CONTRACT_LAST)
                dp_ans = mm(do_own, v_ans, CONTRACT_LAST)
                mean = jnp.sum(p_ctx * dp_ctx, axis=1, keepdims=True) + jnp.sum(
                    p_ans * dp_ans, axis=1, keepdims=True
                )
                ds_ctx = (p_ctx * (dp_ctx - mean)).astype(BF16)
                ds_ans = (p_ans * (dp_ans - mean)).astype(BF16)
                dq.append(mm(ds_ctx, k_ctx) + mm(ds_ans, k_ans))
                new = [
                    mm(ds_ctx, q_own, CONTRACT_FIRST),
                    mm(ds_ans, q_own, CONTRACT_FIRST),
                    mm(p_ctx.astype(BF16), do_own, CONTRACT_FIRST),
                    mm(p_ans.astype(BF16), do_own, CONTRACT_FIRST),
                ]
                sums = new if sums is None else [a + b for a, b in zip(sums, new)]
            dq = turn(jnp.where(lane < HD, dq[0], dq[1]) * root, *turns[0])
            dk_ctx = turn(sums[0] * root, *turns[1])
            dk_ans = turn(sums[1] * root, *turns[0])
            d_ref[:, ans, lanes] = dq.astype(BF16).reshape(n, n_ans, 128)
            d_ref[:, ans, klanes] = dk_ans.astype(BF16).reshape(n, n_ans, 128)
            d_ref[:, ctx, klanes] = dk_ctx.astype(BF16).reshape(n, n_ctx, 128)
            d_ref[:, ans, vlanes] = sums[3].astype(BF16).reshape(n, n_ans, 128)
            d_ref[:, ctx, vlanes] = sums[2].astype(BF16).reshape(n, n_ctx, 128)
    for ref in (gate, down):
        pltpu.make_async_copy(ref, ref, sem).wait()


def attend_back(items, shapes, slot_of, grads, size, *args):
    query, key = args[:2]
    n, rows, width = key.shape
    anywhere = pl.BlockSpec(memory_space=pl.ANY)
    vmem = pl.BlockSpec(memory_space=pltpu.VMEM)
    return pl.pallas_call(
        functools.partial(attend_back_kernel, items, shapes),
        out_shape=[
            jax.ShapeDtypeStruct((n, rows, 3 * width), BF16),
            jax.ShapeDtypeStruct(shapes[1], BF16),
            jax.ShapeDtypeStruct((slot_of.shape[0], size, size), BF16),
        ],
        in_specs=[pl.BlockSpec(memory_space=pltpu.SMEM)] + [vmem] * len(args) + [anywhere] * 2,
        out_specs=[vmem, vmem, anywhere],
        scratch_shapes=[pltpu.VMEM(query.shape, BF16)]
        + [pltpu.VMEM(grad.shape, BF16) for grad in grads]
        + [pltpu.SemaphoreType.DMA((2,)), pltpu.SemaphoreType.DMA],
        compiler_params=pltpu.CompilerParams(vmem_limit_bytes=62 << 20),
        cost_estimate=pl.CostEstimate(flops=0, bytes_accessed=1 << 10, transcendentals=0),
        name="attend_back",
    )(slot_of, *args, *grads)


def in_vmem(kernel, name, outs, scratch, *args):
    return pl.pallas_call(
        kernel,
        out_shape=[jax.ShapeDtypeStruct(shape, dtype) for shape, dtype in outs],
        in_specs=[pl.BlockSpec(memory_space=pltpu.VMEM)] * len(args),
        out_specs=[pl.BlockSpec(memory_space=pltpu.VMEM)] * len(outs),
        scratch_shapes=[pltpu.VMEM(shape, dtype) for shape, dtype in scratch],
        compiler_params=pltpu.CompilerParams(vmem_limit_bytes=62 << 20),
        cost_estimate=pl.CostEstimate(flops=0, bytes_accessed=1 << 10, transcendentals=0),
        name=name,
    )(*args)


def norm_forward(x):
    inverse = lax.rsqrt(jnp.mean(x * x, axis=-1, keepdims=True) + EPS_NORM)
    return (x * inverse, inverse)


def norm_backward(grad, normed, inverse, gain):
    scaled = grad * gain
    dgain = jnp.sum(grad * normed, axis=0)
    dx = inverse * (scaled - normed * jnp.mean(scaled * normed, axis=-1, keepdims=True))
    return (dx, dgain)


def body(
    tokens,
    targets,
    pair_order,
    lengths,
    loss_mask,
    start_pos,
    owner_map,
    block_master,
    left_stat,
    right_stat,
    left_root,
    right_root,
    table_master,
    table_moment,
    table_second,
    gain_master,
    gain_moment,
    gain_second,
):
    dp = lax.axis_index("dp")
    mp = lax.axis_index("mp")
    n_mp = lax.axis_size("mp")
    n_dp = lax.axis_size("dp")
    fused = (n_mp, n_dp) == (8, 4)
    items, length = tokens.shape
    context = length - ANS
    n_ans = ANS // n_mp
    n_ctx = context // n_mp
    rows_ans = items * n_ans
    rows_own = items * (n_ans + n_ctx)
    width = D // n_mp
    units = FF // n_mp
    heads = width // HD
    vocab_part, cols = table_master.shape
    sub = vocab_part // n_dp
    perm = owner_map[0]
    who = mp ^ jnp.array(cube_order(n_mp), jnp.int32)
    near = dp ^ jnp.arange(n_dp, dtype=jnp.int32)

    slots = lax.all_gather(block_master[0].astype(BF16), "dp", axis=0, tiled=True)
    gains = line_gather(gain_master.astype(BF16))
    wide = jnp.zeros((3, D), BF16)
    for o in range(n_dp):
        wide = lax.dynamic_update_slice(wide, gains[o], (0, near[o] * cols))
    gains = wide.astype(F32)
    table_low = table_master.astype(BF16)

    packed = jnp.concatenate([tokens, targets, loss_mask, lengths[:, None]], axis=1)
    packed = jnp.stack(line_gather(packed))
    all_tokens = packed[:, :, :length]
    all_targets = packed[:, :, length : length + ANS]
    all_mask = packed[:, :, length + ANS : length + 2 * ANS]
    all_lengths = packed[:, :, -1]
    column = jnp.arange(ANS)
    weights = jnp.where(
        column == 0,
        1.0,
        jnp.where(column < all_lengths[..., None], all_mask.astype(F32), 0.0),
    )
    pairs_all = pair_order.shape[0] // 2
    pairs = (pair_order // 2).reshape(n_dp, items)[near]
    member = (pairs[..., None] == jnp.arange(pairs_all)).astype(F32)
    counts = jnp.einsum("oip,oi->p", member, jnp.sum(weights, axis=-1))
    scale = weights / (jnp.sum(member * counts, axis=-1)[..., None] * pairs_all)

    def by_owner(x):
        split = x.reshape(n_dp, items, n_mp, n_ans)[:, :, who]
        return split.transpose(2, 0, 1, 3)

    row_scale = by_owner(scale).reshape(-1)
    row_target = by_owner(all_targets).reshape(-1)
    tok_ans = all_tokens[:, :, context:].reshape(n_dp, items, n_mp, n_ans)[:, :, who]
    tok_ctx = all_tokens[:, :, :context].reshape(n_dp, items, n_mp, n_ctx)[:, :, who]
    tok = jnp.concatenate(
        [
            tok_ans.transpose(2, 0, 1, 3).reshape(n_mp, n_dp, -1),
            tok_ctx.transpose(2, 0, 1, 3).reshape(n_mp, n_dp, -1),
        ],
        axis=2,
    )

    shapes = mat_shapes(n_mp)
    number = perm.shape[0]
    slot_of = jnp.zeros_like(perm).at[perm].set(jnp.arange(number, dtype=jnp.int32))

    local = tok - mp * vocab_part
    valid = (local >= 0) & (local < vocab_part)
    safe = jnp.clip(local, 0, vocab_part - 1)
    looked = jnp.where(valid[..., None], jnp.take(table_low, safe, axis=0), 0)
    own_cols = cube_scatter(looked).astype(BF16)
    pieces = line_exchange([own_cols[o] for o in range(n_dp)])
    x0 = jnp.zeros((rows_own, D), BF16)
    for o in range(n_dp):
        x0 = lax.dynamic_update_slice(x0, pieces[o], (0, near[o] * cols))
    x0 = x0.astype(F32)
    normed1, inverse1 = norm_forward(x0)
    h1 = cube_gather((normed1 * gains[0]).astype(BF16))
    h1_all = h1.reshape(-1, D)

    wqkv, wout, wgate, wdown = place_tiles(slot_of, slots, shapes)

    table_late = after(table_low, slots, h1)
    head_parts = lax.all_to_all(table_late.reshape(n_dp, sub, cols), "dp", 0, 0)

    half = HD // 2
    freq = ROPE_BASE ** (-jnp.arange(half).astype(F32) * 2.0 / HD)
    t_ans = context + who[:, None] * n_ans + jnp.arange(n_ans)
    t_ctx = who[:, None] * n_ctx + jnp.arange(n_ctx)

    def angles(t):
        place = (start_pos[None, :, None] + t[:, None, :]).astype(F32)
        angle = place.reshape(n_mp, -1)[..., None] * freq
        return jnp.cos(angle), jnp.sin(angle)

    cosine, sine = (jnp.concatenate(pair, axis=1) for pair in zip(angles(t_ans), angles(t_ctx)))
    cosine = jnp.concatenate([cosine] * 4, axis=-1)
    sine = jnp.concatenate([-sine, sine] * 2, axis=-1)
    t_query = t_ans.reshape(-1)
    place = (t_query[:, None], t_query[None, :])

    ans_shape = ((n_mp, rows_ans, width), BF16)
    key_shape = ((n_mp, rows_own, width), BF16)
    o_rows, query, key, value = in_vmem(
        functools.partial(attend_kernel, items),
        "attend",
        (ans_shape, ans_shape, key_shape, key_shape),
        (((n_mp, rows_own, 3 * width), F32),),
        *(h1, wqkv, cosine, sine, *place),
    )
    own = ((rows_ans, D), F32)
    gain_row = ((1, D), F32)
    plane = ((n_mp, rows_ans, D), BF16)
    if fused:
        x1, h2 = exchange(
            attend_sum_kernel, "attend_sum", 1, n_dp, rows_ans, (own, plane),
            *(o_rows, wout, x0[:rows_ans], gains[1:2]),
        )
    else:
        parts = dot("tw,wd->td", o_rows.reshape(-1, width), wout).astype(BF16)
        x1 = x0[:rows_ans] + cube_scatter(parts.reshape(n_mp, rows_ans, D))
        h2 = cube_gather((norm_forward(x1)[0] * gains[1]).astype(BF16))
    o_rows = o_rows.reshape(-1, width)

    if fused:
        flat_units = n_mp * rows_ans
        x2, gate_up, hidden, final = exchange(
            units_sum_kernel, "units_sum", 2, n_dp, rows_ans,
            (
                own,
                ((flat_units, 2 * units), F32),
                ((flat_units, units), BF16),
                ((rows_ans, D), BF16),
            ),
            *(h2, wgate, wdown, x1, gains[2:3]),
        )
        h2 = h2.reshape(-1, D)
    else:
        h2 = h2.reshape(-1, D)
        gate_up = dot("td,df->tf", h2, wgate)
        gate, upward = gate_up[:, :units], gate_up[:, units:]
        hidden = (jax.nn.silu(gate) * upward).astype(BF16)
        parts = dot("tf,fd->td", hidden, wdown).astype(BF16)
        x2 = x1 + cube_scatter(parts.reshape(n_mp, rows_ans, D))

    def by_line(x):
        return x.reshape(n_mp, n_dp, rows_ans).transpose(1, 0, 2).reshape(n_dp, -1, 1)

    first = mp * vocab_part + dp * sub
    if fused:
        final, dlogits, seen = head_call(
            n_dp, final, head_parts, by_line(row_target - first), by_line(row_scale)
        )
        lse, picked = seen[0, 0], seen[1, 0]
        dlogits = dlogits.reshape(-1, sub)
        final = final.reshape(-1, D)
    else:
        head = jnp.concatenate([head_parts[a] for a in range(n_dp)], axis=1)
        final = (norm_forward(x2)[0] * gains[2]).astype(BF16)
        final = cube_gather(jnp.stack(line_gather(final)).reshape(-1, D))
        final = final.reshape(-1, D)
        logits = dot("rd,vd->rv", final, head)
        hit = jnp.arange(sub, dtype=jnp.int32)[None, :] == (row_target - first)[:, None]
        top = jnp.max(logits, axis=1)
        total = jnp.sum(jnp.exp(logits - top[:, None]), axis=1)
        picked = jnp.sum(jnp.where(hit, logits, 0.0), axis=1)
        top, total, picked = stats_everywhere(jnp.stack([top, total, picked]), rows_ans)
        lse = top + jnp.log(total)
        dlogits = (
            row_scale[:, None] * (jnp.exp(logits - lse[:, None]) - hit.astype(F32))
        ).astype(BF16)
    loss_own = jnp.sum(row_scale[:rows_ans] * (lse - picked)[:rows_ans]) * pairs_all

    if fused:
        cut = (256, 128)
        total = n_dp * rows_ans
        dx2, dgain3, down_in, early_grad, head_grad = exchange(
            functools.partial(head_back_kernel, n_dp, cut), "head_sum", 3, n_dp, total,
            (
                own,
                gain_row,
                plane,
                ((n_dp, sum(cut), cols), BF16),
                ((n_dp, sub - sum(cut), cols), BF16),
            ),
            *(dlogits.reshape(n_mp, -1, sub), head_parts, x2, gains[2:3]),
            final.reshape(n_mp, -1, D),
            more=(
                (total, D),
                (n_dp - 1, rows_ans, D),
                (n_mp, total, D),
                (n_dp - 1, sum(cut), cols),
            ),
            sems=13 + 10 * n_dp,
            far=1,
        )
        dgain3 = dgain3[0]
    else:
        parts = dot("rv,vd->rd", dlogits, head).astype(BF16)
        mine = cube_scatter(parts.reshape(n_mp, n_dp * rows_ans, D)).astype(BF16)
        mine = line_exchange(list(mine.reshape(n_dp, rows_ans, D)))
        dfinal = sum(piece.astype(F32) for piece in mine)
        dx2, dgain3 = norm_backward(dfinal, *norm_forward(x2), gains[2])
        down_in = cube_gather(dx2.astype(BF16))
        head_grad = jnp.stack(
            [
                dot("rv,rd->vd", dlogits, final[:, a * cols : (a + 1) * cols]).astype(BF16)
                for a in range(n_dp)
            ]
        )
    table_grad = lax.all_to_all(head_grad, "dp", 0, 0)
    if fused:
        dx1, dgain2, dgate_up, out_in, grad_down, grad_gate = exchange(
            gate_sum_kernel, "gate_sum", 4, n_dp, rows_ans,
            (
                own,
                gain_row,
                (gate_up.shape, BF16),
                plane,
                (wdown.shape, BF16),
                (wgate.shape, BF16),
            ),
            *(down_in, wdown, wgate, gate_up, x1, gains[1:2], dx2),
            *(h2.reshape(n_mp, rows_ans, D), hidden),
            more=((n_mp, rows_ans, D), hidden.shape, wdown.shape, wgate.shape),
            far=2,
            stored=2,
        )
        dgain2 = dgain2[0]
        down_in = down_in.reshape(-1, D)
    else:
        down_in = down_in.reshape(-1, D)
        dhidden = dot("td,fd->tf", down_in, wdown)
        sigma = jax.nn.sigmoid(gate)
        dgate = dhidden * upward * sigma * (1.0 + gate * (1.0 - sigma))
        dgate_up = jnp.concatenate([dgate, dhidden * gate * sigma], axis=-1).astype(BF16)
        parts = dot("tf,df->td", dgate_up, wgate).astype(BF16)
        dnormed2 = cube_scatter(parts.reshape(n_mp, rows_ans, D))
        dx_mlp, dgain2 = norm_backward(dnormed2, *norm_forward(x1), gains[1])
        dx1 = dx2 + dx_mlp
        out_in = cube_gather(dx1.astype(BF16))
        grad_down = dot("tf,td->fd", hidden, down_in).astype(BF16)
        grad_gate = dot("td,tf->df", h2, dgate_up).astype(BF16)
    dqkv, grad_out, slots = attend_back(
        items, shapes, slot_of, (grad_gate, grad_down), block_master.shape[-1],
        *(query, key, value, out_in, wout, o_rows, cosine, sine, *place),
    )
    dqkv = dqkv.reshape(-1, 3 * width)

    if fused:
        rows_over, dgain1, grad_qkv = exchange(
            functools.partial(input_back_kernel, n_dp), "input_sum", 7, n_dp, rows_own,
            (((n_dp, rows_own, cols), BF16), gain_row, (wqkv.shape, BF16)),
            *(dqkv.reshape(n_mp, rows_own, -1), wqkv, x0, gains[:1], dx1, h1),
            more=((rows_own, D), (n_mp, rows_own, D)),
            sems=(7 + n_dp - 1) * (rows_own // rows_ans),
            far=1,
        )
        dgain1 = dgain1[0]
    else:
        dh1 = dot("te,de->td", dqkv, wqkv).astype(BF16).reshape(n_mp, rows_own, D)
        grad_qkv = dot("td,te->de", h1_all, dqkv).astype(BF16)
        dx0, dgain1 = norm_backward(cube_scatter(dh1), *norm_forward(x0), gains[0])
        dx0 = jnp.concatenate([dx0[:rows_ans] + dx1, dx0[rows_ans:]]).astype(BF16)
        parts = [lax.dynamic_slice_in_dim(dx0, near[o] * cols, cols, 1) for o in range(n_dp)]
        rows_over = jnp.stack(line_exchange(parts))

    slots = collect_tiles(slot_of, (grad_qkv, grad_out), shapes, (0, 1), (slots,))
    slots = after(slots, table_grad, rows_over)
    own_slots = lax.psum_scatter(slots, "dp", scatter_dimension=0, tiled=True)

    if fused:
        table_grad = jnp.concatenate([early_grad, table_grad], axis=1)
    rows_back = cube_gather(rows_over.reshape(-1, cols)).reshape(safe.shape + (cols,))
    picked_rows = jnp.where(valid[..., None], rows_back, 0).astype(F32)
    own_table = table_grad.reshape(vocab_part, cols).astype(F32).at[safe.reshape(-1)].add(picked_rows.reshape(-1, cols))

    gain_grad = jnp.stack([dgain1, dgain2, dgain3])
    gain_total = everywhere(gain_grad, jnp.add)
    own_gain = lax.dynamic_slice_in_dim(gain_total, dp * cols, cols, 1)
    first_mp = (mp == 0).astype(F32)
    squares = jnp.sum(own_table * own_table) + first_mp * jnp.sum(own_gain * own_gain)
    if fused:
        more = jnp.zeros((2, 8, 128), F32).at[:, 0, 0].set(jnp.stack([squares, loss_own]))
        squares_all, loss_total = jnp.sum(total_exchange(own_slots, more, n_dp), axis=(1, 2))
    else:
        squares = squares + jnp.sum(jnp.square(own_slots.astype(F32)))
        more = everywhere(jnp.stack([squares, loss_own])[None], jnp.add)[0]
        squares_all, loss_total = more
    norm = jnp.sqrt(squares_all)
    factor = CLIP_NORM / jnp.maximum(norm, CLIP_NORM)
    roots = (left_stat[0], right_stat[0], left_root[0], right_root[0])
    block_new, block_copy, grad_slots, left_new, right_new, *table_step = owner_step(
        factor.reshape(1, 1),
        (own_slots, block_master[0], *roots),
        (own_table, table_master, table_moment, table_second),
    )
    table_new, table_copy, table_moment_new, table_second_new = table_step
    gain_new, gain_moment_new, gain_second_new = adam(
        gain_master, gain_moment, gain_second, factor * own_gain, LR_GAIN, 0.0
    )
    return (
        loss_total,
        norm,
        block_new[None],
        block_copy[None],
        grad_slots[None],
        left_new[None],
        right_new[None],
        table_new,
        table_copy,
        table_moment_new,
        table_second_new,
        gain_new,
        gain_moment_new,
        gain_second_new,
    )


def solution(mesh):
    in_specs = (
        P("dp", None),
        P("dp", None),
        P(),
        P("dp"),
        P("dp", None),
        P("dp"),
        P("mp", None),
        P("mp", "dp", None, None),
        P("mp", "dp", None, None),
        P("mp", "dp", None, None),
        P("mp", "dp", None, None),
        P("mp", "dp", None, None),
        P("mp", "dp"),
        P("mp", "dp"),
        P("mp", "dp"),
        P(None, "dp"),
        P(None, "dp"),
        P(None, "dp"),
    )
    out_specs = (
        P(),
        P(),
        P("mp", "dp", None, None),
        P("mp", "dp", None, None),
        P("mp", "dp", None, None),
        P("mp", "dp", None, None),
        P("mp", "dp", None, None),
        P("mp", "dp"),
        P("mp", "dp"),
        P("mp", "dp"),
        P("mp", "dp"),
        P(None, "dp"),
        P(None, "dp"),
        P(None, "dp"),
    )
    return jax.shard_map(body, mesh=mesh, in_specs=in_specs, out_specs=out_specs, check_vma=False)
```

```python
import functools

import jax
import jax.numpy as jnp
from jax import lax
from jax.experimental import pallas as pl
from jax.experimental.pallas import tpu as pltpu
from jax.sharding import PartitionSpec as P

D = 2048
HD = 64
FF = 8192
ANS = 256
STEP = 5


EPS_NORM = 1e-05
ROPE_BASE = 130000.0
CLIP_NORM = 0.01
STAT_DECAY = 0.95
LR_MATRIX = 0.05
DECAY_MATRIX = 0.1
LR_TABLE = 0.03
DECAY_TABLE = 0.1
LR_GAIN = 0.2
ADAM_ONE = 0.9
ADAM_TWO = 0.95
ADAM_EPS = 1e-08
MASKED = -1e30
F32 = jnp.float32
BF16 = jnp.bfloat16


def dot(spec, a, b):
    return jnp.einsum(spec, a, b, preferred_element_type=F32)


def cube_bits(n):
    bits = [1 << i for i in range(n.bit_length() - 1)]
    return bits[1:] + bits[:1]


def cube_order(n):
    order = [0]
    for bit in cube_bits(n):
        order = order + [o ^ bit for o in order]
    return order


def swap(x, axis, bit):
    n = lax.axis_size(axis)
    return lax.ppermute(x, axis, [(i, i ^ bit) for i in range(n)])


def cube_gather(x):
    n = lax.axis_size("mp")
    if n != 8:
        held = x[None]
        for bit in cube_bits(n):
            held = jnp.concatenate([held, swap(held, "mp", bit)])
        return held
    half = x.shape[0] // 2
    over_x = swap(x, "mp", 2)
    over_y = swap(x, "mp", 4)
    far = jnp.concatenate([swap(over_x[:half], "mp", 4), swap(over_y[half:], "mp", 2)])
    held = jnp.stack([x, over_x, over_y, far])
    return jnp.concatenate([held, swap(held, "mp", 1)])


def cube_scatter(parts):
    n = lax.axis_size("mp")
    if n != 8:
        held = parts
        for bit in reversed(cube_bits(n)):
            keep = held.shape[0] // 2
            other = swap(held[keep:].astype(BF16), "mp", bit)
            held = held[:keep].astype(F32) + other.astype(F32)
        return held[0]
    got = swap(parts[4:], "mp", 1)
    held = (parts[:4].astype(F32) + got.astype(F32)).astype(BF16)
    half = held.shape[1] // 2
    one, two = held[:, :half], held[:, half:]
    one_x = swap(one[1::2], "mp", 2)
    two_y = swap(two[2:], "mp", 4)
    one = one[0::2].astype(F32) + one_x.astype(F32)
    two = two[:2].astype(F32) + two_y.astype(F32)
    one_y = swap(one[1].astype(BF16), "mp", 4)
    two_x = swap(two[1].astype(BF16), "mp", 2)
    return jnp.concatenate([one[0] + one_y.astype(F32), two[0] + two_x.astype(F32)])


def line_gather(x):
    return [x] + [swap(x, "dp", o) for o in range(1, lax.axis_size("dp"))]


def line_exchange(parts):
    return [parts[0]] + [swap(parts[o], "dp", o) for o in range(1, len(parts))]


def combine_stats(a, b):
    top = jnp.maximum(a[0], b[0])
    total = a[1] * jnp.exp(a[0] - top) + b[1] * jnp.exp(b[0] - top)
    return jnp.stack([top, total, a[2] + b[2]])


def everywhere(x, op):
    for axis in ("mp", "dp"):
        bit = 1
        while bit < lax.axis_size(axis):
            x = op(x, swap(x, axis, bit))
            bit *= 2
    return x


def stats_everywhere(x, rows):
    n_mp, n_dp = lax.axis_size("mp"), lax.axis_size("dp")
    bits = cube_bits(n_mp)
    split = (3,) + (2,) * len(bits) + (n_dp * rows,)
    x = x.reshape(split)
    for i, bit in enumerate(bits):
        x = combine_stats(x, jnp.flip(swap(x, "mp", bit), len(bits) - i))
    x = x.reshape(3, n_mp, n_dp, rows)
    total = x
    for o, other in enumerate(line_gather(x)):
        if o:
            order = [e ^ o for e in range(n_dp)]
            total = combine_stats(total, jnp.stack([other[:, :, e] for e in order], axis=2))
    return total.reshape(3, -1)


def peer_copy(src, dst, sems, k, **device):
    return pltpu.make_async_remote_copy(
        src_ref=src,
        dst_ref=dst,
        send_sem=sems.at[0, k],
        recv_sem=sems.at[1, k],
        device_id=device,
        device_id_type=pl.DeviceIdType.MESH,
    )


def greet(n_dp, bits=(1, 2, 4)):
    me = lax.axis_index("mp")
    a = lax.axis_index("dp")
    barrier = pltpu.get_barrier_semaphore()
    partners = [{"mp": me ^ bit} for bit in bits]
    partners += [{"dp": a ^ o} for o in range(1, n_dp)]
    for partner in partners:
        pl.semaphore_signal(barrier, 1, device_id=partner, device_id_type=pl.DeviceIdType.MESH)
    return lambda: pl.semaphore_wait(barrier, len(partners))


def by_rows(count, step):
    @pl.loop(0, count // 16)
    def _(i):
        step(pl.multiple_of(i * 16, 16))


class PlaneSum:
    def __init__(self, parts, own, core, held, near, last, sems, first, blocks):
        me = lax.axis_index("mp")
        self.refs = parts, own, core, held, near, last
        self.rows = own.shape[0] // blocks
        self.half = half = self.rows // 2
        self.at_core = []
        self.blocks = []
        for b in range(blocks):
            whole = pl.ds(b * self.rows, self.rows)
            top, low = pl.ds(b * self.rows, half), pl.ds(b * self.rows + half, half)
            spot = pl.ds(b * half, half)
            k = first + 7 * b
            self.at_core.append(
                peer_copy(parts.at[4:8, whole], core.at[:, whole], sems, k, mp=me ^ 1)
            )
            sends = (
                (3, top, near, 0, 2),
                (3, low, near, 1, 4),
                (1, top, near, 2, 2),
                (2, low, near, 3, 4),
                (2, top, last, 0, 4),
                (1, low, last, 1, 2),
            )
            self.blocks.append(
                [
                    peer_copy(held.at[s, rows], to.at[at, spot], sems, k + 1 + e, mp=me ^ bit)
                    for e, (s, rows, to, at, bit) in enumerate(sends)
                ]
            )

    def first_sends(self, b):
        self.at_core[b].wait_recv()
        parts, _, core, held, _, _ = self.refs
        copies = self.blocks[b]
        for s, sent in ((3, copies[:2]), (1, copies[2:3]), (2, copies[3:4])):

            def add(at, s=s):
                rows = pl.ds(b * self.rows + at, 16)
                value = parts[s, rows].astype(F32) + core[s, rows].astype(F32)
                held[s, rows] = value.astype(BF16)

            by_rows(self.rows, add)
            for copy in sent:
                copy.start()

    def second_sends(self, b):
        _, _, _, held, near, _ = self.refs
        copies = self.blocks[b]
        for e, s, offset in ((0, 2, 0), (1, 1, self.half)):
            copies[e].wait_recv()

            def add(at, e=e, s=s, offset=offset):
                rows = pl.ds(b * self.rows + offset + at, 16)
                value = held[s, rows].astype(F32) + near[e, pl.ds(b * self.half + at, 16)].astype(F32)
                held[s, rows] = value.astype(BF16)

            by_rows(self.half, add)
            copies[4 + e].start()

    def finish(self, b):
        parts, own, core, _, near, last = self.refs
        for copy in self.blocks[b][2:]:
            copy.wait_recv()

        def total(at):
            spot = pl.ds(b * self.half + at, 16)
            for e, offset in ((0, 0), (1, self.half)):
                rows = pl.ds(b * self.rows + offset + at, 16)
                own[rows] = (
                    (parts[0, rows].astype(F32) + core[0, rows].astype(F32))
                    + near[2 + e, spot].astype(F32)
                    + last[e, spot].astype(F32)
                )

        by_rows(self.half, total)

    def close(self):
        for core, copies in zip(self.at_core, self.blocks):
            core.wait_send()
            for copy in copies:
                copy.wait_send()

    def run(self, fill=lambda: None):
        for b in range(len(self.blocks)):
            self.at_core[b].start()
        for step in (self.first_sends, self.second_sends, self.finish):
            fill()
            for b in range(len(self.blocks)):
                step(b)
        self.close()


class PlaneSpread:
    def __init__(self, x, out, sems, k, start, rows):
        me = lax.axis_index("mp")
        half = rows // 2
        top, low, whole = pl.ds(start, half), pl.ds(start + half, half), pl.ds(start, rows)
        self.own = x, out, start, rows

        def copy(src, slot, part, e, bit):
            return peer_copy(src, out.at[slot, part], sems, k + e, mp=me ^ bit)

        self.x_top = copy(x.at[top], 1, top, 0, 2)
        self.y_low = copy(x.at[low], 2, low, 1, 4)
        self.x_low = copy(x.at[low], 1, low, 2, 2)
        self.y_top = copy(x.at[top], 2, top, 3, 4)
        self.core = copy(x.at[whole], 4, whole, 4, 1)
        self.far_y = copy(out.at[1, top], 3, top, 5, 4)
        self.far_x = copy(out.at[2, low], 3, low, 6, 2)
        self.to_core = {
            (s, r): copy(out.at[s, part], 4 + s, part, 7 + 2 * (s - 1) + r, 1)
            for s in (1, 2, 3)
            for r, part in enumerate((top, low))
        }

    def begin(self):
        for c in (self.x_top, self.y_low, self.x_low, self.y_top, self.core):
            c.start()
        x, out, start, rows = self.own

        def keep(at):
            part = pl.ds(start + at, 16)
            out[0, part] = x[part]

        by_rows(rows, keep)

    def relay(self):
        self.x_top.wait_recv()
        self.far_y.start()
        self.to_core[1, 0].start()
        self.y_low.wait_recv()
        self.far_x.start()
        self.to_core[2, 1].start()
        self.x_low.wait_recv()
        self.to_core[1, 1].start()
        self.y_top.wait_recv()
        self.to_core[2, 0].start()

    def relay_far(self):
        self.far_y.wait_recv()
        self.to_core[3, 0].start()
        self.far_x.wait_recv()
        self.to_core[3, 1].start()

    def arrive(self):
        self.core.wait_recv()
        for c in self.to_core.values():
            c.wait_recv()

    def close(self):
        sent = (self.x_top, self.y_low, self.x_low, self.y_top, self.core, self.far_y, self.far_x)
        for c in (*sent, *self.to_core.values()):
            c.wait_send()

    def run(self, fill=lambda: None):
        self.begin()
        fill()
        self.relay()
        fill()
        self.relay_far()
        self.arrive()
        self.close()


def norm_step(x, gain):
    return (x * lax.rsqrt(jnp.mean(x * x, axis=1, keepdims=True) + EPS_NORM)) * gain


def norm_back_step(grad, x, gain):
    inverse = lax.rsqrt(jnp.mean(x * x, axis=1, keepdims=True) + EPS_NORM)
    normed = x * inverse
    scaled = grad * gain
    dx = inverse * (scaled - normed * jnp.mean(scaled * normed, axis=1, keepdims=True))
    return dx, jnp.sum(grad * normed, axis=0, keepdims=True)


def by_columns(step, width=512):
    for c in range(D // width):
        step(pl.ds(c * width, width))


def forward_step(refs, res, gain, x_out):
    own, core, held, near, last, parts, _, sems = refs
    PlaneSum(parts, own, core, held, near, last, sems, 0, 1).run()
    x = res[...] + own[...]
    x_out[...] = x
    return norm_step(x, gain[...]).astype(BF16)


def attend_sum_kernel(o, wout, res, gain, x_out, out, *refs):
    *_, parts, mine, sems = refs
    met = greet(1)

    def make(c):
        parts[:, :, c] = mm(flat(o[...]), wout[:, c]).astype(BF16).reshape(8, -1, c.size)

    by_columns(make)
    met()
    mine[...] = forward_step(refs, res, gain, x_out)
    PlaneSpread(mine, out, sems, 7, 0, mine.shape[0]).run()


def units_sum_kernel(h2, wgate, wdown, res, gain, x_out, gate_up, hidden, out, *refs):
    *_, parts, _, _ = refs
    units = wdown.shape[0]
    met = greet(1)
    x = flat(h2[...])
    step = min(units, 512)
    for c in range(2 * units // step):
        at = pl.ds(c * step, step)
        gate_up[:, at] = mm(x, wgate[:, at])
    for c in range(units // step):
        at, up = pl.ds(c * step, step), pl.ds(units + c * step, step)
        gate = gate_up[:, at]
        hidden[:, at] = (gate / (1.0 + jnp.exp(-gate)) * gate_up[:, up]).astype(BF16)

    def make(c):
        parts[:, :, c] = mm(hidden[...], wdown[:, c]).astype(BF16).reshape(8, -1, c.size)

    by_columns(make)
    met()
    out[...] = forward_step(refs, res, gain, x_out)


def gate_sum_kernel(down_in, wdown, wgate, gate_up, x_in, gain, res, h2_ref, hidden_ref, *refs):
    dx_out, dgain, dgate_up, out, down_out, gate_out, *refs = refs
    own, core, held, near, last, parts, mine, *refs = refs
    h2, hidden, down_grad, gate_grad, sems, h2_sem, hidden_sem, store_sems = refs
    units = wdown.shape[0]
    loads = [
        pltpu.make_async_copy(h2_ref, h2, h2_sem),
        pltpu.make_async_copy(hidden_ref, hidden, hidden_sem),
    ]
    stores = [
        pltpu.make_async_copy(down_grad, down_out, store_sems.at[0]),
        pltpu.make_async_copy(gate_grad, gate_out, store_sems.at[1]),
    ]
    for copy in loads:
        copy.start()
    met = greet(1)
    x = flat(down_in[...])
    step = min(units, 512)
    for c in range(units // step):
        at, up = pl.ds(c * step, step), pl.ds(units + c * step, step)
        grad = mm(x, wdown[at, :], CONTRACT_LAST)
        gate, upward = gate_up[:, at], gate_up[:, up]
        sigma = 1.0 / (1.0 + jnp.exp(-gate))
        dgate = grad * upward * sigma * (1.0 + gate * (1.0 - sigma))
        dgate_up[:, at] = dgate.astype(BF16)
        dgate_up[:, up] = (grad * gate * sigma).astype(BF16)

    def make(c):
        value = mm(dgate_up[...], wgate[c, :], CONTRACT_LAST)
        parts[:, :, c] = value.astype(BF16).reshape(8, -1, c.size)

    by_columns(make)
    left = [(down_grad, c) for c in range(0, D, step)]
    left += [(gate_grad, c) for c in range(0, 2 * units, step)]

    def fill(count=2):
        for _ in range(min(count, len(left))):
            grad, c = left.pop(0)
            at = pl.ds(c, step)
            if grad is down_grad:
                value = mm(hidden[...], flat(down_in[:, :, at]), CONTRACT_FIRST)
            else:
                value = mm(flat(h2[...]), dgate_up[:, at], CONTRACT_FIRST)
            grad[:, at] = value.astype(BF16)
            if not left:
                stores[1].start()
            elif grad is down_grad and left[0][0] is gate_grad:
                stores[0].start()

    for copy in loads:
        copy.wait()
    met()
    PlaneSum(parts, own, core, held, near, last, sems, 0, 1).run(fill)
    dx, dg = norm_back_step(own[...], x_in[...], gain[...])
    dx = dx + res[...]
    dx_out[...] = dx
    dgain[...] = dg
    mine[...] = dx.astype(BF16)
    PlaneSpread(mine, out, sems, 7, 0, mine.shape[0]).run(fill)
    fill(len(left))
    for copy in stores:
        copy.wait()


def head_kernel(n_dp, rows_ref, target_ref, scale_ref, *refs):
    head_ref, final_out, dlogits_out, seen, final, head, mine, logits, *refs = refs
    stats, plane, mid, line, dlogits, sems, own_sems = refs
    rows, vocab = rows_ref.shape[0], logits.shape[2]
    wide = head.shape[2]
    load = pltpu.make_async_copy(head_ref, head, own_sems.at[0])
    store = pltpu.make_async_copy(final, final_out, own_sems.at[1])
    load.start()
    a = lax.axis_index("dp")
    greet(n_dp, range(1, 8))()
    mine[pl.ds(0, rows)] = rows_ref[...]
    block = [pl.ds(o * rows, rows) for o in range(4)]
    across = [
        peer_copy(rows_ref, mine.at[block[1]], sems, 53, dp=a ^ 1),
        peer_copy(rows_ref, mine.at[block[2]], sems, 54, dp=a ^ 2),
        peer_copy(mine.at[block[2]], mine.at[block[3]], sems, 55, dp=a ^ 1),
    ]
    across[0].start()
    across[1].start()
    blocks = [PlaneSpread(mine, final, sems, 13 * o, o * rows, rows) for o in range(n_dp)]
    tile = 512 if vocab % 512 == 0 else vocab

    def use(b):
        part = pl.ds(b * rows, rows)

        @pl.loop(0, vocab // tile)
        def _(v):
            at = pl.ds(pl.multiple_of(v * tile, tile), tile)
            value = None
            for p in range(n_dp):
                x = flat(final[:, part, pl.ds(p * wide, wide)])
                term = mm(x, head[p, at, :], CONTRACT_LAST)
                value = term if value is None else value + term
            logits[:, part, at] = value.reshape(8, rows, tile)

        value = flat(logits[:, part, :])
        top = jnp.max(value, axis=1, keepdims=True)
        expo = jnp.sum(jnp.exp(value - top), axis=1, keepdims=True)
        column = lax.broadcasted_iota(jnp.int32, value.shape, 1)
        hit = jnp.sum(jnp.where(column == target_ref[b], value, 0.0), axis=1, keepdims=True)
        lane = lax.broadcasted_iota(jnp.int32, (8 * rows, 128), 1)
        packed = jnp.where(lane == 0, top, jnp.where(lane == 1, expo, hit)).T
        for k in range(3):
            stats[k, b : b + 1, :] = packed[k : k + 1]

    blocks[0].begin()
    across[0].wait_recv()
    blocks[1].begin()
    blocks[0].relay()
    across[1].wait_recv()
    across[2].start()
    blocks[2].begin()
    blocks[1].relay()
    blocks[0].relay_far()
    across[2].wait_recv()
    blocks[3].begin()
    blocks[2].relay()
    blocks[1].relay_far()
    blocks[0].arrive()
    load.wait()
    use(0)
    blocks[3].relay()
    blocks[2].relay_far()
    blocks[1].arrive()
    use(1)
    blocks[3].relay_far()
    blocks[2].arrive()
    use(2)
    blocks[3].arrive()
    store.start()
    use(3)
    stats_steps(n_dp, stats, seen, plane, mid, line, sems, 14 * n_dp)

    @pl.loop(0, n_dp)
    def _(b):
        part = pl.ds(pl.multiple_of(b * rows, rows), rows)
        lse = jnp.broadcast_to(seen[0, pl.ds(b, 1), :], (128, 8 * rows)).T[:, :1]
        value = flat(logits[:, part, :])
        column = lax.broadcasted_iota(jnp.int32, value.shape, 1)
        hit = (column == target_ref[b]).astype(F32)
        grad = (scale_ref[b] * (jnp.exp(value - lse) - hit)).astype(BF16)
        dlogits[:, part, :] = grad.reshape(8, rows, vocab)
        pltpu.make_async_copy(
            dlogits.at[:, part, :], dlogits_out.at[:, part, :], own_sems.at[2 + b]
        ).start()

    for b in range(n_dp):
        part = pl.ds(b * rows, rows)
        pltpu.make_async_copy(
            dlogits.at[:, part, :], dlogits_out.at[:, part, :], own_sems.at[2 + b]
        ).wait()
    for copy in across:
        copy.wait_send()
    for each in blocks:
        each.close()
    store.wait()


def head_call(n_dp, rows, head, target, scale):
    total = n_dp * rows.shape[0]
    vocab = head.shape[1]
    stats = (3, n_dp, 8 * rows.shape[0])
    outs = [((8, total, D), BF16), ((8, total, vocab), BF16), ((2,) + stats[1:], F32)]
    anywhere = pl.BlockSpec(memory_space=pl.ANY)
    return pl.pallas_call(
        functools.partial(head_kernel, n_dp),
        out_shape=[jax.ShapeDtypeStruct(shape, dtype) for shape, dtype in outs],
        in_specs=[pl.BlockSpec(memory_space=pltpu.VMEM)] * 3 + [anywhere],
        out_specs=[anywhere, anywhere, pl.BlockSpec(memory_space=pltpu.VMEM)],
        scratch_shapes=[
            pltpu.VMEM((8, total, D), BF16),
            pltpu.VMEM(head.shape, BF16),
            pltpu.VMEM((total, D), BF16),
            pltpu.VMEM((8, total, vocab), F32),
            pltpu.VMEM(stats, F32),
            pltpu.VMEM((7,) + stats, F32),
            pltpu.VMEM(stats, F32),
            pltpu.VMEM((n_dp - 1,) + stats, F32),
            pltpu.VMEM((8, total, vocab), BF16),
            pltpu.SemaphoreType.DMA((2, 14 * n_dp + 6 + n_dp)),
            pltpu.SemaphoreType.DMA((2 + n_dp,)),
        ],
        compiler_params=pltpu.CompilerParams(
            collective_id=5, has_side_effects=True, vmem_limit_bytes=56 << 20
        ),
        cost_estimate=pl.CostEstimate(flops=0, bytes_accessed=1 << 20, transcendentals=0),
        name="head",
    )(rows, target, scale, head)


def head_back_kernel(n_dp, cut, dlogits, head, x_in, gain, final_ref, *refs):
    dx_out, dgain, out, early, grads, own, core, held, near, last, parts, *refs = refs
    mine, sent, got, final, ready, sems, own_sem = refs
    a = lax.axis_index("dp")
    rows = x_in.shape[0]
    _, vocab, wide = head.shape
    load = pltpu.make_async_copy(final_ref, final, own_sem)
    load.start()
    met = greet(n_dp)
    plan = PlaneSum(parts, own, core, held, near, last, sems, 0, n_dp)

    def make(b):
        part = pl.ds(b * rows, rows)
        x = flat(dlogits[:, part, :])
        for p in range(n_dp):
            value = mm(x, head[p]).astype(BF16)
            parts[:, part, pl.ds(p * wide, wide)] = value.reshape(8, rows, wide)
        if b == 2:
            met()
        plan.at_core[b].start()

    def table_part(p, first, number):
        x = flat(final[:, :, pl.ds(pl.multiple_of(p * wide, 128), wide)])
        return mm(flat(dlogits[:, :, pl.ds(first, number)]), x, CONTRACT_FIRST).astype(BF16)

    whole = cut[0] + cut[1]
    left = [(p, v) for p in range(n_dp) for v in range(whole, vocab, 384)]

    def fill(count):
        for _ in range(min(count, len(left))):
            p, v = left.pop(0)
            number = min(384, vocab - v)
            grads[p, pl.ds(v - whole, number), :] = table_part(p, v, number)

    def rows_of(e):
        return pl.ds(e * cut[0], cut[e])

    early_sends = [
        [
            peer_copy(
                ready.at[o - 1, rows_of(e)],
                early.at[a, rows_of(e)],
                sems,
                12 + (8 + e) * n_dp + o,
                dp=a ^ o,
            )
            for o in range(1, n_dp)
        ]
        for e in range(2)
    ]
    across = {
        b: peer_copy(
            sent.at[pl.ds(b * rows, rows)], got.at[b - 1], sems, 13 + 7 * n_dp + b, dp=a ^ b
        )
        for b in range(1, n_dp)
    }

    def finish(b):
        plan.finish(b)
        if b:
            part = pl.ds(b * rows, rows)
            sent[part] = own[part].astype(BF16)
            across[b].start()

    make(2)
    load.wait()
    for o in range(1, n_dp):
        ready[o - 1, rows_of(0)] = table_part(a ^ o, 0, cut[0])
        early_sends[0][o - 1].start()
    plan.first_sends(2)
    make(3)
    plan.second_sends(2)
    plan.first_sends(3)
    make(1)
    early[a, rows_of(0)] = table_part(a, 0, cut[0])
    plan.first_sends(1)
    plan.second_sends(3)
    make(0)
    finish(2)
    plan.first_sends(0)
    fill(2)
    plan.second_sends(1)
    finish(3)
    for o in range(1, n_dp):
        ready[o - 1, rows_of(1)] = table_part(a ^ o, *cut)
    early[a, rows_of(1)] = table_part(a, *cut)
    plan.second_sends(0)
    finish(1)
    for copy in early_sends[1]:
        copy.start()
    fill(7)
    finish(0)
    fill(len(left))
    for copy in across.values():
        copy.wait()
    grad = own[pl.ds(0, rows)]
    for o in range(1, n_dp):
        grad = grad + got[o - 1].astype(F32)
    dx, dg = norm_back_step(grad, x_in[...], gain[...])
    dx_out[...] = dx
    dgain[...] = dg
    mine[...] = dx.astype(BF16)
    PlaneSpread(mine, out, sems, 7 * n_dp, 0, rows).run()
    plan.close()
    for copies in early_sends:
        for copy in copies:
            copy.wait()


def input_back_kernel(n_dp, dqkv, wqkv, x_in, gain, res, h1_ref, over, dgain, grads, *refs):
    own, core, held, near, last, parts, _, dx_out, h1, sems, h1_sem = refs
    rows, wide = res.shape[0], over.shape[2]
    blocks = x_in.shape[0] // rows
    a = lax.axis_index("dp")
    load = pltpu.make_async_copy(h1_ref, h1, h1_sem)
    load.start()
    met = greet(n_dp)
    plan = PlaneSum(parts, own, core, held, near, last, sems, 0, blocks)
    sent = []

    def make(b):
        part = pl.ds(b * rows, rows)
        x = flat(dqkv[:, part, :])
        for c in range(D // 512):
            value = mm(x, wqkv[pl.ds(c * 512, 512), :], CONTRACT_LAST).astype(BF16)
            parts[:, part, pl.ds(c * 512, 512)] = value.reshape(8, rows, 512)
        if b == 0:
            met()
        plan.at_core[b].start()

    left = list(range(D // 512))

    def fill():
        c = pl.ds(left.pop(0) * 512, 512)
        grads[c, :] = mm(flat(h1[:, :, c]), flat(dqkv[...]), CONTRACT_FIRST).astype(BF16)

    def close(b):
        plan.finish(b)
        part = pl.ds(b * rows, rows)
        dx, dg = norm_back_step(own[part], x_in[part], gain[...])
        if b == 0:
            dx = dx + res[...]
            dgain[...] = dg
        else:
            dgain[...] += dg
        dx_out[part] = dx.astype(BF16)

        def columns(o):
            return pl.ds(pl.multiple_of((a ^ o) * wide, 128), wide)

        over[0, part] = dx_out[part, columns(0)]
        for o in range(1, n_dp):
            copy = peer_copy(
                dx_out.at[part, columns(o)], over.at[o, part], sems, 7 * blocks + len(sent), dp=a ^ o
            )
            copy.start()
            sent.append(copy)

    make(0)
    make(1)
    plan.first_sends(0)
    make(2)
    plan.first_sends(1)
    plan.second_sends(0)
    make(3)
    plan.first_sends(2)
    plan.second_sends(1)
    plan.first_sends(3)
    load.wait()
    fill()
    close(0)
    plan.second_sends(2)
    fill()
    close(1)
    plan.second_sends(3)
    fill()
    close(2)
    fill()
    close(3)
    plan.close()
    for copy in sent:
        copy.wait()


def exchange(kernel, name, number, n_dp, total, outs, *args, more=(), sems=20, far=0, stored=0):
    half = total // 2
    rows = outs[0][0][0]
    scratch = [
        pltpu.VMEM((total, D), F32),
        pltpu.VMEM((4, total, D), BF16),
        pltpu.VMEM((4, total, D), BF16),
        pltpu.VMEM((4, half, D), BF16),
        pltpu.VMEM((2, half, D), BF16),
        pltpu.VMEM((8, total, D), BF16),
        pltpu.VMEM((rows, D), BF16),
    ]
    scratch += [pltpu.VMEM(shape, BF16) for shape in more]
    return pl.pallas_call(
        kernel,
        out_shape=[jax.ShapeDtypeStruct(shape, dtype) for shape, dtype in outs],
        in_specs=[pl.BlockSpec(memory_space=pltpu.VMEM)] * (len(args) - far)
        + [pl.BlockSpec(memory_space=pl.ANY)] * far,
        out_specs=[pl.BlockSpec(memory_space=pltpu.VMEM)] * (len(outs) - stored)
        + [pl.BlockSpec(memory_space=pl.ANY)] * stored,
        scratch_shapes=scratch
        + [pltpu.SemaphoreType.DMA((2, sems))]
        + [pltpu.SemaphoreType.DMA] * far
        + [pltpu.SemaphoreType.DMA((stored,))] * (stored > 0),
        compiler_params=pltpu.CompilerParams(
            collective_id=number, has_side_effects=True, vmem_limit_bytes=62 << 20
        ),
        cost_estimate=pl.CostEstimate(flops=0, bytes_accessed=1 << 10, transcendentals=0),
        name=name,
    )(*args)


def stats_steps(n_dp, x_ref, out_ref, plane, mid, line, sems, first):
    me = lax.axis_index("mp")
    a = lax.axis_index("dp")
    order = cube_order(8)
    rows = x_ref.shape[2] // 8
    copies = [
        peer_copy(x_ref, plane.at[s - 1], sems, first + s - 1, mp=me ^ order[s])
        for s in range(1, 8)
    ]
    for copy in copies:
        copy.start()

    def join(have, new):
        top = jnp.maximum(have[0], new[0])
        total = have[1] * jnp.exp(have[0] - top) + new[1] * jnp.exp(new[0] - top)
        return top, total, have[2] + new[2]

    have = tuple(x_ref[k] for k in range(3))
    for s in range(1, 8):
        copies[s - 1].wait_recv()
        got = [plane[s - 1, k] for k in range(3)]
        got = [
            jnp.concatenate([v[:, (e ^ s) * rows : (e ^ s) * rows + rows] for e in range(8)], axis=1)
            for v in got
        ]
        have = join(have, got)
    for k in range(3):
        mid[k] = have[k]
    across = [
        peer_copy(mid, line.at[o - 1], sems, first + 6 + o, dp=a ^ o) for o in range(1, n_dp)
    ]
    for copy in across:
        copy.start()
    for o in range(1, n_dp):
        across[o - 1].wait_recv()
        got = [line[o - 1, k] for k in range(3)]
        got = [jnp.concatenate([v[e ^ o : (e ^ o) + 1] for e in range(n_dp)], axis=0) for v in got]
        have = join(have, got)
    out_ref[0] = have[0] + jnp.log(have[1])
    out_ref[1] = have[2]
    for copy in copies + across:
        copy.wait_send()


def total_kernel(n_dp, slots_ref, more_ref, out_ref, plane, line, sems):
    me = lax.axis_index("mp")
    a = lax.axis_index("dp")
    met = greet(n_dp, range(1, 8))

    def add(k, have):
        g = slots_ref[pl.ds(k * 8, 8)].astype(F32)
        return have + jnp.sum((g * g).reshape(-1, 8, 128), axis=0)

    start = jnp.zeros((8, 128), F32)
    plane[me, 0] = lax.fori_loop(0, slots_ref.shape[0] // 8, add, start) + more_ref[0]
    plane[me, 1] = more_ref[1]
    met()
    copies = [peer_copy(plane.at[me], plane.at[me], sems, k - 1, mp=me ^ k) for k in range(1, 8)]
    for copy in copies:
        copy.start()
    for copy in copies:
        copy.wait()
    line[a] = jnp.sum(plane[...], axis=0)
    across = [
        peer_copy(line.at[a], line.at[a], sems, 6 + o, dp=a ^ o)
        for o in range(1, n_dp)
    ]
    for copy in across:
        copy.start()
    for copy in across:
        copy.wait()
    out_ref[...] = jnp.sum(line[...], axis=0)


def total_exchange(slots, more, n_dp):
    return pl.pallas_call(
        functools.partial(total_kernel, n_dp),
        out_shape=jax.ShapeDtypeStruct(more.shape, F32),
        in_specs=[pl.BlockSpec(memory_space=pltpu.VMEM)] * 2,
        out_specs=pl.BlockSpec(memory_space=pltpu.VMEM),
        scratch_shapes=[
            pltpu.VMEM((8,) + more.shape, F32),
            pltpu.VMEM((n_dp,) + more.shape, F32),
            pltpu.SemaphoreType.DMA((2, 6 + n_dp)),
        ],
        compiler_params=pltpu.CompilerParams(collective_id=6, has_side_effects=True),
        name="total",
    )(slots, more)


def mat_shapes(n_mp):
    width, units = D // n_mp, FF // n_mp
    return ((D, 3 * width), (width, D), (D, 2 * units), (units, D))


def each_tile(shape, size, first, step):
    rows, cols = shape

    @pl.loop(0, rows // size)
    def _(r):
        row = pl.ds(pl.multiple_of(r * size, size), size)
        for c in range(cols // size):
            step(first + r * (cols // size) + c, (row, pl.ds(c * size, size)))


def first_tiles(shapes, size):
    firsts = [0]
    for rows, cols in shapes:
        firsts.append(firsts[-1] + rows * cols // (size * size))
    return firsts


def place_kernel(shapes, slot_ref, slots_ref, *refs):
    count = len(shapes)
    outs, mats, sems = refs[:count], refs[count : 2 * count], refs[-1]
    size = slots_ref.shape[1]
    for k, (shape, first) in enumerate(zip(shapes, first_tiles(shapes, size))):

        def fetch(tile, view, k=k):
            pltpu.make_async_copy(
                slots_ref.at[slot_ref[tile]], mats[k].at[view], sems.at[0, k]
            ).start()

        each_tile(shape, size, first, fetch)
    for k in range(count):
        pltpu.make_async_copy(mats[k], mats[k], sems.at[0, k]).wait()
        pltpu.make_async_copy(mats[k], outs[k], sems.at[1, k]).start()
    for k in range(count):
        pltpu.make_async_copy(mats[k], outs[k], sems.at[1, k]).wait()


def place_tiles(slot_of, slots, shapes):
    anywhere = pl.BlockSpec(memory_space=pl.ANY)
    return pl.pallas_call(
        functools.partial(place_kernel, shapes),
        out_shape=[jax.ShapeDtypeStruct(shape, slots.dtype) for shape in shapes],
        in_specs=[pl.BlockSpec(memory_space=pltpu.SMEM), anywhere],
        out_specs=[anywhere] * len(shapes),
        scratch_shapes=[pltpu.VMEM(shape, slots.dtype) for shape in shapes]
        + [pltpu.SemaphoreType.DMA((2, len(shapes)))],
        compiler_params=pltpu.CompilerParams(vmem_limit_bytes=40 << 20),
        cost_estimate=pl.CostEstimate(flops=0, bytes_accessed=1 << 20, transcendentals=0),
        name="place_tiles",
    )(slot_of, slots)


def collect_kernel(shapes, chosen, slot_ref, *refs):
    mats = refs[: len(chosen)]
    slots_ref, sem = refs[-2:]
    size = slots_ref.shape[1]
    firsts = first_tiles(shapes, size)
    for k, ref in zip(chosen, mats):

        def send(tile, view, ref=ref):
            pltpu.make_async_copy(ref.at[view], slots_ref.at[slot_ref[tile]], sem).start()

        each_tile(shapes[k], size, firsts[k], send)
    for ref in mats:
        pltpu.make_async_copy(ref, ref, sem).wait()


def collect_tiles(slot_of, mats, shapes, chosen, given=()):
    size = 128
    anywhere = pl.BlockSpec(memory_space=pl.ANY)
    return pl.pallas_call(
        functools.partial(collect_kernel, shapes, chosen),
        out_shape=jax.ShapeDtypeStruct((slot_of.shape[0], size, size), BF16),
        in_specs=[pl.BlockSpec(memory_space=pltpu.SMEM)]
        + [pl.BlockSpec(memory_space=pltpu.VMEM)] * len(mats)
        + [anywhere] * len(given),
        out_specs=anywhere,
        scratch_shapes=[pltpu.SemaphoreType.DMA],
        compiler_params=pltpu.CompilerParams(vmem_limit_bytes=40 << 20),
        input_output_aliases={1 + len(mats): 0} if given else {},
        cost_estimate=pl.CostEstimate(flops=0, bytes_accessed=1 << 20, transcendentals=0),
        name="collect_tiles",
    )(slot_of, *mats, *given)


def after(x, *others):
    anywhere = pl.BlockSpec(memory_space=pl.ANY)
    return pl.pallas_call(
        lambda *refs: None,
        out_shape=jax.ShapeDtypeStruct(x.shape, x.dtype),
        in_specs=[anywhere] * (1 + len(others)),
        out_specs=anywhere,
        input_output_aliases={0: 0},
        cost_estimate=pl.CostEstimate(flops=0, bytes_accessed=0, transcendentals=0),
        name="after",
    )(x, *others)


def split(x):
    high = x.astype(BF16)
    return high, (x - high.astype(F32)).astype(BF16)


def adam(master, moment, second, grad, rate, decay):
    moment_new = ADAM_ONE * moment + (1.0 - ADAM_ONE) * grad
    second_new = ADAM_TWO * second + (1.0 - ADAM_TWO) * grad * grad
    corrected = (
        moment_new
        / (1.0 - ADAM_ONE**STEP)
        / (jnp.sqrt(second_new / (1.0 - ADAM_TWO**STEP)) + ADAM_EPS)
    )
    return (master - rate * (corrected + decay * master), moment_new, second_new)


def owner_step_kernel(steps, factor_ref, *refs):
    g_ref, master, left, right, l_root, r_root = refs[:6]
    t_grad, t_master, t_moment, t_second = refs[6:10]
    new, copy, grad, left_new, right_new = refs[10:15]
    t_new, t_copy, t_moment_new, t_second_new = refs[15:]
    factor = factor_ref[0, 0]

    @pl.when(pl.program_id(0) < steps)
    def _():
        for k in range(g_ref.shape[0]):
            g = g_ref[k]
            grad[k] = factor * g.astype(F32)
            outer = (mm(g, g, CONTRACT_LAST) * factor) * factor
            inner = (mm(g, g, CONTRACT_FIRST) * factor) * factor
            left_new[k] = STAT_DECAY * left[k] + (1.0 - STAT_DECAY) * outer
            right_new[k] = STAT_DECAY * right[k] + (1.0 - STAT_DECAY) * inner
            l_high, l_low = split(l_root[k])
            r_high, r_low = split(r_root[k])
            t_high, t_low = split((mm(l_high, g) + mm(l_low, g)) * factor)
            direction = mm(t_high, r_high) + (mm(t_low, r_high) + mm(t_high, r_low))
            value = master[k] - LR_MATRIX * (direction + DECAY_MATRIX * master[k])
            new[k] = value
            copy[k] = value.astype(BF16)

    @pl.when(pl.program_id(0) >= steps)
    def _():
        value, moment, second = adam(
            t_master[...],
            t_moment[...],
            t_second[...],
            factor * t_grad[...],
            LR_TABLE,
            DECAY_TABLE,
        )
        t_new[...] = value
        t_copy[...] = value.astype(BF16)
        t_moment_new[...] = moment
        t_second_new[...] = second


def owner_step(factor, tiles, table):
    number, size, _ = tiles[0].shape
    rows, cols = table[0].shape
    group, band = min(32, number), 512
    steps = number // group

    tile = pl.BlockSpec((group, size, size), lambda i: (jnp.minimum(i, steps - 1), 0, 0))
    part = pl.BlockSpec((band, cols), lambda i: (jnp.maximum(i - steps, 0), 0))
    kinds = (F32, BF16, F32, F32, F32)
    out_shape = [jax.ShapeDtypeStruct((number, size, size), kind) for kind in kinds]
    out_shape += [jax.ShapeDtypeStruct((rows, cols), kind) for kind in kinds[:4]]
    return pl.pallas_call(
        functools.partial(owner_step_kernel, steps),
        grid=(steps + rows // band,),
        out_shape=out_shape,
        in_specs=[pl.BlockSpec(memory_space=pltpu.SMEM)] + [tile] * 6 + [part] * 4,
        out_specs=[tile] * 5 + [part] * 4,
        compiler_params=pltpu.CompilerParams(vmem_limit_bytes=62 << 20),
        name="owner_step",
    )(factor, *tiles, *table)


CONTRACT_LAST = (((1,), (1,)), ((), ()))
CONTRACT_FIRST = (((0,), (0,)), ((), ()))


def mm(a, b, dims=(((1,), (0,)), ((), ()))):
    return lax.dot_general(a, b, dims, preferred_element_type=F32)


def turn(x, cosine, sine):
    lane = lax.broadcasted_iota(jnp.int32, x.shape, 1)
    other = jnp.where(
        lax.rem(lane, HD) < HD // 2, pltpu.roll(x, 128 - HD // 2, 1), pltpu.roll(x, HD // 2, 1)
    )
    return x * cosine + other * sine


def flat(x):
    return x.reshape(x.shape[0] * x.shape[1], x.shape[2])


def head_probs(q, k_ctx, k_ans, causal):
    s_ctx = mm(q, k_ctx, CONTRACT_LAST) * HD ** (-0.5)
    s_ans = jnp.where(causal, mm(q, k_ans, CONTRACT_LAST) * HD ** (-0.5), MASKED)
    top = jnp.maximum(
        jnp.max(s_ctx, axis=1, keepdims=True), jnp.max(s_ans, axis=1, keepdims=True)
    )
    e_ctx = jnp.exp(s_ctx - top)
    e_ans = jnp.exp(s_ans - top)
    total = jnp.sum(e_ctx, axis=1, keepdims=True) + jnp.sum(e_ans, axis=1, keepdims=True)
    return e_ctx / total, e_ans / total


def attend_kernel(items, h1_ref, w_ref, cos_ref, sin_ref, col_ref, row_ref, *outs):
    o_ref, qo_ref, ko_ref, vo_ref, qkv_ref = outs

    @pl.loop(0, h1_ref.shape[0])
    def _(s):
        qkv_ref[s] = mm(h1_ref[s], w_ref[...])

    n, rows_ans, width = o_ref.shape
    n_ans = rows_ans // items
    n_ctx = qkv_ref.shape[1] // items - n_ans
    causal = col_ref[...] >= row_ref[...]
    lane = lax.broadcasted_iota(jnp.int32, (1, 128), 1)

    for item in range(items):
        ans = pl.ds(item * n_ans, n_ans)
        ctx = pl.ds(rows_ans + item * n_ctx, n_ctx)
        turns = [(flat(cos_ref[:, r]), flat(sin_ref[:, r])) for r in (ans, ctx)]
        for g in range(width // 128):
            lanes = pl.ds(g * 128, 128)
            klanes = pl.ds(width + g * 128, 128)
            vlanes = pl.ds(2 * width + g * 128, 128)
            q = turn(flat(qkv_ref[:, ans, lanes]), *turns[0]).astype(BF16)
            k_ans = turn(flat(qkv_ref[:, ans, klanes]), *turns[0]).astype(BF16)
            k_ctx = turn(flat(qkv_ref[:, ctx, klanes]), *turns[1]).astype(BF16)
            v_ans = flat(qkv_ref[:, ans, vlanes]).astype(BF16)
            v_ctx = flat(qkv_ref[:, ctx, vlanes]).astype(BF16)
            qo_ref[:, ans, lanes] = q.reshape(n, n_ans, 128)
            ko_ref[:, ans, lanes] = k_ans.reshape(n, n_ans, 128)
            ko_ref[:, ctx, lanes] = k_ctx.reshape(n, n_ctx, 128)
            vo_ref[:, ans, lanes] = v_ans.reshape(n, n_ans, 128)
            vo_ref[:, ctx, lanes] = v_ctx.reshape(n, n_ctx, 128)
            got = []
            for first in (True, False):
                own = (lane < HD) == first
                p_ctx, p_ans = head_probs(jnp.where(own, q, 0), k_ctx, k_ans, causal)
                got.append(mm(p_ctx.astype(BF16), v_ctx) + mm(p_ans.astype(BF16), v_ans))
            o = jnp.where(lane < HD, got[0], got[1]).astype(BF16)
            o_ref[:, ans, lanes] = o.reshape(n, n_ans, 128)


def attend_back_kernel(items, shapes, slot_ref, *refs):
    q_ref, k_ref, v_ref, dx_ref, w_ref, o_ref, cos_ref, sin_ref, col_ref, row_ref, *refs = refs
    gate_ref, down_ref, d_ref, grad_ref, slots_ref, do_ref, gate, down, load_sems, sem = refs
    loads = [
        pltpu.make_async_copy(gate_ref, gate, load_sems.at[0]),
        pltpu.make_async_copy(down_ref, down, load_sems.at[1]),
    ]
    for copy in loads:
        copy.start()
    n, rows_ans, width = q_ref.shape
    for c in range(D // 512):
        at = pl.ds(c * 512, 512)
        grad_ref[:, at] = mm(o_ref[...], flat(dx_ref[:, :, at]), CONTRACT_FIRST).astype(BF16)
    do_ref[...] = mm(flat(dx_ref[...]), w_ref[...], CONTRACT_LAST).astype(BF16).reshape(q_ref.shape)
    n_ans = rows_ans // items
    n_ctx = k_ref.shape[1] // items - n_ans
    causal = col_ref[...] >= row_ref[...]
    lane = lax.broadcasted_iota(jnp.int32, (1, 128), 1)
    root = HD ** (-0.5)

    def collect():
        size = slots_ref.shape[1]
        firsts = first_tiles(shapes, size)
        for load, k, ref in zip(loads, (2, 3), (gate, down)):
            load.wait()

            def send(tile, view, ref=ref):
                pltpu.make_async_copy(ref.at[view], slots_ref.at[slot_ref[tile]], sem).start()

            each_tile(shapes[k], size, firsts[k], send)

    for item in range(items):
        if item == 1 or items == 1:
            collect()
        ans = pl.ds(item * n_ans, n_ans)
        ctx = pl.ds(rows_ans + item * n_ctx, n_ctx)
        turns = [(flat(cos_ref[:, r]), -flat(sin_ref[:, r])) for r in (ans, ctx)]
        d_ref[:, ctx, pl.ds(0, width)] = jnp.zeros((n, n_ctx, width), BF16)
        for g in range(width // 128):
            lanes = pl.ds(g * 128, 128)
            klanes = pl.ds(width + g * 128, 128)
            vlanes = pl.ds(2 * width + g * 128, 128)
            q, do = flat(q_ref[:, ans, lanes]), flat(do_ref[:, ans, lanes])
            k_ans, k_ctx = flat(k_ref[:, ans, lanes]), flat(k_ref[:, ctx, lanes])
            v_ans, v_ctx = flat(v_ref[:, ans, lanes]), flat(v_ref[:, ctx, lanes])
            dq, sums = [], None
            for first in (True, False):
                own = (lane < HD) == first
                q_own, do_own = jnp.where(own, q, 0), jnp.where(own, do, 0)
                p_ctx, p_ans = head_probs(q_own, k_ctx, k_ans, causal)
                dp_ctx = mm(do_own, v_ctx, CONTRACT_LAST)
                dp_ans = mm(do_own, v_ans, CONTRACT_LAST)
                mean = jnp.sum(p_ctx * dp_ctx, axis=1, keepdims=True) + jnp.sum(
                    p_ans * dp_ans, axis=1, keepdims=True
                )
                ds_ctx = (p_ctx * (dp_ctx - mean)).astype(BF16)
                ds_ans = (p_ans * (dp_ans - mean)).astype(BF16)
                dq.append(mm(ds_ctx, k_ctx) + mm(ds_ans, k_ans))
                new = [
                    mm(ds_ctx, q_own, CONTRACT_FIRST),
                    mm(ds_ans, q_own, CONTRACT_FIRST),
                    mm(p_ctx.astype(BF16), do_own, CONTRACT_FIRST),
                    mm(p_ans.astype(BF16), do_own, CONTRACT_FIRST),
                ]
                sums = new if sums is None else [a + b for a, b in zip(sums, new)]
            dq = turn(jnp.where(lane < HD, dq[0], dq[1]) * root, *turns[0])
            dk_ctx = turn(sums[0] * root, *turns[1])
            dk_ans = turn(sums[1] * root, *turns[0])
            d_ref[:, ans, lanes] = dq.astype(BF16).reshape(n, n_ans, 128)
            d_ref[:, ans, klanes] = dk_ans.astype(BF16).reshape(n, n_ans, 128)
            d_ref[:, ctx, klanes] = dk_ctx.astype(BF16).reshape(n, n_ctx, 128)
            d_ref[:, ans, vlanes] = sums[3].astype(BF16).reshape(n, n_ans, 128)
            d_ref[:, ctx, vlanes] = sums[2].astype(BF16).reshape(n, n_ctx, 128)
    for ref in (gate, down):
        pltpu.make_async_copy(ref, ref, sem).wait()


def attend_back(items, shapes, slot_of, grads, size, *args):
    query, key = args[:2]
    n, rows, width = key.shape
    anywhere = pl.BlockSpec(memory_space=pl.ANY)
    vmem = pl.BlockSpec(memory_space=pltpu.VMEM)
    return pl.pallas_call(
        functools.partial(attend_back_kernel, items, shapes),
        out_shape=[
            jax.ShapeDtypeStruct((n, rows, 3 * width), BF16),
            jax.ShapeDtypeStruct(shapes[1], BF16),
            jax.ShapeDtypeStruct((slot_of.shape[0], size, size), BF16),
        ],
        in_specs=[pl.BlockSpec(memory_space=pltpu.SMEM)] + [vmem] * len(args) + [anywhere] * 2,
        out_specs=[vmem, vmem, anywhere],
        scratch_shapes=[pltpu.VMEM(query.shape, BF16)]
        + [pltpu.VMEM(grad.shape, BF16) for grad in grads]
        + [pltpu.SemaphoreType.DMA((2,)), pltpu.SemaphoreType.DMA],
        compiler_params=pltpu.CompilerParams(vmem_limit_bytes=62 << 20),
        cost_estimate=pl.CostEstimate(flops=0, bytes_accessed=1 << 10, transcendentals=0),
        name="attend_back",
    )(slot_of, *args, *grads)


def in_vmem(kernel, name, outs, scratch, *args):
    return pl.pallas_call(
        kernel,
        out_shape=[jax.ShapeDtypeStruct(shape, dtype) for shape, dtype in outs],
        in_specs=[pl.BlockSpec(memory_space=pltpu.VMEM)] * len(args),
        out_specs=[pl.BlockSpec(memory_space=pltpu.VMEM)] * len(outs),
        scratch_shapes=[pltpu.VMEM(shape, dtype) for shape, dtype in scratch],
        compiler_params=pltpu.CompilerParams(vmem_limit_bytes=62 << 20),
        cost_estimate=pl.CostEstimate(flops=0, bytes_accessed=1 << 10, transcendentals=0),
        name=name,
    )(*args)


def norm_forward(x):
    inverse = lax.rsqrt(jnp.mean(x * x, axis=-1, keepdims=True) + EPS_NORM)
    return (x * inverse, inverse)


def norm_backward(grad, normed, inverse, gain):
    scaled = grad * gain
    dgain = jnp.sum(grad * normed, axis=0)
    dx = inverse * (scaled - normed * jnp.mean(scaled * normed, axis=-1, keepdims=True))
    return (dx, dgain)


def body(
    tokens,
    targets,
    pair_order,
    lengths,
    loss_mask,
    start_pos,
    owner_map,
    block_master,
    left_stat,
    right_stat,
    left_root,
    right_root,
    table_master,
    table_moment,
    table_second,
    gain_master,
    gain_moment,
    gain_second,
):
    dp = lax.axis_index("dp")
    mp = lax.axis_index("mp")
    n_mp = lax.axis_size("mp")
    n_dp = lax.axis_size("dp")
    fused = (n_mp, n_dp) == (8, 4)
    items, length = tokens.shape
    context = length - ANS
    n_ans = ANS // n_mp
    n_ctx = context // n_mp
    rows_ans = items * n_ans
    rows_own = items * (n_ans + n_ctx)
    width = D // n_mp
    units = FF // n_mp
    heads = width // HD
    vocab_part, cols = table_master.shape
    sub = vocab_part // n_dp
    perm = owner_map[0]
    who = mp ^ jnp.array(cube_order(n_mp), jnp.int32)
    near = dp ^ jnp.arange(n_dp, dtype=jnp.int32)

    slots = lax.all_gather(block_master[0].astype(BF16), "dp", axis=0, tiled=True)
    gains = line_gather(gain_master.astype(BF16))
    wide = jnp.zeros((3, D), BF16)
    for o in range(n_dp):
        wide = lax.dynamic_update_slice(wide, gains[o], (0, near[o] * cols))
    gains = wide.astype(F32)
    table_low = table_master.astype(BF16)

    packed = jnp.concatenate([tokens, targets, loss_mask, lengths[:, None]], axis=1)
    packed = jnp.stack(line_gather(packed))
    all_tokens = packed[:, :, :length]
    all_targets = packed[:, :, length : length + ANS]
    all_mask = packed[:, :, length + ANS : length + 2 * ANS]
    all_lengths = packed[:, :, -1]
    column = jnp.arange(ANS)
    weights = jnp.where(
        column == 0,
        1.0,
        jnp.where(column < all_lengths[..., None], all_mask.astype(F32), 0.0),
    )
    pairs_all = pair_order.shape[0] // 2
    pairs = (pair_order // 2).reshape(n_dp, items)[near]
    member = (pairs[..., None] == jnp.arange(pairs_all)).astype(F32)
    counts = jnp.einsum("oip,oi->p", member, jnp.sum(weights, axis=-1))
    scale = weights / (jnp.sum(member * counts, axis=-1)[..., None] * pairs_all)

    def by_owner(x):
        split = x.reshape(n_dp, items, n_mp, n_ans)[:, :, who]
        return split.transpose(2, 0, 1, 3)

    row_scale = by_owner(scale).reshape(-1)
    row_target = by_owner(all_targets).reshape(-1)
    tok_ans = all_tokens[:, :, context:].reshape(n_dp, items, n_mp, n_ans)[:, :, who]
    tok_ctx = all_tokens[:, :, :context].reshape(n_dp, items, n_mp, n_ctx)[:, :, who]
    tok = jnp.concatenate(
        [
            tok_ans.transpose(2, 0, 1, 3).reshape(n_mp, n_dp, -1),
            tok_ctx.transpose(2, 0, 1, 3).reshape(n_mp, n_dp, -1),
        ],
        axis=2,
    )

    shapes = mat_shapes(n_mp)
    number = perm.shape[0]
    slot_of = jnp.zeros_like(perm).at[perm].set(jnp.arange(number, dtype=jnp.int32))

    local = tok - mp * vocab_part
    valid = (local >= 0) & (local < vocab_part)
    safe = jnp.clip(local, 0, vocab_part - 1)
    looked = jnp.where(valid[..., None], jnp.take(table_low, safe, axis=0), 0)
    own_cols = cube_scatter(looked).astype(BF16)
    pieces = line_exchange([own_cols[o] for o in range(n_dp)])
    x0 = jnp.zeros((rows_own, D), BF16)
    for o in range(n_dp):
        x0 = lax.dynamic_update_slice(x0, pieces[o], (0, near[o] * cols))
    x0 = x0.astype(F32)
    normed1, inverse1 = norm_forward(x0)
    h1 = cube_gather((normed1 * gains[0]).astype(BF16))
    h1_all = h1.reshape(-1, D)

    wqkv, wout, wgate, wdown = place_tiles(slot_of, slots, shapes)

    table_late = after(table_low, slots, h1)
    head_parts = lax.all_to_all(table_late.reshape(n_dp, sub, cols), "dp", 0, 0)

    half = HD // 2
    freq = ROPE_BASE ** (-jnp.arange(half).astype(F32) * 2.0 / HD)
    t_ans = context + who[:, None] * n_ans + jnp.arange(n_ans)
    t_ctx = who[:, None] * n_ctx + jnp.arange(n_ctx)

    def angles(t):
        place = (start_pos[None, :, None] + t[:, None, :]).astype(F32)
        angle = place.reshape(n_mp, -1)[..., None] * freq
        return jnp.cos(angle), jnp.sin(angle)

    cosine, sine = (jnp.concatenate(pair, axis=1) for pair in zip(angles(t_ans), angles(t_ctx)))
    cosine = jnp.concatenate([cosine] * 4, axis=-1)
    sine = jnp.concatenate([-sine, sine] * 2, axis=-1)
    t_query = t_ans.reshape(-1)
    place = (t_query[:, None], t_query[None, :])

    ans_shape = ((n_mp, rows_ans, width), BF16)
    key_shape = ((n_mp, rows_own, width), BF16)
    o_rows, query, key, value = in_vmem(
        functools.partial(attend_kernel, items),
        "attend",
        (ans_shape, ans_shape, key_shape, key_shape),
        (((n_mp, rows_own, 3 * width), F32),),
        *(h1, wqkv, cosine, sine, *place),
    )
    own = ((rows_ans, D), F32)
    gain_row = ((1, D), F32)
    plane = ((n_mp, rows_ans, D), BF16)
    if fused:
        x1, h2 = exchange(
            attend_sum_kernel, "attend_sum", 1, n_dp, rows_ans, (own, plane),
            *(o_rows, wout, x0[:rows_ans], gains[1:2]),
        )
    else:
        parts = dot("tw,wd->td", o_rows.reshape(-1, width), wout).astype(BF16)
        x1 = x0[:rows_ans] + cube_scatter(parts.reshape(n_mp, rows_ans, D))
        h2 = cube_gather((norm_forward(x1)[0] * gains[1]).astype(BF16))
    o_rows = o_rows.reshape(-1, width)

    if fused:
        flat_units = n_mp * rows_ans
        x2, gate_up, hidden, final = exchange(
            units_sum_kernel, "units_sum", 2, n_dp, rows_ans,
            (
                own,
                ((flat_units, 2 * units), F32),
                ((flat_units, units), BF16),
                ((rows_ans, D), BF16),
            ),
            *(h2, wgate, wdown, x1, gains[2:3]),
        )
        h2 = h2.reshape(-1, D)
    else:
        h2 = h2.reshape(-1, D)
        gate_up = dot("td,df->tf", h2, wgate)
        gate, upward = gate_up[:, :units], gate_up[:, units:]
        hidden = (jax.nn.silu(gate) * upward).astype(BF16)
        parts = dot("tf,fd->td", hidden, wdown).astype(BF16)
        x2 = x1 + cube_scatter(parts.reshape(n_mp, rows_ans, D))

    def by_line(x):
        return x.reshape(n_mp, n_dp, rows_ans).transpose(1, 0, 2).reshape(n_dp, -1, 1)

    first = mp * vocab_part + dp * sub
    if fused:
        final, dlogits, seen = head_call(
            n_dp, final, head_parts, by_line(row_target - first), by_line(row_scale)
        )
        lse, picked = seen[0, 0], seen[1, 0]
        dlogits = dlogits.reshape(-1, sub)
        final = final.reshape(-1, D)
    else:
        head = jnp.concatenate([head_parts[a] for a in range(n_dp)], axis=1)
        final = (norm_forward(x2)[0] * gains[2]).astype(BF16)
        final = cube_gather(jnp.stack(line_gather(final)).reshape(-1, D))
        final = final.reshape(-1, D)
        logits = dot("rd,vd->rv", final, head)
        hit = jnp.arange(sub, dtype=jnp.int32)[None, :] == (row_target - first)[:, None]
        top = jnp.max(logits, axis=1)
        total = jnp.sum(jnp.exp(logits - top[:, None]), axis=1)
        picked = jnp.sum(jnp.where(hit, logits, 0.0), axis=1)
        top, total, picked = stats_everywhere(jnp.stack([top, total, picked]), rows_ans)
        lse = top + jnp.log(total)
        dlogits = (
            row_scale[:, None] * (jnp.exp(logits - lse[:, None]) - hit.astype(F32))
        ).astype(BF16)
    loss_own = jnp.sum(row_scale[:rows_ans] * (lse - picked)[:rows_ans]) * pairs_all

    if fused:
        cut = (256, 128)
        total = n_dp * rows_ans
        dx2, dgain3, down_in, early_grad, head_grad = exchange(
            functools.partial(head_back_kernel, n_dp, cut), "head_sum", 3, n_dp, total,
            (
                own,
                gain_row,
                plane,
                ((n_dp, sum(cut), cols), BF16),
                ((n_dp, sub - sum(cut), cols), BF16),
            ),
            *(dlogits.reshape(n_mp, -1, sub), head_parts, x2, gains[2:3]),
            final.reshape(n_mp, -1, D),
            more=(
                (total, D),
                (n_dp - 1, rows_ans, D),
                (n_mp, total, D),
                (n_dp - 1, sum(cut), cols),
            ),
            sems=13 + 10 * n_dp,
            far=1,
        )
        dgain3 = dgain3[0]
    else:
        parts = dot("rv,vd->rd", dlogits, head).astype(BF16)
        mine = cube_scatter(parts.reshape(n_mp, n_dp * rows_ans, D)).astype(BF16)
        mine = line_exchange(list(mine.reshape(n_dp, rows_ans, D)))
        dfinal = sum(piece.astype(F32) for piece in mine)
        dx2, dgain3 = norm_backward(dfinal, *norm_forward(x2), gains[2])
        down_in = cube_gather(dx2.astype(BF16))
        head_grad = jnp.stack(
            [
                dot("rv,rd->vd", dlogits, final[:, a * cols : (a + 1) * cols]).astype(BF16)
                for a in range(n_dp)
            ]
        )
    table_grad = lax.all_to_all(head_grad, "dp", 0, 0)
    if fused:
        dx1, dgain2, dgate_up, out_in, grad_down, grad_gate = exchange(
            gate_sum_kernel, "gate_sum", 4, n_dp, rows_ans,
            (
                own,
                gain_row,
                (gate_up.shape, BF16),
                plane,
                (wdown.shape, BF16),
                (wgate.shape, BF16),
            ),
            *(down_in, wdown, wgate, gate_up, x1, gains[1:2], dx2),
            *(h2.reshape(n_mp, rows_ans, D), hidden),
            more=((n_mp, rows_ans, D), hidden.shape, wdown.shape, wgate.shape),
            far=2,
            stored=2,
        )
        dgain2 = dgain2[0]
        down_in = down_in.reshape(-1, D)
    else:
        down_in = down_in.reshape(-1, D)
        dhidden = dot("td,fd->tf", down_in, wdown)
        sigma = jax.nn.sigmoid(gate)
        dgate = dhidden * upward * sigma * (1.0 + gate * (1.0 - sigma))
        dgate_up = jnp.concatenate([dgate, dhidden * gate * sigma], axis=-1).astype(BF16)
        parts = dot("tf,df->td", dgate_up, wgate).astype(BF16)
        dnormed2 = cube_scatter(parts.reshape(n_mp, rows_ans, D))
        dx_mlp, dgain2 = norm_backward(dnormed2, *norm_forward(x1), gains[1])
        dx1 = dx2 + dx_mlp
        out_in = cube_gather(dx1.astype(BF16))
        grad_down = dot("tf,td->fd", hidden, down_in).astype(BF16)
        grad_gate = dot("td,tf->df", h2, dgate_up).astype(BF16)
    dqkv, grad_out, slots = attend_back(
        items, shapes, slot_of, (grad_gate, grad_down), block_master.shape[-1],
        *(query, key, value, out_in, wout, o_rows, cosine, sine, *place),
    )
    dqkv = dqkv.reshape(-1, 3 * width)

    if fused:
        rows_over, dgain1, grad_qkv = exchange(
            functools.partial(input_back_kernel, n_dp), "input_sum", 7, n_dp, rows_own,
            (((n_dp, rows_own, cols), BF16), gain_row, (wqkv.shape, BF16)),
            *(dqkv.reshape(n_mp, rows_own, -1), wqkv, x0, gains[:1], dx1, h1),
            more=((rows_own, D), (n_mp, rows_own, D)),
            sems=(7 + n_dp - 1) * (rows_own // rows_ans),
            far=1,
        )
        dgain1 = dgain1[0]
    else:
        dh1 = dot("te,de->td", dqkv, wqkv).astype(BF16).reshape(n_mp, rows_own, D)
        grad_qkv = dot("td,te->de", h1_all, dqkv).astype(BF16)
        dx0, dgain1 = norm_backward(cube_scatter(dh1), *norm_forward(x0), gains[0])
        dx0 = jnp.concatenate([dx0[:rows_ans] + dx1, dx0[rows_ans:]]).astype(BF16)
        parts = [lax.dynamic_slice_in_dim(dx0, near[o] * cols, cols, 1) for o in range(n_dp)]
        rows_over = jnp.stack(line_exchange(parts))

    slots = collect_tiles(slot_of, (grad_qkv, grad_out), shapes, (0, 1), (slots,))
    slots = after(slots, table_grad, rows_over)
    own_slots = lax.psum_scatter(slots, "dp", scatter_dimension=0, tiled=True)

    if fused:
        table_grad = jnp.concatenate([early_grad, table_grad], axis=1)
    rows_back = cube_gather(rows_over.reshape(-1, cols)).reshape(safe.shape + (cols,))
    picked_rows = jnp.where(valid[..., None], rows_back, 0).astype(F32)
    own_table = table_grad.reshape(vocab_part, cols).astype(F32).at[safe.reshape(-1)].add(picked_rows.reshape(-1, cols))

    gain_grad = jnp.stack([dgain1, dgain2, dgain3])
    gain_total = everywhere(gain_grad, jnp.add)
    own_gain = lax.dynamic_slice_in_dim(gain_total, dp * cols, cols, 1)
    first_mp = (mp == 0).astype(F32)
    squares = jnp.sum(own_table * own_table) + first_mp * jnp.sum(own_gain * own_gain)
    if fused:
        more = jnp.zeros((2, 8, 128), F32).at[:, 0, 0].set(jnp.stack([squares, loss_own]))
        squares_all, loss_total = jnp.sum(total_exchange(own_slots, more, n_dp), axis=(1, 2))
    else:
        squares = squares + jnp.sum(jnp.square(own_slots.astype(F32)))
        more = everywhere(jnp.stack([squares, loss_own])[None], jnp.add)[0]
        squares_all, loss_total = more
    norm = jnp.sqrt(squares_all)
    factor = CLIP_NORM / jnp.maximum(norm, CLIP_NORM)
    roots = (left_stat[0], right_stat[0], left_root[0], right_root[0])
    block_new, block_copy, grad_slots, left_new, right_new, *table_step = owner_step(
        factor.reshape(1, 1),
        (own_slots, block_master[0], *roots),
        (own_table, table_master, table_moment, table_second),
    )
    table_new, table_copy, table_moment_new, table_second_new = table_step
    gain_new, gain_moment_new, gain_second_new = adam(
        gain_master, gain_moment, gain_second, factor * own_gain, LR_GAIN, 0.0
    )
    return (
        loss_total,
        norm,
        block_new[None],
        block_copy[None],
        grad_slots[None],
        left_new[None],
        right_new[None],
        table_new,
        table_copy,
        table_moment_new,
        table_second_new,
        gain_new,
        gain_moment_new,
        gain_second_new,
    )


def solution(mesh):
    in_specs = (
        P("dp", None),
        P("dp", None),
        P(),
        P("dp"),
        P("dp", None),
        P("dp"),
        P("mp", None),
        P("mp", "dp", None, None),
        P("mp", "dp", None, None),
        P("mp", "dp", None, None),
        P("mp", "dp", None, None),
        P("mp", "dp", None, None),
        P("mp", "dp"),
        P("mp", "dp"),
        P("mp", "dp"),
        P(None, "dp"),
        P(None, "dp"),
        P(None, "dp"),
    )
    out_specs = (
        P(),
        P(),
        P("mp", "dp", None, None),
        P("mp", "dp", None, None),
        P("mp", "dp", None, None),
        P("mp", "dp", None, None),
        P("mp", "dp", None, None),
        P("mp", "dp"),
        P("mp", "dp"),
        P("mp", "dp"),
        P("mp", "dp"),
        P(None, "dp"),
        P(None, "dp"),
        P(None, "dp"),
    )
    return jax.shard_map(body, mesh=mesh, in_specs=in_specs, out_specs=out_specs, check_vma=False)
```

```python
import functools

import jax
import jax.numpy as jnp
from jax import lax
from jax.experimental import pallas as pl
from jax.experimental.pallas import tpu as pltpu
from jax.sharding import PartitionSpec as P

D = 2048
HD = 64
FF = 8192
ANS = 256
STEP = 5


EPS_NORM = 1e-05
ROPE_BASE = 130000.0
CLIP_NORM = 0.01
STAT_DECAY = 0.95
LR_MATRIX = 0.05
DECAY_MATRIX = 0.1
LR_TABLE = 0.03
DECAY_TABLE = 0.1
LR_GAIN = 0.2
ADAM_ONE = 0.9
ADAM_TWO = 0.95
ADAM_EPS = 1e-08
MASKED = -1e30
F32 = jnp.float32
BF16 = jnp.bfloat16


def dot(spec, a, b):
    return jnp.einsum(spec, a, b, preferred_element_type=F32)


def cube_bits(n):
    bits = [1 << i for i in range(n.bit_length() - 1)]
    return bits[1:] + bits[:1]


def cube_order(n):
    order = [0]
    for bit in cube_bits(n):
        order = order + [o ^ bit for o in order]
    return order


def swap(x, axis, bit):
    n = lax.axis_size(axis)
    return lax.ppermute(x, axis, [(i, i ^ bit) for i in range(n)])


def cube_gather(x):
    n = lax.axis_size("mp")
    if n != 8:
        held = x[None]
        for bit in cube_bits(n):
            held = jnp.concatenate([held, swap(held, "mp", bit)])
        return held
    half = x.shape[0] // 2
    over_x = swap(x, "mp", 2)
    over_y = swap(x, "mp", 4)
    far = jnp.concatenate([swap(over_x[:half], "mp", 4), swap(over_y[half:], "mp", 2)])
    held = jnp.stack([x, over_x, over_y, far])
    return jnp.concatenate([held, swap(held, "mp", 1)])


def cube_scatter(parts):
    n = lax.axis_size("mp")
    if n != 8:
        held = parts
        for bit in reversed(cube_bits(n)):
            keep = held.shape[0] // 2
            other = swap(held[keep:].astype(BF16), "mp", bit)
            held = held[:keep].astype(F32) + other.astype(F32)
        return held[0]
    got = swap(parts[4:], "mp", 1)
    held = (parts[:4].astype(F32) + got.astype(F32)).astype(BF16)
    half = held.shape[1] // 2
    one, two = held[:, :half], held[:, half:]
    one_x = swap(one[1::2], "mp", 2)
    two_y = swap(two[2:], "mp", 4)
    one = one[0::2].astype(F32) + one_x.astype(F32)
    two = two[:2].astype(F32) + two_y.astype(F32)
    one_y = swap(one[1].astype(BF16), "mp", 4)
    two_x = swap(two[1].astype(BF16), "mp", 2)
    return jnp.concatenate([one[0] + one_y.astype(F32), two[0] + two_x.astype(F32)])


def line_gather(x):
    return [x] + [swap(x, "dp", o) for o in range(1, lax.axis_size("dp"))]


def line_exchange(parts):
    return [parts[0]] + [swap(parts[o], "dp", o) for o in range(1, len(parts))]


def combine_stats(a, b):
    top = jnp.maximum(a[0], b[0])
    total = a[1] * jnp.exp(a[0] - top) + b[1] * jnp.exp(b[0] - top)
    return jnp.stack([top, total, a[2] + b[2]])


def everywhere(x, op):
    for axis in ("mp", "dp"):
        bit = 1
        while bit < lax.axis_size(axis):
            x = op(x, swap(x, axis, bit))
            bit *= 2
    return x


def stats_everywhere(x, rows):
    n_mp, n_dp = lax.axis_size("mp"), lax.axis_size("dp")
    bits = cube_bits(n_mp)
    split = (3,) + (2,) * len(bits) + (n_dp * rows,)
    x = x.reshape(split)
    for i, bit in enumerate(bits):
        x = combine_stats(x, jnp.flip(swap(x, "mp", bit), len(bits) - i))
    x = x.reshape(3, n_mp, n_dp, rows)
    total = x
    for o, other in enumerate(line_gather(x)):
        if o:
            order = [e ^ o for e in range(n_dp)]
            total = combine_stats(total, jnp.stack([other[:, :, e] for e in order], axis=2))
    return total.reshape(3, -1)


def peer_copy(src, dst, sems, k, **device):
    return pltpu.make_async_remote_copy(
        src_ref=src,
        dst_ref=dst,
        send_sem=sems.at[0, k],
        recv_sem=sems.at[1, k],
        device_id=device,
        device_id_type=pl.DeviceIdType.MESH,
    )


def greet(n_dp, bits=(1, 2, 4)):
    me = lax.axis_index("mp")
    a = lax.axis_index("dp")
    barrier = pltpu.get_barrier_semaphore()
    partners = [{"mp": me ^ bit} for bit in bits]
    partners += [{"dp": a ^ o} for o in range(1, n_dp)]
    for partner in partners:
        pl.semaphore_signal(barrier, 1, device_id=partner, device_id_type=pl.DeviceIdType.MESH)
    return lambda: pl.semaphore_wait(barrier, len(partners))


def by_rows(count, step):
    @pl.loop(0, count // 16)
    def _(i):
        step(pl.multiple_of(i * 16, 16))


class PlaneSum:
    def __init__(self, parts, own, core, held, near, last, sems, first, blocks):
        me = lax.axis_index("mp")
        self.refs = parts, own, core, held, near, last
        self.rows = own.shape[0] // blocks
        self.half = half = self.rows // 2
        self.at_core = []
        self.blocks = []
        for b in range(blocks):
            whole = pl.ds(b * self.rows, self.rows)
            top, low = pl.ds(b * self.rows, half), pl.ds(b * self.rows + half, half)
            spot = pl.ds(b * half, half)
            k = first + 7 * b
            self.at_core.append(
                peer_copy(parts.at[4:8, whole], core.at[:, whole], sems, k, mp=me ^ 1)
            )
            sends = (
                (3, top, near, 0, 2),
                (3, low, near, 1, 4),
                (1, top, near, 2, 2),
                (2, low, near, 3, 4),
                (2, top, last, 0, 4),
                (1, low, last, 1, 2),
            )
            self.blocks.append(
                [
                    peer_copy(held.at[s, rows], to.at[at, spot], sems, k + 1 + e, mp=me ^ bit)
                    for e, (s, rows, to, at, bit) in enumerate(sends)
                ]
            )

    def first_sends(self, b):
        self.at_core[b].wait_recv()
        parts, _, core, held, _, _ = self.refs
        copies = self.blocks[b]
        for s, sent in ((3, copies[:2]), (1, copies[2:3]), (2, copies[3:4])):

            def add(at, s=s):
                rows = pl.ds(b * self.rows + at, 16)
                value = parts[s, rows].astype(F32) + core[s, rows].astype(F32)
                held[s, rows] = value.astype(BF16)

            by_rows(self.rows, add)
            for copy in sent:
                copy.start()

    def second_sends(self, b):
        _, _, _, held, near, _ = self.refs
        copies = self.blocks[b]
        for e, s, offset in ((0, 2, 0), (1, 1, self.half)):
            copies[e].wait_recv()

            def add(at, e=e, s=s, offset=offset):
                rows = pl.ds(b * self.rows + offset + at, 16)
                value = held[s, rows].astype(F32) + near[e, pl.ds(b * self.half + at, 16)].astype(F32)
                held[s, rows] = value.astype(BF16)

            by_rows(self.half, add)
            copies[4 + e].start()

    def finish(self, b):
        parts, own, core, _, near, last = self.refs
        for copy in self.blocks[b][2:]:
            copy.wait_recv()

        def total(at):
            spot = pl.ds(b * self.half + at, 16)
            for e, offset in ((0, 0), (1, self.half)):
                rows = pl.ds(b * self.rows + offset + at, 16)
                own[rows] = (
                    (parts[0, rows].astype(F32) + core[0, rows].astype(F32))
                    + near[2 + e, spot].astype(F32)
                    + last[e, spot].astype(F32)
                )

        by_rows(self.half, total)

    def close(self):
        for core, copies in zip(self.at_core, self.blocks):
            core.wait_send()
            for copy in copies:
                copy.wait_send()

    def run(self, fill=lambda: None):
        for b in range(len(self.blocks)):
            self.at_core[b].start()
        for step in (self.first_sends, self.second_sends, self.finish):
            fill()
            for b in range(len(self.blocks)):
                step(b)
        self.close()


class PlaneSpread:
    def __init__(self, x, out, sems, k, start, rows):
        me = lax.axis_index("mp")
        half = rows // 2
        top, low, whole = pl.ds(start, half), pl.ds(start + half, half), pl.ds(start, rows)
        self.own = x, out, start, rows

        def copy(src, slot, part, e, bit):
            return peer_copy(src, out.at[slot, part], sems, k + e, mp=me ^ bit)

        self.x_top = copy(x.at[top], 1, top, 0, 2)
        self.y_low = copy(x.at[low], 2, low, 1, 4)
        self.x_low = copy(x.at[low], 1, low, 2, 2)
        self.y_top = copy(x.at[top], 2, top, 3, 4)
        self.core = copy(x.at[whole], 4, whole, 4, 1)
        self.far_y = copy(out.at[1, top], 3, top, 5, 4)
        self.far_x = copy(out.at[2, low], 3, low, 6, 2)
        self.to_core = {
            (s, r): copy(out.at[s, part], 4 + s, part, 7 + 2 * (s - 1) + r, 1)
            for s in (1, 2, 3)
            for r, part in enumerate((top, low))
        }

    def begin(self):
        for c in (self.x_top, self.y_low, self.x_low, self.y_top, self.core):
            c.start()
        x, out, start, rows = self.own

        def keep(at):
            part = pl.ds(start + at, 16)
            out[0, part] = x[part]

        by_rows(rows, keep)

    def relay(self):
        self.x_top.wait_recv()
        self.far_y.start()
        self.to_core[1, 0].start()
        self.y_low.wait_recv()
        self.far_x.start()
        self.to_core[2, 1].start()
        self.x_low.wait_recv()
        self.to_core[1, 1].start()
        self.y_top.wait_recv()
        self.to_core[2, 0].start()

    def relay_far(self):
        self.far_y.wait_recv()
        self.to_core[3, 0].start()
        self.far_x.wait_recv()
        self.to_core[3, 1].start()

    def arrive(self):
        self.core.wait_recv()
        for c in self.to_core.values():
            c.wait_recv()

    def close(self):
        sent = (self.x_top, self.y_low, self.x_low, self.y_top, self.core, self.far_y, self.far_x)
        for c in (*sent, *self.to_core.values()):
            c.wait_send()

    def run(self, fill=lambda: None):
        self.begin()
        fill()
        self.relay()
        fill()
        self.relay_far()
        self.arrive()
        self.close()


def norm_step(x, gain):
    return (x * lax.rsqrt(jnp.mean(x * x, axis=1, keepdims=True) + EPS_NORM)) * gain


def norm_back_step(grad, x, gain):
    inverse = lax.rsqrt(jnp.mean(x * x, axis=1, keepdims=True) + EPS_NORM)
    normed = x * inverse
    scaled = grad * gain
    dx = inverse * (scaled - normed * jnp.mean(scaled * normed, axis=1, keepdims=True))
    return dx, jnp.sum(grad * normed, axis=0, keepdims=True)


def by_columns(step, width=512):
    for c in range(D // width):
        step(pl.ds(c * width, width))


def forward_step(refs, res, gain, x_out):
    own, core, held, near, last, parts, _, sems = refs
    PlaneSum(parts, own, core, held, near, last, sems, 0, 1).run()
    x = res[...] + own[...]
    x_out[...] = x
    return norm_step(x, gain[...]).astype(BF16)


def attend_sum_kernel(o, wout, res, gain, x_out, out, *refs):
    *_, parts, mine, sems = refs
    met = greet(1)

    def make(c):
        parts[:, :, c] = mm(flat(o[...]), wout[:, c]).astype(BF16).reshape(8, -1, c.size)

    by_columns(make)
    met()
    mine[...] = forward_step(refs, res, gain, x_out)
    PlaneSpread(mine, out, sems, 7, 0, mine.shape[0]).run()


def units_sum_kernel(h2, wgate, wdown, res, gain, x_out, gate_up, hidden, out, *refs):
    *_, parts, _, _ = refs
    units = wdown.shape[0]
    met = greet(1)
    x = flat(h2[...])
    step = min(units, 512)
    for c in range(2 * units // step):
        at = pl.ds(c * step, step)
        gate_up[:, at] = mm(x, wgate[:, at])
    for c in range(units // step):
        at, up = pl.ds(c * step, step), pl.ds(units + c * step, step)
        gate = gate_up[:, at]
        hidden[:, at] = (gate / (1.0 + jnp.exp(-gate)) * gate_up[:, up]).astype(BF16)

    def make(c):
        parts[:, :, c] = mm(hidden[...], wdown[:, c]).astype(BF16).reshape(8, -1, c.size)

    by_columns(make)
    met()
    out[...] = forward_step(refs, res, gain, x_out)


def gate_sum_kernel(down_in, wdown, wgate, gate_up, x_in, gain, res, h2_ref, hidden_ref, *refs):
    dx_out, dgain, dgate_up, out, down_out, gate_out, *refs = refs
    own, core, held, near, last, parts, mine, *refs = refs
    h2, hidden, down_grad, gate_grad, sems, h2_sem, hidden_sem, store_sems = refs
    units = wdown.shape[0]
    loads = [
        pltpu.make_async_copy(h2_ref, h2, h2_sem),
        pltpu.make_async_copy(hidden_ref, hidden, hidden_sem),
    ]
    stores = [
        pltpu.make_async_copy(down_grad, down_out, store_sems.at[0]),
        pltpu.make_async_copy(gate_grad, gate_out, store_sems.at[1]),
    ]
    for copy in loads:
        copy.start()
    met = greet(1)
    x = flat(down_in[...])
    step = min(units, 512)
    for c in range(units // step):
        at, up = pl.ds(c * step, step), pl.ds(units + c * step, step)
        grad = mm(x, wdown[at, :], CONTRACT_LAST)
        gate, upward = gate_up[:, at], gate_up[:, up]
        sigma = 1.0 / (1.0 + jnp.exp(-gate))
        dgate = grad * upward * sigma * (1.0 + gate * (1.0 - sigma))
        dgate_up[:, at] = dgate.astype(BF16)
        dgate_up[:, up] = (grad * gate * sigma).astype(BF16)

    def make(c):
        value = mm(dgate_up[...], wgate[c, :], CONTRACT_LAST)
        parts[:, :, c] = value.astype(BF16).reshape(8, -1, c.size)

    by_columns(make)
    left = [(down_grad, c) for c in range(0, D, step)]
    left += [(gate_grad, c) for c in range(0, 2 * units, step)]

    def fill(count=2):
        for _ in range(min(count, len(left))):
            grad, c = left.pop(0)
            at = pl.ds(c, step)
            if grad is down_grad:
                value = mm(hidden[...], flat(down_in[:, :, at]), CONTRACT_FIRST)
            else:
                value = mm(flat(h2[...]), dgate_up[:, at], CONTRACT_FIRST)
            grad[:, at] = value.astype(BF16)
            if not left:
                stores[1].start()
            elif grad is down_grad and left[0][0] is gate_grad:
                stores[0].start()

    for copy in loads:
        copy.wait()
    met()
    PlaneSum(parts, own, core, held, near, last, sems, 0, 1).run(fill)
    dx, dg = norm_back_step(own[...], x_in[...], gain[...])
    dx = dx + res[...]
    dx_out[...] = dx
    dgain[...] = dg
    mine[...] = dx.astype(BF16)
    PlaneSpread(mine, out, sems, 7, 0, mine.shape[0]).run(fill)
    fill(len(left))
    for copy in stores:
        copy.wait()


def head_kernel(n_dp, rows_ref, target_ref, scale_ref, late_ref, *refs):
    head_ref, final_out, dlogits_out, head_out, seen, final, head, mine, logits, *refs = refs
    stats, plane, mid, line, dlogits, sems, own_sems = refs
    rows, vocab = rows_ref.shape[0], logits.shape[2]
    wide = head.shape[2]
    count = late_ref.shape[1]
    soon, late = pl.ds(0, vocab - count), pl.ds(vocab - count, count)
    load = pltpu.make_async_copy(head_ref, head.at[:, soon], own_sems.at[0])
    store_head = pltpu.make_async_copy(head, head_out, own_sems.at[2 + n_dp])
    store = pltpu.make_async_copy(final, final_out, own_sems.at[1])
    load.start()
    a = lax.axis_index("dp")
    greet(n_dp, range(1, 8))()
    mine[pl.ds(0, rows)] = rows_ref[...]
    block = [pl.ds(o * rows, rows) for o in range(4)]
    across = [
        peer_copy(rows_ref, mine.at[block[1]], sems, 53, dp=a ^ 1),
        peer_copy(rows_ref, mine.at[block[2]], sems, 54, dp=a ^ 2),
        peer_copy(mine.at[block[2]], mine.at[block[3]], sems, 55, dp=a ^ 1),
    ]
    across[0].start()
    across[1].start()
    blocks = [PlaneSpread(mine, final, sems, 13 * o, o * rows, rows) for o in range(n_dp)]
    late_rows = [
        peer_copy(late_ref.at[a ^ o], head.at[a, late], sems, 15 * n_dp + 5 + o, dp=a ^ o)
        for o in range(1, n_dp)
    ]

    def multiply(b, first, number):
        part = pl.ds(b * rows, rows)

        @pl.loop(0, number // 256)
        def _(v):
            at = pl.ds(pl.multiple_of(first + v * 256, 256), 256)
            value = None
            for p in range(n_dp):
                x = flat(final[:, part, pl.ds(p * wide, wide)])
                term = mm(x, head[p, at, :], CONTRACT_LAST)
                value = term if value is None else value + term
            logits[:, part, at] = value.reshape(8, rows, 256)

    def use(b):
        part = pl.ds(b * rows, rows)
        value = flat(logits[:, part, :])
        top = jnp.max(value, axis=1, keepdims=True)
        expo = jnp.sum(jnp.exp(value - top), axis=1, keepdims=True)
        column = lax.broadcasted_iota(jnp.int32, value.shape, 1)
        hit = jnp.sum(jnp.where(column == target_ref[b], value, 0.0), axis=1, keepdims=True)
        lane = lax.broadcasted_iota(jnp.int32, (8 * rows, 128), 1)
        packed = jnp.where(lane == 0, top, jnp.where(lane == 1, expo, hit)).T
        for k in range(3):
            stats[k, b : b + 1, :] = packed[k : k + 1]

    most = vocab - count
    blocks[0].begin()
    across[0].wait_recv()
    blocks[1].begin()
    blocks[0].relay()
    across[1].wait_recv()
    across[2].start()
    for copy in late_rows:
        copy.start()
    blocks[2].begin()
    blocks[1].relay()
    blocks[0].relay_far()
    across[2].wait_recv()
    blocks[3].begin()
    blocks[2].relay()
    blocks[1].relay_far()
    head[a, late] = late_ref[a]
    blocks[0].arrive()
    load.wait()
    multiply(0, 0, most)
    blocks[3].relay()
    blocks[2].relay_far()
    blocks[1].arrive()
    multiply(1, 0, most)
    blocks[3].relay_far()
    blocks[2].arrive()
    multiply(2, 0, most)
    for copy in late_rows:
        copy.wait_recv()
    store_head.start()
    for b in range(3):
        multiply(b, most, count)
        use(b)
    blocks[3].arrive()
    store.start()
    multiply(3, 0, vocab)
    use(3)
    stats_steps(n_dp, stats, seen, plane, mid, line, sems, 14 * n_dp)

    @pl.loop(0, n_dp)
    def _(b):
        part = pl.ds(pl.multiple_of(b * rows, rows), rows)
        lse = jnp.broadcast_to(seen[0, pl.ds(b, 1), :], (128, 8 * rows)).T[:, :1]
        value = flat(logits[:, part, :])
        column = lax.broadcasted_iota(jnp.int32, value.shape, 1)
        hit = (column == target_ref[b]).astype(F32)
        grad = (scale_ref[b] * (jnp.exp(value - lse) - hit)).astype(BF16)
        dlogits[:, part, :] = grad.reshape(8, rows, vocab)
        pltpu.make_async_copy(
            dlogits.at[:, part, :], dlogits_out.at[:, part, :], own_sems.at[2 + b]
        ).start()

    for b in range(n_dp):
        part = pl.ds(b * rows, rows)
        pltpu.make_async_copy(
            dlogits.at[:, part, :], dlogits_out.at[:, part, :], own_sems.at[2 + b]
        ).wait()
    for copy in across:
        copy.wait_send()
    for each in blocks:
        each.close()
    for copy in late_rows:
        copy.wait_send()
    store.wait()
    store_head.wait()


def head_call(n_dp, rows, head, late, target, scale):
    total = n_dp * rows.shape[0]
    vocab = head.shape[1] + late.shape[1]
    whole = (n_dp, vocab, head.shape[2])
    stats = (3, n_dp, 8 * rows.shape[0])
    outs = [((8, total, D), BF16), ((8, total, vocab), BF16), (whole, BF16)]
    outs.append(((2,) + stats[1:], F32))
    anywhere = pl.BlockSpec(memory_space=pl.ANY)
    return pl.pallas_call(
        functools.partial(head_kernel, n_dp),
        out_shape=[jax.ShapeDtypeStruct(shape, dtype) for shape, dtype in outs],
        in_specs=[pl.BlockSpec(memory_space=pltpu.VMEM)] * 4 + [anywhere],
        out_specs=[anywhere] * 3 + [pl.BlockSpec(memory_space=pltpu.VMEM)],
        scratch_shapes=[
            pltpu.VMEM((8, total, D), BF16),
            pltpu.VMEM(whole, BF16),
            pltpu.VMEM((total, D), BF16),
            pltpu.VMEM((8, total, vocab), F32),
            pltpu.VMEM(stats, F32),
            pltpu.VMEM((7,) + stats, F32),
            pltpu.VMEM(stats, F32),
            pltpu.VMEM((n_dp - 1,) + stats, F32),
            pltpu.VMEM((8, total, vocab), BF16),
            pltpu.SemaphoreType.DMA((2, 16 * n_dp + 5)),
            pltpu.SemaphoreType.DMA((3 + n_dp,)),
        ],
        compiler_params=pltpu.CompilerParams(
            collective_id=5, has_side_effects=True, vmem_limit_bytes=60 << 20
        ),
        cost_estimate=pl.CostEstimate(flops=0, bytes_accessed=1 << 20, transcendentals=0),
        name="head",
    )(rows, target, scale, late, head)


def head_back_kernel(n_dp, cut, dlogits, head, x_in, gain, final_ref, *refs):
    dx_out, dgain, out, early, grads, own, core, held, near, last, parts, *refs = refs
    mine, sent, got, final, ready, sems, own_sem = refs
    a = lax.axis_index("dp")
    rows = x_in.shape[0]
    _, vocab, wide = head.shape
    load = pltpu.make_async_copy(final_ref, final, own_sem)
    load.start()
    met = greet(n_dp)
    plan = PlaneSum(parts, own, core, held, near, last, sems, 0, n_dp)

    def make(b):
        part = pl.ds(b * rows, rows)
        x = flat(dlogits[:, part, :])
        for p in range(n_dp):
            value = mm(x, head[p]).astype(BF16)
            parts[:, part, pl.ds(p * wide, wide)] = value.reshape(8, rows, wide)
        if b == 2:
            met()
        plan.at_core[b].start()

    def table_part(p, first, number):
        x = flat(final[:, :, pl.ds(pl.multiple_of(p * wide, 128), wide)])
        return mm(flat(dlogits[:, :, pl.ds(first, number)]), x, CONTRACT_FIRST).astype(BF16)

    whole = cut[0] + cut[1]
    left = [(p, v) for p in range(n_dp) for v in range(whole, vocab, 384)]

    def fill(count):
        for _ in range(min(count, len(left))):
            p, v = left.pop(0)
            number = min(384, vocab - v)
            grads[p, pl.ds(v - whole, number), :] = table_part(p, v, number)

    def rows_of(e):
        return pl.ds(e * cut[0], cut[e])

    early_sends = [
        [
            peer_copy(
                ready.at[o - 1, rows_of(e)],
                early.at[a, rows_of(e)],
                sems,
                12 + (8 + e) * n_dp + o,
                dp=a ^ o,
            )
            for o in range(1, n_dp)
        ]
        for e in range(2)
    ]
    across = {
        b: peer_copy(
            sent.at[pl.ds(b * rows, rows)], got.at[b - 1], sems, 13 + 7 * n_dp + b, dp=a ^ b
        )
        for b in range(1, n_dp)
    }

    def finish(b):
        plan.finish(b)
        if b:
            part = pl.ds(b * rows, rows)
            sent[part] = own[part].astype(BF16)
            across[b].start()

    make(2)
    load.wait()
    for o in range(1, n_dp):
        ready[o - 1, rows_of(0)] = table_part(a ^ o, 0, cut[0])
        early_sends[0][o - 1].start()
    plan.first_sends(2)
    make(3)
    plan.second_sends(2)
    plan.first_sends(3)
    make(1)
    early[a, rows_of(0)] = table_part(a, 0, cut[0])
    plan.first_sends(1)
    plan.second_sends(3)
    make(0)
    finish(2)
    plan.first_sends(0)
    fill(2)
    plan.second_sends(1)
    finish(3)
    for o in range(1, n_dp):
        ready[o - 1, rows_of(1)] = table_part(a ^ o, *cut)
    early[a, rows_of(1)] = table_part(a, *cut)
    plan.second_sends(0)
    finish(1)
    for copy in early_sends[1]:
        copy.start()
    fill(7)
    finish(0)
    fill(len(left))
    for copy in across.values():
        copy.wait()
    grad = own[pl.ds(0, rows)]
    for o in range(1, n_dp):
        grad = grad + got[o - 1].astype(F32)
    dx, dg = norm_back_step(grad, x_in[...], gain[...])
    dx_out[...] = dx
    dgain[...] = dg
    mine[...] = dx.astype(BF16)
    PlaneSpread(mine, out, sems, 7 * n_dp, 0, rows).run()
    plan.close()
    for copies in early_sends:
        for copy in copies:
            copy.wait()


def input_back_kernel(n_dp, dqkv, wqkv, x_in, gain, res, h1_ref, over, dgain, grads, *refs):
    own, core, held, near, last, parts, _, dx_out, h1, sems, h1_sem = refs
    rows, wide = res.shape[0], over.shape[2]
    blocks = x_in.shape[0] // rows
    a = lax.axis_index("dp")
    load = pltpu.make_async_copy(h1_ref, h1, h1_sem)
    load.start()
    met = greet(n_dp)
    plan = PlaneSum(parts, own, core, held, near, last, sems, 0, blocks)
    sent = []

    def make(b):
        part = pl.ds(b * rows, rows)
        x = flat(dqkv[:, part, :])
        for c in range(D // 512):
            value = mm(x, wqkv[pl.ds(c * 512, 512), :], CONTRACT_LAST).astype(BF16)
            parts[:, part, pl.ds(c * 512, 512)] = value.reshape(8, rows, 512)
        if b == 0:
            met()
        plan.at_core[b].start()

    left = list(range(D // 512))

    def fill():
        c = pl.ds(left.pop(0) * 512, 512)
        grads[c, :] = mm(flat(h1[:, :, c]), flat(dqkv[...]), CONTRACT_FIRST).astype(BF16)

    def close(b):
        plan.finish(b)
        part = pl.ds(b * rows, rows)
        dx, dg = norm_back_step(own[part], x_in[part], gain[...])
        if b == 0:
            dx = dx + res[...]
            dgain[...] = dg
        else:
            dgain[...] += dg
        dx_out[part] = dx.astype(BF16)

        def columns(o):
            return pl.ds(pl.multiple_of((a ^ o) * wide, 128), wide)

        over[0, part] = dx_out[part, columns(0)]
        for o in range(1, n_dp):
            copy = peer_copy(
                dx_out.at[part, columns(o)], over.at[o, part], sems, 7 * blocks + len(sent), dp=a ^ o
            )
            copy.start()
            sent.append(copy)

    make(0)
    make(1)
    plan.first_sends(0)
    make(2)
    plan.first_sends(1)
    plan.second_sends(0)
    make(3)
    plan.first_sends(2)
    plan.second_sends(1)
    plan.first_sends(3)
    load.wait()
    fill()
    close(0)
    plan.second_sends(2)
    fill()
    close(1)
    plan.second_sends(3)
    fill()
    close(2)
    fill()
    close(3)
    plan.close()
    for copy in sent:
        copy.wait()


def exchange(kernel, name, number, n_dp, total, outs, *args, more=(), sems=20, far=0, stored=0):
    half = total // 2
    rows = outs[0][0][0]
    scratch = [
        pltpu.VMEM((total, D), F32),
        pltpu.VMEM((4, total, D), BF16),
        pltpu.VMEM((4, total, D), BF16),
        pltpu.VMEM((4, half, D), BF16),
        pltpu.VMEM((2, half, D), BF16),
        pltpu.VMEM((8, total, D), BF16),
        pltpu.VMEM((rows, D), BF16),
    ]
    scratch += [pltpu.VMEM(shape, BF16) for shape in more]
    return pl.pallas_call(
        kernel,
        out_shape=[jax.ShapeDtypeStruct(shape, dtype) for shape, dtype in outs],
        in_specs=[pl.BlockSpec(memory_space=pltpu.VMEM)] * (len(args) - far)
        + [pl.BlockSpec(memory_space=pl.ANY)] * far,
        out_specs=[pl.BlockSpec(memory_space=pltpu.VMEM)] * (len(outs) - stored)
        + [pl.BlockSpec(memory_space=pl.ANY)] * stored,
        scratch_shapes=scratch
        + [pltpu.SemaphoreType.DMA((2, sems))]
        + [pltpu.SemaphoreType.DMA] * far
        + [pltpu.SemaphoreType.DMA((stored,))] * (stored > 0),
        compiler_params=pltpu.CompilerParams(
            collective_id=number, has_side_effects=True, vmem_limit_bytes=62 << 20
        ),
        cost_estimate=pl.CostEstimate(flops=0, bytes_accessed=1 << 10, transcendentals=0),
        name=name,
    )(*args)


def stats_steps(n_dp, x_ref, out_ref, plane, mid, line, sems, first):
    me = lax.axis_index("mp")
    a = lax.axis_index("dp")
    order = cube_order(8)
    rows = x_ref.shape[2] // 8
    copies = [
        peer_copy(x_ref, plane.at[s - 1], sems, first + s - 1, mp=me ^ order[s])
        for s in range(1, 8)
    ]
    for copy in copies:
        copy.start()

    def join(have, new):
        top = jnp.maximum(have[0], new[0])
        total = have[1] * jnp.exp(have[0] - top) + new[1] * jnp.exp(new[0] - top)
        return top, total, have[2] + new[2]

    have = tuple(x_ref[k] for k in range(3))
    for s in range(1, 8):
        copies[s - 1].wait_recv()
        got = [plane[s - 1, k] for k in range(3)]
        got = [
            jnp.concatenate([v[:, (e ^ s) * rows : (e ^ s) * rows + rows] for e in range(8)], axis=1)
            for v in got
        ]
        have = join(have, got)
    for k in range(3):
        mid[k] = have[k]
    across = [
        peer_copy(mid, line.at[o - 1], sems, first + 6 + o, dp=a ^ o) for o in range(1, n_dp)
    ]
    for copy in across:
        copy.start()
    for o in range(1, n_dp):
        across[o - 1].wait_recv()
        got = [line[o - 1, k] for k in range(3)]
        got = [jnp.concatenate([v[e ^ o : (e ^ o) + 1] for e in range(n_dp)], axis=0) for v in got]
        have = join(have, got)
    out_ref[0] = have[0] + jnp.log(have[1])
    out_ref[1] = have[2]
    for copy in copies + across:
        copy.wait_send()


def total_kernel(n_dp, slots_ref, more_ref, out_ref, plane, line, sems):
    me = lax.axis_index("mp")
    a = lax.axis_index("dp")
    met = greet(n_dp, range(1, 8))

    def add(k, have):
        g = slots_ref[pl.ds(k * 8, 8)].astype(F32)
        return have + jnp.sum((g * g).reshape(-1, 8, 128), axis=0)

    start = jnp.zeros((8, 128), F32)
    plane[me, 0] = lax.fori_loop(0, slots_ref.shape[0] // 8, add, start) + more_ref[0]
    plane[me, 1] = more_ref[1]
    met()
    copies = [peer_copy(plane.at[me], plane.at[me], sems, k - 1, mp=me ^ k) for k in range(1, 8)]
    for copy in copies:
        copy.start()
    for copy in copies:
        copy.wait()
    line[a] = jnp.sum(plane[...], axis=0)
    across = [
        peer_copy(line.at[a], line.at[a], sems, 6 + o, dp=a ^ o)
        for o in range(1, n_dp)
    ]
    for copy in across:
        copy.start()
    for copy in across:
        copy.wait()
    out_ref[...] = jnp.sum(line[...], axis=0)


def total_exchange(slots, more, n_dp):
    return pl.pallas_call(
        functools.partial(total_kernel, n_dp),
        out_shape=jax.ShapeDtypeStruct(more.shape, F32),
        in_specs=[pl.BlockSpec(memory_space=pltpu.VMEM)] * 2,
        out_specs=pl.BlockSpec(memory_space=pltpu.VMEM),
        scratch_shapes=[
            pltpu.VMEM((8,) + more.shape, F32),
            pltpu.VMEM((n_dp,) + more.shape, F32),
            pltpu.SemaphoreType.DMA((2, 6 + n_dp)),
        ],
        compiler_params=pltpu.CompilerParams(collective_id=6, has_side_effects=True),
        name="total",
    )(slots, more)


def mat_shapes(n_mp):
    width, units = D // n_mp, FF // n_mp
    return ((D, 3 * width), (width, D), (D, 2 * units), (units, D))


def each_tile(shape, size, first, step):
    rows, cols = shape

    @pl.loop(0, rows // size)
    def _(r):
        row = pl.ds(pl.multiple_of(r * size, size), size)
        for c in range(cols // size):
            step(first + r * (cols // size) + c, (row, pl.ds(c * size, size)))


def first_tiles(shapes, size):
    firsts = [0]
    for rows, cols in shapes:
        firsts.append(firsts[-1] + rows * cols // (size * size))
    return firsts


def place_kernel(shapes, slot_ref, slots_ref, *refs):
    count = len(shapes)
    outs, mats, sems = refs[:count], refs[count : 2 * count], refs[-1]
    size = slots_ref.shape[1]
    for k, (shape, first) in enumerate(zip(shapes, first_tiles(shapes, size))):

        def fetch(tile, view, k=k):
            pltpu.make_async_copy(
                slots_ref.at[slot_ref[tile]], mats[k].at[view], sems.at[0, k]
            ).start()

        each_tile(shape, size, first, fetch)
    for k in range(count):
        pltpu.make_async_copy(mats[k], mats[k], sems.at[0, k]).wait()
        pltpu.make_async_copy(mats[k], outs[k], sems.at[1, k]).start()
    for k in range(count):
        pltpu.make_async_copy(mats[k], outs[k], sems.at[1, k]).wait()


def place_tiles(slot_of, slots, shapes):
    anywhere = pl.BlockSpec(memory_space=pl.ANY)
    return pl.pallas_call(
        functools.partial(place_kernel, shapes),
        out_shape=[jax.ShapeDtypeStruct(shape, slots.dtype) for shape in shapes],
        in_specs=[pl.BlockSpec(memory_space=pltpu.SMEM), anywhere],
        out_specs=[anywhere] * len(shapes),
        scratch_shapes=[pltpu.VMEM(shape, slots.dtype) for shape in shapes]
        + [pltpu.SemaphoreType.DMA((2, len(shapes)))],
        compiler_params=pltpu.CompilerParams(vmem_limit_bytes=40 << 20),
        cost_estimate=pl.CostEstimate(flops=0, bytes_accessed=1 << 20, transcendentals=0),
        name="place_tiles",
    )(slot_of, slots)


def collect_kernel(shapes, chosen, slot_ref, *refs):
    mats = refs[: len(chosen)]
    slots_ref, sem = refs[-2:]
    size = slots_ref.shape[1]
    firsts = first_tiles(shapes, size)
    for k, ref in zip(chosen, mats):

        def send(tile, view, ref=ref):
            pltpu.make_async_copy(ref.at[view], slots_ref.at[slot_ref[tile]], sem).start()

        each_tile(shapes[k], size, firsts[k], send)
    for ref in mats:
        pltpu.make_async_copy(ref, ref, sem).wait()


def collect_tiles(slot_of, mats, shapes, chosen, given=()):
    size = 128
    anywhere = pl.BlockSpec(memory_space=pl.ANY)
    return pl.pallas_call(
        functools.partial(collect_kernel, shapes, chosen),
        out_shape=jax.ShapeDtypeStruct((slot_of.shape[0], size, size), BF16),
        in_specs=[pl.BlockSpec(memory_space=pltpu.SMEM)]
        + [pl.BlockSpec(memory_space=pltpu.VMEM)] * len(mats)
        + [anywhere] * len(given),
        out_specs=anywhere,
        scratch_shapes=[pltpu.SemaphoreType.DMA],
        compiler_params=pltpu.CompilerParams(vmem_limit_bytes=40 << 20),
        input_output_aliases={1 + len(mats): 0} if given else {},
        cost_estimate=pl.CostEstimate(flops=0, bytes_accessed=1 << 20, transcendentals=0),
        name="collect_tiles",
    )(slot_of, *mats, *given)


def after(x, *others):
    anywhere = pl.BlockSpec(memory_space=pl.ANY)
    return pl.pallas_call(
        lambda *refs: None,
        out_shape=jax.ShapeDtypeStruct(x.shape, x.dtype),
        in_specs=[anywhere] * (1 + len(others)),
        out_specs=anywhere,
        input_output_aliases={0: 0},
        cost_estimate=pl.CostEstimate(flops=0, bytes_accessed=0, transcendentals=0),
        name="after",
    )(x, *others)


def split(x):
    high = x.astype(BF16)
    return high, (x - high.astype(F32)).astype(BF16)


def adam(master, moment, second, grad, rate, decay):
    moment_new = ADAM_ONE * moment + (1.0 - ADAM_ONE) * grad
    second_new = ADAM_TWO * second + (1.0 - ADAM_TWO) * grad * grad
    corrected = (
        moment_new
        / (1.0 - ADAM_ONE**STEP)
        / (jnp.sqrt(second_new / (1.0 - ADAM_TWO**STEP)) + ADAM_EPS)
    )
    return (master - rate * (corrected + decay * master), moment_new, second_new)


def owner_step_kernel(steps, factor_ref, *refs):
    g_ref, master, left, right, l_root, r_root = refs[:6]
    t_grad, t_master, t_moment, t_second = refs[6:10]
    new, copy, grad, left_new, right_new = refs[10:15]
    t_new, t_copy, t_moment_new, t_second_new = refs[15:]
    factor = factor_ref[0, 0]

    @pl.when(pl.program_id(0) < steps)
    def _():
        for k in range(g_ref.shape[0]):
            g = g_ref[k]
            grad[k] = factor * g.astype(F32)
            outer = (mm(g, g, CONTRACT_LAST) * factor) * factor
            inner = (mm(g, g, CONTRACT_FIRST) * factor) * factor
            left_new[k] = STAT_DECAY * left[k] + (1.0 - STAT_DECAY) * outer
            right_new[k] = STAT_DECAY * right[k] + (1.0 - STAT_DECAY) * inner
            l_high, l_low = split(l_root[k])
            r_high, r_low = split(r_root[k])
            t_high, t_low = split((mm(l_high, g) + mm(l_low, g)) * factor)
            direction = mm(t_high, r_high) + (mm(t_low, r_high) + mm(t_high, r_low))
            value = master[k] - LR_MATRIX * (direction + DECAY_MATRIX * master[k])
            new[k] = value
            copy[k] = value.astype(BF16)

    @pl.when(pl.program_id(0) >= steps)
    def _():
        value, moment, second = adam(
            t_master[...],
            t_moment[...],
            t_second[...],
            factor * t_grad[...],
            LR_TABLE,
            DECAY_TABLE,
        )
        t_new[...] = value
        t_copy[...] = value.astype(BF16)
        t_moment_new[...] = moment
        t_second_new[...] = second


def owner_step(factor, tiles, table):
    number, size, _ = tiles[0].shape
    rows, cols = table[0].shape
    group, band = min(32, number), 512
    steps = number // group

    tile = pl.BlockSpec((group, size, size), lambda i: (jnp.minimum(i, steps - 1), 0, 0))
    part = pl.BlockSpec((band, cols), lambda i: (jnp.maximum(i - steps, 0), 0))
    kinds = (F32, BF16, F32, F32, F32)
    out_shape = [jax.ShapeDtypeStruct((number, size, size), kind) for kind in kinds]
    out_shape += [jax.ShapeDtypeStruct((rows, cols), kind) for kind in kinds[:4]]
    return pl.pallas_call(
        functools.partial(owner_step_kernel, steps),
        grid=(steps + rows // band,),
        out_shape=out_shape,
        in_specs=[pl.BlockSpec(memory_space=pltpu.SMEM)] + [tile] * 6 + [part] * 4,
        out_specs=[tile] * 5 + [part] * 4,
        compiler_params=pltpu.CompilerParams(vmem_limit_bytes=62 << 20),
        name="owner_step",
    )(factor, *tiles, *table)


CONTRACT_LAST = (((1,), (1,)), ((), ()))
CONTRACT_FIRST = (((0,), (0,)), ((), ()))


def mm(a, b, dims=(((1,), (0,)), ((), ()))):
    return lax.dot_general(a, b, dims, preferred_element_type=F32)


def turn(x, cosine, sine):
    lane = lax.broadcasted_iota(jnp.int32, x.shape, 1)
    other = jnp.where(
        lax.rem(lane, HD) < HD // 2, pltpu.roll(x, 128 - HD // 2, 1), pltpu.roll(x, HD // 2, 1)
    )
    return x * cosine + other * sine


def flat(x):
    return x.reshape(x.shape[0] * x.shape[1], x.shape[2])


def head_probs(q, k_ctx, k_ans, causal):
    s_ctx = mm(q, k_ctx, CONTRACT_LAST) * HD ** (-0.5)
    s_ans = jnp.where(causal, mm(q, k_ans, CONTRACT_LAST) * HD ** (-0.5), MASKED)
    top = jnp.maximum(
        jnp.max(s_ctx, axis=1, keepdims=True), jnp.max(s_ans, axis=1, keepdims=True)
    )
    e_ctx = jnp.exp(s_ctx - top)
    e_ans = jnp.exp(s_ans - top)
    total = jnp.sum(e_ctx, axis=1, keepdims=True) + jnp.sum(e_ans, axis=1, keepdims=True)
    return e_ctx / total, e_ans / total


def attend_kernel(items, h1_ref, w_ref, cos_ref, sin_ref, col_ref, row_ref, *outs):
    o_ref, qo_ref, ko_ref, vo_ref, qkv_ref = outs

    @pl.loop(0, h1_ref.shape[0])
    def _(s):
        qkv_ref[s] = mm(h1_ref[s], w_ref[...])

    n, rows_ans, width = o_ref.shape
    n_ans = rows_ans // items
    n_ctx = qkv_ref.shape[1] // items - n_ans
    causal = col_ref[...] >= row_ref[...]
    lane = lax.broadcasted_iota(jnp.int32, (1, 128), 1)

    for item in range(items):
        ans = pl.ds(item * n_ans, n_ans)
        ctx = pl.ds(rows_ans + item * n_ctx, n_ctx)
        turns = [(flat(cos_ref[:, r]), flat(sin_ref[:, r])) for r in (ans, ctx)]
        for g in range(width // 128):
            lanes = pl.ds(g * 128, 128)
            klanes = pl.ds(width + g * 128, 128)
            vlanes = pl.ds(2 * width + g * 128, 128)
            q = turn(flat(qkv_ref[:, ans, lanes]), *turns[0]).astype(BF16)
            k_ans = turn(flat(qkv_ref[:, ans, klanes]), *turns[0]).astype(BF16)
            k_ctx = turn(flat(qkv_ref[:, ctx, klanes]), *turns[1]).astype(BF16)
            v_ans = flat(qkv_ref[:, ans, vlanes]).astype(BF16)
            v_ctx = flat(qkv_ref[:, ctx, vlanes]).astype(BF16)
            qo_ref[:, ans, lanes] = q.reshape(n, n_ans, 128)
            ko_ref[:, ans, lanes] = k_ans.reshape(n, n_ans, 128)
            ko_ref[:, ctx, lanes] = k_ctx.reshape(n, n_ctx, 128)
            vo_ref[:, ans, lanes] = v_ans.reshape(n, n_ans, 128)
            vo_ref[:, ctx, lanes] = v_ctx.reshape(n, n_ctx, 128)
            got = []
            for first in (True, False):
                own = (lane < HD) == first
                p_ctx, p_ans = head_probs(jnp.where(own, q, 0), k_ctx, k_ans, causal)
                got.append(mm(p_ctx.astype(BF16), v_ctx) + mm(p_ans.astype(BF16), v_ans))
            o = jnp.where(lane < HD, got[0], got[1]).astype(BF16)
            o_ref[:, ans, lanes] = o.reshape(n, n_ans, 128)


def attend_back_kernel(items, shapes, slot_ref, *refs):
    q_ref, k_ref, v_ref, dx_ref, w_ref, o_ref, cos_ref, sin_ref, col_ref, row_ref, *refs = refs
    gate_ref, down_ref, d_ref, grad_ref, slots_ref, do_ref, gate, down, load_sems, sem = refs
    loads = [
        pltpu.make_async_copy(gate_ref, gate, load_sems.at[0]),
        pltpu.make_async_copy(down_ref, down, load_sems.at[1]),
    ]
    for copy in loads:
        copy.start()
    n, rows_ans, width = q_ref.shape
    for c in range(D // 512):
        at = pl.ds(c * 512, 512)
        grad_ref[:, at] = mm(o_ref[...], flat(dx_ref[:, :, at]), CONTRACT_FIRST).astype(BF16)
    do_ref[...] = mm(flat(dx_ref[...]), w_ref[...], CONTRACT_LAST).astype(BF16).reshape(q_ref.shape)
    n_ans = rows_ans // items
    n_ctx = k_ref.shape[1] // items - n_ans
    causal = col_ref[...] >= row_ref[...]
    lane = lax.broadcasted_iota(jnp.int32, (1, 128), 1)
    root = HD ** (-0.5)

    def collect():
        size = slots_ref.shape[1]
        firsts = first_tiles(shapes, size)
        for load, k, ref in zip(loads, (2, 3), (gate, down)):
            load.wait()

            def send(tile, view, ref=ref):
                pltpu.make_async_copy(ref.at[view], slots_ref.at[slot_ref[tile]], sem).start()

            each_tile(shapes[k], size, firsts[k], send)

    for item in range(items):
        if item == 1 or items == 1:
            collect()
        ans = pl.ds(item * n_ans, n_ans)
        ctx = pl.ds(rows_ans + item * n_ctx, n_ctx)
        turns = [(flat(cos_ref[:, r]), -flat(sin_ref[:, r])) for r in (ans, ctx)]
        d_ref[:, ctx, pl.ds(0, width)] = jnp.zeros((n, n_ctx, width), BF16)
        for g in range(width // 128):
            lanes = pl.ds(g * 128, 128)
            klanes = pl.ds(width + g * 128, 128)
            vlanes = pl.ds(2 * width + g * 128, 128)
            q, do = flat(q_ref[:, ans, lanes]), flat(do_ref[:, ans, lanes])
            k_ans, k_ctx = flat(k_ref[:, ans, lanes]), flat(k_ref[:, ctx, lanes])
            v_ans, v_ctx = flat(v_ref[:, ans, lanes]), flat(v_ref[:, ctx, lanes])
            dq, sums = [], None
            for first in (True, False):
                own = (lane < HD) == first
                q_own, do_own = jnp.where(own, q, 0), jnp.where(own, do, 0)
                p_ctx, p_ans = head_probs(q_own, k_ctx, k_ans, causal)
                dp_ctx = mm(do_own, v_ctx, CONTRACT_LAST)
                dp_ans = mm(do_own, v_ans, CONTRACT_LAST)
                mean = jnp.sum(p_ctx * dp_ctx, axis=1, keepdims=True) + jnp.sum(
                    p_ans * dp_ans, axis=1, keepdims=True
                )
                ds_ctx = (p_ctx * (dp_ctx - mean)).astype(BF16)
                ds_ans = (p_ans * (dp_ans - mean)).astype(BF16)
                dq.append(mm(ds_ctx, k_ctx) + mm(ds_ans, k_ans))
                new = [
                    mm(ds_ctx, q_own, CONTRACT_FIRST),
                    mm(ds_ans, q_own, CONTRACT_FIRST),
                    mm(p_ctx.astype(BF16), do_own, CONTRACT_FIRST),
                    mm(p_ans.astype(BF16), do_own, CONTRACT_FIRST),
                ]
                sums = new if sums is None else [a + b for a, b in zip(sums, new)]
            dq = turn(jnp.where(lane < HD, dq[0], dq[1]) * root, *turns[0])
            dk_ctx = turn(sums[0] * root, *turns[1])
            dk_ans = turn(sums[1] * root, *turns[0])
            d_ref[:, ans, lanes] = dq.astype(BF16).reshape(n, n_ans, 128)
            d_ref[:, ans, klanes] = dk_ans.astype(BF16).reshape(n, n_ans, 128)
            d_ref[:, ctx, klanes] = dk_ctx.astype(BF16).reshape(n, n_ctx, 128)
            d_ref[:, ans, vlanes] = sums[3].astype(BF16).reshape(n, n_ans, 128)
            d_ref[:, ctx, vlanes] = sums[2].astype(BF16).reshape(n, n_ctx, 128)
    for ref in (gate, down):
        pltpu.make_async_copy(ref, ref, sem).wait()


def attend_back(items, shapes, slot_of, grads, size, *args):
    query, key = args[:2]
    n, rows, width = key.shape
    anywhere = pl.BlockSpec(memory_space=pl.ANY)
    vmem = pl.BlockSpec(memory_space=pltpu.VMEM)
    return pl.pallas_call(
        functools.partial(attend_back_kernel, items, shapes),
        out_shape=[
            jax.ShapeDtypeStruct((n, rows, 3 * width), BF16),
            jax.ShapeDtypeStruct(shapes[1], BF16),
            jax.ShapeDtypeStruct((slot_of.shape[0], size, size), BF16),
        ],
        in_specs=[pl.BlockSpec(memory_space=pltpu.SMEM)] + [vmem] * len(args) + [anywhere] * 2,
        out_specs=[vmem, vmem, anywhere],
        scratch_shapes=[pltpu.VMEM(query.shape, BF16)]
        + [pltpu.VMEM(grad.shape, BF16) for grad in grads]
        + [pltpu.SemaphoreType.DMA((2,)), pltpu.SemaphoreType.DMA],
        compiler_params=pltpu.CompilerParams(vmem_limit_bytes=62 << 20),
        cost_estimate=pl.CostEstimate(flops=0, bytes_accessed=1 << 10, transcendentals=0),
        name="attend_back",
    )(slot_of, *args, *grads)


def in_vmem(kernel, name, outs, scratch, *args):
    return pl.pallas_call(
        kernel,
        out_shape=[jax.ShapeDtypeStruct(shape, dtype) for shape, dtype in outs],
        in_specs=[pl.BlockSpec(memory_space=pltpu.VMEM)] * len(args),
        out_specs=[pl.BlockSpec(memory_space=pltpu.VMEM)] * len(outs),
        scratch_shapes=[pltpu.VMEM(shape, dtype) for shape, dtype in scratch],
        compiler_params=pltpu.CompilerParams(vmem_limit_bytes=62 << 20),
        cost_estimate=pl.CostEstimate(flops=0, bytes_accessed=1 << 10, transcendentals=0),
        name=name,
    )(*args)


def norm_forward(x):
    inverse = lax.rsqrt(jnp.mean(x * x, axis=-1, keepdims=True) + EPS_NORM)
    return (x * inverse, inverse)


def norm_backward(grad, normed, inverse, gain):
    scaled = grad * gain
    dgain = jnp.sum(grad * normed, axis=0)
    dx = inverse * (scaled - normed * jnp.mean(scaled * normed, axis=-1, keepdims=True))
    return (dx, dgain)


def body(
    tokens,
    targets,
    pair_order,
    lengths,
    loss_mask,
    start_pos,
    owner_map,
    block_master,
    left_stat,
    right_stat,
    left_root,
    right_root,
    table_master,
    table_moment,
    table_second,
    gain_master,
    gain_moment,
    gain_second,
):
    dp = lax.axis_index("dp")
    mp = lax.axis_index("mp")
    n_mp = lax.axis_size("mp")
    n_dp = lax.axis_size("dp")
    fused = (n_mp, n_dp) == (8, 4)
    items, length = tokens.shape
    context = length - ANS
    n_ans = ANS // n_mp
    n_ctx = context // n_mp
    rows_ans = items * n_ans
    rows_own = items * (n_ans + n_ctx)
    width = D // n_mp
    units = FF // n_mp
    heads = width // HD
    vocab_part, cols = table_master.shape
    sub = vocab_part // n_dp
    perm = owner_map[0]
    who = mp ^ jnp.array(cube_order(n_mp), jnp.int32)
    near = dp ^ jnp.arange(n_dp, dtype=jnp.int32)

    slots = lax.all_gather(block_master[0].astype(BF16), "dp", axis=0, tiled=True)
    gains = line_gather(gain_master.astype(BF16))
    wide = jnp.zeros((3, D), BF16)
    for o in range(n_dp):
        wide = lax.dynamic_update_slice(wide, gains[o], (0, near[o] * cols))
    gains = wide.astype(F32)
    table_low = table_master.astype(BF16)

    packed = jnp.concatenate([tokens, targets, loss_mask, lengths[:, None]], axis=1)
    packed = jnp.stack(line_gather(packed))
    all_tokens = packed[:, :, :length]
    all_targets = packed[:, :, length : length + ANS]
    all_mask = packed[:, :, length + ANS : length + 2 * ANS]
    all_lengths = packed[:, :, -1]
    column = jnp.arange(ANS)
    weights = jnp.where(
        column == 0,
        1.0,
        jnp.where(column < all_lengths[..., None], all_mask.astype(F32), 0.0),
    )
    pairs_all = pair_order.shape[0] // 2
    pairs = (pair_order // 2).reshape(n_dp, items)[near]
    member = (pairs[..., None] == jnp.arange(pairs_all)).astype(F32)
    counts = jnp.einsum("oip,oi->p", member, jnp.sum(weights, axis=-1))
    scale = weights / (jnp.sum(member * counts, axis=-1)[..., None] * pairs_all)

    def by_owner(x):
        split = x.reshape(n_dp, items, n_mp, n_ans)[:, :, who]
        return split.transpose(2, 0, 1, 3)

    row_scale = by_owner(scale).reshape(-1)
    row_target = by_owner(all_targets).reshape(-1)
    tok_ans = all_tokens[:, :, context:].reshape(n_dp, items, n_mp, n_ans)[:, :, who]
    tok_ctx = all_tokens[:, :, :context].reshape(n_dp, items, n_mp, n_ctx)[:, :, who]
    tok = jnp.concatenate(
        [
            tok_ans.transpose(2, 0, 1, 3).reshape(n_mp, n_dp, -1),
            tok_ctx.transpose(2, 0, 1, 3).reshape(n_mp, n_dp, -1),
        ],
        axis=2,
    )

    shapes = mat_shapes(n_mp)
    number = perm.shape[0]
    slot_of = jnp.zeros_like(perm).at[perm].set(jnp.arange(number, dtype=jnp.int32))

    local = tok - mp * vocab_part
    valid = (local >= 0) & (local < vocab_part)
    safe = jnp.clip(local, 0, vocab_part - 1)
    looked = jnp.where(valid[..., None], jnp.take(table_low, safe, axis=0), 0)
    own_cols = cube_scatter(looked).astype(BF16)
    pieces = line_exchange([own_cols[o] for o in range(n_dp)])
    x0 = jnp.zeros((rows_own, D), BF16)
    for o in range(n_dp):
        x0 = lax.dynamic_update_slice(x0, pieces[o], (0, near[o] * cols))
    x0 = x0.astype(F32)
    normed1, inverse1 = norm_forward(x0)
    h1 = cube_gather((normed1 * gains[0]).astype(BF16))
    h1_all = h1.reshape(-1, D)

    wqkv, wout, wgate, wdown = place_tiles(slot_of, slots, shapes)

    soon = sub - 256 if fused else sub
    by_part = table_low.reshape(n_dp, sub, cols)
    table_late = after(by_part[:, :soon], slots, h1)
    head_parts = lax.all_to_all(table_late, "dp", 0, 0)

    half = HD // 2
    freq = ROPE_BASE ** (-jnp.arange(half).astype(F32) * 2.0 / HD)
    t_ans = context + who[:, None] * n_ans + jnp.arange(n_ans)
    t_ctx = who[:, None] * n_ctx + jnp.arange(n_ctx)

    def angles(t):
        place = (start_pos[None, :, None] + t[:, None, :]).astype(F32)
        angle = place.reshape(n_mp, -1)[..., None] * freq
        return jnp.cos(angle), jnp.sin(angle)

    cosine, sine = (jnp.concatenate(pair, axis=1) for pair in zip(angles(t_ans), angles(t_ctx)))
    cosine = jnp.concatenate([cosine] * 4, axis=-1)
    sine = jnp.concatenate([-sine, sine] * 2, axis=-1)
    t_query = t_ans.reshape(-1)
    place = (t_query[:, None], t_query[None, :])

    ans_shape = ((n_mp, rows_ans, width), BF16)
    key_shape = ((n_mp, rows_own, width), BF16)
    o_rows, query, key, value = in_vmem(
        functools.partial(attend_kernel, items),
        "attend",
        (ans_shape, ans_shape, key_shape, key_shape),
        (((n_mp, rows_own, 3 * width), F32),),
        *(h1, wqkv, cosine, sine, *place),
    )
    own = ((rows_ans, D), F32)
    gain_row = ((1, D), F32)
    plane = ((n_mp, rows_ans, D), BF16)
    if fused:
        x1, h2 = exchange(
            attend_sum_kernel, "attend_sum", 1, n_dp, rows_ans, (own, plane),
            *(o_rows, wout, x0[:rows_ans], gains[1:2]),
        )
    else:
        parts = dot("tw,wd->td", o_rows.reshape(-1, width), wout).astype(BF16)
        x1 = x0[:rows_ans] + cube_scatter(parts.reshape(n_mp, rows_ans, D))
        h2 = cube_gather((norm_forward(x1)[0] * gains[1]).astype(BF16))
    o_rows = o_rows.reshape(-1, width)

    if fused:
        flat_units = n_mp * rows_ans
        x2, gate_up, hidden, final = exchange(
            units_sum_kernel, "units_sum", 2, n_dp, rows_ans,
            (
                own,
                ((flat_units, 2 * units), F32),
                ((flat_units, units), BF16),
                ((rows_ans, D), BF16),
            ),
            *(h2, wgate, wdown, x1, gains[2:3]),
        )
        h2 = h2.reshape(-1, D)
    else:
        h2 = h2.reshape(-1, D)
        gate_up = dot("td,df->tf", h2, wgate)
        gate, upward = gate_up[:, :units], gate_up[:, units:]
        hidden = (jax.nn.silu(gate) * upward).astype(BF16)
        parts = dot("tf,fd->td", hidden, wdown).astype(BF16)
        x2 = x1 + cube_scatter(parts.reshape(n_mp, rows_ans, D))

    def by_line(x):
        return x.reshape(n_mp, n_dp, rows_ans).transpose(1, 0, 2).reshape(n_dp, -1, 1)

    first = mp * vocab_part + dp * sub
    if fused:
        final, dlogits, head_parts, seen = head_call(
            n_dp,
            *(final, head_parts, by_part[:, soon:]),
            *(by_line(row_target - first), by_line(row_scale)),
        )
        lse, picked = seen[0, 0], seen[1, 0]
        dlogits = dlogits.reshape(-1, sub)
        final = final.reshape(-1, D)
    else:
        head = jnp.concatenate([head_parts[a] for a in range(n_dp)], axis=1)
        final = (norm_forward(x2)[0] * gains[2]).astype(BF16)
        final = cube_gather(jnp.stack(line_gather(final)).reshape(-1, D))
        final = final.reshape(-1, D)
        logits = dot("rd,vd->rv", final, head)
        hit = jnp.arange(sub, dtype=jnp.int32)[None, :] == (row_target - first)[:, None]
        top = jnp.max(logits, axis=1)
        total = jnp.sum(jnp.exp(logits - top[:, None]), axis=1)
        picked = jnp.sum(jnp.where(hit, logits, 0.0), axis=1)
        top, total, picked = stats_everywhere(jnp.stack([top, total, picked]), rows_ans)
        lse = top + jnp.log(total)
        dlogits = (
            row_scale[:, None] * (jnp.exp(logits - lse[:, None]) - hit.astype(F32))
        ).astype(BF16)
    loss_own = jnp.sum(row_scale[:rows_ans] * (lse - picked)[:rows_ans]) * pairs_all

    if fused:
        cut = (256, 128)
        total = n_dp * rows_ans
        dx2, dgain3, down_in, early_grad, head_grad = exchange(
            functools.partial(head_back_kernel, n_dp, cut), "head_sum", 3, n_dp, total,
            (
                own,
                gain_row,
                plane,
                ((n_dp, sum(cut), cols), BF16),
                ((n_dp, sub - sum(cut), cols), BF16),
            ),
            *(dlogits.reshape(n_mp, -1, sub), head_parts, x2, gains[2:3]),
            final.reshape(n_mp, -1, D),
            more=(
                (total, D),
                (n_dp - 1, rows_ans, D),
                (n_mp, total, D),
                (n_dp - 1, sum(cut), cols),
            ),
            sems=13 + 10 * n_dp,
            far=1,
        )
        dgain3 = dgain3[0]
    else:
        parts = dot("rv,vd->rd", dlogits, head).astype(BF16)
        mine = cube_scatter(parts.reshape(n_mp, n_dp * rows_ans, D)).astype(BF16)
        mine = line_exchange(list(mine.reshape(n_dp, rows_ans, D)))
        dfinal = sum(piece.astype(F32) for piece in mine)
        dx2, dgain3 = norm_backward(dfinal, *norm_forward(x2), gains[2])
        down_in = cube_gather(dx2.astype(BF16))
        head_grad = jnp.stack(
            [
                dot("rv,rd->vd", dlogits, final[:, a * cols : (a + 1) * cols]).astype(BF16)
                for a in range(n_dp)
            ]
        )
    table_grad = lax.all_to_all(head_grad, "dp", 0, 0)
    if fused:
        dx1, dgain2, dgate_up, out_in, grad_down, grad_gate = exchange(
            gate_sum_kernel, "gate_sum", 4, n_dp, rows_ans,
            (
                own,
                gain_row,
                (gate_up.shape, BF16),
                plane,
                (wdown.shape, BF16),
                (wgate.shape, BF16),
            ),
            *(down_in, wdown, wgate, gate_up, x1, gains[1:2], dx2),
            *(h2.reshape(n_mp, rows_ans, D), hidden),
            more=((n_mp, rows_ans, D), hidden.shape, wdown.shape, wgate.shape),
            far=2,
            stored=2,
        )
        dgain2 = dgain2[0]
        down_in = down_in.reshape(-1, D)
    else:
        down_in = down_in.reshape(-1, D)
        dhidden = dot("td,fd->tf", down_in, wdown)
        sigma = jax.nn.sigmoid(gate)
        dgate = dhidden * upward * sigma * (1.0 + gate * (1.0 - sigma))
        dgate_up = jnp.concatenate([dgate, dhidden * gate * sigma], axis=-1).astype(BF16)
        parts = dot("tf,df->td", dgate_up, wgate).astype(BF16)
        dnormed2 = cube_scatter(parts.reshape(n_mp, rows_ans, D))
        dx_mlp, dgain2 = norm_backward(dnormed2, *norm_forward(x1), gains[1])
        dx1 = dx2 + dx_mlp
        out_in = cube_gather(dx1.astype(BF16))
        grad_down = dot("tf,td->fd", hidden, down_in).astype(BF16)
        grad_gate = dot("td,tf->df", h2, dgate_up).astype(BF16)
    dqkv, grad_out, slots = attend_back(
        items, shapes, slot_of, (grad_gate, grad_down), block_master.shape[-1],
        *(query, key, value, out_in, wout, o_rows, cosine, sine, *place),
    )
    dqkv = dqkv.reshape(-1, 3 * width)

    if fused:
        rows_over, dgain1, grad_qkv = exchange(
            functools.partial(input_back_kernel, n_dp), "input_sum", 7, n_dp, rows_own,
            (((n_dp, rows_own, cols), BF16), gain_row, (wqkv.shape, BF16)),
            *(dqkv.reshape(n_mp, rows_own, -1), wqkv, x0, gains[:1], dx1, h1),
            more=((rows_own, D), (n_mp, rows_own, D)),
            sems=(7 + n_dp - 1) * (rows_own // rows_ans),
            far=1,
        )
        dgain1 = dgain1[0]
    else:
        dh1 = dot("te,de->td", dqkv, wqkv).astype(BF16).reshape(n_mp, rows_own, D)
        grad_qkv = dot("td,te->de", h1_all, dqkv).astype(BF16)
        dx0, dgain1 = norm_backward(cube_scatter(dh1), *norm_forward(x0), gains[0])
        dx0 = jnp.concatenate([dx0[:rows_ans] + dx1, dx0[rows_ans:]]).astype(BF16)
        parts = [lax.dynamic_slice_in_dim(dx0, near[o] * cols, cols, 1) for o in range(n_dp)]
        rows_over = jnp.stack(line_exchange(parts))

    slots = collect_tiles(slot_of, (grad_qkv, grad_out), shapes, (0, 1), (slots,))
    slots = after(slots, table_grad, rows_over)
    own_slots = lax.psum_scatter(slots, "dp", scatter_dimension=0, tiled=True)

    if fused:
        table_grad = jnp.concatenate([early_grad, table_grad], axis=1)
    rows_back = cube_gather(rows_over.reshape(-1, cols)).reshape(safe.shape + (cols,))
    picked_rows = jnp.where(valid[..., None], rows_back, 0).astype(F32)
    own_table = table_grad.reshape(vocab_part, cols).astype(F32).at[safe.reshape(-1)].add(picked_rows.reshape(-1, cols))

    gain_grad = jnp.stack([dgain1, dgain2, dgain3])
    gain_total = everywhere(gain_grad, jnp.add)
    own_gain = lax.dynamic_slice_in_dim(gain_total, dp * cols, cols, 1)
    first_mp = (mp == 0).astype(F32)
    squares = jnp.sum(own_table * own_table) + first_mp * jnp.sum(own_gain * own_gain)
    if fused:
        more = jnp.zeros((2, 8, 128), F32).at[:, 0, 0].set(jnp.stack([squares, loss_own]))
        squares_all, loss_total = jnp.sum(total_exchange(own_slots, more, n_dp), axis=(1, 2))
    else:
        squares = squares + jnp.sum(jnp.square(own_slots.astype(F32)))
        more = everywhere(jnp.stack([squares, loss_own])[None], jnp.add)[0]
        squares_all, loss_total = more
    norm = jnp.sqrt(squares_all)
    factor = CLIP_NORM / jnp.maximum(norm, CLIP_NORM)
    roots = (left_stat[0], right_stat[0], left_root[0], right_root[0])
    block_new, block_copy, grad_slots, left_new, right_new, *table_step = owner_step(
        factor.reshape(1, 1),
        (own_slots, block_master[0], *roots),
        (own_table, table_master, table_moment, table_second),
    )
    table_new, table_copy, table_moment_new, table_second_new = table_step
    gain_new, gain_moment_new, gain_second_new = adam(
        gain_master, gain_moment, gain_second, factor * own_gain, LR_GAIN, 0.0
    )
    return (
        loss_total,
        norm,
        block_new[None],
        block_copy[None],
        grad_slots[None],
        left_new[None],
        right_new[None],
        table_new,
        table_copy,
        table_moment_new,
        table_second_new,
        gain_new,
        gain_moment_new,
        gain_second_new,
    )


def solution(mesh):
    in_specs = (
        P("dp", None),
        P("dp", None),
        P(),
        P("dp"),
        P("dp", None),
        P("dp"),
        P("mp", None),
        P("mp", "dp", None, None),
        P("mp", "dp", None, None),
        P("mp", "dp", None, None),
        P("mp", "dp", None, None),
        P("mp", "dp", None, None),
        P("mp", "dp"),
        P("mp", "dp"),
        P("mp", "dp"),
        P(None, "dp"),
        P(None, "dp"),
        P(None, "dp"),
    )
    out_specs = (
        P(),
        P(),
        P("mp", "dp", None, None),
        P("mp", "dp", None, None),
        P("mp", "dp", None, None),
        P("mp", "dp", None, None),
        P("mp", "dp", None, None),
        P("mp", "dp"),
        P("mp", "dp"),
        P("mp", "dp"),
        P("mp", "dp"),
        P(None, "dp"),
        P(None, "dp"),
        P(None, "dp"),
    )
    return jax.shard_map(body, mesh=mesh, in_specs=in_specs, out_specs=out_specs, check_vma=False)
```
